32 devices in a mesh: dp: 8 (over z, y), seq: 4 (over x, core).
Axes of the slice: x: 2, y: 2, z: 4, core: 2. Of those that a mesh axis runs over, the one named last changes fastest.
Arguments:
- tokens: bfloat16 [8, 2048, 1024], P('dp', 'seq'), may hold values from -6 to 6
- positions: int32 [3, 8, 2048], P(None, 'dp', 'seq'), may hold values from 0 to 15, as said below
- adapter_index: int32 [8, 1], P('dp'), may hold values from 0 to 7
- qkv_weight: bfloat16 [1024, 3072], P('dp', 'seq'), may hold values from -0.1875 to 0.1875
- proj_weight: bfloat16 [1024, 1024], P('dp', 'seq'), may hold values from -0.75 to 0.75
- fc1_weight: bfloat16 [1024, 4096], P('dp', 'seq'), may hold values from -0.1875 to 0.1875
- fc2_weight: bfloat16 [4096, 1024], P('dp', 'seq'), may hold values from -0.09375 to 0.09375
- vectors: bfloat16 [9, 1024], P(None, 'seq')
- fc1_bias: bfloat16 [4096], P('seq'), may hold values from -3 to 3
- adapter_down: bfloat16 [8, 16, 7168], P(None, 'dp', 'seq'), may hold values from -0.1875 to 0.1875
- adapter_up: bfloat16 [8, 16, 9216], P(None, 'dp', 'seq'), may hold values from -1.5 to 1.5
- cotangent: bfloat16 [8, 2048, 1024], P('dp', 'seq'), may hold values from -6 to 6
Outputs:
- output: bfloat16 [8, 2048, 1024], P('dp', 'seq')
- input_grad: bfloat16 [8, 2048, 1024], P('dp', 'seq')
- down_grad: float32 [8, 16, 7168], P(None, 'dp', 'seq')
- up_grad: float32 [8, 16, 9216], P(None, 'dp', 'seq')
The draws below stay inside these ranges and needn't reach their ends.
Inputs may be any that keep to these rules, and one draw needn't show every extreme that they name: `adapter_index`: every adapter is used by at least one clip. `positions`: each clip's tokens sit on 2048 distinct cells of a grid of 16 frames by 16 rows by 16 columns, in raster order (frame, then row, then column); every clip holds the last cell of the grid.
All inputs are finite; a program needn't handle non-finite values.
Results may differ from the reference program's by a relative error of at most 0.019.
Values may be sent and summed in bfloat16 or wider, within the bound.
A program may use at most 320 MiB of HBM per device.

```python
import math
import jax
import jax.numpy as jnp
from jax import lax

D = 1024
HEADS = 16
HD = 64
FF = 4096
R = 16
NA = 8
FRAMES = 16
GRID = 16
LENGTH = 2048
CLIPS = 8


def draw_positions(key, part):
    cell_count = FRAMES * GRID * GRID

    def one_clip_draw(clip_key):
        shuffled = jax.random.permutation(clip_key, cell_count)
        ranking = jnp.where(jnp.arange(cell_count) == cell_count - 1, -1, shuffled)
        picked = jnp.sort(jnp.argsort(ranking, stable=True)[:LENGTH])
        return jnp.stack([picked // (GRID * GRID), picked // GRID % GRID, picked % GRID])
    clip_keys = jax.random.split(jax.random.fold_in(key, 11), CLIPS)
    drawn = jax.vmap(one_clip_draw)(clip_keys)
    return jnp.transpose(drawn, (1, 0, 2)).astype(jnp.int32)


def draw_vectors(key, part):
    inner_key = jax.random.fold_in(key, 23)
    random_part = jnp.clip(jax.random.normal(inner_key, (9, D), jnp.float32), -2.5, 2.5)
    row_ids = jnp.arange(9)
    is_gain = (row_ids == 0) | (row_ids == 2)
    return jnp.where(is_gain[:, None], 1.0 + 0.3 * random_part, 0.5 * random_part).astype(jnp.bfloat16)


def levels(stream_key, dims, shards, least, top_value):
    level = 1.0
    for axis_at, blocks in shards:
        steps = jax.random.uniform(jax.random.fold_in(jax.random.fold_in(stream_key, 6), axis_at), (blocks,), jnp.float32, least / len(shards), top_value / len(shards))
        level = level * jnp.repeat(jnp.exp(steps), dims[axis_at] // blocks).reshape((-1,) + (1,) * (len(dims) - 1 - axis_at))
    return level


def different_ones(stream_key, rows, number_of, top, lift):
    order = jax.random.permutation(jax.random.fold_in(stream_key, 1), number_of)
    boost = order
    for power in range(3):
        boost = boost * boost // number_of
    boost = boost * lift // number_of
    lots = jax.random.randint(jax.random.fold_in(stream_key, 2), (rows, number_of), 0, 4096) + boost
    sure = jax.random.permutation(jax.random.fold_in(stream_key, 3), rows)[jnp.arange(number_of) % rows]
    lots = jnp.where(jnp.arange(rows)[:, None] == sure[None, :], 1 << 14, lots)
    merit = lots * number_of + jnp.arange(number_of)
    return lax.top_k(merit.astype(jnp.int32), top)[1].astype(jnp.int32)


def gaussian(key, extent, scale, most, cuts=(), held_as=jnp.bfloat16):
    values = jax.random.normal(key, extent, jnp.float32) * scale
    if len(cuts) > 0:
        values = levels(key, extent, cuts, -0.22, 0.18) * values
    return jnp.clip(values, min=-most, max=most).astype(held_as)


def setup_inputs(seed: int = 0) -> dict:
    seeds = jax.random.split(jax.random.key(seed), 13)
    tokens = gaussian(seeds[0], (CLIPS, LENGTH, D), 1.0, 6.0, ((0, 8), (1, 4)))
    positions = draw_positions(jax.random.fold_in(seeds[12], 71), 0)
    adapter_index = different_ones(seeds[2], CLIPS, NA, 1, 0)
    qkv_weight = gaussian(seeds[3], (D, 3 * D), D ** -0.5, 0.1875, ((0, 8), (1, 4)))
    proj_weight = gaussian(seeds[4], (D, D), (D // 16) ** -0.5, 0.75, ((0, 8), (1, 4)))
    fc1_weight = gaussian(seeds[5], (D, FF), D ** -0.5, 0.1875, ((0, 8), (1, 4)))
    fc2_weight = gaussian(seeds[6], (FF, D), FF ** -0.5, 0.09375, ((0, 8), (1, 4)))
    vectors = draw_vectors(jax.random.fold_in(seeds[12], 71), 0)
    fc1_bias = gaussian(seeds[8], (FF,), 0.5, 3.0, ((0, 4),))
    adapter_down = gaussian(seeds[9], (NA, R, 3 * D + FF), D ** -0.5, 0.1875, ((1, 8), (2, 4)))
    adapter_up = gaussian(seeds[10], (NA, R, 5 * D + FF), R ** -0.5, 1.5, ((1, 8), (2, 4)))
    cotangent = gaussian(seeds[11], (CLIPS, LENGTH, D), 1.0, 6.0, ((0, 8), (1, 4)))
    return {"tokens": tokens, "positions": positions, "adapter_index": adapter_index, "qkv_weight": qkv_weight, "proj_weight": proj_weight, "fc1_weight": fc1_weight, "fc2_weight": fc2_weight, "vectors": vectors, "fc1_bias": fc1_bias, "adapter_down": adapter_down, "adapter_up": adapter_up, "cotangent": cotangent}


@jax.custom_vjp
def low(v):
    return lax.optimization_barrier(v.astype(jnp.bfloat16)).astype(jnp.float32)

@jax.custom_vjp
def low_back(v):
    return v

def low_keep(v):
    return (low(v), None)

def low_pass(kept, grad):
    return (grad,)

def back_keep(v):
    return (v, None)

def back_low(kept, grad):
    return (low(grad),)
low.defvjp(low_keep, low_pass)
low_back.defvjp(back_keep, back_low)
best_precision = lax.Precision.HIGHEST

def layer_norm(values, gain_row, shift_row):
    centre = values - lax.optimization_barrier(jnp.mean(values, axis=-1, keepdims=True))
    spread = lax.optimization_barrier(jnp.mean(centre * centre, axis=-1, keepdims=True))
    return centre * lax.rsqrt(spread + 1e-06) * gain_row + shift_row

def rotate(values, places, direction):
    rot_span = 2 * (values.shape[-1] // 3 // 2)
    half_span = rot_span // 2
    inverse_freq = 10000.0 ** (-jnp.arange(half_span, dtype=jnp.float32) / half_span)
    pieces = []
    for axis_id in range(3):
        segment = values[..., axis_id * rot_span:(axis_id + 1) * rot_span]
        angles = places[axis_id].astype(jnp.float32)[..., None, None] * inverse_freq
        cosine = jnp.cos(angles)
        sine_wave = direction * jnp.sin(angles)
        lower_part = segment[..., :half_span]
        upper_part = segment[..., half_span:]
        pieces.append(lower_part * cosine - upper_part * sine_wave)
        pieces.append(lower_part * sine_wave + upper_part * cosine)
    pieces.append(values[..., 3 * rot_span:])
    return jnp.concatenate(pieces, axis=-1)

def exact_gelu(values):
    return jax.nn.gelu(values, approximate=False)

def adapted(inputs, weight, shift_row, down_part, up_part):
    reduced = low_back(low(jnp.dot(inputs, down_part.T, precision=best_precision)))
    base = jnp.dot(inputs, weight, precision=best_precision) + shift_row
    return base + jnp.dot(reduced, up_part, precision=best_precision)

def attend(queries, keys_all, values_all):
    length = queries.shape[0]
    block_len = math.gcd(length, 512)
    score_scale = HD ** (-0.5)

    def one_block(query_block):
        scores = low_back(jnp.einsum('qhd,khd->hqk', query_block, keys_all, precision=best_precision) * score_scale)
        top_score = lax.optimization_barrier(jnp.max(scores, axis=-1, keepdims=True))
        weights = jnp.exp(scores - top_score)
        probabilities = low(weights / lax.optimization_barrier(jnp.sum(weights, axis=-1, keepdims=True)))
        return jnp.einsum('hqk,khd->qhd', probabilities, values_all, precision=best_precision)
    blocks = lax.map(jax.checkpoint(one_block), queries.reshape(length // block_len, block_len, HEADS, HD))
    return blocks.reshape(length, HEADS * HD)

def clip_forward(inputs, places, choose_row, down_all, up_all, frozen):
    qkv_weight, proj_weight, fc1_weight, fc2_weight, vectors, fc1_bias = frozen
    length = inputs.shape[0]
    down_sel = jnp.einsum('a,ari->ri', choose_row, down_all, precision=best_precision)
    up_sel = jnp.einsum('a,aro->ro', choose_row, up_all, precision=best_precision)
    normed_one = low(layer_norm(inputs, vectors[0], vectors[1]))
    mixed_qkv = low_back(adapted(normed_one, qkv_weight, vectors[4:7].reshape(3 * D), down_sel[:, :D], up_sel[:, :3 * D]))
    queries = low(rotate(mixed_qkv[:, :D].reshape(length, HEADS, HD), places, 1.0))
    keys_all = low(rotate(mixed_qkv[:, D:2 * D].reshape(length, HEADS, HD), places, 1.0))
    values_all = low(mixed_qkv[:, 2 * D:].reshape(length, HEADS, HD))
    attended = low_back(low(attend(queries, keys_all, values_all)))
    projected = low_back(adapted(attended, proj_weight, vectors[7], down_sel[:, D:2 * D], up_sel[:, 3 * D:4 * D]))
    residual = inputs + projected
    normed_two = low(layer_norm(residual, vectors[2], vectors[3]))
    hidden = low_back(adapted(normed_two, fc1_weight, fc1_bias, down_sel[:, 2 * D:3 * D], up_sel[:, 4 * D:4 * D + FF]))
    activated = low(exact_gelu(hidden))
    branch = low_back(adapted(activated, fc2_weight, vectors[8], down_sel[:, 3 * D:], up_sel[:, 4 * D + FF:]))
    return residual + branch

def reference(tokens, positions, adapter_index, qkv_weight, proj_weight, fc1_weight, fc2_weight, vectors, fc1_bias, adapter_down, adapter_up, cotangent):
    frozen = (qkv_weight.astype(jnp.float32), proj_weight.astype(jnp.float32), fc1_weight.astype(jnp.float32), fc2_weight.astype(jnp.float32), vectors.astype(jnp.float32), fc1_bias.astype(jnp.float32))
    down_all = adapter_down.astype(jnp.float32)
    up_all = adapter_up.astype(jnp.float32)
    choose = (adapter_index == jnp.arange(NA, dtype=jnp.int32)[None, :]).astype(jnp.float32)

    def one_clip(totals, inputs):
        clip_tokens, places, choose_row, clip_cotangent = inputs

        def forward(clip_in, down_in, up_in):
            return clip_forward(clip_in, places, choose_row, down_in, up_in, frozen)
        result, pullback = jax.vjp(forward, clip_tokens.astype(jnp.float32), down_all, up_all)
        grad_in, grad_down, grad_up = pullback(clip_cotangent.astype(jnp.float32))
        return ((totals[0] + grad_down, totals[1] + grad_up), (result.astype(jnp.bfloat16), grad_in.astype(jnp.bfloat16)))
    start_totals = (jnp.zeros(down_all.shape, jnp.float32), jnp.zeros(up_all.shape, jnp.float32))
    totals, outputs = lax.scan(one_clip, start_totals, (tokens, jnp.transpose(positions, (1, 0, 2)), choose, cotangent))
    return (outputs[0], outputs[1], totals[0], totals[1])
```

```python
import functools
import math

import jax
import jax.numpy as jnp
from jax import lax
from jax.experimental import pallas as pl
from jax.experimental.pallas import tpu as pltpu
from jax.sharding import PartitionSpec as P

D = 1024
HEADS = 16
HD = 64
FF = 4096
NA = 8


def layer_norm(values, gain_row, shift_row):
    centre = values - jnp.mean(values, axis=-1, keepdims=True)
    spread = jnp.mean(centre * centre, axis=-1, keepdims=True)
    return centre * lax.rsqrt(spread + 1e-06) * gain_row + shift_row


def rotate(values, places, direction):
    rot_span = 2 * (values.shape[-1] // 3 // 2)
    half_span = rot_span // 2
    inverse_freq = 10000.0 ** (-jnp.arange(half_span, dtype=jnp.float32) / half_span)
    pieces = []
    for axis_id in range(3):
        segment = values[..., axis_id * rot_span : (axis_id + 1) * rot_span]
        angles = places[axis_id].astype(jnp.float32)[..., None, None] * inverse_freq
        cosine = jnp.cos(angles)
        sine_wave = direction * jnp.sin(angles)
        lower_part = segment[..., :half_span]
        upper_part = segment[..., half_span:]
        pieces.append(lower_part * cosine - upper_part * sine_wave)
        pieces.append(lower_part * sine_wave + upper_part * cosine)
    pieces.append(values[..., 3 * rot_span :])
    return jnp.concatenate(pieces, axis=-1)


def exact_gelu(values):
    return jax.nn.gelu(values, approximate=False)


def fetch_weight(weight):
    joined = lax.all_gather(weight, "seq", axis=1, tiled=True)
    return lax.all_gather(joined, "dp", axis=0, tiled=True)


def adapted(inputs, weight, shift_row, down_part, up_part):
    base = jnp.einsum("cti,io->cto", inputs, weight, preferred_element_type=jnp.float32)
    reduced = jnp.einsum(
        "cti,cri->ctr", inputs, down_part, preferred_element_type=jnp.float32
    ).astype(jnp.bfloat16)
    result = (
        base
        + shift_row
        + jnp.einsum("ctr,cro->cto", reduced, up_part, preferred_element_type=jnp.float32)
    )
    return (result, reduced)


def adapted_back(grad_out, inputs, weight, down_part, up_part, reduced):
    grad_in = jnp.einsum("cto,io->cti", grad_out, weight, preferred_element_type=jnp.float32)
    grad_reduced = jnp.einsum(
        "cto,cro->ctr", grad_out, up_part, preferred_element_type=jnp.float32
    ).astype(jnp.bfloat16)
    grad_in = grad_in + jnp.einsum(
        "ctr,cri->cti", grad_reduced, down_part, preferred_element_type=jnp.float32
    )
    grad_down = jnp.einsum("ctr,cti->cri", grad_reduced, inputs, preferred_element_type=jnp.float32)
    grad_up = jnp.einsum("ctr,cto->cro", reduced, grad_out, preferred_element_type=jnp.float32)
    return (grad_in, grad_down, grad_up)


def split_tokens(source, split_count):
    old_shape = source.shape
    shaped = source.reshape(
        (old_shape[0], split_count, old_shape[1] // split_count) + old_shape[2:]
    )
    return jnp.moveaxis(shaped, 1, 0)


def score_grads(
    query_block, key_block, value_block, grad_block, log_block, delta_block, score_scale
):
    scores = (
        jnp.einsum("cqhd,ckhd->chqk", query_block, key_block, preferred_element_type=jnp.float32)
        * score_scale
    )
    probabilities = jnp.exp(scores - log_block[..., None])
    grad_probs = jnp.einsum(
        "cqhd,ckhd->chqk", grad_block, value_block, preferred_element_type=jnp.float32
    )
    grad_scores = (probabilities * (grad_probs - delta_block[..., None])).astype(jnp.bfloat16)
    return (probabilities.astype(jnp.bfloat16), grad_scores)


def shards(
    tokens,
    positions,
    adapter_index,
    qkv_weight,
    proj_weight,
    fc1_weight,
    fc2_weight,
    vectors,
    fc1_bias,
    adapter_down,
    adapter_up,
    cotangent,
):
    clip_count, tok_count = (tokens.shape[0], tokens.shape[1])
    head_shape = (clip_count, tok_count, HEADS, HD)
    score_scale = HD ** (-0.5)
    small_parts = (
        lax.all_gather(adapter_down, "seq", axis=2, tiled=True),
        lax.all_gather(adapter_up, "seq", axis=2, tiled=True),
        lax.all_gather(vectors, "seq", axis=1, tiled=True),
        lax.all_gather(fc1_bias, "seq", axis=0, tiled=True),
    )
    down_all, up_all = (
        lax.all_gather(small_parts[0], "dp", axis=1, tiled=True),
        lax.all_gather(small_parts[1], "dp", axis=1, tiled=True),
    )
    vector_rows = small_parts[2].astype(jnp.float32)
    hidden_bias = small_parts[3].astype(jnp.float32)
    choose = (adapter_index == jnp.arange(NA, dtype=jnp.int32)[None, :]).astype(jnp.bfloat16)
    down_sel = jnp.einsum(
        "ca,ari->cri", choose, down_all, preferred_element_type=jnp.float32
    ).astype(jnp.bfloat16)
    up_sel = jnp.einsum("ca,aro->cro", choose, up_all, preferred_element_type=jnp.float32).astype(
        jnp.bfloat16
    )
    down_parts = (
        down_sel[:, :, :D],
        down_sel[:, :, D : 2 * D],
        down_sel[:, :, 2 * D : 3 * D],
        down_sel[:, :, 3 * D :],
    )
    up_parts = (
        up_sel[:, :, : 3 * D],
        up_sel[:, :, 3 * D : 4 * D],
        up_sel[:, :, 4 * D : 4 * D + FF],
        up_sel[:, :, 4 * D + FF :],
    )
    inputs = tokens.astype(jnp.float32)
    normed_one = layer_norm(inputs, vector_rows[0], vector_rows[1]).astype(jnp.bfloat16)
    weight_qkv = fetch_weight(qkv_weight)
    mixed_qkv, reduced_qkv = adapted(
        normed_one, weight_qkv, vector_rows[4:7].reshape(3 * D), down_parts[0], up_parts[0]
    )
    queries = rotate(mixed_qkv[..., :D].reshape(head_shape), positions, 1.0).astype(jnp.bfloat16)
    keys_local = rotate(mixed_qkv[..., D : 2 * D].reshape(head_shape), positions, 1.0).astype(
        jnp.bfloat16
    )
    values_local = mixed_qkv[..., 2 * D :].reshape(head_shape).astype(jnp.bfloat16)
    stat_shape = (clip_count, HEADS, tok_count)
    start_state = (
        jnp.full(stat_shape, -jnp.inf, jnp.float32),
        jnp.zeros(stat_shape, jnp.float32),
        jnp.zeros(stat_shape + (HD,), jnp.float32),
    )
    key_piece = lax.all_gather(keys_local, "seq", axis=1, tiled=True)
    value_piece = lax.all_gather(values_local, "seq", axis=1, tiled=True)
    split_count = key_piece.shape[1] // math.gcd(key_piece.shape[1], 256)

    def inner_step(running, block_pair):
        top_score, row_total, weighted = running
        key_block, value_block = block_pair
        scores = (
            jnp.einsum("cqhd,ckhd->chqk", queries, key_block, preferred_element_type=jnp.float32)
            * score_scale
        )
        new_top = jnp.maximum(top_score, jnp.max(scores, axis=-1))
        factor = jnp.exp(top_score - new_top)
        weights = jnp.exp(scores - new_top[..., None])
        row_total = row_total * factor + jnp.sum(weights, axis=-1)
        weighted = weighted * factor[..., None] + jnp.einsum(
            "chqk,ckhd->chqd",
            weights.astype(jnp.bfloat16),
            value_block,
            preferred_element_type=jnp.float32,
        )
        return ((new_top, row_total, weighted), None)

    result, unused = lax.scan(
        inner_step,
        start_state,
        (split_tokens(key_piece, split_count), split_tokens(value_piece, split_count)),
    )
    top_score, row_total, weighted = result
    log_total = top_score + jnp.log(row_total)
    heads_tok = jnp.swapaxes(weighted / row_total[..., None], 1, 2)
    attended = heads_tok.reshape(clip_count, tok_count, D).astype(jnp.bfloat16)
    weight_proj = fetch_weight(proj_weight)
    projected, reduced_proj = adapted(
        attended, weight_proj, vector_rows[7], down_parts[1], up_parts[1]
    )
    residual = inputs + projected
    normed_two = layer_norm(residual, vector_rows[2], vector_rows[3]).astype(jnp.bfloat16)
    weight_up = fetch_weight(fc1_weight)
    hidden, reduced_up = adapted(normed_two, weight_up, hidden_bias, down_parts[2], up_parts[2])
    activated = exact_gelu(hidden).astype(jnp.bfloat16)
    weight_down = fetch_weight(fc2_weight)
    branch, reduced_down = adapted(
        activated, weight_down, vector_rows[8], down_parts[3], up_parts[3]
    )
    output = (residual + branch).astype(jnp.bfloat16)
    weight_down = fetch_weight(fc2_weight)
    grad_act, gdown_four, gup_four = adapted_back(
        cotangent, activated, weight_down, down_parts[3], up_parts[3], reduced_down
    )
    unused, gelu_back = jax.vjp(exact_gelu, hidden)
    grad_hidden = gelu_back(grad_act)[0].astype(jnp.bfloat16)
    weight_up = fetch_weight(fc1_weight)
    grad_normed_two, gdown_three, gup_three = adapted_back(
        grad_hidden, normed_two, weight_up, down_parts[2], up_parts[2], reduced_up
    )

    def norm_two(values):
        return layer_norm(values, vector_rows[2], vector_rows[3])

    unused, norm_two_back = jax.vjp(norm_two, residual)
    grad_residual = cotangent.astype(jnp.float32) + norm_two_back(grad_normed_two)[0]
    weight_proj = fetch_weight(proj_weight)
    grad_attended, gdown_two, gup_two = adapted_back(
        grad_residual.astype(jnp.bfloat16),
        attended,
        weight_proj,
        down_parts[1],
        up_parts[1],
        reduced_proj,
    )
    grad_tok = grad_attended.astype(jnp.bfloat16).reshape(head_shape)
    delta_heads = jnp.swapaxes(jnp.sum(grad_tok.astype(jnp.float32) * heads_tok, axis=-1), 1, 2)
    whole_keys, whole_values = (
        lax.all_gather(keys_local, "seq", axis=1, tiled=True),
        lax.all_gather(values_local, "seq", axis=1, tiled=True),
    )
    block_count = whole_keys.shape[1] // math.gcd(whole_keys.shape[1], 256)
    key_blocks = split_tokens(whole_keys, block_count)
    value_blocks = split_tokens(whole_values, block_count)
    zero_heads = jnp.zeros(head_shape, jnp.float32)

    def back_step(grad_query, block_pair):
        key_block, value_block = block_pair
        probs_low, grad_scores = score_grads(
            queries, key_block, value_block, grad_tok, log_total, delta_heads, score_scale
        )
        grad_query = (
            grad_query
            + jnp.einsum(
                "chqk,ckhd->cqhd", grad_scores, key_block, preferred_element_type=jnp.float32
            )
            * score_scale
        )
        grad_key = (
            jnp.einsum("chqk,cqhd->ckhd", grad_scores, queries, preferred_element_type=jnp.float32)
            * score_scale
        )
        grad_value = jnp.einsum(
            "chqk,cqhd->ckhd", probs_low, grad_tok, preferred_element_type=jnp.float32
        )
        return (grad_query, jnp.concatenate([grad_key, grad_value], axis=-1))

    grad_query, key_terms = lax.scan(back_step, zero_heads, (key_blocks, value_blocks))
    key_terms = jnp.moveaxis(key_terms, 0, 1).reshape(
        clip_count, whole_keys.shape[1], HEADS, 2 * HD
    )
    summed = lax.psum_scatter(
        key_terms.astype(jnp.bfloat16), "seq", scatter_dimension=1, tiled=True
    ).astype(jnp.float32)
    grad_key = summed[..., :HD]
    grad_value = summed[..., HD:]
    grad_mixed = jnp.concatenate(
        [
            rotate(grad_query, positions, -1.0).reshape(clip_count, tok_count, D),
            rotate(grad_key, positions, -1.0).reshape(clip_count, tok_count, D),
            grad_value.reshape(clip_count, tok_count, D),
        ],
        axis=-1,
    ).astype(jnp.bfloat16)
    weight_qkv = fetch_weight(qkv_weight)
    grad_normed_one, gdown_one, gup_one = adapted_back(
        grad_mixed, normed_one, weight_qkv, down_parts[0], up_parts[0], reduced_qkv
    )

    def norm_one(values):
        return layer_norm(values, vector_rows[0], vector_rows[1])

    unused, norm_one_back = jax.vjp(norm_one, inputs)
    input_grad = (grad_residual + norm_one_back(grad_normed_one)[0]).astype(jnp.bfloat16)
    choose_wide = choose.astype(jnp.float32)
    clip_down = jnp.concatenate([gdown_one, gdown_two, gdown_three, gdown_four], axis=-1)
    clip_up = jnp.concatenate([gup_one, gup_two, gup_three, gup_four], axis=-1)
    down_term = jnp.einsum("ca,cri->ari", choose_wide, clip_down, precision=lax.Precision.HIGHEST)
    up_term = jnp.einsum("ca,cro->aro", choose_wide, clip_up, precision=lax.Precision.HIGHEST)
    down_grad, up_grad = (
        lax.psum_scatter(
            down_term.astype(jnp.bfloat16), "seq", scatter_dimension=2, tiled=True
        ).astype(jnp.float32),
        lax.psum_scatter(
            up_term.astype(jnp.bfloat16), "seq", scatter_dimension=2, tiled=True
        ).astype(jnp.float32),
    )
    down_grad, up_grad = (
        lax.psum_scatter(
            down_grad.astype(jnp.bfloat16), "dp", scatter_dimension=1, tiled=True
        ).astype(jnp.float32),
        lax.psum_scatter(
            up_grad.astype(jnp.bfloat16), "dp", scatter_dimension=1, tiled=True
        ).astype(jnp.float32),
    )
    return (output, input_grad, down_grad, up_grad)

MESH = pl.DeviceIdType.MESH
BF = jnp.bfloat16
F32 = jnp.float32
LOG2E = 1.4426950408889634
LN2 = 0.6931471805599453
VM = 60 * 1024 * 1024


def mm(a, b):
    return lax.dot_general(a, b, (((1,), (0,)), ((), ())), preferred_element_type=F32)


def mm_nt(a, b):
    return lax.dot_general(a, b, (((1,), (1,)), ((), ())), preferred_element_type=F32)


def mm_tn(a, b):
    return lax.dot_general(a, b, (((0,), (0,)), ((), ())), preferred_element_type=F32)


class Links:
    def __init__(self, ssem, rsem, lsem, nz):
        self.ssem, self.rsem, self.lsem = ssem, rsem, lsem
        self.nr, self.nl = 0, 0
        d, s = lax.axis_index("dp"), lax.axis_index("seq")
        self.d, self.s, self.nz = d, s, nz
        self.z, self.y, self.x, self.c = d // 2, lax.rem(d, 2), s // 2, lax.rem(s, 2)
        self.core = (d, s + 1 - 2 * self.c)
        self.xn = (d, s + 2 - 4 * self.x)
        self.diag = (d, 3 - s)
        self.yn = (d + 1 - 2 * self.y, s)
        self.up, self.down = (d + 2, s), (d - 2, s)
        self.tail = []

    def barrier(self):
        bar = pltpu.get_barrier_semaphore()
        for dev in (self.core, self.xn, self.yn):
            pl.semaphore_signal(bar, inc=1, device_id=dev, device_id_type=MESH)

        @pl.when(self.z < self.nz - 1)
        def _():
            pl.semaphore_signal(bar, inc=1, device_id=self.up, device_id_type=MESH)

        @pl.when(self.z > 0)
        def _():
            pl.semaphore_signal(bar, inc=1, device_id=self.down, device_id_type=MESH)

        edge = (self.z == 0).astype(jnp.int32) + (self.z == self.nz - 1).astype(jnp.int32)
        pl.semaphore_wait(bar, 5 - edge)

    def new(self, count=1):
        self.nr += count
        return self.nr - count

    def newl(self):
        self.nl += 1
        return self.nl - 1

    def remote(self, i, src, dst, dev):
        return pltpu.make_async_remote_copy(
            src_ref=src,
            dst_ref=dst,
            send_sem=self.ssem.at[i],
            recv_sem=self.rsem.at[i],
            device_id=dev,
            device_id_type=MESH,
        )

    def local(self, i, src, dst):
        return pltpu.make_async_copy(src, dst, self.lsem.at[i])


def guard(cond, body):
    if cond is None:
        body()
    else:
        pl.when(cond)(body)


class Part:
    def __init__(self, links, order, own, region, handover):
        self.k, self.order, self.own = links, order, own
        self.region, self.handover = region, handover
        k = links
        self.s_own = k.newl()
        self.s_up, self.s_dn = k.new(k.nz - 1), k.new(k.nz - 1)
        self.s_f, self.s_g1, self.s_g2 = k.new(), k.new(), k.new()
        self.pend = []
        self.steps = self.steps_zlast() if order == "xyz" else self.steps_zfirst()

    def reg(self, fi, gi, zs):
        return self.region(fi, zs, gi) if self.order == "zxy" else self.region(gi, zs, fi)

    def hand(self, cond, x, zs, y):
        k = self.k
        loc, rem = self.handover(x, zs, y)
        ls = [(k.newl(), a, b) for a, b in loc]
        rs = [(k.new(), a, b, w) for a, b, w in rem]

        def start():
            for i, a, b in ls:
                k.local(i, a, b).start()
            for i, a, b, _ in rs:
                k.remote(i, a, b, k.core).start()

        def finish():
            for i, a, b in ls:
                k.local(i, a, b).wait()
            for i, a, b, w in rs:
                k.remote(i, a, w, k.core).wait_recv()
                k.remote(i, a, b, k.core).wait_send()

        guard(cond, start)
        self.pend.append((cond, finish))

    def line(self, src, at, zs_hand, first_hand):
        k = self.k
        z, nz = k.z, k.nz
        can_up, can_dn = z < nz - 1, z > 0
        guard(can_up, lambda: k.remote(self.s_up, src, at(z), k.up).start())
        guard(can_dn, lambda: k.remote(self.s_dn, src, at(z), k.down).start())
        k.tail.append((can_up, lambda: k.remote(self.s_up, src, at(z), k.up).wait_send()))
        k.tail.append((can_dn, lambda: k.remote(self.s_dn, src, at(z), k.down).wait_send()))
        yield
        for r in range(nz - 1):
            for sem, here, origin, dev, can in (
                (self.s_up, z > r, z - 1 - r, k.up, can_up),
                (self.s_dn, z + r < nz - 1, z + 1 + r, k.down, can_dn),
            ):
                guard(
                    here,
                    lambda: k.remote(sem + r, at(origin), at(origin), dev).wait_recv(),
                )
                if r < nz - 2:
                    go = jnp.logical_and(here, can)
                    guard(
                        go, lambda: k.remote(sem + r + 1, at(origin), at(origin), dev).start()
                    )
                    k.tail.append(
                        (
                            go,
                            lambda sem=sem, r=r, origin=origin, dev=dev: k.remote(
                                sem + r + 1, at(origin), at(origin), dev
                            ).wait_send(),
                        )
                    )
                if zs_hand is not None:
                    zs_hand(here, origin)
            if r < nz - 2:
                yield

    def steps_zfirst(self):
        k = self.k
        f, g = (k.x, k.y) if self.order == "zxy" else (k.y, k.x)
        fd, gd = (k.xn, k.yn) if self.order == "zxy" else (k.yn, k.xn)
        xy = (lambda a, b: (a, b)) if self.order == "zxy" else (lambda a, b: (b, a))
        al = slice(None)

        def hand(a, b):
            x, y = xy(a, b)
            self.hand(None, x, al, y)

        own_copy = k.local(self.s_own, self.own, self.reg(f, g, k.z))
        own_copy.start()
        yield from self.line(self.own, lambda z: self.reg(f, g, z), None, None)
        own_copy.wait()
        mine, nf = self.reg(f, g, al), self.reg(1 - f, g, al)
        ng, nfg = self.reg(f, 1 - g, al), self.reg(1 - f, 1 - g, al)
        c_f = k.remote(self.s_f, mine, mine, fd)
        c_g1 = k.remote(self.s_g1, mine, mine, gd)
        c_g2 = k.remote(self.s_g2, nf, nf, gd)
        c_f.start()
        c_g1.start()
        hand(f, g)
        yield
        k.remote(self.s_f, mine, nf, fd).wait_recv()
        c_g2.start()
        hand(1 - f, g)
        yield
        k.remote(self.s_g1, mine, ng, gd).wait_recv()
        hand(f, 1 - g)
        yield
        k.remote(self.s_g2, nf, nfg, gd).wait_recv()
        hand(1 - f, 1 - g)
        for cp in (c_f, c_g1, c_g2):
            k.tail.append((None, cp.wait_send))
        yield

    def steps_zlast(self):
        k = self.k
        x, y, z = k.x, k.y, k.z
        al = slice(None)
        own_copy = k.local(self.s_own, self.own, self.region(x, z, y))
        own_copy.start()
        c_f = k.remote(self.s_f, self.own, self.region(x, z, y), k.xn)
        c_g1 = k.remote(self.s_g1, self.own, self.region(x, z, y), k.yn)
        c_f.start()
        c_g1.start()
        yield
        k.remote(self.s_f, self.own, self.region(1 - x, z, y), k.xn).wait_recv()
        c_g2 = k.remote(self.s_g2, self.region(1 - x, z, y), self.region(1 - x, z, y), k.yn)
        c_g2.start()
        yield
        k.remote(self.s_g1, self.own, self.region(x, z, 1 - y), k.yn).wait_recv()
        k.remote(
            self.s_g2, self.region(1 - x, z, y), self.region(1 - x, z, 1 - y), k.yn
        ).wait_recv()
        own_copy.wait()
        for cp in (c_f, c_g1, c_g2):
            k.tail.append((None, cp.wait_send))
        self.hand(None, al, z, al)
        yield from self.line(
            self.region(al, z, al),
            lambda o: self.region(al, o, al),
            lambda here, o: self.hand(here, al, o, al),
            None,
        )
        yield

    def finish(self):
        for cond, body in self.pend:
            guard(cond, body)


def wide_parts(links, shard, buf, cuts):
    c = links.c
    parts = []
    for r0, n, order in cuts:
        rows = pl.ds(r0, n)

        def region(x, z, y, rows=rows):
            return buf.at[x, c, z, y, rows]

        def handover(x, z, y, rows=rows):
            at = buf.at[x, c, z, y, rows]
            return [], [(at, at, buf.at[x, 1 - c, z, y, rows])]

        parts.append(Part(links, order, shard.at[rows], region, handover))
    return parts


def qkv_parts(links, shard, lane, buf, cuts):
    c = links.c
    parts = []
    for r0, n, order in cuts:
        rows = pl.ds(r0, n)

        def region(x, z, y, rows=rows):
            return lane.at[x, z, y, rows]

        def handover(x, z, y, rows=rows):
            loc, rem = [], []
            for xx in (0, 1) if isinstance(x, slice) else (x,):
                for col, role in ((0, 3 * xx + c), (512, 3 * xx + c + 1)):
                    loc.append((lane.at[xx, z, y, rows, pl.ds(col, 256)], buf.at[role, z, y, rows]))
                rem.append(
                    (
                        lane.at[xx, z, y, rows, pl.ds(256, 256)],
                        buf.at[3 * xx + 2 * c, z, y, rows],
                        buf.at[3 * xx + 2 - 2 * c, z, y, rows],
                    )
                )
            return loc, rem

        parts.append(Part(links, order, shard.at[rows], region, handover))
    return parts


def wavefront(steps):
    steps = list(steps)
    live = []
    while steps or live:
        if steps:
            live.append(steps.pop(0))
        for gen in list(live):
            try:
                next(gen)
            except StopIteration:
                live.remove(gen)


def gather_kernel(nz, tok, qkv, proj, fc1, fc2, tok4, lane, wq, wp, w1, w2, ssem, rsem, lsem):
    k = Links(ssem, rsem, lsem, nz)
    k.barrier()
    i_own, i_core, i_x, i_d = k.newl(), k.new(), k.new(), k.new()
    own = k.local(i_own, tok, tok4.at[0])
    own.start()
    to_core = k.remote(i_core, tok, tok4.at[1], k.core)
    to_x = k.remote(i_x, tok, tok4.at[2], k.xn)
    to_core.start()
    to_x.start()
    parts = (
        qkv_parts(k, qkv, lane, wq, ((0, 80, "zxy"), (80, 48, "xyz")))
        + wide_parts(k, proj, wp, ((0, 128, "zyx"),))
        + wide_parts(k, fc1, w1, ((0, 96, "zxy"), (96, 32, "zyx")))
        + wide_parts(k, fc2, w2, ((0, 256, "zxy"), (256, 256, "xyz")))
    )

    def tokens():
        yield
        yield
        yield
        to_x.wait_recv()
        fwd = k.remote(i_d, tok4.at[2], tok4.at[3], k.core)
        fwd.start()
        yield
        fwd.wait()

    wavefront([p.steps for p in parts[:2]] + [tokens()] + [p.steps for p in parts[2:]])
    for p in parts:
        p.finish()
    own.wait()
    to_core.wait()
    to_x.wait_send()
    for cond, body in k.tail:
        guard(cond, body)


def gather_all(nz, tok, qkv, proj, fc1, fc2):
    anyspec = pl.BlockSpec(memory_space=pl.ANY)
    out = [
        jax.ShapeDtypeStruct((4,) + tok.shape, BF),
        jax.ShapeDtypeStruct((2, nz, 2) + qkv.shape, BF),
        jax.ShapeDtypeStruct((6, nz, 2, qkv.shape[0], 256), BF),
    ] + [jax.ShapeDtypeStruct((2, 2, nz, 2) + w.shape, BF) for w in (proj, fc1, fc2)]
    return pl.pallas_call(
        functools.partial(gather_kernel, nz),
        out_shape=out,
        in_specs=[anyspec] * 5,
        out_specs=[anyspec] * 6,
        scratch_shapes=[
            pltpu.SemaphoreType.DMA((160,)),
            pltpu.SemaphoreType.DMA((160,)),
            pltpu.SemaphoreType.DMA((64,)),
        ],
        compiler_params=pltpu.CompilerParams(collective_id=0, has_side_effects=True),
    )(tok, qkv, proj, fc1, fc2)


def norm_parts(values):
    centre = values - jnp.mean(values, axis=-1, keepdims=True)
    inv = lax.rsqrt(jnp.mean(centre * centre, axis=-1, keepdims=True) + 1e-06)
    return centre * inv, inv


def swap_pairs(v):
    n = v.shape[1]
    j = lax.rem(lax.broadcasted_iota(jnp.int32, (1, n), 1), HD)
    lower = lax.rem(j, 20) < 10
    return jnp.where(lower, pltpu.roll(v, n - 10, 1), pltpu.roll(v, 10, 1))


def turn(v, cos, sin):
    cc, ss = jnp.concatenate([cos, cos], axis=1), jnp.concatenate([sin, sin], axis=1)
    return v * cc + swap_pairs(v) * ss


def qkv_body(tok4, tab, wq, down, up6, bias6, gain, shift, n1, red, q, k, v):
    for slot in range(4):
        xhat, _ = norm_parts(tok4[slot].astype(F32))
        h = (xhat * gain[...] + shift[...]).astype(BF)
        n1[slot] = h
        low = mm_nt(h, down[...]).astype(BF)
        red[slot] = low
        cos, sin = tab[slot, :, :128], tab[slot, :, 128:]
        rows = pl.ds(slot * 512, 512)
        for role in range(0 if slot < 2 else 2, 6):
            val = mm(h, wq[role]) + bias6[role] + mm(low, up6[role])
            cols = pl.ds((role % 2) * 256, 256)
            if role < 2:
                q[rows, cols] = (turn(val, cos, sin) * (LOG2E * HD**-0.5)).astype(BF)
            elif role < 4:
                k[rows, cols] = turn(val, cos, sin).astype(BF)
            else:
                v[rows, cols] = val.astype(BF)


def attend_body(q_ref, k_ref, v_ref, o_ref, l_ref):
    lane = lax.broadcasted_iota(jnp.int32, (1, 128), 1)
    ks, qs = k_ref[...], q_ref[...]
    vt = v_ref[...].T
    outs = []
    for e in range(2):
        keep = (lane < 64) if e == 0 else (lane >= 64)
        st = mm_nt(ks, jnp.where(keep, qs, jnp.zeros_like(qs)))
        top = jnp.max(st, axis=0, keepdims=True)
        pr = jnp.exp2(st - top)
        total = jnp.sum(pr, axis=0, keepdims=True)
        outs.append(mm(vt[64 * e : 64 * e + 64], pr.astype(BF)) / total)
        l_ref[e : e + 1, :] = top + jnp.log2(total)
    o_ref[...] = jnp.concatenate(outs, axis=0).T.astype(BF)


def attend(q, k, v):
    nq, nk = q.shape[0], k.shape[0]
    qb = min(1024, nq)
    return pl.pallas_call(
        attend_body,
        grid=(4, nq // qb),
        in_specs=[
            pl.BlockSpec((qb, 128), lambda h, i: (i, h)),
            pl.BlockSpec((nk, 128), lambda h, i: (0, h)),
            pl.BlockSpec((nk, 128), lambda h, i: (0, h)),
        ],
        out_specs=[
            pl.BlockSpec((qb, 128), lambda h, i: (i, h)),
            pl.BlockSpec((None, 2, qb), lambda h, i: (h, 0, i)),
        ],
        out_shape=[
            jax.ShapeDtypeStruct((nq, 512), BF),
            jax.ShapeDtypeStruct((4, 2, nq), F32),
        ],
        compiler_params=pltpu.CompilerParams(vmem_limit_bytes=VM),
    )(q, k, v)


def attend_back_body(q_ref, do_ref, o_ref, k_ref, v_ref, lse_ref, dq_ref, dk_ref, dv_ref, acc, dl):
    lane = lax.broadcasted_iota(jnp.int32, (1, 128), 1)
    kb = pl.program_id(1)
    q, do, ks, vs = q_ref[...], do_ref[...], k_ref[...], v_ref[...]

    @pl.when(kb == 0)
    def _():
        prod = do.astype(F32) * o_ref[...].astype(F32)
        r8 = lax.broadcasted_iota(jnp.int32, (8, 128), 0)
        l8 = lax.broadcasted_iota(jnp.int32, (8, 128), 1) // 64
        pick = (r8 == l8).astype(F32)
        dl[...] = lax.dot_general(
            pick,
            prod,
            (((1,), (1,)), ((), ())),
            precision=lax.Precision.HIGHEST,
            preferred_element_type=F32,
        )

    dks, dvs, dqs = [], [], []
    for e in range(2):
        keep = (lane < 64) if e == 0 else (lane >= 64)
        st = mm_nt(jnp.where(keep, ks, jnp.zeros_like(ks)), q)
        pr = jnp.exp2(st - lse_ref[e : e + 1, :])
        dp = mm_nt(jnp.where(keep, vs, jnp.zeros_like(vs)), do)
        ds = (pr * (dp - dl[e : e + 1, :])).astype(BF)
        dvs.append(mm(pr.astype(BF), do))
        dks.append(mm(ds, q))
        dqs.append(mm(ks.T[64 * e : 64 * e + 64], ds))
    dk_ref[...] = jnp.where(lane < 64, dks[0], dks[1]) * LN2
    dv_ref[...] = jnp.where(lane < 64, dvs[0], dvs[1])
    dq = jnp.concatenate(dqs, axis=0)

    @pl.when(kb == 0)
    def _():
        acc[...] = dq

    @pl.when(kb > 0)
    def _():
        acc[...] += dq

    @pl.when(kb == pl.num_programs(1) - 1)
    def _():
        dq_ref[...] = acc[...].T * (HD**-0.5)


def attend_back(q, do, o, k, v, lse):
    nq, nk = q.shape[0], k.shape[0]
    kb = 1024
    full = pl.BlockSpec((nq, 128), lambda h, i: (0, h))
    part = pl.BlockSpec((kb, 128), lambda h, i: (i, h))
    return pl.pallas_call(
        attend_back_body,
        grid=(4, nk // kb),
        in_specs=[full, full, full, part, part, pl.BlockSpec((None, 2, nq), lambda h, i: (h, 0, 0))],
        out_specs=[full, part, part],
        out_shape=[
            jax.ShapeDtypeStruct((nq, 512), F32),
            jax.ShapeDtypeStruct((nk, 512), F32),
            jax.ShapeDtypeStruct((nk, 512), F32),
        ],
        scratch_shapes=[pltpu.VMEM((128, nq), F32), pltpu.VMEM((8, nq), F32)],
        compiler_params=pltpu.CompilerParams(vmem_limit_bytes=VM),
    )(q, do, o, k, v, lse)


def norm_back(grad, xhat, inv, gain):
    q = grad * gain
    return inv * (
        q - jnp.mean(q, axis=-1, keepdims=True) - xhat * jnp.mean(q * xhat, axis=-1, keepdims=True)
    )


def ffn_body(
    att, tok, cot, wp, w1, w2, dp_, d1, d2, up, u1, u2, bp, b1, b2, gain, shift,
    out, gres, gatt, gap, gbp, ga1, gb1, ga2, gb2,
    act, slope, accs, gn2, res, n2s,
):
    r_p = jnp.zeros((512, 16), F32)
    for g in range(4):
        r_p += mm_nt(att[g], dp_[:, g * 256 : g * 256 + 256])
    r_p = r_p.astype(BF)
    for s in range(4):
        cols = pl.ds(s * 256, 256)
        val = mm(r_p, up[:, cols]) + bp[:, cols]
        for g in range(4):
            val += mm(att[g], wp[s, g * 256 : g * 256 + 256, :])
        res[:, cols] = tok[:, cols].astype(F32) + val
    xhat, inv = norm_parts(res[...])
    n2 = (xhat * gain[...] + shift[...]).astype(BF)
    n2s[...] = n2
    r_1 = mm_nt(n2, d1[...]).astype(BF)

    def up_step(i, carry):
        s = i // 2
        cols = pl.ds(pl.multiple_of(lax.rem(i, 2) * 512, 512), 512)
        hid = mm(n2s[...], w1[s, :, cols]) + b1[i] + mm(r_1, u1[i])
        cdf = 0.5 * (1.0 + lax.erf(hid * (0.5**0.5)))
        act[i] = (hid * cdf).astype(BF)
        slope[i] = cdf + hid * jnp.exp(-0.5 * hid * hid) * 0.3989422804014327
        return carry

    lax.fori_loop(0, 8, up_step, 0)
    g_r2 = mm_nt(cot[...], u2[...]).astype(BF)
    accs[...] = jnp.zeros_like(accs)
    gn2[...] = jnp.zeros_like(gn2)

    def down_step(i, carry):
        r_2, g_r1 = carry
        a = act[i]
        r_2 += mm_nt(a, d2[i])
        g = mm(g_r2, d2[i])
        rows = pl.ds(pl.multiple_of(i * 512, 512), 512)
        for s in range(4):
            w = w2[s, rows, :]
            accs[:, s * 256 : s * 256 + 256] += mm(a, w)
            g += mm_nt(cot[:, s * 256 : s * 256 + 256], w)
        gh = (g * slope[i]).astype(BF)
        cols = pl.ds(pl.multiple_of(lax.rem(i, 2) * 512, 512), 512)
        gn2[...] += mm_nt(gh, w1[i // 2, :, cols])
        g_r1 += mm_nt(gh, u1[i])
        ga2[i] = mm_tn(g_r2, a)
        gb1[i] = mm_tn(r_1, gh)
        return r_2, g_r1

    r_2, g_r1 = lax.fori_loop(
        0, 8, down_step, (jnp.zeros((512, 16), F32), jnp.zeros((512, 16), F32))
    )
    r_2, g_r1 = r_2.astype(BF), g_r1.astype(BF)
    out[...] = (res[...] + accs[...] + b2[...] + mm(r_2, u2[...])).astype(BF)
    gb2[...] = mm_tn(r_2, cot[...])
    ga1[...] = mm_tn(g_r1, n2s[...])
    g_n2 = gn2[...] + mm(g_r1, d1[...])
    xhat, inv = norm_parts(res[...])
    g_res = cot[...].astype(F32) + norm_back(g_n2, xhat, inv, gain[...])
    gres[...] = g_res
    gb = g_res.astype(BF)
    g_rp = mm_nt(gb, up[...]).astype(BF)
    gbp[...] = mm_tn(r_p, gb)
    for g in range(4):
        rows = pl.ds(g * 256, 256)
        val = mm(g_rp, dp_[:, g * 256 : g * 256 + 256])
        for s in range(4):
            val += mm_nt(gb[:, s * 256 : s * 256 + 256], wp[s, rows, :])
        gatt[g] = val.astype(BF)
        gap[:, g * 256 : g * 256 + 256] = mm_tn(g_rp, att[g])


def qkv_back_body(dq, dk, dv, tab, n1, red, wq, down, up6, parts, ga, gb6, gm):
    gb_acc = [None] * 6
    ga_acc = None
    for slot in range(4):
        cos, sin = tab[slot, :, :128], -tab[slot, :, 128:]
        rows = pl.ds(slot * 512, 512)
        first = 0 if slot < 2 else 2
        g_red = jnp.zeros((512, 16), F32)
        for role in range(first, 6):
            cols = pl.ds((role % 2) * 256, 256)
            if role < 2:
                g = turn(dq[rows, cols], cos, sin)
            elif role < 4:
                g = turn(dk[rows, cols], cos, sin)
            else:
                g = dv[rows, cols]
            g = g.astype(BF)
            gm[role] = g
            g_red += mm_nt(g, up6[role])
            t = mm_tn(red[slot], g)
            gb_acc[role] = t if gb_acc[role] is None else gb_acc[role] + t
        g_red = g_red.astype(BF)
        t = mm_tn(g_red, n1[slot])
        ga_acc = t if ga_acc is None else ga_acc + t
        total = mm(g_red, down[...])
        for role in range(first, 6):
            total += mm_nt(gm[role], wq[role])
        parts[slot] = total
    ga[...] = ga_acc
    for role in range(6):
        gb6[role] = gb_acc[role]


def local_call(body, outs, scratch, *args):
    vm = pl.BlockSpec(memory_space=pltpu.VMEM)
    return pl.pallas_call(
        body,
        out_shape=outs,
        in_specs=[vm] * len(args),
        out_specs=[vm] * len(outs),
        scratch_shapes=scratch,
        compiler_params=pltpu.CompilerParams(vmem_limit_bytes=VM),
    )(*args)


def sds(shape, dtype):
    return jax.ShapeDtypeStruct(shape, dtype)


def rotary_table(places):
    half = 10
    freq = 10000.0 ** (-jnp.arange(half, dtype=F32) / half)
    ang = places.astype(F32)[:, :, None] * freq
    cos = [jnp.cos(ang[p]) for p in range(3)]
    sin = [jnp.sin(ang[p]) for p in range(3)]
    rest = places.shape[1:] + (HD - 60,)
    c64 = jnp.concatenate([v for p in cos for v in (p, p)] + [jnp.ones(rest, F32)], axis=-1)
    s64 = jnp.concatenate([v for p in sin for v in (-p, p)] + [jnp.zeros(rest, F32)], axis=-1)
    return jnp.concatenate([c64, c64, s64, s64], axis=-1)


SWAP = [(0, 1), (1, 0), (2, 3), (3, 2)]
CROSS = [(0, 2), (2, 0), (1, 3), (3, 1)]


def fast_shards(
    nz, tokens, positions, adapter_index, qkv_weight, proj_weight, fc1_weight, fc2_weight,
    vectors, fc1_bias, adapter_down, adapter_up, cotangent,
):
    seq = lax.axis_index("seq")
    core = lax.rem(seq, 2)
    tok4, _, wq, wp, w1, w2 = gather_all(
        nz, tokens[0], qkv_weight, proj_weight, fc1_weight, fc2_weight
    )
    wq = wq.reshape(6, D, 256)
    wp, w1, w2 = wp.reshape(4, D, 256), w1.reshape(4, D, 1024), w2.reshape(4, FF, 256)
    vec = lax.all_gather(vectors, "seq", axis=1, tiled=True).astype(F32)
    hb = lax.all_gather(fc1_bias, "seq", axis=0, tiled=True).astype(F32)
    places = lax.all_gather(positions[:, 0], "seq", axis=1)
    places = jnp.where(core == 1, jnp.stack([places[:, i] for i in (1, 0, 3, 2)], axis=1), places)
    places = jnp.where(seq >= 2, jnp.stack([places[:, i] for i in (2, 3, 0, 1)], axis=1), places)
    tab = rotary_table(places.reshape(3, 2048)).reshape(4, 512, 256)
    index = lax.all_gather(adapter_index[:, 0], "dp", axis=0, tiled=True)
    choose = index[:, None] == jnp.arange(NA, dtype=jnp.int32)[None, :]
    mine = jnp.concatenate([adapter_down, adapter_up], axis=-1)
    rk = mine.shape[1]
    sel = jnp.sum(
        jnp.where(choose[:, :, None, None], mine[None].astype(F32), 0.0), axis=1
    ).astype(BF)
    sel = lax.all_to_all(sel, "dp", 0, 0, tiled=True)
    sel = sel.reshape(-1, sel.shape[-1])
    sel = lax.all_gather(sel, "seq", axis=0)
    nd = adapter_down.shape[-1]
    down = jnp.moveaxis(sel[:, :, :nd], 0, 1).reshape(16, -1)
    upm = jnp.moveaxis(sel[:, :, nd:], 0, 1).reshape(16, -1)
    aq, ap, a1, a2 = down[:, :D], down[:, D : 2 * D], down[:, 2 * D : 3 * D], down[:, 3 * D :]
    bq, bp_, b1_, b2_ = (
        upm[:, : 3 * D], upm[:, 3 * D : 4 * D], upm[:, 4 * D : 4 * D + FF], upm[:, 4 * D + FF :],
    )
    up6 = lax.dynamic_index_in_dim(
        jnp.moveaxis(bq.reshape(16, 6, 2, 256), 0, 2), core, 1, keepdims=False
    )
    bias6 = lax.dynamic_index_in_dim(
        vec[4:7].reshape(6, 2, 1, 256), core, 1, keepdims=False
    )
    n1, red, q, k, v = local_call(
        qkv_body,
        [sds((4, 512, D), BF), sds((4, 512, 16), BF), sds((1024, 512), BF), sds((2048, 512), BF), sds((2048, 512), BF)],
        [],
        tok4, tab, wq, aq, up6, bias6, vec[0:1], vec[1:2],
    )
    o, lse = attend(q, k, v)
    other = lax.ppermute(o[512:], "seq", SWAP)

    def by_group(mine_, other_):
        m, t = (
            jnp.moveaxis(w.reshape(512, 2, 256), 1, 0) for w in (mine_, other_)
        )
        first = jnp.where(core == 0, m, t)
        second = jnp.where(core == 0, t, m)
        return jnp.stack([first[0], second[0], first[1], second[1]])

    att = by_group(o[:512], other)
    outs = local_call(
        ffn_body,
        [sds((512, D), BF), sds((512, D), F32), sds((4, 512, 256), BF),
         sds((16, D), F32), sds((16, D), F32), sds((16, D), F32), sds((8, 16, 512), F32),
         sds((8, 16, 512), F32), sds((16, D), F32)],
        [pltpu.VMEM((8, 512, 512), BF), pltpu.VMEM((8, 512, 512), F32), pltpu.VMEM((512, D), F32),
         pltpu.VMEM((512, D), F32), pltpu.VMEM((512, D), F32), pltpu.VMEM((512, D), BF)],
        att, tokens[0], cotangent[0], wp, w1, w2,
        ap, a1, jnp.moveaxis(a2.reshape(16, 8, 512), 1, 0),
        bp_, jnp.moveaxis(b1_.reshape(16, 8, 512), 1, 0), b2_,
        vec[7:8], hb.reshape(8, 1, 512), vec[8:9], vec[2:3], vec[3:4],
    )
    output, gres, gatt, gap, gbp, ga1, gb1, ga2, gb2 = outs
    mine_ = jnp.where(core == 0, jnp.stack([gatt[0], gatt[2]]), jnp.stack([gatt[1], gatt[3]]))
    send_ = jnp.where(core == 0, jnp.stack([gatt[1], gatt[3]]), jnp.stack([gatt[0], gatt[2]]))
    other = lax.ppermute(send_, "seq", SWAP)
    do = jnp.concatenate([mine_, other], axis=1)
    do = jnp.moveaxis(do, 0, 1).reshape(1024, 512)
    dq, dk, dv = attend_back(q, do, o, k, v, lse)
    parts, gaq, gbq = local_call(
        qkv_back_body,
        [sds((4, 512, D), F32), sds((16, D), F32), sds((6, 16, 256), F32)],
        [pltpu.VMEM((6, 512, 256), BF)],
        dq, dk, dv, tab, n1, red, wq, aq, up6,
    )
    r13 = lax.ppermute(jnp.stack([parts[1], parts[3]]).astype(BF), "seq", SWAP)
    r2 = lax.ppermute((parts[2] + r13[1].astype(F32)).astype(BF), "seq", CROSS)
    g_n1 = parts[0] + r13[0].astype(F32) + r2.astype(F32)
    xhat, inv = norm_parts(tokens[0].astype(F32))
    input_grad = (gres + norm_back(g_n1, xhat, inv, vec[0:1])).astype(BF)
    gbq_full = jnp.zeros((6, 2, 16, 256), F32)
    gbq_full = lax.dynamic_update_index_in_dim(gbq_full, gbq[:, None], core, 1)
    gbq_full = jnp.moveaxis(gbq_full, 2, 0).reshape(16, 3 * D)
    flat8 = lambda w: jnp.moveaxis(w, 0, 1).reshape(16, FF)
    cd = jnp.concatenate([gaq, gap, ga1, flat8(ga2)], axis=1).astype(BF)
    cu = jnp.concatenate([gbq_full, gbp, flat8(gb1), gb2], axis=1).astype(BF)
    cd = lax.psum_scatter(cd, "seq", scatter_dimension=1, tiled=True)
    cu = lax.psum_scatter(cu, "seq", scatter_dimension=1, tiled=True)
    both = jnp.concatenate([cd, cu], axis=1)
    both = lax.all_to_all(both, "dp", 0, 0, tiled=True).reshape(-1, rk, both.shape[1])
    grads = jnp.sum(
        jnp.where(choose[:, :, None, None], both[:, None].astype(F32), 0.0), axis=0
    )
    return output[None], input_grad[None], grads[:, :, :nd], grads[:, :, nd:]


def solution(mesh):
    in_specs = (
        P("dp", "seq", None),
        P(None, "dp", "seq"),
        P("dp", None),
        P("dp", "seq"),
        P("dp", "seq"),
        P("dp", "seq"),
        P("dp", "seq"),
        P(None, "seq"),
        P("seq"),
        P(None, "dp", "seq"),
        P(None, "dp", "seq"),
        P("dp", "seq", None),
    )
    out_specs = (
        P("dp", "seq", None),
        P("dp", "seq", None),
        P(None, "dp", "seq"),
        P(None, "dp", "seq"),
    )
    body = shards
    if mesh.shape["seq"] == 4 and mesh.shape["dp"] % 2 == 0:

        def body(tokens, *rest):
            if tokens.shape[0] == 1 and tokens.shape[1] == 512:
                return fast_shards(mesh.shape["dp"] // 2, tokens, *rest)
            return shards(tokens, *rest)

    return jax.shard_map(body, mesh=mesh, in_specs=in_specs, out_specs=out_specs, check_vma=False)
```

```python
import functools
import math

import jax
import jax.numpy as jnp
import numpy as np
from jax import lax
from jax.experimental import pallas as pl
from jax.experimental.pallas import tpu as pltpu
from jax.sharding import PartitionSpec as P

D = 1024
HEADS = 16
HD = 64
FF = 4096
NA = 8


def layer_norm(values, gain_row, shift_row):
    centre = values - jnp.mean(values, axis=-1, keepdims=True)
    spread = jnp.mean(centre * centre, axis=-1, keepdims=True)
    return centre * lax.rsqrt(spread + 1e-06) * gain_row + shift_row


def rotate(values, places, direction):
    rot_span = 2 * (values.shape[-1] // 3 // 2)
    half_span = rot_span // 2
    inverse_freq = 10000.0 ** (-jnp.arange(half_span, dtype=jnp.float32) / half_span)
    pieces = []
    for axis_id in range(3):
        segment = values[..., axis_id * rot_span : (axis_id + 1) * rot_span]
        angles = places[axis_id].astype(jnp.float32)[..., None, None] * inverse_freq
        cosine = jnp.cos(angles)
        sine_wave = direction * jnp.sin(angles)
        lower_part = segment[..., :half_span]
        upper_part = segment[..., half_span:]
        pieces.append(lower_part * cosine - upper_part * sine_wave)
        pieces.append(lower_part * sine_wave + upper_part * cosine)
    pieces.append(values[..., 3 * rot_span :])
    return jnp.concatenate(pieces, axis=-1)


def exact_gelu(values):
    return jax.nn.gelu(values, approximate=False)


def fetch_weight(weight):
    joined = lax.all_gather(weight, "seq", axis=1, tiled=True)
    return lax.all_gather(joined, "dp", axis=0, tiled=True)


def adapted(inputs, weight, shift_row, down_part, up_part):
    base = jnp.einsum("cti,io->cto", inputs, weight, preferred_element_type=jnp.float32)
    reduced = jnp.einsum(
        "cti,cri->ctr", inputs, down_part, preferred_element_type=jnp.float32
    ).astype(jnp.bfloat16)
    result = (
        base
        + shift_row
        + jnp.einsum("ctr,cro->cto", reduced, up_part, preferred_element_type=jnp.float32)
    )
    return (result, reduced)


def adapted_back(grad_out, inputs, weight, down_part, up_part, reduced):
    grad_in = jnp.einsum("cto,io->cti", grad_out, weight, preferred_element_type=jnp.float32)
    grad_reduced = jnp.einsum(
        "cto,cro->ctr", grad_out, up_part, preferred_element_type=jnp.float32
    ).astype(jnp.bfloat16)
    grad_in = grad_in + jnp.einsum(
        "ctr,cri->cti", grad_reduced, down_part, preferred_element_type=jnp.float32
    )
    grad_down = jnp.einsum("ctr,cti->cri", grad_reduced, inputs, preferred_element_type=jnp.float32)
    grad_up = jnp.einsum("ctr,cto->cro", reduced, grad_out, preferred_element_type=jnp.float32)
    return (grad_in, grad_down, grad_up)


def split_tokens(source, split_count):
    old_shape = source.shape
    shaped = source.reshape(
        (old_shape[0], split_count, old_shape[1] // split_count) + old_shape[2:]
    )
    return jnp.moveaxis(shaped, 1, 0)


def score_grads(
    query_block, key_block, value_block, grad_block, log_block, delta_block, score_scale
):
    scores = (
        jnp.einsum("cqhd,ckhd->chqk", query_block, key_block, preferred_element_type=jnp.float32)
        * score_scale
    )
    probabilities = jnp.exp(scores - log_block[..., None])
    grad_probs = jnp.einsum(
        "cqhd,ckhd->chqk", grad_block, value_block, preferred_element_type=jnp.float32
    )
    grad_scores = (probabilities * (grad_probs - delta_block[..., None])).astype(jnp.bfloat16)
    return (probabilities.astype(jnp.bfloat16), grad_scores)


def shards(
    tokens,
    positions,
    adapter_index,
    qkv_weight,
    proj_weight,
    fc1_weight,
    fc2_weight,
    vectors,
    fc1_bias,
    adapter_down,
    adapter_up,
    cotangent,
):
    clip_count, tok_count = (tokens.shape[0], tokens.shape[1])
    head_shape = (clip_count, tok_count, HEADS, HD)
    score_scale = HD ** (-0.5)
    small_parts = (
        lax.all_gather(adapter_down, "seq", axis=2, tiled=True),
        lax.all_gather(adapter_up, "seq", axis=2, tiled=True),
        lax.all_gather(vectors, "seq", axis=1, tiled=True),
        lax.all_gather(fc1_bias, "seq", axis=0, tiled=True),
    )
    down_all, up_all = (
        lax.all_gather(small_parts[0], "dp", axis=1, tiled=True),
        lax.all_gather(small_parts[1], "dp", axis=1, tiled=True),
    )
    vector_rows = small_parts[2].astype(jnp.float32)
    hidden_bias = small_parts[3].astype(jnp.float32)
    choose = (adapter_index == jnp.arange(NA, dtype=jnp.int32)[None, :]).astype(jnp.bfloat16)
    down_sel = jnp.einsum(
        "ca,ari->cri", choose, down_all, preferred_element_type=jnp.float32
    ).astype(jnp.bfloat16)
    up_sel = jnp.einsum("ca,aro->cro", choose, up_all, preferred_element_type=jnp.float32).astype(
        jnp.bfloat16
    )
    down_parts = (
        down_sel[:, :, :D],
        down_sel[:, :, D : 2 * D],
        down_sel[:, :, 2 * D : 3 * D],
        down_sel[:, :, 3 * D :],
    )
    up_parts = (
        up_sel[:, :, : 3 * D],
        up_sel[:, :, 3 * D : 4 * D],
        up_sel[:, :, 4 * D : 4 * D + FF],
        up_sel[:, :, 4 * D + FF :],
    )
    inputs = tokens.astype(jnp.float32)
    normed_one = layer_norm(inputs, vector_rows[0], vector_rows[1]).astype(jnp.bfloat16)
    weight_qkv = fetch_weight(qkv_weight)
    mixed_qkv, reduced_qkv = adapted(
        normed_one, weight_qkv, vector_rows[4:7].reshape(3 * D), down_parts[0], up_parts[0]
    )
    queries = rotate(mixed_qkv[..., :D].reshape(head_shape), positions, 1.0).astype(jnp.bfloat16)
    keys_local = rotate(mixed_qkv[..., D : 2 * D].reshape(head_shape), positions, 1.0).astype(
        jnp.bfloat16
    )
    values_local = mixed_qkv[..., 2 * D :].reshape(head_shape).astype(jnp.bfloat16)
    stat_shape = (clip_count, HEADS, tok_count)
    start_state = (
        jnp.full(stat_shape, -jnp.inf, jnp.float32),
        jnp.zeros(stat_shape, jnp.float32),
        jnp.zeros(stat_shape + (HD,), jnp.float32),
    )
    key_piece = lax.all_gather(keys_local, "seq", axis=1, tiled=True)
    value_piece = lax.all_gather(values_local, "seq", axis=1, tiled=True)
    split_count = key_piece.shape[1] // math.gcd(key_piece.shape[1], 256)

    def inner_step(running, block_pair):
        top_score, row_total, weighted = running
        key_block, value_block = block_pair
        scores = (
            jnp.einsum("cqhd,ckhd->chqk", queries, key_block, preferred_element_type=jnp.float32)
            * score_scale
        )
        new_top = jnp.maximum(top_score, jnp.max(scores, axis=-1))
        factor = jnp.exp(top_score - new_top)
        weights = jnp.exp(scores - new_top[..., None])
        row_total = row_total * factor + jnp.sum(weights, axis=-1)
        weighted = weighted * factor[..., None] + jnp.einsum(
            "chqk,ckhd->chqd",
            weights.astype(jnp.bfloat16),
            value_block,
            preferred_element_type=jnp.float32,
        )
        return ((new_top, row_total, weighted), None)

    result, unused = lax.scan(
        inner_step,
        start_state,
        (split_tokens(key_piece, split_count), split_tokens(value_piece, split_count)),
    )
    top_score, row_total, weighted = result
    log_total = top_score + jnp.log(row_total)
    heads_tok = jnp.swapaxes(weighted / row_total[..., None], 1, 2)
    attended = heads_tok.reshape(clip_count, tok_count, D).astype(jnp.bfloat16)
    weight_proj = fetch_weight(proj_weight)
    projected, reduced_proj = adapted(
        attended, weight_proj, vector_rows[7], down_parts[1], up_parts[1]
    )
    residual = inputs + projected
    normed_two = layer_norm(residual, vector_rows[2], vector_rows[3]).astype(jnp.bfloat16)
    weight_up = fetch_weight(fc1_weight)
    hidden, reduced_up = adapted(normed_two, weight_up, hidden_bias, down_parts[2], up_parts[2])
    activated = exact_gelu(hidden).astype(jnp.bfloat16)
    weight_down = fetch_weight(fc2_weight)
    branch, reduced_down = adapted(
        activated, weight_down, vector_rows[8], down_parts[3], up_parts[3]
    )
    output = (residual + branch).astype(jnp.bfloat16)
    weight_down = fetch_weight(fc2_weight)
    grad_act, gdown_four, gup_four = adapted_back(
        cotangent, activated, weight_down, down_parts[3], up_parts[3], reduced_down
    )
    unused, gelu_back = jax.vjp(exact_gelu, hidden)
    grad_hidden = gelu_back(grad_act)[0].astype(jnp.bfloat16)
    weight_up = fetch_weight(fc1_weight)
    grad_normed_two, gdown_three, gup_three = adapted_back(
        grad_hidden, normed_two, weight_up, down_parts[2], up_parts[2], reduced_up
    )

    def norm_two(values):
        return layer_norm(values, vector_rows[2], vector_rows[3])

    unused, norm_two_back = jax.vjp(norm_two, residual)
    grad_residual = cotangent.astype(jnp.float32) + norm_two_back(grad_normed_two)[0]
    weight_proj = fetch_weight(proj_weight)
    grad_attended, gdown_two, gup_two = adapted_back(
        grad_residual.astype(jnp.bfloat16),
        attended,
        weight_proj,
        down_parts[1],
        up_parts[1],
        reduced_proj,
    )
    grad_tok = grad_attended.astype(jnp.bfloat16).reshape(head_shape)
    delta_heads = jnp.swapaxes(jnp.sum(grad_tok.astype(jnp.float32) * heads_tok, axis=-1), 1, 2)
    whole_keys, whole_values = (
        lax.all_gather(keys_local, "seq", axis=1, tiled=True),
        lax.all_gather(values_local, "seq", axis=1, tiled=True),
    )
    block_count = whole_keys.shape[1] // math.gcd(whole_keys.shape[1], 256)
    key_blocks = split_tokens(whole_keys, block_count)
    value_blocks = split_tokens(whole_values, block_count)
    zero_heads = jnp.zeros(head_shape, jnp.float32)

    def back_step(grad_query, block_pair):
        key_block, value_block = block_pair
        probs_low, grad_scores = score_grads(
            queries, key_block, value_block, grad_tok, log_total, delta_heads, score_scale
        )
        grad_query = (
            grad_query
            + jnp.einsum(
                "chqk,ckhd->cqhd", grad_scores, key_block, preferred_element_type=jnp.float32
            )
            * score_scale
        )
        grad_key = (
            jnp.einsum("chqk,cqhd->ckhd", grad_scores, queries, preferred_element_type=jnp.float32)
            * score_scale
        )
        grad_value = jnp.einsum(
            "chqk,cqhd->ckhd", probs_low, grad_tok, preferred_element_type=jnp.float32
        )
        return (grad_query, jnp.concatenate([grad_key, grad_value], axis=-1))

    grad_query, key_terms = lax.scan(back_step, zero_heads, (key_blocks, value_blocks))
    key_terms = jnp.moveaxis(key_terms, 0, 1).reshape(
        clip_count, whole_keys.shape[1], HEADS, 2 * HD
    )
    summed = lax.psum_scatter(
        key_terms.astype(jnp.bfloat16), "seq", scatter_dimension=1, tiled=True
    ).astype(jnp.float32)
    grad_key = summed[..., :HD]
    grad_value = summed[..., HD:]
    grad_mixed = jnp.concatenate(
        [
            rotate(grad_query, positions, -1.0).reshape(clip_count, tok_count, D),
            rotate(grad_key, positions, -1.0).reshape(clip_count, tok_count, D),
            grad_value.reshape(clip_count, tok_count, D),
        ],
        axis=-1,
    ).astype(jnp.bfloat16)
    weight_qkv = fetch_weight(qkv_weight)
    grad_normed_one, gdown_one, gup_one = adapted_back(
        grad_mixed, normed_one, weight_qkv, down_parts[0], up_parts[0], reduced_qkv
    )

    def norm_one(values):
        return layer_norm(values, vector_rows[0], vector_rows[1])

    unused, norm_one_back = jax.vjp(norm_one, inputs)
    input_grad = (grad_residual + norm_one_back(grad_normed_one)[0]).astype(jnp.bfloat16)
    choose_wide = choose.astype(jnp.float32)
    clip_down = jnp.concatenate([gdown_one, gdown_two, gdown_three, gdown_four], axis=-1)
    clip_up = jnp.concatenate([gup_one, gup_two, gup_three, gup_four], axis=-1)
    down_term = jnp.einsum("ca,cri->ari", choose_wide, clip_down, precision=lax.Precision.HIGHEST)
    up_term = jnp.einsum("ca,cro->aro", choose_wide, clip_up, precision=lax.Precision.HIGHEST)
    down_grad, up_grad = (
        lax.psum_scatter(
            down_term.astype(jnp.bfloat16), "seq", scatter_dimension=2, tiled=True
        ).astype(jnp.float32),
        lax.psum_scatter(
            up_term.astype(jnp.bfloat16), "seq", scatter_dimension=2, tiled=True
        ).astype(jnp.float32),
    )
    down_grad, up_grad = (
        lax.psum_scatter(
            down_grad.astype(jnp.bfloat16), "dp", scatter_dimension=1, tiled=True
        ).astype(jnp.float32),
        lax.psum_scatter(
            up_grad.astype(jnp.bfloat16), "dp", scatter_dimension=1, tiled=True
        ).astype(jnp.float32),
    )
    return (output, input_grad, down_grad, up_grad)

MESH = pl.DeviceIdType.MESH
BF = jnp.bfloat16
F32 = jnp.float32
LOG2E = 1.4426950408889634
LN2 = 0.6931471805599453
VM = 60 * 1024 * 1024


def mm(a, b):
    return lax.dot_general(a, b, (((1,), (0,)), ((), ())), preferred_element_type=F32)


def mm_nt(a, b):
    return lax.dot_general(a, b, (((1,), (1,)), ((), ())), preferred_element_type=F32)


def mm_tn(a, b):
    return lax.dot_general(a, b, (((0,), (0,)), ((), ())), preferred_element_type=F32)


class Links:
    def __init__(self, ssem, rsem, lsem, nz):
        self.ssem, self.rsem, self.lsem = ssem, rsem, lsem
        self.nr, self.nl = 0, 0
        d, s = lax.axis_index("dp"), lax.axis_index("seq")
        self.d, self.s, self.nz = d, s, nz
        self.z, self.y, self.x, self.c = d // 2, lax.rem(d, 2), s // 2, lax.rem(s, 2)
        self.core = (d, s + 1 - 2 * self.c)
        self.xn = (d, s + 2 - 4 * self.x)
        self.diag = (d, 3 - s)
        self.yn = (d + 1 - 2 * self.y, s)
        self.up, self.down = (d + 2, s), (d - 2, s)
        self.zpeer = [(lax.rem(d + 2 * j, 2 * nz), s) for j in range(nz)]

    def barrier(self, peers):
        bar = pltpu.get_barrier_semaphore()
        for dev in peers:
            pl.semaphore_signal(bar, inc=1, device_id=dev, device_id_type=MESH)
        pl.semaphore_wait(bar, len(peers))

    def new(self, count=1):
        self.nr += count
        return self.nr - count

    def newl(self):
        self.nl += 1
        return self.nl - 1

    def remote(self, i, src, dst, dev):
        return pltpu.make_async_remote_copy(
            src_ref=src,
            dst_ref=dst,
            send_sem=self.ssem.at[i],
            recv_sem=self.rsem.at[i],
            device_id=dev,
            device_id_type=MESH,
        )

    def local(self, i, src, dst):
        return pltpu.make_async_copy(src, dst, self.lsem.at[i])


def guard(cond, body):
    if cond is None:
        body()
    else:
        pl.when(cond)(body)


class Part:
    def __init__(self, links, order, own, region, handover):
        self.k, self.order, self.own = links, order, own
        self.region, self.handover = region, handover
        k = links
        self.s_own = k.newl()
        n = k.nz - 1
        self.s_z = k.new(2 * n if order == "xyz" else n)
        self.s_f, self.s_g1, self.s_g2 = k.new(), k.new(), k.new()
        self.pend, self.tail = [], []
        xfirst = order != "zyx"
        self.f, self.g = (k.x, k.y) if xfirst else (k.y, k.x)
        self.fd, self.gd = (k.xn, k.yn) if xfirst else (k.yn, k.xn)

    def reg(self, fi, gi, zs):
        return self.region(gi, zs, fi) if self.order == "zyx" else self.region(fi, zs, gi)

    def hand(self, cond, fi, zs, gi):
        k = self.k
        x, y = (gi, fi) if self.order == "zyx" else (fi, gi)
        loc, rem = self.handover(x, zs, y)
        ls = [(k.newl(), a, b) for a, b in loc]
        rs = [(k.new(), a, b, w) for a, b, w in rem]

        def start():
            for i, a, b in ls:
                k.local(i, a, b).start()
            for i, a, b, _ in rs:
                k.remote(i, a, b, k.core).start()

        def arrive():
            for i, a, b in ls:
                k.local(i, a, b).wait()
            for i, a, b, w in rs:
                k.remote(i, a, w, k.core).wait_recv()

        def sent():
            for i, a, b, _ in rs:
                k.remote(i, a, b, k.core).wait_send()

        guard(cond, start)
        self.pend.append((cond, arrive))
        self.tail.append((cond, sent))

    def go(self, cond, copy):
        guard(cond, copy.start)
        self.tail.append((cond, copy.wait_send))

    def step(self, name):
        getattr(self, ("l_" if self.order == "xyz" else "z_") + name)()

    def z_s(self):
        k, f, g = self.k, self.f, self.g
        k.local(self.s_own, self.own, self.reg(f, g, k.z)).start()
        for j in range(1, k.nz):
            self.go(None, k.remote(self.s_z + j - 1, self.own, self.reg(f, g, k.z), k.zpeer[j]))

    def z_m(self):
        k, f, g = self.k, self.f, self.g
        al = slice(None)
        for j in range(1, k.nz):
            at = self.reg(f, g, lax.rem(k.z + k.nz - j, k.nz))
            k.remote(self.s_z + j - 1, self.own, at, k.zpeer[j]).wait_recv()
        k.local(self.s_own, self.own, self.reg(f, g, k.z)).wait()
        mine = self.reg(f, g, al)
        self.go(None, k.remote(self.s_f, mine, mine, self.fd))
        self.go(None, k.remote(self.s_g1, mine, mine, self.gd))
        self.hand(None, f, al, g)

    def z_f(self):
        k, f, g = self.k, self.f, self.g
        al = slice(None)
        new = self.reg(1 - f, g, al)
        k.remote(self.s_f, new, new, self.fd).wait_recv()
        self.go(None, k.remote(self.s_g2, new, new, self.gd))
        self.hand(None, 1 - f, al, g)

    def z_g1(self):
        k, f, g = self.k, self.f, self.g
        al = slice(None)
        new = self.reg(f, 1 - g, al)
        k.remote(self.s_g1, new, new, self.gd).wait_recv()
        self.hand(None, f, al, 1 - g)

    def z_g2(self):
        k, f, g = self.k, self.f, self.g
        al = slice(None)
        new = self.reg(1 - f, 1 - g, al)
        k.remote(self.s_g2, new, new, self.gd).wait_recv()
        self.hand(None, 1 - f, al, 1 - g)

    def l_s(self):
        k, f, g, z = self.k, self.f, self.g, self.k.z
        k.local(self.s_own, self.own, self.reg(f, g, z)).start()
        self.go(None, k.remote(self.s_f, self.own, self.reg(f, g, z), self.fd))
        self.go(None, k.remote(self.s_g1, self.own, self.reg(f, g, z), self.gd))

    def l_f(self):
        k, f, g, z = self.k, self.f, self.g, self.k.z
        new = self.reg(1 - f, g, z)
        k.remote(self.s_f, self.own, new, self.fd).wait_recv()
        self.go(None, k.remote(self.s_g2, new, new, self.gd))

    def l_m(self):
        k, f, g, z = self.k, self.f, self.g, self.k.z
        al = slice(None)
        k.remote(self.s_g1, self.own, self.reg(f, 1 - g, z), self.gd).wait_recv()
        new = self.reg(1 - f, 1 - g, z)
        k.remote(self.s_g2, new, new, self.gd).wait_recv()
        k.local(self.s_own, self.own, self.reg(f, g, z)).wait()
        four = self.reg(al, al, z)
        self.go(z < k.nz - 1, k.remote(self.s_z, four, four, k.up))
        self.go(z > 0, k.remote(self.s_z + k.nz - 1, four, four, k.down))
        self.hand(None, al, z, al)

    def relay(self, r):
        k, z = self.k, self.k.z
        al = slice(None)
        for sem, here, origin, dev, can in (
            (self.s_z, z > r, z - 1 - r, k.up, z < k.nz - 1),
            (self.s_z + k.nz - 1, z + r < k.nz - 1, z + 1 + r, k.down, z > 0),
        ):
            four = self.reg(al, al, origin)
            guard(here, k.remote(sem + r, four, four, dev).wait_recv)
            if r < k.nz - 2:
                self.go(jnp.logical_and(here, can), k.remote(sem + r + 1, four, four, dev))
            self.hand(here, al, origin, al)

    def l_r0(self):
        self.relay(0)

    def l_r1(self):
        self.relay(1)

    def l_r2(self):
        self.relay(2)

    def arrive(self):
        for cond, body in self.pend:
            guard(cond, body)

    def finish(self):
        for cond, body in self.tail:
            guard(cond, body)


def wide_parts(links, shard, buf, cuts):
    c = links.c
    parts = []
    for r0, n, order in cuts:
        rows = pl.ds(r0, n)

        def region(x, z, y, rows=rows):
            return buf.at[x, c, z, y, rows]

        def handover(x, z, y, rows=rows):
            at = buf.at[x, c, z, y, rows]
            return [], [(at, at, buf.at[x, 1 - c, z, y, rows])]

        parts.append(Part(links, order, shard.at[rows], region, handover))
    return parts


def qkv_parts(links, shard, lane, buf, cuts):
    c = links.c
    parts = []
    for r0, n, order in cuts:
        rows = pl.ds(r0, n)

        def region(x, z, y, rows=rows):
            return lane.at[x, z, y, rows]

        def handover(x, z, y, rows=rows):
            loc, rem = [], []
            for xx in (0, 1) if isinstance(x, slice) else (x,):
                for col, role in ((0, 3 * xx + c), (512, 3 * xx + c + 1)):
                    loc.append((lane.at[xx, z, y, rows, pl.ds(col, 256)], buf.at[role, z, y, rows]))
                rem.append(
                    (
                        lane.at[xx, z, y, rows, pl.ds(256, 256)],
                        buf.at[3 * xx + 2 * c, z, y, rows],
                        buf.at[3 * xx + 2 - 2 * c, z, y, rows],
                    )
                )
            return loc, rem

        parts.append(Part(links, order, shard.at[rows], region, handover))
    return parts


def norm_parts(values):
    centre = values - jnp.mean(values, axis=-1, keepdims=True)
    inv = lax.rsqrt(jnp.mean(centre * centre, axis=-1, keepdims=True) + 1e-06)
    return centre * inv, inv


def swap_pairs(v):
    n = v.shape[1]
    j = lax.rem(lax.broadcasted_iota(jnp.int32, (1, n), 1), HD)
    lower = lax.rem(j, 20) < 10
    return jnp.where(lower, pltpu.roll(v, n - 10, 1), pltpu.roll(v, 10, 1))


def turn(v, cos, sin):
    cc, ss = jnp.concatenate([cos, cos], axis=1), jnp.concatenate([sin, sin], axis=1)
    return v * cc + swap_pairs(v) * ss


def attend_back_body(q_ref, do_ref, o_ref, k_ref, v_ref, lse_ref, dq_ref, dk_ref, dv_ref, acc, dl):
    lane = lax.broadcasted_iota(jnp.int32, (1, 128), 1)
    kb = pl.program_id(1)
    q, do, ks, vs = q_ref[...], do_ref[...], k_ref[...], v_ref[...]

    @pl.when(kb == 0)
    def _():
        prod = do.astype(F32) * o_ref[...].astype(F32)
        r8 = lax.broadcasted_iota(jnp.int32, (8, 128), 0)
        l8 = lax.broadcasted_iota(jnp.int32, (8, 128), 1) // 64
        pick = (r8 == l8).astype(F32)
        dl[...] = lax.dot_general(
            pick,
            prod,
            (((1,), (1,)), ((), ())),
            precision=lax.Precision.HIGHEST,
            preferred_element_type=F32,
        )

    dks, dvs, dqs = [], [], []
    for e in range(2):
        keep = (lane < 64) if e == 0 else (lane >= 64)
        st = mm_nt(jnp.where(keep, ks, jnp.zeros_like(ks)), q)
        pr = jnp.exp2(st - lse_ref[e : e + 1, :])
        dp = mm_nt(jnp.where(keep, vs, jnp.zeros_like(vs)), do)
        ds = (pr * (dp - dl[e : e + 1, :])).astype(BF)
        dvs.append(mm(pr.astype(BF), do))
        dks.append(mm(ds, q))
        dqs.append(mm(ks.T[64 * e : 64 * e + 64], ds))
    dk_ref[...] = jnp.where(lane < 64, dks[0], dks[1]) * LN2
    dv_ref[...] = jnp.where(lane < 64, dvs[0], dvs[1])
    dq = jnp.concatenate(dqs, axis=0)

    @pl.when(kb == 0)
    def _():
        acc[...] = dq

    @pl.when(kb > 0)
    def _():
        acc[...] += dq

    @pl.when(kb == pl.num_programs(1) - 1)
    def _():
        dq_ref[...] = acc[...].T * (HD**-0.5)


def attend_back(q, do, o, k, v, lse):
    nq, nk = q.shape[0], k.shape[0]
    kb = 1024
    full = pl.BlockSpec((nq, 128), lambda h, i: (0, h))
    part = pl.BlockSpec((kb, 128), lambda h, i: (i, h))
    return pl.pallas_call(
        attend_back_body,
        grid=(4, nk // kb),
        in_specs=[full, full, full, part, part, pl.BlockSpec((None, 2, nq), lambda h, i: (h, 0, 0))],
        out_specs=[full, part, part],
        out_shape=[
            jax.ShapeDtypeStruct((nq, 512), F32),
            jax.ShapeDtypeStruct((nk, 512), F32),
            jax.ShapeDtypeStruct((nk, 512), F32),
        ],
        scratch_shapes=[pltpu.VMEM((128, nq), F32), pltpu.VMEM((8, nq), F32)],
        compiler_params=pltpu.CompilerParams(vmem_limit_bytes=VM),
    )(q, do, o, k, v, lse)


def norm_back(grad, xhat, inv, gain):
    q = grad * gain
    return inv * (
        q - jnp.mean(q, axis=-1, keepdims=True) - xhat * jnp.mean(q * xhat, axis=-1, keepdims=True)
    )


def qkv_back_body(dq, dk, dv, pall, table, n1, red, wq, down, up6, parts, ga, gb6, gm):
    gb_acc = [None] * 6
    ga_acc = None
    for slot in range(4):
        tab = turns(pall[slot], table)
        cos, sin = tab[:, :128], -tab[:, 128:]
        rows = pl.ds(slot * 512, 512)
        first = 0 if slot < 2 else 2
        g_red = jnp.zeros((512, 16), F32)
        for role in range(first, 6):
            cols = pl.ds((role % 2) * 256, 256)
            if role < 2:
                g = turn(dq[rows, cols], cos, sin)
            elif role < 4:
                g = turn(dk[rows, cols], cos, sin)
            else:
                g = dv[rows, cols]
            g = g.astype(BF)
            gm[role] = g
            g_red += mm_nt(g, up6[role])
            t = mm_tn(red[slot], g)
            gb_acc[role] = t if gb_acc[role] is None else gb_acc[role] + t
        g_red = g_red.astype(BF)
        t = mm_tn(g_red, n1[slot])
        ga_acc = t if ga_acc is None else ga_acc + t
        total = mm(g_red, down[...])
        for role in range(first, 6):
            total += mm_nt(gm[role], wq[role])
        parts[slot] = total
    ga[...] = ga_acc
    for role in range(6):
        gb6[role] = gb_acc[role]


def local_call(body, outs, scratch, *args):
    vm = pl.BlockSpec(memory_space=pltpu.VMEM)
    return pl.pallas_call(
        body,
        out_shape=outs,
        in_specs=[vm] * len(args),
        out_specs=[vm] * len(outs),
        scratch_shapes=scratch,
        compiler_params=pltpu.CompilerParams(vmem_limit_bytes=VM),
    )(*args)


def sds(shape, dtype):
    return jax.ShapeDtypeStruct(shape, dtype)


PLAN = (
    (((0, 48, 'zxy'), (48, 48, 'zxy'), (96, 32, 'xyz')), ((0, 128, 'zxy'),), ((0, 32, 'zxy'), (32, 32, 'zyx'), (64, 32, 'xyz'), (96, 32, 'zxy')), ((0, 128, 'xyz'), (128, 128, 'zxy'), (256, 128, 'zyx'), (384, 128, 'zxy'))),
    (
        (0, 's'), (1, 's'), (2, 's'), ('tok', 1), ('vec',), ('norm', 0), ('pick',), (3, 's'), (2, 'f'),
        ('pass',), (2, 'm'), ('maps',), ('norm', 1), ('red', 0), ('red', 1), ('tok', 0), (0, 'm'), (6, 's'),
        ('tokfwd', 1), (1, 'm'), (0, 'f'), (0, 'g1'), (2, 'r0'), (4, 's'), (7, 's'), (1, 'f'), (1, 'g1'),
        (8, 's'), (3, 'm'), (5, 's'), (0, 'g2'), (2, 'r1'), (10, 's'), (2, 'r2'), ('tokfwd', 0), ('norm', 2),
        (6, 'f'), (4, 'm'), (1, 'g2'), ('norm', 3), ('red', 2), ('red', 3), (9, 's'), ('wq',),
        ('qkv', 0, 0, 2), ('qkv', 0, 2, 4), ('qkv', 0, 4, 6), (3, 'f'), (3, 'g1'), ('qkv', 1, 0, 2),
        ('qkv', 1, 2, 4), (8, 'f'), ('qkv', 1, 4, 6), (7, 'm'), ('qkv', 2, 2, 4), ('qkv', 2, 4, 6),
        ('qkv', 3, 2, 4), ('qkv', 3, 4, 6), ('keep',), ('att', 0, 0), (6, 'm'), ('att', 0, 1), (4, 'f'),
        (5, 'm'), (4, 'g1'), ('att', 0, 2), ('att', 0, 3), (7, 'f'), (10, 'm'), ('att', 1, 0), ('att', 1, 1),
        (3, 'g2'), (8, 'm'), ('att', 1, 2), (6, 'r0'), (11, 's'), (7, 'g1'), ('att', 1, 3), ('att', 2, 0),
        (9, 'm'), ('att', 2, 1), ('att', 2, 2), (4, 'g2'), (6, 'r1'), ('att', 2, 3), (9, 'f'), (5, 'f'),
        (5, 'g1'), ('att', 3, 0), ('att', 3, 1), (8, 'r0'), ('att', 3, 2), (5, 'g2'), (7, 'g2'),
        ('att', 3, 3), (6, 'r2'), ('swap',), ('proj',), (10, 'f'), (10, 'g1'), ('norm2',), (11, 'm'),
        ('fc1', 0), ('fc1', 1), (9, 'g1'), (10, 'g2'), ('fc1', 2), ('fc1', 3), (8, 'r1'), ('fc1', 4),
        (9, 'g2'), ('fc1', 5), (11, 'f'), ('fc1', 6), (8, 'r2'), ('fc1', 7), (11, 'g1'), ('fc2', 2),
        ('fc2', 1), (11, 'g2'), ('fc2', 0), ('fc2', 3), ('end',),
    ),
)
QB = 256
NSEM = (230, 90)


def row_table():
    half = 10
    freq = 10000.0 ** (-np.arange(half) / half)
    ang = np.arange(16)[:, None] * freq
    whole = np.zeros((48, 256))
    for p in range(3):
        rows = slice(16 * p, 16 * p + 16)
        for head in range(2):
            at = head * HD + p * 2 * half
            whole[rows, at : at + half] = np.cos(ang)
            whole[rows, at + half : at + 2 * half] = np.cos(ang)
            whole[rows, 128 + at : 128 + at + half] = -np.sin(ang)
            whole[rows, 128 + at + half : 128 + at + 2 * half] = np.sin(ang)
    for head in range(2):
        whole[:16, head * HD + 60 : head * HD + HD] = 1.0
    whole = whole.astype(np.float32)
    pieces = []
    for _ in range(3):
        piece = whole.astype(BF)
        pieces.append(np.asarray(piece))
        whole = whole - piece.astype(np.float32)
    return np.stack(pieces)


def turns(places, table):
    level = lax.broadcasted_iota(jnp.int32, (16, places.shape[1]), 0).astype(F32)
    hot = jnp.concatenate([(level == places[p : p + 1]).astype(F32) for p in range(3)], axis=0)
    hot = hot.astype(BF)
    return mm_tn(hot, table[0]) + mm_tn(hot, table[1]) + mm_tn(hot, table[2])


def unshuffle():
    i = lax.broadcasted_iota(jnp.int32, (128, 128), 0)
    j = lax.broadcasted_iota(jnp.int32, (128, 128), 1)
    k, dp, r = i // 16, lax.rem(i, 16) // 2, lax.rem(i, 2)
    return (j == dp * 16 + r * 8 + k).astype(F32).astype(BF)


def front_kernel(nz, cfg, *refs):
    (tok, cot, qkv, proj, fc1, fc2, vecs, places, index, ad, table) = refs[:11]
    (out, gres, do_o, q_o, k_o, v_o, o_o, lse_o, n1_o, red_o, wq_o, dn, up, pall, idxs,
     gap, gbp, ga1, gb1, ga2, gb2, lane) = refs[11:33]
    (buf4, wq, wp, w1, w2, q, kv, att, accs, res, n2s,
     vall, vf, selb, adall, small, ssem, rsem, lsem) = refs[33:]
    (r_p_s, r_1_s, g_r2_s, r_2_s, g_r1_s) = [small.at[i] for i in range(5)]
    k = Links(ssem, rsem, lsem, nz)
    c, d, s = k.c, k.d, k.s
    ndp = 2 * nz
    slope, o, gatt, gn2 = kv, q, att, gres
    seqs = [k.core, k.xn, k.diag]
    dps = [(lax.rem(d + j, ndp), s) for j in range(1, ndp)]
    k.barrier(seqs + [k.yn] + [p for p in dps])
    late = []

    def push(src, dst, land, dev):
        i = k.new()
        cp = k.remote(i, src, dst, dev)
        cp.start()
        late.append(cp.wait_send)
        return k.remote(i, src, land, dev).wait_recv

    def send_later(src, dst, land, dev):
        i = k.new()
        cp = k.remote(i, src, dst, dev)

        def start():
            cp.start()
            late.append(cp.wait_send)

        return start, k.remote(i, src, land, dev).wait_recv

    def keep(src, dst):
        i = k.newl()
        cp = k.local(i, src, dst)
        cp.start()
        return cp.wait

    idxs[d] = index[...]
    wait_idx = [
        push(index, idxs.at[d], idxs.at[lax.rem(d + ndp - j, ndp)], dps[j - 1])
        for j in range(1, ndp)
    ]
    vall[s] = vecs[...]
    seq_of = [s + 1 - 2 * c, s + 2 - 4 * k.x, 3 - s]
    wait_vec = [push(vecs, vall.at[s], vall.at[seq_of[r]], seqs[r]) for r in range(3)]
    pall[0] = places[...]
    wait_pos = [push(places, pall.at[r + 1], pall.at[r + 1], seqs[r]) for r in range(3)]
    own_tok = keep(tok, buf4.at[0])
    tok_core = push(tok, buf4.at[1], buf4.at[1], k.core)
    halves = [pl.ds(0, 256), pl.ds(256, 256)]
    tok_x = [send_later(tok.at[h], buf4.at[2, h], buf4.at[2, h], k.xn) for h in halves]
    tok_on = [k.remote(k.new(), buf4.at[2, h], buf4.at[3, h], k.core) for h in halves]
    cuts, order = cfg
    parts = (
        qkv_parts(k, qkv, lane, wq, cuts[0])
        + wide_parts(k, proj, wp, cuts[1])
        + wide_parts(k, fc1, w1, cuts[2])
        + wide_parts(k, fc2, w2, cuts[3])
    )
    groups = []
    n = 0
    for cs in cuts:
        groups.append(parts[n : n + len(cs)])
        n += len(cs)
    state = {}

    def a_tok(h):
        tok_x[h][0]()

    def a_tokfwd(h):
        tok_x[h][1]()
        tok_on[h].start()

    def a_pick():
        for w in wait_idx:
            w()
        for j in range(ndp):
            dest = lax.rem(d + j, ndp)
            who = idxs[dest]
            total = jnp.zeros((16, 512), F32)
            for a in range(NA):
                total += jnp.where(who[0:1, 0:1] == float(a), ad[a].astype(F32), 0.0)
            selb[j] = total.astype(BF)
        adall[s, d] = selb[0]
        state["ad"] = [
            push(selb.at[j], adall.at[s, d], adall.at[s, lax.rem(d + ndp - j, ndp)], dps[j - 1])
            for j in range(1, ndp)
        ]

    def a_pass():
        for w in state["ad"]:
            w()
        state["ad4"] = [
            push(adall.at[s], adall.at[s], adall.at[seq_of[r]], seqs[r]) for r in range(3)
        ]

    def a_maps():
        for w in state["ad4"]:
            w()
        shuffle = unshuffle()
        for t in range(4):
            rows = mm(shuffle, adall[t].reshape(128, 512)).astype(BF)
            for b in range(8):
                piece = rows[16 * b : 16 * b + 16]
                at = b * 512
                nd = dn.shape[1] // 4
                nu = up.shape[1] // 4
                cut = min(max(nd - at, 0), 512)
                if cut:
                    dn[:, t * nd + at : t * nd + at + cut] = piece[:, :cut]
                if cut < 512:
                    b0 = t * nu + at + cut - nd
                    up[:, b0 : b0 + 512 - cut] = piece[:, cut:]

    def a_vec():
        for w in wait_vec:
            w()
        for t in range(4):
            vf[:, t * 256 : t * 256 + 256] = vall[t].astype(F32)

    def a_norm(slot):
        if slot < 2:
            (own_tok, tok_core)[slot]()
        else:
            for cp in tok_on:
                cp.wait_send() if slot == 2 else cp.wait_recv()
        if slot == 0:
            for w in wait_pos:
                w()
        xhat, _ = norm_parts(buf4[slot].astype(F32))
        buf4[slot] = (xhat * vf[0:1, :] + vf[1:2, :]).astype(BF)

    def a_wq():
        for p in groups[0]:
            p.arrive()
        late.append(keep(wq, wq_o))

    def role_cols(role):
        return pl.ds(pl.multiple_of((4 * (role // 2) + 2 * (role % 2) + c) * 256, 256), 256)

    def role_bias(role):
        lg = pl.multiple_of((2 * (role % 2) + c) * 256, 256)
        return vf[4 + role // 2 : 5 + role // 2, pl.ds(lg, 256)]

    def a_red(slot):
        red_o[slot] = mm_nt(buf4[slot], dn[:, :D]).astype(BF)

    def a_qkv(slot, first, last):
        tab = turns(pall[slot], table)
        cos, sin = tab[:, :128], tab[:, 128:]
        h, low = buf4[slot], red_o[slot]
        rows = pl.ds(slot * 512, 512)
        for role in range(first, last):
            val = mm(h, wq[role].reshape(D, 256)) + role_bias(role) + mm(low, up[:, role_cols(role)])
            cols = pl.ds((role % 2) * 256, 256)
            if role < 2:
                q[rows, cols] = (turn(val, cos, sin) * (LOG2E * HD**-0.5)).astype(BF)
            elif role < 4:
                kv[slot, :, (role % 2) * 256 : (role % 2) * 256 + 256] = turn(val, cos, sin).astype(BF)
            else:
                kv[slot, :, 512 + (role % 2) * 256 : 768 + (role % 2) * 256] = val.astype(BF)

    def a_keep():
        state["n1"] = keep(buf4, n1_o)
        state["q"] = keep(q, q_o)
        state["kv"] = [keep(kv.at[:, :, pl.ds(512 * i, 512)], (k_o, v_o)[i]) for i in range(2)]

    def a_att(pair, qb):
        lane_i = lax.broadcasted_iota(jnp.int32, (1, 128), 1)
        if "q" in state:
            state.pop("q")()
        cols = pl.ds(pair * 128, 128)
        rows = pl.ds(qb * QB, QB)
        ks, qs = kv[:, :, cols].reshape(-1, 128), q[rows, cols]
        vt = kv[:, :, pl.ds(512 + pair * 128, 128)].reshape(-1, 128).T
        outs = []
        for e in range(2):
            mine = (lane_i < 64) if e == 0 else (lane_i >= 64)
            st = mm_nt(ks, jnp.where(mine, qs, jnp.zeros_like(qs)))
            top = jnp.max(st, axis=0, keepdims=True)
            pr = jnp.exp2(st - top)
            total = jnp.sum(pr, axis=0, keepdims=True)
            outs.append(mm(vt[64 * e : 64 * e + 64], pr.astype(BF)) / total)
            lse_o[pair, e : e + 1, pl.ds(qb * QB, QB)] = top + jnp.log2(total)
        o[rows, cols] = jnp.concatenate(outs, axis=0).T.astype(BF)

    def a_swap():
        late.append(keep(o, o_o))
        state["att"] = []
        for lg in range(2):
            cols = pl.ds(lg * 256, 256)
            state["att"].append(keep(o.at[pl.ds(0, 512), cols], att.at[2 * lg + c]))
            state["att"].append(
                push(o.at[pl.ds(512, 512), cols], att.at[2 * lg + c], att.at[2 * lg + 1 - c], k.core)
            )

    def a_proj():
        for w in state["att"] + state["kv"]:
            w()
        own = keep(tok, n2s)
        own()
        for p in groups[1]:
            p.arrive()
        low = jnp.zeros((512, 16), F32)
        for g in range(4):
            low += mm_nt(att[g], dn[:, D + g * 256 : D + g * 256 + 256])
        low = low.astype(BF)
        r_p_s[...] = low
        for t in range(4):
            cols = pl.ds(t * 256, 256)
            val = mm(low, up[:, 3 * D + t * 256 : 3 * D + t * 256 + 256]) + vf[7:8, cols]
            for g in range(4):
                val += mm(att[g], wp[t // 2, t % 2, g].reshape(256, 256))
            res[:, cols] = n2s[:, cols].astype(F32) + val

    def a_norm2():
        xhat, _ = norm_parts(res[...])
        n2 = (xhat * vf[2:3, :] + vf[3:4, :]).astype(BF)
        n2s[...] = n2
        r_1_s[...] = mm_nt(n2, dn[:, 2 * D : 3 * D]).astype(BF)
        g_r2_s[...] = mm_nt(cot[...], up[:, 4 * D + FF :]).astype(BF)
        accs[...] = jnp.zeros_like(accs)
        gn2[...] = jnp.zeros_like(gn2)
        state["n1"]()

    def a_fc1(i):
        if i == 0:
            for p in groups[2]:
                p.arrive()
        t, h = i // 2, i % 2
        w = w1[t // 2, t % 2, :, :, :, h * 512 : h * 512 + 512].reshape(D, 512)
        bias = jnp.concatenate(
            [vf[9 + 2 * h + b : 10 + 2 * h + b, t * 256 : t * 256 + 256] for b in range(2)], axis=1
        )
        hid = mm(n2s[...], w) + bias
        hid += mm(r_1_s[...], up[:, 4 * D + i * 512 : 4 * D + i * 512 + 512])
        cdf = 0.5 * (1.0 + lax.erf(hid * (0.5**0.5)))
        a = (hid * cdf).astype(BF)
        sl = cdf + hid * jnp.exp(-0.5 * hid * hid) * 0.3989422804014327
        for j in range(4):
            buf4[j, :, i * 128 : i * 128 + 128] = a[:, j * 128 : j * 128 + 128]
            slope[j, :, i * 128 : i * 128 + 128] = sl[:, j * 128 : j * 128 + 128].astype(BF)

    def a_fc2(j):
        groups[3][j].arrive()
        a = buf4[j]
        hcols = [3 * D + i * 512 + j * 128 for i in range(8)]
        d2 = jnp.concatenate([dn[:, h : h + 128] for h in hcols], axis=1)
        low2 = mm_nt(a, d2)
        g = mm(g_r2_s[...], d2)
        for t in range(4):
            w = w2[t // 2, t % 2, :, :, j * 128 : j * 128 + 128, :].reshape(1024, 256)
            cols = pl.ds(t * 256, 256)
            accs[:, cols] += mm(a, w)
            g += mm_nt(cot[:, cols], w)
        gh = (g * slope[j].astype(F32)).astype(BF)
        w = jnp.concatenate(
            [
                w1[i // 4, (i // 2) % 2, :, :, :, (i % 2) * 512 + j * 128 : (i % 2) * 512 + j * 128 + 128].reshape(D, 128)
                for i in range(8)
            ],
            axis=1,
        )
        gn2[...] += mm_nt(gh, w)
        u1 = jnp.concatenate(
            [up[:, 4 * D + i * 512 + j * 128 : 4 * D + i * 512 + j * 128 + 128] for i in range(8)],
            axis=1,
        )
        low1 = mm_nt(gh, u1)
        state["r2"] = low2 if "r2" not in state else state["r2"] + low2
        state["g1"] = low1 if "g1" not in state else state["g1"] + low1
        ga2[j] = mm_tn(g_r2_s[...], a)
        gb1[j] = mm_tn(r_1_s[...], gh)

    def a_end():
        r_2, g_r1 = state["r2"].astype(BF), state["g1"].astype(BF)
        g_n2 = gn2[...] + mm(g_r1, dn[:, 2 * D : 3 * D])
        xhat, inv = norm_parts(res[...])
        g_res = cot[...].astype(F32) + norm_back(g_n2, xhat, inv, vf[2:3, :])
        gres[...] = g_res
        gb = g_res.astype(BF)
        g_rp = mm_nt(gb, up[:, 3 * D : 4 * D]).astype(BF)
        for g in range(4):
            gap[:, g * 256 : g * 256 + 256] = mm_tn(g_rp, att[g])
            val = mm(g_rp, dn[:, D + g * 256 : D + g * 256 + 256])
            for t in range(4):
                w = wp[t // 2, t % 2, g].reshape(256, 256)
                val += mm_nt(gb[:, t * 256 : t * 256 + 256], w)
            gatt[g] = val.astype(BF)
        waits = []
        for lg in range(2):
            cols = pl.ds(lg * 256, 256)
            top, low = pl.ds(0, 512), pl.ds(512, 512)
            waits.append(keep(gatt.at[2 * lg + c], do_o.at[top, cols]))
            waits.append(
                push(gatt.at[2 * lg + 1 - c], do_o.at[low, cols], do_o.at[low, cols], k.core)
            )
        u2 = up[:, 4 * D + FF :]
        out[...] = (res[...] + accs[...] + vf[8:9, :] + mm(r_2, u2)).astype(BF)
        gb2[...] = mm_tn(r_2, cot[...])
        ga1[...] = mm_tn(g_r1, n2s[...])
        gbp[...] = mm_tn(r_p_s[...], gb)
        for w in waits:
            w()

    acts = {
        "tok": a_tok, "tokfwd": a_tokfwd, "pick": a_pick, "pass": a_pass, "maps": a_maps, "vec": a_vec,
        "norm": a_norm, "wq": a_wq, "red": a_red, "qkv": a_qkv, "keep": a_keep, "att": a_att,
        "swap": a_swap, "proj": a_proj, "norm2": a_norm2, "fc1": a_fc1, "fc2": a_fc2, "end": a_end,
    }
    for name, *args in order:
        if isinstance(name, int):
            parts[name].step(args[0])
        else:
            acts[name](*args)
    for w in late:
        w()
    for p in parts:
        p.finish()
    assert k.nr <= NSEM[0] and k.nl <= NSEM[1]


def front(nz, cfg, tok, cot, qkv, proj, fc1, fc2, vecs, places, index, ad):
    anys, vm = pl.BlockSpec(memory_space=pl.ANY), pl.BlockSpec(memory_space=pltpu.VMEM)
    ndp = 2 * nz
    rows = tok.shape[0]
    nd, nu = 3 * D + FF, 5 * D + FF
    outs = [
        (vm, (rows, D), BF), (vm, (rows, D), F32), (anys, (2 * rows, 512), BF),
        (anys, (2 * rows, 512), BF), (anys, (4, rows, 512), BF), (anys, (4, rows, 512), BF),
        (anys, (2 * rows, 512), BF), (vm, (4, 2, 2 * rows), F32), (anys, (4, rows, D), BF),
        (vm, (4, rows, 16), BF), (anys, (6, nz, 2, qkv.shape[0], 256), BF), (vm, (16, nd), BF),
        (vm, (16, nu), BF), (vm, (4, 8, rows), F32), (vm, (ndp, 8, 128), F32),
        (vm, (16, D), F32), (vm, (16, D), F32), (vm, (16, D), F32), (vm, (4, 16, 1024), F32),
        (vm, (4, 16, 1024), F32), (vm, (16, D), F32), (anys, (2, nz, 2) + qkv.shape, BF),
    ]
    scratch = [
        ((4, rows, D), BF), ((6, nz, 2, qkv.shape[0], 256), BF),
        ((2, 2, nz, 2) + proj.shape, BF), ((2, 2, nz, 2) + fc1.shape, BF), ((2, 2, nz, 2) + fc2.shape, BF),
        ((2 * rows, 512), BF), ((4, rows, 1024), BF), ((4, rows, 256), BF), ((rows, D), F32),
        ((rows, D), F32), ((rows, D), BF), ((4, 16, 256), BF), ((16, D), F32),
        ((ndp, 16, 512), BF), ((4, ndp, 16, 512), BF), ((5, rows, 16), BF),
    ]
    return pl.pallas_call(
        functools.partial(front_kernel, nz, cfg),
        out_shape=[sds(sh, t) for _, sh, t in outs],
        in_specs=[anys, vm, anys, anys, anys, anys, vm, vm, vm, vm, vm],
        out_specs=[m for m, _, _ in outs],
        scratch_shapes=[pltpu.VMEM(sh, t) for sh, t in scratch]
        + [
            pltpu.SemaphoreType.DMA((NSEM[0],)),
            pltpu.SemaphoreType.DMA((NSEM[0],)),
            pltpu.SemaphoreType.DMA((NSEM[1],)),
        ],
        compiler_params=pltpu.CompilerParams(
            collective_id=0, has_side_effects=True, vmem_limit_bytes=VM
        ),
    )(tok, cot, qkv, proj, fc1, fc2, vecs, places, index, ad, jnp.asarray(row_table()))


SWAP = [(0, 1), (1, 0), (2, 3), (3, 2)]
CROSS = [(0, 2), (2, 0), (1, 3), (3, 1)]


def fast_shards(
    nz, tokens, positions, adapter_index, qkv_weight, proj_weight, fc1_weight, fc2_weight,
    vectors, fc1_bias, adapter_down, adapter_up, cotangent,
):
    core = lax.rem(lax.axis_index("seq"), 2)
    vecs = jnp.concatenate([vectors, fc1_bias.reshape(4, 256), jnp.zeros((3, 256), BF)], axis=0)
    places = jnp.pad(positions[:, 0].astype(F32), ((0, 5), (0, 0)))
    index = jnp.broadcast_to(adapter_index.astype(F32), (8, 128))
    rk, nd = adapter_down.shape[1:]
    ad = jnp.concatenate([adapter_down, adapter_up], axis=-1).reshape(NA, 16, 512)
    (output, gres, do, q, k, v, o, lse, n1, red, wq, dn, up, pall, idxs,
     gap, gbp, ga1, gb1, ga2, gb2, _) = front(
        nz, PLAN, tokens[0], cotangent[0], qkv_weight, proj_weight, fc1_weight, fc2_weight,
        vecs, places, index, ad,
    )
    wq = wq.reshape(6, D, 256)
    up6 = lax.dynamic_index_in_dim(
        jnp.moveaxis(up[:, : 3 * D].reshape(16, 6, 2, 256), 0, 2), core, 1, keepdims=False
    )
    k, v = k.reshape(-1, 512), v.reshape(-1, 512)
    dq, dk, dv = attend_back(q, do, o, k, v, lse)
    parts, gaq, gbq = local_call(
        qkv_back_body,
        [sds((4, 512, D), F32), sds((16, D), F32), sds((6, 16, 256), F32)],
        [pltpu.VMEM((6, 512, 256), BF)],
        dq, dk, dv, pall, jnp.asarray(row_table()), n1, red, wq, dn[:, :D], up6,
    )
    r13 = lax.ppermute(jnp.stack([parts[1], parts[3]]).astype(BF), "seq", SWAP)
    r2 = lax.ppermute((parts[2] + r13[1].astype(F32)).astype(BF), "seq", CROSS)
    g_n1 = parts[0] + r13[0].astype(F32) + r2.astype(F32)
    gain = lax.all_gather(vectors[0:1], "seq", axis=1, tiled=True).astype(F32)
    xhat, inv = norm_parts(tokens[0].astype(F32))
    input_grad = (gres + norm_back(g_n1, xhat, inv, gain)).astype(BF)
    gbq_full = jnp.zeros((6, 2, 16, 256), F32)
    gbq_full = lax.dynamic_update_index_in_dim(gbq_full, gbq[:, None], core, 1)
    gbq_full = jnp.moveaxis(gbq_full, 2, 0).reshape(16, 3 * D)

    def by_row(w):
        return jnp.transpose(w.reshape(4, 16, 8, 128), (1, 2, 0, 3)).reshape(16, FF)

    cd = jnp.concatenate([gaq, gap, ga1, by_row(ga2)], axis=1).astype(BF)
    cu = jnp.concatenate([gbq_full, gbp, by_row(gb1), gb2], axis=1).astype(BF)
    cd = lax.psum_scatter(cd, "seq", scatter_dimension=1, tiled=True)
    cu = lax.psum_scatter(cu, "seq", scatter_dimension=1, tiled=True)
    both = jnp.concatenate([cd, cu], axis=1)
    both = lax.all_to_all(both, "dp", 0, 0, tiled=True).reshape(-1, rk, both.shape[1])
    choose = idxs[:, 0, :1] == jnp.arange(NA, dtype=F32)[None, :]
    grads = jnp.sum(
        jnp.where(choose[:, :, None, None], both[:, None].astype(F32), 0.0), axis=0
    )
    return output[None], input_grad[None], grads[:, :, :nd], grads[:, :, nd:]


def solution(mesh):
    in_specs = (
        P("dp", "seq", None),
        P(None, "dp", "seq"),
        P("dp", None),
        P("dp", "seq"),
        P("dp", "seq"),
        P("dp", "seq"),
        P("dp", "seq"),
        P(None, "seq"),
        P("seq"),
        P(None, "dp", "seq"),
        P(None, "dp", "seq"),
        P("dp", "seq", None),
    )
    out_specs = (
        P("dp", "seq", None),
        P("dp", "seq", None),
        P(None, "dp", "seq"),
        P(None, "dp", "seq"),
    )
    body = shards
    if mesh.shape["seq"] == 4 and mesh.shape["dp"] == 8:

        def body(tokens, *rest):
            if tokens.shape[0] == 1 and tokens.shape[1] == 512:
                return fast_shards(mesh.shape["dp"] // 2, tokens, *rest)
            return shards(tokens, *rest)

    return jax.shard_map(body, mesh=mesh, in_specs=in_specs, out_specs=out_specs, check_vma=False)
```

```python
import functools
import math

import jax
import jax.numpy as jnp
import numpy as np
from jax import lax
from jax.experimental import pallas as pl
from jax.experimental.pallas import tpu as pltpu
from jax.sharding import PartitionSpec as P

D = 1024
HEADS = 16
HD = 64
FF = 4096
NA = 8


def layer_norm(values, gain_row, shift_row):
    centre = values - jnp.mean(values, axis=-1, keepdims=True)
    spread = jnp.mean(centre * centre, axis=-1, keepdims=True)
    return centre * lax.rsqrt(spread + 1e-06) * gain_row + shift_row


def rotate(values, places, direction):
    rot_span = 2 * (values.shape[-1] // 3 // 2)
    half_span = rot_span // 2
    inverse_freq = 10000.0 ** (-jnp.arange(half_span, dtype=jnp.float32) / half_span)
    pieces = []
    for axis_id in range(3):
        segment = values[..., axis_id * rot_span : (axis_id + 1) * rot_span]
        angles = places[axis_id].astype(jnp.float32)[..., None, None] * inverse_freq
        cosine = jnp.cos(angles)
        sine_wave = direction * jnp.sin(angles)
        lower_part = segment[..., :half_span]
        upper_part = segment[..., half_span:]
        pieces.append(lower_part * cosine - upper_part * sine_wave)
        pieces.append(lower_part * sine_wave + upper_part * cosine)
    pieces.append(values[..., 3 * rot_span :])
    return jnp.concatenate(pieces, axis=-1)


def exact_gelu(values):
    return jax.nn.gelu(values, approximate=False)


def fetch_weight(weight):
    joined = lax.all_gather(weight, "seq", axis=1, tiled=True)
    return lax.all_gather(joined, "dp", axis=0, tiled=True)


def adapted(inputs, weight, shift_row, down_part, up_part):
    base = jnp.einsum("cti,io->cto", inputs, weight, preferred_element_type=jnp.float32)
    reduced = jnp.einsum(
        "cti,cri->ctr", inputs, down_part, preferred_element_type=jnp.float32
    ).astype(jnp.bfloat16)
    result = (
        base
        + shift_row
        + jnp.einsum("ctr,cro->cto", reduced, up_part, preferred_element_type=jnp.float32)
    )
    return (result, reduced)


def adapted_back(grad_out, inputs, weight, down_part, up_part, reduced):
    grad_in = jnp.einsum("cto,io->cti", grad_out, weight, preferred_element_type=jnp.float32)
    grad_reduced = jnp.einsum(
        "cto,cro->ctr", grad_out, up_part, preferred_element_type=jnp.float32
    ).astype(jnp.bfloat16)
    grad_in = grad_in + jnp.einsum(
        "ctr,cri->cti", grad_reduced, down_part, preferred_element_type=jnp.float32
    )
    grad_down = jnp.einsum("ctr,cti->cri", grad_reduced, inputs, preferred_element_type=jnp.float32)
    grad_up = jnp.einsum("ctr,cto->cro", reduced, grad_out, preferred_element_type=jnp.float32)
    return (grad_in, grad_down, grad_up)


def split_tokens(source, split_count):
    old_shape = source.shape
    shaped = source.reshape(
        (old_shape[0], split_count, old_shape[1] // split_count) + old_shape[2:]
    )
    return jnp.moveaxis(shaped, 1, 0)


def score_grads(
    query_block, key_block, value_block, grad_block, log_block, delta_block, score_scale
):
    scores = (
        jnp.einsum("cqhd,ckhd->chqk", query_block, key_block, preferred_element_type=jnp.float32)
        * score_scale
    )
    probabilities = jnp.exp(scores - log_block[..., None])
    grad_probs = jnp.einsum(
        "cqhd,ckhd->chqk", grad_block, value_block, preferred_element_type=jnp.float32
    )
    grad_scores = (probabilities * (grad_probs - delta_block[..., None])).astype(jnp.bfloat16)
    return (probabilities.astype(jnp.bfloat16), grad_scores)


def shards(
    tokens,
    positions,
    adapter_index,
    qkv_weight,
    proj_weight,
    fc1_weight,
    fc2_weight,
    vectors,
    fc1_bias,
    adapter_down,
    adapter_up,
    cotangent,
):
    clip_count, tok_count = (tokens.shape[0], tokens.shape[1])
    head_shape = (clip_count, tok_count, HEADS, HD)
    score_scale = HD ** (-0.5)
    small_parts = (
        lax.all_gather(adapter_down, "seq", axis=2, tiled=True),
        lax.all_gather(adapter_up, "seq", axis=2, tiled=True),
        lax.all_gather(vectors, "seq", axis=1, tiled=True),
        lax.all_gather(fc1_bias, "seq", axis=0, tiled=True),
    )
    down_all, up_all = (
        lax.all_gather(small_parts[0], "dp", axis=1, tiled=True),
        lax.all_gather(small_parts[1], "dp", axis=1, tiled=True),
    )
    vector_rows = small_parts[2].astype(jnp.float32)
    hidden_bias = small_parts[3].astype(jnp.float32)
    choose = (adapter_index == jnp.arange(NA, dtype=jnp.int32)[None, :]).astype(jnp.bfloat16)
    down_sel = jnp.einsum(
        "ca,ari->cri", choose, down_all, preferred_element_type=jnp.float32
    ).astype(jnp.bfloat16)
    up_sel = jnp.einsum("ca,aro->cro", choose, up_all, preferred_element_type=jnp.float32).astype(
        jnp.bfloat16
    )
    down_parts = (
        down_sel[:, :, :D],
        down_sel[:, :, D : 2 * D],
        down_sel[:, :, 2 * D : 3 * D],
        down_sel[:, :, 3 * D :],
    )
    up_parts = (
        up_sel[:, :, : 3 * D],
        up_sel[:, :, 3 * D : 4 * D],
        up_sel[:, :, 4 * D : 4 * D + FF],
        up_sel[:, :, 4 * D + FF :],
    )
    inputs = tokens.astype(jnp.float32)
    normed_one = layer_norm(inputs, vector_rows[0], vector_rows[1]).astype(jnp.bfloat16)
    weight_qkv = fetch_weight(qkv_weight)
    mixed_qkv, reduced_qkv = adapted(
        normed_one, weight_qkv, vector_rows[4:7].reshape(3 * D), down_parts[0], up_parts[0]
    )
    queries = rotate(mixed_qkv[..., :D].reshape(head_shape), positions, 1.0).astype(jnp.bfloat16)
    keys_local = rotate(mixed_qkv[..., D : 2 * D].reshape(head_shape), positions, 1.0).astype(
        jnp.bfloat16
    )
    values_local = mixed_qkv[..., 2 * D :].reshape(head_shape).astype(jnp.bfloat16)
    stat_shape = (clip_count, HEADS, tok_count)
    start_state = (
        jnp.full(stat_shape, -jnp.inf, jnp.float32),
        jnp.zeros(stat_shape, jnp.float32),
        jnp.zeros(stat_shape + (HD,), jnp.float32),
    )
    key_piece = lax.all_gather(keys_local, "seq", axis=1, tiled=True)
    value_piece = lax.all_gather(values_local, "seq", axis=1, tiled=True)
    split_count = key_piece.shape[1] // math.gcd(key_piece.shape[1], 256)

    def inner_step(running, block_pair):
        top_score, row_total, weighted = running
        key_block, value_block = block_pair
        scores = (
            jnp.einsum("cqhd,ckhd->chqk", queries, key_block, preferred_element_type=jnp.float32)
            * score_scale
        )
        new_top = jnp.maximum(top_score, jnp.max(scores, axis=-1))
        factor = jnp.exp(top_score - new_top)
        weights = jnp.exp(scores - new_top[..., None])
        row_total = row_total * factor + jnp.sum(weights, axis=-1)
        weighted = weighted * factor[..., None] + jnp.einsum(
            "chqk,ckhd->chqd",
            weights.astype(jnp.bfloat16),
            value_block,
            preferred_element_type=jnp.float32,
        )
        return ((new_top, row_total, weighted), None)

    result, unused = lax.scan(
        inner_step,
        start_state,
        (split_tokens(key_piece, split_count), split_tokens(value_piece, split_count)),
    )
    top_score, row_total, weighted = result
    log_total = top_score + jnp.log(row_total)
    heads_tok = jnp.swapaxes(weighted / row_total[..., None], 1, 2)
    attended = heads_tok.reshape(clip_count, tok_count, D).astype(jnp.bfloat16)
    weight_proj = fetch_weight(proj_weight)
    projected, reduced_proj = adapted(
        attended, weight_proj, vector_rows[7], down_parts[1], up_parts[1]
    )
    residual = inputs + projected
    normed_two = layer_norm(residual, vector_rows[2], vector_rows[3]).astype(jnp.bfloat16)
    weight_up = fetch_weight(fc1_weight)
    hidden, reduced_up = adapted(normed_two, weight_up, hidden_bias, down_parts[2], up_parts[2])
    activated = exact_gelu(hidden).astype(jnp.bfloat16)
    weight_down = fetch_weight(fc2_weight)
    branch, reduced_down = adapted(
        activated, weight_down, vector_rows[8], down_parts[3], up_parts[3]
    )
    output = (residual + branch).astype(jnp.bfloat16)
    weight_down = fetch_weight(fc2_weight)
    grad_act, gdown_four, gup_four = adapted_back(
        cotangent, activated, weight_down, down_parts[3], up_parts[3], reduced_down
    )
    unused, gelu_back = jax.vjp(exact_gelu, hidden)
    grad_hidden = gelu_back(grad_act)[0].astype(jnp.bfloat16)
    weight_up = fetch_weight(fc1_weight)
    grad_normed_two, gdown_three, gup_three = adapted_back(
        grad_hidden, normed_two, weight_up, down_parts[2], up_parts[2], reduced_up
    )

    def norm_two(values):
        return layer_norm(values, vector_rows[2], vector_rows[3])

    unused, norm_two_back = jax.vjp(norm_two, residual)
    grad_residual = cotangent.astype(jnp.float32) + norm_two_back(grad_normed_two)[0]
    weight_proj = fetch_weight(proj_weight)
    grad_attended, gdown_two, gup_two = adapted_back(
        grad_residual.astype(jnp.bfloat16),
        attended,
        weight_proj,
        down_parts[1],
        up_parts[1],
        reduced_proj,
    )
    grad_tok = grad_attended.astype(jnp.bfloat16).reshape(head_shape)
    delta_heads = jnp.swapaxes(jnp.sum(grad_tok.astype(jnp.float32) * heads_tok, axis=-1), 1, 2)
    whole_keys, whole_values = (
        lax.all_gather(keys_local, "seq", axis=1, tiled=True),
        lax.all_gather(values_local, "seq", axis=1, tiled=True),
    )
    block_count = whole_keys.shape[1] // math.gcd(whole_keys.shape[1], 256)
    key_blocks = split_tokens(whole_keys, block_count)
    value_blocks = split_tokens(whole_values, block_count)
    zero_heads = jnp.zeros(head_shape, jnp.float32)

    def back_step(grad_query, block_pair):
        key_block, value_block = block_pair
        probs_low, grad_scores = score_grads(
            queries, key_block, value_block, grad_tok, log_total, delta_heads, score_scale
        )
        grad_query = (
            grad_query
            + jnp.einsum(
                "chqk,ckhd->cqhd", grad_scores, key_block, preferred_element_type=jnp.float32
            )
            * score_scale
        )
        grad_key = (
            jnp.einsum("chqk,cqhd->ckhd", grad_scores, queries, preferred_element_type=jnp.float32)
            * score_scale
        )
        grad_value = jnp.einsum(
            "chqk,cqhd->ckhd", probs_low, grad_tok, preferred_element_type=jnp.float32
        )
        return (grad_query, jnp.concatenate([grad_key, grad_value], axis=-1))

    grad_query, key_terms = lax.scan(back_step, zero_heads, (key_blocks, value_blocks))
    key_terms = jnp.moveaxis(key_terms, 0, 1).reshape(
        clip_count, whole_keys.shape[1], HEADS, 2 * HD
    )
    summed = lax.psum_scatter(
        key_terms.astype(jnp.bfloat16), "seq", scatter_dimension=1, tiled=True
    ).astype(jnp.float32)
    grad_key = summed[..., :HD]
    grad_value = summed[..., HD:]
    grad_mixed = jnp.concatenate(
        [
            rotate(grad_query, positions, -1.0).reshape(clip_count, tok_count, D),
            rotate(grad_key, positions, -1.0).reshape(clip_count, tok_count, D),
            grad_value.reshape(clip_count, tok_count, D),
        ],
        axis=-1,
    ).astype(jnp.bfloat16)
    weight_qkv = fetch_weight(qkv_weight)
    grad_normed_one, gdown_one, gup_one = adapted_back(
        grad_mixed, normed_one, weight_qkv, down_parts[0], up_parts[0], reduced_qkv
    )

    def norm_one(values):
        return layer_norm(values, vector_rows[0], vector_rows[1])

    unused, norm_one_back = jax.vjp(norm_one, inputs)
    input_grad = (grad_residual + norm_one_back(grad_normed_one)[0]).astype(jnp.bfloat16)
    choose_wide = choose.astype(jnp.float32)
    clip_down = jnp.concatenate([gdown_one, gdown_two, gdown_three, gdown_four], axis=-1)
    clip_up = jnp.concatenate([gup_one, gup_two, gup_three, gup_four], axis=-1)
    down_term = jnp.einsum("ca,cri->ari", choose_wide, clip_down, precision=lax.Precision.HIGHEST)
    up_term = jnp.einsum("ca,cro->aro", choose_wide, clip_up, precision=lax.Precision.HIGHEST)
    down_grad, up_grad = (
        lax.psum_scatter(
            down_term.astype(jnp.bfloat16), "seq", scatter_dimension=2, tiled=True
        ).astype(jnp.float32),
        lax.psum_scatter(
            up_term.astype(jnp.bfloat16), "seq", scatter_dimension=2, tiled=True
        ).astype(jnp.float32),
    )
    down_grad, up_grad = (
        lax.psum_scatter(
            down_grad.astype(jnp.bfloat16), "dp", scatter_dimension=1, tiled=True
        ).astype(jnp.float32),
        lax.psum_scatter(
            up_grad.astype(jnp.bfloat16), "dp", scatter_dimension=1, tiled=True
        ).astype(jnp.float32),
    )
    return (output, input_grad, down_grad, up_grad)

MESH = pl.DeviceIdType.MESH
BF = jnp.bfloat16
F32 = jnp.float32
LOG2E = 1.4426950408889634
LN2 = 0.6931471805599453
VM = 60 * 1024 * 1024


def mm(a, b):
    return lax.dot_general(a, b, (((1,), (0,)), ((), ())), preferred_element_type=F32)


def mm_nt(a, b):
    return lax.dot_general(a, b, (((1,), (1,)), ((), ())), preferred_element_type=F32)


def mm_tn(a, b):
    return lax.dot_general(a, b, (((0,), (0,)), ((), ())), preferred_element_type=F32)


class Links:
    def __init__(self, ssem, rsem, lsem, nz):
        self.ssem, self.rsem, self.lsem = ssem, rsem, lsem
        self.nr, self.nl = 0, 0
        d, s = lax.axis_index("dp"), lax.axis_index("seq")
        self.d, self.s, self.nz = d, s, nz
        self.z, self.y, self.x, self.c = d // 2, lax.rem(d, 2), s // 2, lax.rem(s, 2)
        self.core = (d, s + 1 - 2 * self.c)
        self.xn = (d, s + 2 - 4 * self.x)
        self.diag = (d, 3 - s)
        self.yn = (d + 1 - 2 * self.y, s)
        self.up, self.down = (d + 2, s), (d - 2, s)
        self.zpeer = [(lax.rem(d + 2 * j, 2 * nz), s) for j in range(nz)]

    def barrier(self, peers):
        bar = pltpu.get_barrier_semaphore()
        for dev in peers:
            pl.semaphore_signal(bar, inc=1, device_id=dev, device_id_type=MESH)
        pl.semaphore_wait(bar, len(peers))

    def new(self, count=1):
        self.nr += count
        return self.nr - count

    def newl(self):
        self.nl += 1
        return self.nl - 1

    def remote(self, i, src, dst, dev):
        return pltpu.make_async_remote_copy(
            src_ref=src,
            dst_ref=dst,
            send_sem=self.ssem.at[i],
            recv_sem=self.rsem.at[i],
            device_id=dev,
            device_id_type=MESH,
        )

    def local(self, i, src, dst):
        return pltpu.make_async_copy(src, dst, self.lsem.at[i])


def guard(cond, body):
    if cond is None:
        body()
    else:
        pl.when(cond)(body)


class Part:
    def __init__(self, links, order, own, region, handover):
        self.k, self.order, self.own = links, order, own
        self.region, self.handover = region, handover
        k = links
        self.s_own = k.newl()
        n = k.nz - 1
        self.s_z = k.new(2 * n if order == "xyz" else n)
        self.s_f, self.s_g1, self.s_g2 = k.new(), k.new(), k.new()
        self.pend, self.tail = [], []
        xfirst = order != "zyx"
        self.f, self.g = (k.x, k.y) if xfirst else (k.y, k.x)
        self.fd, self.gd = (k.xn, k.yn) if xfirst else (k.yn, k.xn)

    def reg(self, fi, gi, zs):
        return self.region(gi, zs, fi) if self.order == "zyx" else self.region(fi, zs, gi)

    def hand(self, cond, fi, zs, gi):
        k = self.k
        x, y = (gi, fi) if self.order == "zyx" else (fi, gi)
        loc, rem = self.handover(x, zs, y)
        ls = [(k.newl(), a, b) for a, b in loc]
        rs = [(k.new(), a, b, w) for a, b, w in rem]

        def start():
            for i, a, b in ls:
                k.local(i, a, b).start()
            for i, a, b, _ in rs:
                k.remote(i, a, b, k.core).start()

        def arrive():
            for i, a, b in ls:
                k.local(i, a, b).wait()
            for i, a, b, w in rs:
                k.remote(i, a, w, k.core).wait_recv()

        def sent():
            for i, a, b, _ in rs:
                k.remote(i, a, b, k.core).wait_send()

        guard(cond, start)
        self.pend.append((cond, arrive))
        self.tail.append((cond, sent))

    def go(self, cond, copy):
        guard(cond, copy.start)
        self.tail.append((cond, copy.wait_send))

    def step(self, name):
        getattr(self, ("l_" if self.order == "xyz" else "z_") + name)()

    def z_s(self):
        k, f, g = self.k, self.f, self.g
        k.local(self.s_own, self.own, self.reg(f, g, k.z)).start()
        for j in range(1, k.nz):
            self.go(None, k.remote(self.s_z + j - 1, self.own, self.reg(f, g, k.z), k.zpeer[j]))

    def z_m(self):
        k, f, g = self.k, self.f, self.g
        al = slice(None)
        for j in range(1, k.nz):
            at = self.reg(f, g, lax.rem(k.z + k.nz - j, k.nz))
            k.remote(self.s_z + j - 1, self.own, at, k.zpeer[j]).wait_recv()
        k.local(self.s_own, self.own, self.reg(f, g, k.z)).wait()
        mine = self.reg(f, g, al)
        self.go(None, k.remote(self.s_f, mine, mine, self.fd))
        self.go(None, k.remote(self.s_g1, mine, mine, self.gd))
        self.hand(None, f, al, g)

    def z_f(self):
        k, f, g = self.k, self.f, self.g
        al = slice(None)
        new = self.reg(1 - f, g, al)
        k.remote(self.s_f, new, new, self.fd).wait_recv()
        self.go(None, k.remote(self.s_g2, new, new, self.gd))
        self.hand(None, 1 - f, al, g)

    def z_g1(self):
        k, f, g = self.k, self.f, self.g
        al = slice(None)
        new = self.reg(f, 1 - g, al)
        k.remote(self.s_g1, new, new, self.gd).wait_recv()
        self.hand(None, f, al, 1 - g)

    def z_g2(self):
        k, f, g = self.k, self.f, self.g
        al = slice(None)
        new = self.reg(1 - f, 1 - g, al)
        k.remote(self.s_g2, new, new, self.gd).wait_recv()
        self.hand(None, 1 - f, al, 1 - g)

    def l_s(self):
        k, f, g, z = self.k, self.f, self.g, self.k.z
        k.local(self.s_own, self.own, self.reg(f, g, z)).start()
        self.go(None, k.remote(self.s_f, self.own, self.reg(f, g, z), self.fd))
        self.go(None, k.remote(self.s_g1, self.own, self.reg(f, g, z), self.gd))

    def l_f(self):
        k, f, g, z = self.k, self.f, self.g, self.k.z
        new = self.reg(1 - f, g, z)
        k.remote(self.s_f, self.own, new, self.fd).wait_recv()
        self.go(None, k.remote(self.s_g2, new, new, self.gd))

    def l_m(self):
        k, f, g, z = self.k, self.f, self.g, self.k.z
        al = slice(None)
        k.remote(self.s_g1, self.own, self.reg(f, 1 - g, z), self.gd).wait_recv()
        new = self.reg(1 - f, 1 - g, z)
        k.remote(self.s_g2, new, new, self.gd).wait_recv()
        k.local(self.s_own, self.own, self.reg(f, g, z)).wait()
        four = self.reg(al, al, z)
        self.go(z < k.nz - 1, k.remote(self.s_z, four, four, k.up))
        self.go(z > 0, k.remote(self.s_z + k.nz - 1, four, four, k.down))
        self.hand(None, al, z, al)

    def relay(self, r):
        k, z = self.k, self.k.z
        al = slice(None)
        for sem, here, origin, dev, can in (
            (self.s_z, z > r, z - 1 - r, k.up, z < k.nz - 1),
            (self.s_z + k.nz - 1, z + r < k.nz - 1, z + 1 + r, k.down, z > 0),
        ):
            four = self.reg(al, al, origin)
            guard(here, k.remote(sem + r, four, four, dev).wait_recv)
            if r < k.nz - 2:
                self.go(jnp.logical_and(here, can), k.remote(sem + r + 1, four, four, dev))
            self.hand(here, al, origin, al)

    def l_r0(self):
        self.relay(0)

    def l_r1(self):
        self.relay(1)

    def l_r2(self):
        self.relay(2)

    def arrive(self):
        for cond, body in self.pend:
            guard(cond, body)

    def finish(self):
        for cond, body in self.tail:
            guard(cond, body)


def wide_parts(links, shard, buf, cuts):
    c = links.c
    parts = []
    for r0, n, order in cuts:
        rows = pl.ds(r0, n)

        def region(x, z, y, rows=rows):
            return buf.at[x, c, z, y, rows]

        def handover(x, z, y, rows=rows):
            at = buf.at[x, c, z, y, rows]
            return [], [(at, at, buf.at[x, 1 - c, z, y, rows])]

        parts.append(Part(links, order, shard.at[rows], region, handover))
    return parts


def qkv_parts(links, shard, lane, buf, cuts):
    c = links.c
    parts = []
    for r0, n, order in cuts:
        rows = pl.ds(r0, n)

        def region(x, z, y, rows=rows):
            return lane.at[x, z, y, rows]

        def handover(x, z, y, rows=rows):
            loc, rem = [], []
            for xx in (0, 1) if isinstance(x, slice) else (x,):
                for col, role in ((0, 3 * xx + c), (512, 3 * xx + c + 1)):
                    loc.append((lane.at[xx, z, y, rows, pl.ds(col, 256)], buf.at[role, z, y, rows]))
                rem.append(
                    (
                        lane.at[xx, z, y, rows, pl.ds(256, 256)],
                        buf.at[3 * xx + 2 * c, z, y, rows],
                        buf.at[3 * xx + 2 - 2 * c, z, y, rows],
                    )
                )
            return loc, rem

        parts.append(Part(links, order, shard.at[rows], region, handover))
    return parts


def norm_parts(values):
    centre = values - jnp.mean(values, axis=-1, keepdims=True)
    inv = lax.rsqrt(jnp.mean(centre * centre, axis=-1, keepdims=True) + 1e-06)
    return centre * inv, inv


def swap_pairs(v):
    n = v.shape[1]
    j = lax.rem(lax.broadcasted_iota(jnp.int32, (1, n), 1), HD)
    lower = lax.rem(j, 20) < 10
    return jnp.where(lower, pltpu.roll(v, n - 10, 1), pltpu.roll(v, 10, 1))


def turn(v, cos, sin):
    cc, ss = jnp.concatenate([cos, cos], axis=1), jnp.concatenate([sin, sin], axis=1)
    return v * cc + swap_pairs(v) * ss


def norm_back(grad, xhat, inv, gain):
    q = grad * gain
    return inv * (
        q - jnp.mean(q, axis=-1, keepdims=True) - xhat * jnp.mean(q * xhat, axis=-1, keepdims=True)
    )


def sds(shape, dtype):
    return jax.ShapeDtypeStruct(shape, dtype)


PLAN = (
    (((0, 48, 'zxy'), (48, 48, 'zxy'), (96, 32, 'xyz')), ((0, 128, 'zxy'),), ((0, 32, 'zxy'), (32, 32, 'zyx'), (64, 32, 'xyz'), (96, 32, 'zxy')), ((0, 128, 'xyz'), (128, 128, 'zxy'), (256, 128, 'zyx'), (384, 128, 'zxy'))),
    (
        (0, 's'), (1, 's'), (2, 's'), ('tok', 1), ('vec',), ('norm', 0), ('pick',), (3, 's'), (2, 'f'),
        ('pass',), (2, 'm'), ('maps',), ('norm', 1), ('red', 0), ('red', 1), ('tok', 0), (0, 'm'), (6, 's'),
        ('tokfwd', 1), (1, 'm'), (0, 'f'), (0, 'g1'), (2, 'r0'), (4, 's'), (7, 's'), (1, 'f'), (1, 'g1'),
        (8, 's'), (3, 'm'), (5, 's'), (0, 'g2'), (2, 'r1'), (10, 's'), (2, 'r2'), ('tokfwd', 0), ('norm', 2),
        (6, 'f'), (4, 'm'), (1, 'g2'), ('norm', 3), ('red', 2), ('red', 3), (9, 's'), ('wq',),
        ('qkv', 0, 0, 2), ('qkv', 0, 2, 4), ('qkv', 0, 4, 6), (3, 'f'), (3, 'g1'), ('qkv', 1, 0, 2),
        ('qkv', 1, 2, 4), (8, 'f'), ('qkv', 1, 4, 6), (7, 'm'), ('qkv', 2, 2, 4), ('qkv', 2, 4, 6),
        ('qkv', 3, 2, 4), ('qkv', 3, 4, 6), ('keep',), ('att', 0, 0), (6, 'm'), ('att', 0, 1), (4, 'f'),
        (5, 'm'), (4, 'g1'), ('att', 0, 2), ('att', 0, 3), (7, 'f'), (10, 'm'), ('att', 1, 0), ('att', 1, 1),
        (3, 'g2'), (8, 'm'), ('att', 1, 2), (6, 'r0'), (11, 's'), (7, 'g1'), ('att', 1, 3), ('att', 2, 0),
        (9, 'm'), ('att', 2, 1), ('att', 2, 2), (4, 'g2'), (6, 'r1'), ('att', 2, 3), (9, 'f'), (5, 'f'),
        (5, 'g1'), ('att', 3, 0), ('att', 3, 1), (8, 'r0'), ('att', 3, 2), (5, 'g2'), (7, 'g2'),
        ('att', 3, 3), (6, 'r2'), ('swap',), ('proj',), (10, 'f'), (10, 'g1'), ('norm2',), (11, 'm'),
        ('fc1', 0), ('fc1', 1), (9, 'g1'), (10, 'g2'), ('fc1', 2), ('fc1', 3), (8, 'r1'), ('fc1', 4),
        (9, 'g2'), ('fc1', 5), (11, 'f'), ('fc1', 6), (8, 'r2'), ('fc1', 7), (11, 'g1'), ('fc2', 2),
        ('fc2', 1), (11, 'g2'), ('fc2', 0), ('fc2', 3), ('end',),
    ),
)
QB = 256
NSEM = (230, 90)


def row_table():
    half = 10
    freq = 10000.0 ** (-np.arange(half) / half)
    ang = np.arange(16)[:, None] * freq
    whole = np.zeros((48, 256))
    for p in range(3):
        rows = slice(16 * p, 16 * p + 16)
        for head in range(2):
            at = head * HD + p * 2 * half
            whole[rows, at : at + half] = np.cos(ang)
            whole[rows, at + half : at + 2 * half] = np.cos(ang)
            whole[rows, 128 + at : 128 + at + half] = -np.sin(ang)
            whole[rows, 128 + at + half : 128 + at + 2 * half] = np.sin(ang)
    for head in range(2):
        whole[:16, head * HD + 60 : head * HD + HD] = 1.0
    whole = whole.astype(np.float32)
    pieces = []
    for _ in range(3):
        piece = whole.astype(BF)
        pieces.append(np.asarray(piece))
        whole = whole - piece.astype(np.float32)
    return np.stack(pieces)


def turns(places, table):
    level = lax.broadcasted_iota(jnp.int32, (16, places.shape[1]), 0).astype(F32)
    hot = jnp.concatenate([(level == places[p : p + 1]).astype(F32) for p in range(3)], axis=0)
    hot = hot.astype(BF)
    return mm_tn(hot, table[0]) + mm_tn(hot, table[1]) + mm_tn(hot, table[2])


def unshuffle():
    i = lax.broadcasted_iota(jnp.int32, (128, 128), 0)
    j = lax.broadcasted_iota(jnp.int32, (128, 128), 1)
    k, dp, r = i // 16, lax.rem(i, 16) // 2, lax.rem(i, 2)
    return (j == dp * 16 + r * 8 + k).astype(F32).astype(BF)


def front_kernel(nz, cfg, *refs):
    (tok, cot, qkv, proj, fc1, fc2, vecs, places, index, ad, table) = refs[:11]
    (out, gres, do_o, q_o, k_o, v_o, o_o, lse_o, n1_o, red_o, wq_o, dn, up, pall, idxs,
     gap, gbp, ga1, gb1, ga2, gb2, lane, vf) = refs[11:34]
    (buf4, wq, wp, w1, w2, q, kv, att, accs, res, n2s,
     vall, selb, adall, small, ssem, rsem, lsem) = refs[34:]
    (r_p_s, r_1_s, g_r2_s, r_2_s, g_r1_s) = [small.at[i] for i in range(5)]
    k = Links(ssem, rsem, lsem, nz)
    c, d, s = k.c, k.d, k.s
    ndp = 2 * nz
    slope, o, gatt, gn2 = kv, q, att, gres
    seqs = [k.core, k.xn, k.diag]
    dps = [(lax.rem(d + j, ndp), s) for j in range(1, ndp)]
    k.barrier(seqs + [k.yn] + [p for p in dps])
    late = []

    def push(src, dst, land, dev):
        i = k.new()
        cp = k.remote(i, src, dst, dev)
        cp.start()
        late.append(cp.wait_send)
        return k.remote(i, src, land, dev).wait_recv

    def send_later(src, dst, land, dev):
        i = k.new()
        cp = k.remote(i, src, dst, dev)

        def start():
            cp.start()
            late.append(cp.wait_send)

        return start, k.remote(i, src, land, dev).wait_recv

    def keep(src, dst):
        i = k.newl()
        cp = k.local(i, src, dst)
        cp.start()
        return cp.wait

    idxs[d] = index[...]
    wait_idx = [
        push(index, idxs.at[d], idxs.at[lax.rem(d + ndp - j, ndp)], dps[j - 1])
        for j in range(1, ndp)
    ]
    vall[s] = vecs[...]
    seq_of = [s + 1 - 2 * c, s + 2 - 4 * k.x, 3 - s]
    wait_vec = [push(vecs, vall.at[s], vall.at[seq_of[r]], seqs[r]) for r in range(3)]
    pall[0] = places[...]
    wait_pos = [push(places, pall.at[r + 1], pall.at[r + 1], seqs[r]) for r in range(3)]
    own_tok = keep(tok, buf4.at[0])
    tok_core = push(tok, buf4.at[1], buf4.at[1], k.core)
    halves = [pl.ds(0, 256), pl.ds(256, 256)]
    tok_x = [send_later(tok.at[h], buf4.at[2, h], buf4.at[2, h], k.xn) for h in halves]
    tok_on = [k.remote(k.new(), buf4.at[2, h], buf4.at[3, h], k.core) for h in halves]
    cuts, order = cfg
    parts = (
        qkv_parts(k, qkv, lane, wq, cuts[0])
        + wide_parts(k, proj, wp, cuts[1])
        + wide_parts(k, fc1, w1, cuts[2])
        + wide_parts(k, fc2, w2, cuts[3])
    )
    groups = []
    n = 0
    for cs in cuts:
        groups.append(parts[n : n + len(cs)])
        n += len(cs)
    state = {}

    def a_tok(h):
        tok_x[h][0]()

    def a_tokfwd(h):
        tok_x[h][1]()
        tok_on[h].start()

    def a_pick():
        for w in wait_idx:
            w()
        for j in range(ndp):
            dest = lax.rem(d + j, ndp)
            who = idxs[dest]
            total = jnp.zeros((16, 512), F32)
            for a in range(NA):
                total += jnp.where(who[0:1, 0:1] == float(a), ad[a].astype(F32), 0.0)
            selb[j] = total.astype(BF)
        adall[s, d] = selb[0]
        state["ad"] = [
            push(selb.at[j], adall.at[s, d], adall.at[s, lax.rem(d + ndp - j, ndp)], dps[j - 1])
            for j in range(1, ndp)
        ]

    def a_pass():
        for w in state["ad"]:
            w()
        state["ad4"] = [
            push(adall.at[s], adall.at[s], adall.at[seq_of[r]], seqs[r]) for r in range(3)
        ]

    def a_maps():
        for w in state["ad4"]:
            w()
        shuffle = unshuffle()
        for t in range(4):
            rows = mm(shuffle, adall[t].reshape(128, 512)).astype(BF)
            for b in range(8):
                piece = rows[16 * b : 16 * b + 16]
                at = b * 512
                nd = dn.shape[1] // 4
                nu = up.shape[1] // 4
                cut = min(max(nd - at, 0), 512)
                if cut:
                    dn[:, t * nd + at : t * nd + at + cut] = piece[:, :cut]
                if cut < 512:
                    b0 = t * nu + at + cut - nd
                    up[:, b0 : b0 + 512 - cut] = piece[:, cut:]

    def a_vec():
        for w in wait_vec:
            w()
        for t in range(4):
            vf[:, t * 256 : t * 256 + 256] = vall[t].astype(F32)

    def a_norm(slot):
        if slot < 2:
            (own_tok, tok_core)[slot]()
        else:
            for cp in tok_on:
                cp.wait_send() if slot == 2 else cp.wait_recv()
        if slot == 0:
            for w in wait_pos:
                w()
        xhat, _ = norm_parts(buf4[slot].astype(F32))
        buf4[slot] = (xhat * vf[0:1, :] + vf[1:2, :]).astype(BF)

    def a_wq():
        for p in groups[0]:
            p.arrive()
        late.append(keep(wq, wq_o))

    def role_cols(role):
        return pl.ds(pl.multiple_of((4 * (role // 2) + 2 * (role % 2) + c) * 256, 256), 256)

    def role_bias(role):
        lg = pl.multiple_of((2 * (role % 2) + c) * 256, 256)
        return vf[4 + role // 2 : 5 + role // 2, pl.ds(lg, 256)]

    def a_red(slot):
        red_o[slot] = mm_nt(buf4[slot], dn[:, :D]).astype(BF)

    def a_qkv(slot, first, last):
        tab = turns(pall[slot], table)
        cos, sin = tab[:, :128], tab[:, 128:]
        h, low = buf4[slot], red_o[slot]
        rows = pl.ds(slot * 512, 512)
        for role in range(first, last):
            val = mm(h, wq[role].reshape(D, 256)) + role_bias(role) + mm(low, up[:, role_cols(role)])
            cols = pl.ds((role % 2) * 256, 256)
            if role < 2:
                q[rows, cols] = (turn(val, cos, sin) * (LOG2E * HD**-0.5)).astype(BF)
            elif role < 4:
                kv[slot, :, (role % 2) * 256 : (role % 2) * 256 + 256] = turn(val, cos, sin).astype(BF)
            else:
                kv[slot, :, 512 + (role % 2) * 256 : 768 + (role % 2) * 256] = val.astype(BF)

    def a_keep():
        state["n1"] = keep(buf4, n1_o)
        state["q"] = keep(q, q_o)
        state["kv"] = [keep(kv.at[:, :, pl.ds(512 * i, 512)], (k_o, v_o)[i]) for i in range(2)]

    def a_att(pair, qb):
        lane_i = lax.broadcasted_iota(jnp.int32, (1, 128), 1)
        if "q" in state:
            state.pop("q")()
        cols = pl.ds(pair * 128, 128)
        rows = pl.ds(qb * QB, QB)
        ks, qs = kv[:, :, cols].reshape(-1, 128), q[rows, cols]
        vt = kv[:, :, pl.ds(512 + pair * 128, 128)].reshape(-1, 128).T
        outs = []
        for e in range(2):
            mine = (lane_i < 64) if e == 0 else (lane_i >= 64)
            st = mm_nt(ks, jnp.where(mine, qs, jnp.zeros_like(qs)))
            top = jnp.max(st, axis=0, keepdims=True)
            pr = jnp.exp2(st - top)
            total = jnp.sum(pr, axis=0, keepdims=True)
            outs.append(mm(vt[64 * e : 64 * e + 64], pr.astype(BF)) / total)
            lse_o[pair, e : e + 1, pl.ds(qb * QB, QB)] = top + jnp.log2(total)
        o[rows, cols] = jnp.concatenate(outs, axis=0).T.astype(BF)

    def a_swap():
        late.append(keep(o, o_o))
        state["att"] = []
        for lg in range(2):
            cols = pl.ds(lg * 256, 256)
            state["att"].append(keep(o.at[pl.ds(0, 512), cols], att.at[2 * lg + c]))
            state["att"].append(
                push(o.at[pl.ds(512, 512), cols], att.at[2 * lg + c], att.at[2 * lg + 1 - c], k.core)
            )

    def a_proj():
        for w in state["att"] + state["kv"]:
            w()
        own = keep(tok, n2s)
        own()
        for p in groups[1]:
            p.arrive()
        low = jnp.zeros((512, 16), F32)
        for g in range(4):
            low += mm_nt(att[g], dn[:, D + g * 256 : D + g * 256 + 256])
        low = low.astype(BF)
        r_p_s[...] = low
        for t in range(4):
            cols = pl.ds(t * 256, 256)
            val = mm(low, up[:, 3 * D + t * 256 : 3 * D + t * 256 + 256]) + vf[7:8, cols]
            for g in range(4):
                val += mm(att[g], wp[t // 2, t % 2, g].reshape(256, 256))
            res[:, cols] = n2s[:, cols].astype(F32) + val

    def a_norm2():
        xhat, _ = norm_parts(res[...])
        n2 = (xhat * vf[2:3, :] + vf[3:4, :]).astype(BF)
        n2s[...] = n2
        r_1_s[...] = mm_nt(n2, dn[:, 2 * D : 3 * D]).astype(BF)
        g_r2_s[...] = mm_nt(cot[...], up[:, 4 * D + FF :]).astype(BF)
        accs[...] = jnp.zeros_like(accs)
        gn2[...] = jnp.zeros_like(gn2)
        state["n1"]()

    def a_fc1(i):
        if i == 0:
            for p in groups[2]:
                p.arrive()
        t, h = i // 2, i % 2
        w = w1[t // 2, t % 2, :, :, :, h * 512 : h * 512 + 512].reshape(D, 512)
        bias = jnp.concatenate(
            [vf[9 + 2 * h + b : 10 + 2 * h + b, t * 256 : t * 256 + 256] for b in range(2)], axis=1
        )
        hid = mm(n2s[...], w) + bias
        hid += mm(r_1_s[...], up[:, 4 * D + i * 512 : 4 * D + i * 512 + 512])
        cdf = 0.5 * (1.0 + lax.erf(hid * (0.5**0.5)))
        a = (hid * cdf).astype(BF)
        sl = cdf + hid * jnp.exp(-0.5 * hid * hid) * 0.3989422804014327
        for j in range(4):
            buf4[j, :, i * 128 : i * 128 + 128] = a[:, j * 128 : j * 128 + 128]
            slope[j, :, i * 128 : i * 128 + 128] = sl[:, j * 128 : j * 128 + 128].astype(BF)

    def a_fc2(j):
        groups[3][j].arrive()
        a = buf4[j]
        hcols = [3 * D + i * 512 + j * 128 for i in range(8)]
        d2 = jnp.concatenate([dn[:, h : h + 128] for h in hcols], axis=1)
        low2 = mm_nt(a, d2)
        g = mm(g_r2_s[...], d2)
        for t in range(4):
            w = w2[t // 2, t % 2, :, :, j * 128 : j * 128 + 128, :].reshape(1024, 256)
            cols = pl.ds(t * 256, 256)
            accs[:, cols] += mm(a, w)
            g += mm_nt(cot[:, cols], w)
        gh = (g * slope[j].astype(F32)).astype(BF)
        w = jnp.concatenate(
            [
                w1[i // 4, (i // 2) % 2, :, :, :, (i % 2) * 512 + j * 128 : (i % 2) * 512 + j * 128 + 128].reshape(D, 128)
                for i in range(8)
            ],
            axis=1,
        )
        gn2[...] += mm_nt(gh, w)
        u1 = jnp.concatenate(
            [up[:, 4 * D + i * 512 + j * 128 : 4 * D + i * 512 + j * 128 + 128] for i in range(8)],
            axis=1,
        )
        low1 = mm_nt(gh, u1)
        state["r2"] = low2 if "r2" not in state else state["r2"] + low2
        state["g1"] = low1 if "g1" not in state else state["g1"] + low1
        ga2[j] = mm_tn(g_r2_s[...], a)
        gb1[j] = mm_tn(r_1_s[...], gh)

    def a_end():
        r_2, g_r1 = state["r2"].astype(BF), state["g1"].astype(BF)
        g_n2 = gn2[...] + mm(g_r1, dn[:, 2 * D : 3 * D])
        xhat, inv = norm_parts(res[...])
        g_res = cot[...].astype(F32) + norm_back(g_n2, xhat, inv, vf[2:3, :])
        gres[...] = g_res
        gb = g_res.astype(BF)
        g_rp = mm_nt(gb, up[:, 3 * D : 4 * D]).astype(BF)
        for g in range(4):
            gap[:, g * 256 : g * 256 + 256] = mm_tn(g_rp, att[g])
            val = mm(g_rp, dn[:, D + g * 256 : D + g * 256 + 256])
            for t in range(4):
                w = wp[t // 2, t % 2, g].reshape(256, 256)
                val += mm_nt(gb[:, t * 256 : t * 256 + 256], w)
            gatt[g] = val.astype(BF)
        waits = []
        for lg in range(2):
            cols = pl.ds(lg * 256, 256)
            top, low = pl.ds(0, 512), pl.ds(512, 512)
            waits.append(keep(gatt.at[2 * lg + c], do_o.at[top, cols]))
            waits.append(
                push(gatt.at[2 * lg + 1 - c], do_o.at[low, cols], do_o.at[low, cols], k.core)
            )
        u2 = up[:, 4 * D + FF :]
        out[...] = (res[...] + accs[...] + vf[8:9, :] + mm(r_2, u2)).astype(BF)
        gb2[...] = mm_tn(r_2, cot[...])
        ga1[...] = mm_tn(g_r1, n2s[...])
        gbp[...] = mm_tn(r_p_s[...], gb)
        for w in waits:
            w()

    acts = {
        "tok": a_tok, "tokfwd": a_tokfwd, "pick": a_pick, "pass": a_pass, "maps": a_maps, "vec": a_vec,
        "norm": a_norm, "wq": a_wq, "red": a_red, "qkv": a_qkv, "keep": a_keep, "att": a_att,
        "swap": a_swap, "proj": a_proj, "norm2": a_norm2, "fc1": a_fc1, "fc2": a_fc2, "end": a_end,
    }
    for name, *args in order:
        if isinstance(name, int):
            parts[name].step(args[0])
        else:
            acts[name](*args)
    for w in late:
        w()
    for p in parts:
        p.finish()
    assert k.nr <= NSEM[0] and k.nl <= NSEM[1]


def front(nz, cfg, tok, cot, qkv, proj, fc1, fc2, vecs, places, index, ad):
    anys, vm = pl.BlockSpec(memory_space=pl.ANY), pl.BlockSpec(memory_space=pltpu.VMEM)
    ndp = 2 * nz
    rows = tok.shape[0]
    nd, nu = 3 * D + FF, 5 * D + FF
    outs = [
        (vm, (rows, D), BF), (vm, (rows, D), F32), (anys, (2 * rows, 512), BF),
        (anys, (2 * rows, 512), BF), (anys, (4, rows, 512), BF), (anys, (4, rows, 512), BF),
        (anys, (2 * rows, 512), BF), (vm, (4, 2, 2 * rows), F32), (anys, (4, rows, D), BF),
        (vm, (4, rows, 16), BF), (anys, (6, nz, 2, qkv.shape[0], 256), BF), (vm, (16, nd), BF),
        (vm, (16, nu), BF), (vm, (4, 8, rows), F32), (vm, (ndp, 8, 128), F32),
        (vm, (16, D), F32), (vm, (16, D), F32), (vm, (16, D), F32), (vm, (4, 16, 1024), F32),
        (vm, (4, 16, 1024), F32), (vm, (16, D), F32), (anys, (2, nz, 2) + qkv.shape, BF), (vm, (16, D), F32),
    ]
    scratch = [
        ((4, rows, D), BF), ((6, nz, 2, qkv.shape[0], 256), BF),
        ((2, 2, nz, 2) + proj.shape, BF), ((2, 2, nz, 2) + fc1.shape, BF), ((2, 2, nz, 2) + fc2.shape, BF),
        ((2 * rows, 512), BF), ((4, rows, 1024), BF), ((4, rows, 256), BF), ((rows, D), F32),
        ((rows, D), F32), ((rows, D), BF), ((4, 16, 256), BF),
        ((ndp, 16, 512), BF), ((4, ndp, 16, 512), BF), ((5, rows, 16), BF),
    ]
    return pl.pallas_call(
        functools.partial(front_kernel, nz, cfg),
        out_shape=[sds(sh, t) for _, sh, t in outs],
        in_specs=[anys, vm, anys, anys, anys, anys, vm, vm, vm, vm, vm],
        out_specs=[m for m, _, _ in outs],
        scratch_shapes=[pltpu.VMEM(sh, t) for sh, t in scratch]
        + [
            pltpu.SemaphoreType.DMA((NSEM[0],)),
            pltpu.SemaphoreType.DMA((NSEM[0],)),
            pltpu.SemaphoreType.DMA((NSEM[1],)),
        ],
        compiler_params=pltpu.CompilerParams(
            collective_id=0, has_side_effects=True, vmem_limit_bytes=VM
        ),
    )(tok, cot, qkv, proj, fc1, fc2, vecs, places, index, ad, jnp.asarray(row_table()))


def back_kernel(nz, *refs):
    (q_i, k_i, v_i, o_i, do_i, n1_i, wq_i, tok_i, gres_i, lse, red, dn, up, pall, idxs, vf,
     gap, gbp, ga1, gb1, ga2, gb2, table) = refs[:23]
    ig, grads = refs[23:25]
    (q, kk, vv, o, do, n1, wcat, tok, gres, acc, dl, dk, dv, gm, upc, gaq, gbq, own, part, gd, gu,
     blk, got, selo, selr, ssem, rsem, lsem) = refs[25:]
    k = Links(ssem, rsem, lsem, nz)
    c, d, s = k.c, k.d, k.s
    ndp = 2 * nz
    rows = tok.shape[0]
    nq = 2 * rows
    seqs = [k.core, k.xn, k.diag]
    seq_of = [s + 1 - 2 * c, s + 2 - 4 * k.x, 3 - s]
    dps = [(lax.rem(d + j, ndp), s) for j in range(1, ndp)]
    late = []

    def keep(src, dst):
        i = k.newl()
        cp = k.local(i, src, dst)
        cp.start()
        return cp.wait

    def push(src, dst, land, dev):
        i = k.new()
        cp = k.remote(i, src, dst, dev)
        cp.start()
        late.append(cp.wait_send)
        return k.remote(i, src, land, dev).wait_recv

    first = [keep(a, b) for a, b in ((q_i, q), (k_i, kk), (v_i, vv), (o_i, o), (do_i, do))]
    later = [keep(wq_i.at[r], wcat.at[:, pl.ds(256 * r, 256)]) for r in range(6)]
    later += [keep(a, b) for a, b in ((n1_i, n1), (tok_i, tok), (gres_i, gres))]
    k.barrier(seqs + dps)
    for w in first:
        w()
    lane = lax.broadcasted_iota(jnp.int32, (1, 128), 1)

    def attend_back(pair, half):
        cols = pl.ds(pair * 128, 128)
        krows = pl.ds(half * nq, nq)
        qs, dos, ks, vs = q[:, cols], do[:, cols], kk[krows, cols], vv[krows, cols]
        if half == 1:
            r8 = lax.broadcasted_iota(jnp.int32, (8, 128), 0)
            l8 = lax.broadcasted_iota(jnp.int32, (8, 128), 1) // 64
            dl[pair] = lax.dot_general(
                (r8 == l8).astype(F32),
                dos.astype(F32) * o[:, cols].astype(F32),
                (((1,), (1,)), ((), ())),
                precision=lax.Precision.HIGHEST,
                preferred_element_type=F32,
            )
        dks, dvs, dqs = [], [], []
        for e in range(2):
            mine = (lane < 64) if e == 0 else (lane >= 64)
            st = mm_nt(jnp.where(mine, ks, jnp.zeros_like(ks)), qs)
            pr = jnp.exp2(st - lse[pair, e : e + 1, :])
            dp = mm_nt(jnp.where(mine, vs, jnp.zeros_like(vs)), dos)
            ds = (pr * (dp - dl[pair, e : e + 1, :])).astype(BF)
            dvs.append(mm(pr.astype(BF), dos))
            dks.append(mm(ds, qs))
            dqs.append(mm(ks.T[64 * e : 64 * e + 64], ds))
        dk[:, cols] = jnp.where(lane < 64, dks[0], dks[1]) * LN2
        dv[:, cols] = jnp.where(lane < 64, dvs[0], dvs[1])
        dq = jnp.concatenate(dqs, axis=0)
        frows = pl.ds(pair * 128, 128)
        if half == 1:
            acc[frows, :] = dq
        else:
            acc[frows, :] += dq

    def mixed(slot):
        tab = turns(pall[slot], table)
        cos, sin = tab[:, :128], -tab[:, 128:]
        at = pl.ds((slot % 2) * rows, rows)
        f = 0 if slot < 2 else 512
        for role in range(0 if slot < 2 else 2, 6):
            cols = pl.ds((role % 2) * 256, 256)
            if role < 2:
                g = acc[cols, at].T * (HD**-0.5)
                g = turn(g, cos, sin)
            elif role < 4:
                g = turn(dk[at, cols], cos, sin)
            else:
                g = dv[at, cols]
            gm[at, role * 256 : role * 256 + 256] = g.astype(BF)
        g = gm[at, f:]
        low = mm_nt(g, upc[:, f:]).astype(BF)
        ta, tb = mm_tn(low, n1[slot]), mm_tn(red[slot], g)
        if slot == 2:
            gaq[...] = ta
            gbq[:, :512] = jnp.zeros((16, 512), F32)
            gbq[:, f:] = tb
        else:
            gaq[...] += ta
            gbq[:, f:] += tb
        return low

    def into_h(slot, low):
        at = pl.ds((slot % 2) * rows, rows)
        f = 0 if slot < 2 else 512
        return mm_nt(gm[at, f:], wcat[:, f:]) + mm(low, dn[:, :D])

    for pair in range(4):
        attend_back(pair, 1)
    for w in later:
        w()
    for role in range(6):
        at = pl.multiple_of((4 * (role // 2) + 2 * (role % 2) + c) * 256, 256)
        upc[:, role * 256 : role * 256 + 256] = up[:, pl.ds(at, 256)]
    low2 = mixed(2)
    low3 = mixed(3)
    part[0] = into_h(3, low3).astype(BF)
    from_core = push(part.at[0], part.at[1], part.at[1], k.core)
    own[...] = into_h(2, low2)
    from_core()
    part[2] = (own[...] + part[1].astype(F32)).astype(BF)
    from_x = push(part.at[2], part.at[3], part.at[3], k.xn)
    gd[:, D : 2 * D] = gap[...]
    gd[:, 2 * D : 3 * D] = ga1[...]
    gu[:, : 3 * D] = jnp.zeros((16, 3 * D), F32)
    gu[:, 3 * D : 4 * D] = gbp[...]
    gu[:, 4 * D + FF :] = gb2[...]
    for j in range(4):
        for i in range(8):
            at = i * 512 + j * 128
            gd[:, 3 * D + at : 3 * D + at + 128] = ga2[j, :, i * 128 : i * 128 + 128]
            gu[:, 4 * D + at : 4 * D + at + 128] = gb1[j, :, i * 128 : i * 128 + 128]
    for pair in range(4):
        attend_back(pair, 0)
    low1 = mixed(1)
    low0 = mixed(0)
    gd[:, :D] = gaq[...]
    for role in range(6):
        at = pl.multiple_of((4 * (role // 2) + 2 * (role % 2) + c) * 256, 256)
        gu[:, pl.ds(at, 256)] = gbq[:, role * 256 : role * 256 + 256]
    nd, nu = gd.shape[1] // 4, gu.shape[1] // 4
    for t in range(4):
        blk[t, :, :nd] = gd[:, t * nd : t * nd + nd].astype(BF)
        blk[t, :, nd:] = gu[:, t * nu : t * nu + nu].astype(BF)
    sums = [push(blk.at[seq_of[r]], got.at[r], got.at[r], seqs[r]) for r in range(3)]
    part[4] = into_h(1, low1).astype(BF)
    from_core = push(part.at[4], part.at[5], part.at[5], k.core)
    for w in sums:
        w()
    total = blk[s].astype(F32)
    for r in range(3):
        total += got[r].astype(F32)
    total = total.astype(BF)
    stack = jnp.concatenate([total[:, b * 512 : b * 512 + 512] for b in range(8)], axis=0)
    selo[...] = mm_tn(unshuffle(), stack).astype(BF).reshape(ndp, 16, 512)
    selr[d] = selo[d]
    ends = [
        push(selo.at[lax.rem(d + j, ndp)], selr.at[d], selr.at[lax.rem(d + ndp - j, ndp)], dps[j - 1])
        for j in range(1, ndp)
    ]
    own[...] = into_h(0, low0)
    xhat, inv = norm_parts(tok[...].astype(F32))
    from_core()
    from_x()
    g_n1 = own[...] + part[5].astype(F32) + part[3].astype(F32)
    ig[...] = (gres[...] + norm_back(g_n1, xhat, inv, vf[0:1, :])).astype(BF)
    for w in ends:
        w()
    for a in range(NA):
        out = jnp.zeros((16, 512), F32)
        for j in range(ndp):
            out += jnp.where(idxs[j][0:1, 0:1] == float(a), selr[j].astype(F32), 0.0)
        grads[a] = out
    for w in late:
        w()
    assert k.nr <= 40 and k.nl <= 20


def back(nz, *args):
    anys, vm = pl.BlockSpec(memory_space=pl.ANY), pl.BlockSpec(memory_space=pltpu.VMEM)
    rows = args[7].shape[0]
    nq = 2 * rows
    ndp = 2 * nz
    scratch = [
        ((nq, 512), BF), ((2 * nq, 512), BF), ((2 * nq, 512), BF), ((nq, 512), BF), ((nq, 512), BF),
        ((4, rows, D), BF), ((D, 1536), BF), ((rows, D), BF), ((rows, D), F32),
        ((512, nq), F32), ((4, 8, nq), F32), ((nq, 512), F32), ((nq, 512), F32),
        ((nq, 1536), BF), ((16, 1536), BF), ((16, D), F32), ((16, 1536), F32), ((rows, D), F32),
        ((6, rows, D), BF), ((16, 3 * D + FF), F32), ((16, 5 * D + FF), F32),
        ((4, 16, 4096), BF), ((3, 16, 4096), BF), ((ndp, 16, 512), BF), ((ndp, 16, 512), BF),
    ]
    return pl.pallas_call(
        functools.partial(back_kernel, nz),
        out_shape=[sds((rows, D), BF), sds((NA, 16, 512), F32)],
        in_specs=[anys] * 9 + [vm] * (len(args) - 8),
        out_specs=[vm, vm],
        scratch_shapes=[pltpu.VMEM(sh, t) for sh, t in scratch]
        + [
            pltpu.SemaphoreType.DMA((40,)),
            pltpu.SemaphoreType.DMA((40,)),
            pltpu.SemaphoreType.DMA((20,)),
        ],
        compiler_params=pltpu.CompilerParams(
            collective_id=1, has_side_effects=True, vmem_limit_bytes=VM
        ),
    )(*args, jnp.asarray(row_table()))


def fast_shards(
    nz, tokens, positions, adapter_index, qkv_weight, proj_weight, fc1_weight, fc2_weight,
    vectors, fc1_bias, adapter_down, adapter_up, cotangent,
):
    vecs = jnp.concatenate([vectors, fc1_bias.reshape(4, 256), jnp.zeros((3, 256), BF)], axis=0)
    places = jnp.pad(positions[:, 0].astype(F32), ((0, 5), (0, 0)))
    index = jnp.broadcast_to(adapter_index.astype(F32), (8, 128))
    rk, nd = adapter_down.shape[1:]
    ad = jnp.concatenate([adapter_down, adapter_up], axis=-1).reshape(NA, 16, 512)
    (output, gres, do, q, k, v, o, lse, n1, red, wq, dn, up, pall, idxs,
     gap, gbp, ga1, gb1, ga2, gb2, _, vf) = front(
        nz, PLAN, tokens[0], cotangent[0], qkv_weight, proj_weight, fc1_weight, fc2_weight,
        vecs, places, index, ad,
    )
    input_grad, grads = back(
        nz, q, k.reshape(-1, 512), v.reshape(-1, 512), o, do, n1, wq.reshape(6, D, 256), tokens[0],
        gres, lse, red, dn, up, pall, idxs, vf, gap, gbp, ga1, gb1, ga2, gb2,
    )
    grads = grads.reshape(NA, rk, -1)
    return output[None], input_grad[None], grads[:, :, :nd], grads[:, :, nd:]


def solution(mesh):
    in_specs = (
        P("dp", "seq", None),
        P(None, "dp", "seq"),
        P("dp", None),
        P("dp", "seq"),
        P("dp", "seq"),
        P("dp", "seq"),
        P("dp", "seq"),
        P(None, "seq"),
        P("seq"),
        P(None, "dp", "seq"),
        P(None, "dp", "seq"),
        P("dp", "seq", None),
    )
    out_specs = (
        P("dp", "seq", None),
        P("dp", "seq", None),
        P(None, "dp", "seq"),
        P(None, "dp", "seq"),
    )
    body = shards
    if mesh.shape["seq"] == 4 and mesh.shape["dp"] == 8:

        def body(tokens, *rest):
            if tokens.shape[0] == 1 and tokens.shape[1] == 512:
                return fast_shards(mesh.shape["dp"] // 2, tokens, *rest)
            return shards(tokens, *rest)

    return jax.shard_map(body, mesh=mesh, in_specs=in_specs, out_specs=out_specs, check_vma=False)
```

```python
import functools
import math

import jax
import jax.numpy as jnp
import numpy as np
from jax import lax
from jax.experimental import pallas as pl
from jax.experimental.pallas import tpu as pltpu
from jax.sharding import PartitionSpec as P

D = 1024
HEADS = 16
HD = 64
FF = 4096
NA = 8


def layer_norm(values, gain_row, shift_row):
    centre = values - jnp.mean(values, axis=-1, keepdims=True)
    spread = jnp.mean(centre * centre, axis=-1, keepdims=True)
    return centre * lax.rsqrt(spread + 1e-06) * gain_row + shift_row


def rotate(values, places, direction):
    rot_span = 2 * (values.shape[-1] // 3 // 2)
    half_span = rot_span // 2
    inverse_freq = 10000.0 ** (-jnp.arange(half_span, dtype=jnp.float32) / half_span)
    pieces = []
    for axis_id in range(3):
        segment = values[..., axis_id * rot_span : (axis_id + 1) * rot_span]
        angles = places[axis_id].astype(jnp.float32)[..., None, None] * inverse_freq
        cosine = jnp.cos(angles)
        sine_wave = direction * jnp.sin(angles)
        lower_part = segment[..., :half_span]
        upper_part = segment[..., half_span:]
        pieces.append(lower_part * cosine - upper_part * sine_wave)
        pieces.append(lower_part * sine_wave + upper_part * cosine)
    pieces.append(values[..., 3 * rot_span :])
    return jnp.concatenate(pieces, axis=-1)


def exact_gelu(values):
    return jax.nn.gelu(values, approximate=False)


def fetch_weight(weight):
    joined = lax.all_gather(weight, "seq", axis=1, tiled=True)
    return lax.all_gather(joined, "dp", axis=0, tiled=True)


def adapted(inputs, weight, shift_row, down_part, up_part):
    base = jnp.einsum("cti,io->cto", inputs, weight, preferred_element_type=jnp.float32)
    reduced = jnp.einsum(
        "cti,cri->ctr", inputs, down_part, preferred_element_type=jnp.float32
    ).astype(jnp.bfloat16)
    result = (
        base
        + shift_row
        + jnp.einsum("ctr,cro->cto", reduced, up_part, preferred_element_type=jnp.float32)
    )
    return (result, reduced)


def adapted_back(grad_out, inputs, weight, down_part, up_part, reduced):
    grad_in = jnp.einsum("cto,io->cti", grad_out, weight, preferred_element_type=jnp.float32)
    grad_reduced = jnp.einsum(
        "cto,cro->ctr", grad_out, up_part, preferred_element_type=jnp.float32
    ).astype(jnp.bfloat16)
    grad_in = grad_in + jnp.einsum(
        "ctr,cri->cti", grad_reduced, down_part, preferred_element_type=jnp.float32
    )
    grad_down = jnp.einsum("ctr,cti->cri", grad_reduced, inputs, preferred_element_type=jnp.float32)
    grad_up = jnp.einsum("ctr,cto->cro", reduced, grad_out, preferred_element_type=jnp.float32)
    return (grad_in, grad_down, grad_up)


def split_tokens(source, split_count):
    old_shape = source.shape
    shaped = source.reshape(
        (old_shape[0], split_count, old_shape[1] // split_count) + old_shape[2:]
    )
    return jnp.moveaxis(shaped, 1, 0)


def score_grads(
    query_block, key_block, value_block, grad_block, log_block, delta_block, score_scale
):
    scores = (
        jnp.einsum("cqhd,ckhd->chqk", query_block, key_block, preferred_element_type=jnp.float32)
        * score_scale
    )
    probabilities = jnp.exp(scores - log_block[..., None])
    grad_probs = jnp.einsum(
        "cqhd,ckhd->chqk", grad_block, value_block, preferred_element_type=jnp.float32
    )
    grad_scores = (probabilities * (grad_probs - delta_block[..., None])).astype(jnp.bfloat16)
    return (probabilities.astype(jnp.bfloat16), grad_scores)


def shards(
    tokens,
    positions,
    adapter_index,
    qkv_weight,
    proj_weight,
    fc1_weight,
    fc2_weight,
    vectors,
    fc1_bias,
    adapter_down,
    adapter_up,
    cotangent,
):
    clip_count, tok_count = (tokens.shape[0], tokens.shape[1])
    head_shape = (clip_count, tok_count, HEADS, HD)
    score_scale = HD ** (-0.5)
    small_parts = (
        lax.all_gather(adapter_down, "seq", axis=2, tiled=True),
        lax.all_gather(adapter_up, "seq", axis=2, tiled=True),
        lax.all_gather(vectors, "seq", axis=1, tiled=True),
        lax.all_gather(fc1_bias, "seq", axis=0, tiled=True),
    )
    down_all, up_all = (
        lax.all_gather(small_parts[0], "dp", axis=1, tiled=True),
        lax.all_gather(small_parts[1], "dp", axis=1, tiled=True),
    )
    vector_rows = small_parts[2].astype(jnp.float32)
    hidden_bias = small_parts[3].astype(jnp.float32)
    choose = (adapter_index == jnp.arange(NA, dtype=jnp.int32)[None, :]).astype(jnp.bfloat16)
    down_sel = jnp.einsum(
        "ca,ari->cri", choose, down_all, preferred_element_type=jnp.float32
    ).astype(jnp.bfloat16)
    up_sel = jnp.einsum("ca,aro->cro", choose, up_all, preferred_element_type=jnp.float32).astype(
        jnp.bfloat16
    )
    down_parts = (
        down_sel[:, :, :D],
        down_sel[:, :, D : 2 * D],
        down_sel[:, :, 2 * D : 3 * D],
        down_sel[:, :, 3 * D :],
    )
    up_parts = (
        up_sel[:, :, : 3 * D],
        up_sel[:, :, 3 * D : 4 * D],
        up_sel[:, :, 4 * D : 4 * D + FF],
        up_sel[:, :, 4 * D + FF :],
    )
    inputs = tokens.astype(jnp.float32)
    normed_one = layer_norm(inputs, vector_rows[0], vector_rows[1]).astype(jnp.bfloat16)
    weight_qkv = fetch_weight(qkv_weight)
    mixed_qkv, reduced_qkv = adapted(
        normed_one, weight_qkv, vector_rows[4:7].reshape(3 * D), down_parts[0], up_parts[0]
    )
    queries = rotate(mixed_qkv[..., :D].reshape(head_shape), positions, 1.0).astype(jnp.bfloat16)
    keys_local = rotate(mixed_qkv[..., D : 2 * D].reshape(head_shape), positions, 1.0).astype(
        jnp.bfloat16
    )
    values_local = mixed_qkv[..., 2 * D :].reshape(head_shape).astype(jnp.bfloat16)
    stat_shape = (clip_count, HEADS, tok_count)
    start_state = (
        jnp.full(stat_shape, -jnp.inf, jnp.float32),
        jnp.zeros(stat_shape, jnp.float32),
        jnp.zeros(stat_shape + (HD,), jnp.float32),
    )
    key_piece = lax.all_gather(keys_local, "seq", axis=1, tiled=True)
    value_piece = lax.all_gather(values_local, "seq", axis=1, tiled=True)
    split_count = key_piece.shape[1] // math.gcd(key_piece.shape[1], 256)

    def inner_step(running, block_pair):
        top_score, row_total, weighted = running
        key_block, value_block = block_pair
        scores = (
            jnp.einsum("cqhd,ckhd->chqk", queries, key_block, preferred_element_type=jnp.float32)
            * score_scale
        )
        new_top = jnp.maximum(top_score, jnp.max(scores, axis=-1))
        factor = jnp.exp(top_score - new_top)
        weights = jnp.exp(scores - new_top[..., None])
        row_total = row_total * factor + jnp.sum(weights, axis=-1)
        weighted = weighted * factor[..., None] + jnp.einsum(
            "chqk,ckhd->chqd",
            weights.astype(jnp.bfloat16),
            value_block,
            preferred_element_type=jnp.float32,
        )
        return ((new_top, row_total, weighted), None)

    result, unused = lax.scan(
        inner_step,
        start_state,
        (split_tokens(key_piece, split_count), split_tokens(value_piece, split_count)),
    )
    top_score, row_total, weighted = result
    log_total = top_score + jnp.log(row_total)
    heads_tok = jnp.swapaxes(weighted / row_total[..., None], 1, 2)
    attended = heads_tok.reshape(clip_count, tok_count, D).astype(jnp.bfloat16)
    weight_proj = fetch_weight(proj_weight)
    projected, reduced_proj = adapted(
        attended, weight_proj, vector_rows[7], down_parts[1], up_parts[1]
    )
    residual = inputs + projected
    normed_two = layer_norm(residual, vector_rows[2], vector_rows[3]).astype(jnp.bfloat16)
    weight_up = fetch_weight(fc1_weight)
    hidden, reduced_up = adapted(normed_two, weight_up, hidden_bias, down_parts[2], up_parts[2])
    activated = exact_gelu(hidden).astype(jnp.bfloat16)
    weight_down = fetch_weight(fc2_weight)
    branch, reduced_down = adapted(
        activated, weight_down, vector_rows[8], down_parts[3], up_parts[3]
    )
    output = (residual + branch).astype(jnp.bfloat16)
    weight_down = fetch_weight(fc2_weight)
    grad_act, gdown_four, gup_four = adapted_back(
        cotangent, activated, weight_down, down_parts[3], up_parts[3], reduced_down
    )
    unused, gelu_back = jax.vjp(exact_gelu, hidden)
    grad_hidden = gelu_back(grad_act)[0].astype(jnp.bfloat16)
    weight_up = fetch_weight(fc1_weight)
    grad_normed_two, gdown_three, gup_three = adapted_back(
        grad_hidden, normed_two, weight_up, down_parts[2], up_parts[2], reduced_up
    )

    def norm_two(values):
        return layer_norm(values, vector_rows[2], vector_rows[3])

    unused, norm_two_back = jax.vjp(norm_two, residual)
    grad_residual = cotangent.astype(jnp.float32) + norm_two_back(grad_normed_two)[0]
    weight_proj = fetch_weight(proj_weight)
    grad_attended, gdown_two, gup_two = adapted_back(
        grad_residual.astype(jnp.bfloat16),
        attended,
        weight_proj,
        down_parts[1],
        up_parts[1],
        reduced_proj,
    )
    grad_tok = grad_attended.astype(jnp.bfloat16).reshape(head_shape)
    delta_heads = jnp.swapaxes(jnp.sum(grad_tok.astype(jnp.float32) * heads_tok, axis=-1), 1, 2)
    whole_keys, whole_values = (
        lax.all_gather(keys_local, "seq", axis=1, tiled=True),
        lax.all_gather(values_local, "seq", axis=1, tiled=True),
    )
    block_count = whole_keys.shape[1] // math.gcd(whole_keys.shape[1], 256)
    key_blocks = split_tokens(whole_keys, block_count)
    value_blocks = split_tokens(whole_values, block_count)
    zero_heads = jnp.zeros(head_shape, jnp.float32)

    def back_step(grad_query, block_pair):
        key_block, value_block = block_pair
        probs_low, grad_scores = score_grads(
            queries, key_block, value_block, grad_tok, log_total, delta_heads, score_scale
        )
        grad_query = (
            grad_query
            + jnp.einsum(
                "chqk,ckhd->cqhd", grad_scores, key_block, preferred_element_type=jnp.float32
            )
            * score_scale
        )
        grad_key = (
            jnp.einsum("chqk,cqhd->ckhd", grad_scores, queries, preferred_element_type=jnp.float32)
            * score_scale
        )
        grad_value = jnp.einsum(
            "chqk,cqhd->ckhd", probs_low, grad_tok, preferred_element_type=jnp.float32
        )
        return (grad_query, jnp.concatenate([grad_key, grad_value], axis=-1))

    grad_query, key_terms = lax.scan(back_step, zero_heads, (key_blocks, value_blocks))
    key_terms = jnp.moveaxis(key_terms, 0, 1).reshape(
        clip_count, whole_keys.shape[1], HEADS, 2 * HD
    )
    summed = lax.psum_scatter(
        key_terms.astype(jnp.bfloat16), "seq", scatter_dimension=1, tiled=True
    ).astype(jnp.float32)
    grad_key = summed[..., :HD]
    grad_value = summed[..., HD:]
    grad_mixed = jnp.concatenate(
        [
            rotate(grad_query, positions, -1.0).reshape(clip_count, tok_count, D),
            rotate(grad_key, positions, -1.0).reshape(clip_count, tok_count, D),
            grad_value.reshape(clip_count, tok_count, D),
        ],
        axis=-1,
    ).astype(jnp.bfloat16)
    weight_qkv = fetch_weight(qkv_weight)
    grad_normed_one, gdown_one, gup_one = adapted_back(
        grad_mixed, normed_one, weight_qkv, down_parts[0], up_parts[0], reduced_qkv
    )

    def norm_one(values):
        return layer_norm(values, vector_rows[0], vector_rows[1])

    unused, norm_one_back = jax.vjp(norm_one, inputs)
    input_grad = (grad_residual + norm_one_back(grad_normed_one)[0]).astype(jnp.bfloat16)
    choose_wide = choose.astype(jnp.float32)
    clip_down = jnp.concatenate([gdown_one, gdown_two, gdown_three, gdown_four], axis=-1)
    clip_up = jnp.concatenate([gup_one, gup_two, gup_three, gup_four], axis=-1)
    down_term = jnp.einsum("ca,cri->ari", choose_wide, clip_down, precision=lax.Precision.HIGHEST)
    up_term = jnp.einsum("ca,cro->aro", choose_wide, clip_up, precision=lax.Precision.HIGHEST)
    down_grad, up_grad = (
        lax.psum_scatter(
            down_term.astype(jnp.bfloat16), "seq", scatter_dimension=2, tiled=True
        ).astype(jnp.float32),
        lax.psum_scatter(
            up_term.astype(jnp.bfloat16), "seq", scatter_dimension=2, tiled=True
        ).astype(jnp.float32),
    )
    down_grad, up_grad = (
        lax.psum_scatter(
            down_grad.astype(jnp.bfloat16), "dp", scatter_dimension=1, tiled=True
        ).astype(jnp.float32),
        lax.psum_scatter(
            up_grad.astype(jnp.bfloat16), "dp", scatter_dimension=1, tiled=True
        ).astype(jnp.float32),
    )
    return (output, input_grad, down_grad, up_grad)

MESH = pl.DeviceIdType.MESH
BF = jnp.bfloat16
F32 = jnp.float32
LOG2E = 1.4426950408889634
LN2 = 0.6931471805599453
VM = 60 * 1024 * 1024


def mm(a, b):
    return lax.dot_general(a, b, (((1,), (0,)), ((), ())), preferred_element_type=F32)


def mm_nt(a, b):
    return lax.dot_general(a, b, (((1,), (1,)), ((), ())), preferred_element_type=F32)


def mm_tn(a, b):
    return lax.dot_general(a, b, (((0,), (0,)), ((), ())), preferred_element_type=F32)


class Links:
    def __init__(self, ssem, rsem, lsem, nz):
        self.ssem, self.rsem, self.lsem = ssem, rsem, lsem
        self.nr, self.nl = 0, 0
        d, s = lax.axis_index("dp"), lax.axis_index("seq")
        self.d, self.s, self.nz = d, s, nz
        self.z, self.y, self.x, self.c = d // 2, lax.rem(d, 2), s // 2, lax.rem(s, 2)
        self.core = (d, s + 1 - 2 * self.c)
        self.xn = (d, s + 2 - 4 * self.x)
        self.diag = (d, 3 - s)
        self.yn = (d + 1 - 2 * self.y, s)
        self.up, self.down = (d + 2, s), (d - 2, s)
        self.zpeer = [(lax.rem(d + 2 * j, 2 * nz), s) for j in range(nz)]

    def greet(self, peers):
        bar = pltpu.get_barrier_semaphore()
        for dev in peers:
            pl.semaphore_signal(bar, inc=1, device_id=dev, device_id_type=MESH)
        return lambda: pl.semaphore_wait(bar, len(peers))

    def barrier(self, peers):
        self.greet(peers)()

    def new(self, count=1):
        self.nr += count
        return self.nr - count

    def newl(self):
        self.nl += 1
        return self.nl - 1

    def remote(self, i, src, dst, dev):
        return pltpu.make_async_remote_copy(
            src_ref=src,
            dst_ref=dst,
            send_sem=self.ssem.at[i],
            recv_sem=self.rsem.at[i],
            device_id=dev,
            device_id_type=MESH,
        )

    def local(self, i, src, dst):
        return pltpu.make_async_copy(src, dst, self.lsem.at[i])


def guard(cond, body):
    if cond is None:
        body()
    else:
        pl.when(cond)(body)


class Part:
    def __init__(self, links, order, own, region, handover):
        self.k, self.order, self.own = links, order, own
        self.region, self.handover = region, handover
        k = links
        self.s_own = k.newl()
        n = k.nz - 1
        self.s_z = k.new(2 * n if order == "xyz" else n)
        self.s_f, self.s_g1, self.s_g2 = k.new(), k.new(), k.new()
        self.pend, self.tail = [], []
        xfirst = order != "zyx"
        self.f, self.g = (k.x, k.y) if xfirst else (k.y, k.x)
        self.fd, self.gd = (k.xn, k.yn) if xfirst else (k.yn, k.xn)

    def reg(self, fi, gi, zs):
        return self.region(gi, zs, fi) if self.order == "zyx" else self.region(fi, zs, gi)

    def hand(self, cond, fi, zs, gi):
        k = self.k
        x, y = (gi, fi) if self.order == "zyx" else (fi, gi)
        loc, rem = self.handover(x, zs, y)
        ls = [(k.newl(), a, b) for a, b in loc]
        rs = [(k.new(), a, b, w) for a, b, w in rem]

        def start():
            for i, a, b in ls:
                k.local(i, a, b).start()
            for i, a, b, _ in rs:
                k.remote(i, a, b, k.core).start()

        def arrive():
            for i, a, b in ls:
                k.local(i, a, b).wait()
            for i, a, b, w in rs:
                k.remote(i, a, w, k.core).wait_recv()

        def sent():
            for i, a, b, _ in rs:
                k.remote(i, a, b, k.core).wait_send()

        guard(cond, start)
        self.pend.append((cond, arrive))
        self.tail.append((cond, sent))

    def go(self, cond, copy):
        guard(cond, copy.start)
        self.tail.append((cond, copy.wait_send))

    def step(self, name):
        getattr(self, ("l_" if self.order == "xyz" else "z_") + name)()

    def z_s(self):
        k, f, g = self.k, self.f, self.g
        k.local(self.s_own, self.own, self.reg(f, g, k.z)).start()
        for j in range(1, k.nz):
            self.go(None, k.remote(self.s_z + j - 1, self.own, self.reg(f, g, k.z), k.zpeer[j]))

    def z_m(self):
        k, f, g = self.k, self.f, self.g
        al = slice(None)
        for j in range(1, k.nz):
            at = self.reg(f, g, lax.rem(k.z + k.nz - j, k.nz))
            k.remote(self.s_z + j - 1, self.own, at, k.zpeer[j]).wait_recv()
        k.local(self.s_own, self.own, self.reg(f, g, k.z)).wait()
        mine = self.reg(f, g, al)
        self.go(None, k.remote(self.s_f, mine, mine, self.fd))
        self.go(None, k.remote(self.s_g1, mine, mine, self.gd))
        self.hand(None, f, al, g)

    def z_f(self):
        k, f, g = self.k, self.f, self.g
        al = slice(None)
        new = self.reg(1 - f, g, al)
        k.remote(self.s_f, new, new, self.fd).wait_recv()
        self.go(None, k.remote(self.s_g2, new, new, self.gd))
        self.hand(None, 1 - f, al, g)

    def z_g1(self):
        k, f, g = self.k, self.f, self.g
        al = slice(None)
        new = self.reg(f, 1 - g, al)
        k.remote(self.s_g1, new, new, self.gd).wait_recv()
        self.hand(None, f, al, 1 - g)

    def z_g2(self):
        k, f, g = self.k, self.f, self.g
        al = slice(None)
        new = self.reg(1 - f, 1 - g, al)
        k.remote(self.s_g2, new, new, self.gd).wait_recv()
        self.hand(None, 1 - f, al, 1 - g)

    def l_s(self):
        k, f, g, z = self.k, self.f, self.g, self.k.z
        k.local(self.s_own, self.own, self.reg(f, g, z)).start()
        self.go(None, k.remote(self.s_f, self.own, self.reg(f, g, z), self.fd))
        self.go(None, k.remote(self.s_g1, self.own, self.reg(f, g, z), self.gd))

    def l_f(self):
        k, f, g, z = self.k, self.f, self.g, self.k.z
        new = self.reg(1 - f, g, z)
        k.remote(self.s_f, self.own, new, self.fd).wait_recv()
        self.go(None, k.remote(self.s_g2, new, new, self.gd))

    def l_m(self):
        k, f, g, z = self.k, self.f, self.g, self.k.z
        al = slice(None)
        k.remote(self.s_g1, self.own, self.reg(f, 1 - g, z), self.gd).wait_recv()
        new = self.reg(1 - f, 1 - g, z)
        k.remote(self.s_g2, new, new, self.gd).wait_recv()
        k.local(self.s_own, self.own, self.reg(f, g, z)).wait()
        four = self.reg(al, al, z)
        self.go(z < k.nz - 1, k.remote(self.s_z, four, four, k.up))
        self.go(z > 0, k.remote(self.s_z + k.nz - 1, four, four, k.down))
        self.hand(None, al, z, al)

    def relay(self, r):
        k, z = self.k, self.k.z
        al = slice(None)
        for sem, here, origin, dev, can in (
            (self.s_z, z > r, z - 1 - r, k.up, z < k.nz - 1),
            (self.s_z + k.nz - 1, z + r < k.nz - 1, z + 1 + r, k.down, z > 0),
        ):
            four = self.reg(al, al, origin)
            guard(here, k.remote(sem + r, four, four, dev).wait_recv)
            if r < k.nz - 2:
                self.go(jnp.logical_and(here, can), k.remote(sem + r + 1, four, four, dev))
            self.hand(here, al, origin, al)

    def l_r0(self):
        self.relay(0)

    def l_r1(self):
        self.relay(1)

    def l_r2(self):
        self.relay(2)

    def arrive(self):
        for cond, body in self.pend:
            guard(cond, body)

    def finish(self):
        for cond, body in self.tail:
            guard(cond, body)


def wide_parts(links, shard, buf, cuts):
    c = links.c
    parts = []
    for r0, n, order in cuts:
        rows = pl.ds(r0, n)

        def region(x, z, y, rows=rows):
            return buf.at[x, c, z, y, rows]

        def handover(x, z, y, rows=rows):
            at = buf.at[x, c, z, y, rows]
            return [], [(at, at, buf.at[x, 1 - c, z, y, rows])]

        parts.append(Part(links, order, shard.at[rows], region, handover))
    return parts


def qkv_parts(links, shard, buf, cuts):
    parts = []
    for r0, n, order in cuts:
        rows = pl.ds(r0, n)

        def region(x, z, y, rows=rows):
            return buf.at[x, pl.ds(0, 3), z, y, rows]

        def handover(x, z, y, rows=rows):
            return [], [
                (buf.at[x, 2, z, y, rows], buf.at[x, 3, z, y, rows], buf.at[x, 3, z, y, rows])
            ]

        parts.append(Part(links, order, shard.at[:, rows], region, handover))
    return parts


def role_slot(role, c):
    return role // 3, (3 * c, 1 - c, 3 - 2 * c)[role % 3]


def norm_parts(values):
    centre = values - jnp.mean(values, axis=-1, keepdims=True)
    inv = lax.rsqrt(jnp.mean(centre * centre, axis=-1, keepdims=True) + 1e-06)
    return centre * inv, inv


def swap_pairs(v):
    n = v.shape[1]
    j = lax.rem(lax.broadcasted_iota(jnp.int32, (1, n), 1), HD)
    lower = lax.rem(j, 20) < 10
    return jnp.where(lower, pltpu.roll(v, n - 10, 1), pltpu.roll(v, 10, 1))


def turn(v, cos, sin):
    cc, ss = jnp.concatenate([cos, cos], axis=1), jnp.concatenate([sin, sin], axis=1)
    return v * cc + swap_pairs(v) * ss


def norm_back(grad, xhat, inv, gain):
    q = grad * gain
    return inv * (
        q - jnp.mean(q, axis=-1, keepdims=True) - xhat * jnp.mean(q * xhat, axis=-1, keepdims=True)
    )


def sds(shape, dtype):
    return jax.ShapeDtypeStruct(shape, dtype)


PLAN = (
    (((0, 48, 'zxy'), (48, 48, 'zxy'), (96, 32, 'xyz')), ((0, 128, 'zyx'),), ((0, 32, 'zxy'), (32, 32, 'zxy'), (64, 32, 'zyx'), (96, 32, 'zxy')), ((0, 128, 'xyz'), (128, 128, 'zxy'), (256, 128, 'zyx'), (384, 128, 'zxy'))),
    (
        (2, 's'), (8, 's'), (1, 's'), ('tok', 0), ('vec',), (0, 's'), (2, 'f'), ('norm', 0), (8, 'f'),
        ('pick',), (2, 'm'), (1, 'm'), (0, 'm'), (3, 's'), ('pass',), ('tok', 1), (2, 'r0'), (1, 'f'),
        (4, 's'), (2, 'r1'), (0, 'f'), (5, 's'), (4, 'm'), (3, 'm'), (6, 's'), (7, 's'), ('maps',),
        (1, 'g1'), ('norm', 1), (2, 'r2'), ('tokfwd', 0), (9, 's'), (10, 's'), (1, 'g2'), ('tokfwd', 1),
        (0, 'g1'), ('red', 0), (8, 'm'), (5, 'm'), ('red', 1), (11, 's'), (0, 'g2'), ('norm', 2),
        ('norm', 3), ('red', 2), ('red', 3), ('wq',), ('qkv', 0, 0, 2), (6, 'm'), ('qkv', 0, 2, 4), (4, 'f'),
        ('qkv', 0, 4, 6), ('qkv', 1, 0, 2), ('qkv', 1, 2, 4), ('qkv', 1, 4, 6), ('qkv', 2, 2, 4),
        ('qkv', 2, 4, 6), (7, 'm'), (4, 'g1'), ('qkv', 3, 2, 4), ('qkv', 3, 4, 6), ('keep',), (3, 'f'),
        ('att', 0, 0), (10, 'm'), ('att', 0, 1), (8, 'r0'), (5, 'f'), (6, 'f'), (9, 'm'), ('att', 1, 0),
        ('att', 1, 1), ('att', 2, 0), ('att', 2, 1), (8, 'r1'), (5, 'g1'), (7, 'f'), ('att', 3, 0),
        (3, 'g1'), (11, 'm'), ('att', 3, 1), (3, 'g2'), ('swap',), (10, 'f'), (4, 'g2'), (6, 'g1'),
        (7, 'g1'), (9, 'f'), (6, 'g2'), (5, 'g2'), ('proj',), (7, 'g2'), (9, 'g1'), ('norm2',), (10, 'g1'),
        ('fc1', 0), (11, 'f'), ('fc1', 1), ('fc1', 2), (10, 'g2'), ('fc1', 3), (11, 'g1'), ('fc1', 4),
        ('fc1', 5), ('fc1', 6), (8, 'r2'), (11, 'g2'), ('fc1', 7), (9, 'g2'), ('fc2', 2), ('fc2', 1),
        ('fc2', 3), ('fc2', 0), ('end',),
    ),
)
QB = 512
NSEM = (230, 90)


def gelu_parts(h):
    bell = jnp.exp(-0.5 * h * h)
    t = 1.0 / (1.0 + (0.3275911 * 0.5**0.5) * jnp.abs(h))
    poly = 1.061405429 * t - 1.453152027
    for co in (1.421413741, -0.284496736, 0.254829592):
        poly = poly * t + co
    tail = 0.5 * poly * t * bell
    cdf = jnp.where(h < 0.0, tail, 1.0 - tail)
    return h * cdf, cdf + h * bell * 0.3989422804014327


def row_table():
    half = 10
    freq = 10000.0 ** (-np.arange(half) / half)
    ang = np.arange(16)[:, None] * freq
    whole = np.zeros((48, 256))
    for p in range(3):
        rows = slice(16 * p, 16 * p + 16)
        for head in range(2):
            at = head * HD + p * 2 * half
            whole[rows, at : at + half] = np.cos(ang)
            whole[rows, at + half : at + 2 * half] = np.cos(ang)
            whole[rows, 128 + at : 128 + at + half] = -np.sin(ang)
            whole[rows, 128 + at + half : 128 + at + 2 * half] = np.sin(ang)
    for head in range(2):
        whole[:16, head * HD + 60 : head * HD + HD] = 1.0
    whole = whole.astype(np.float32)
    pieces = []
    for _ in range(3):
        piece = whole.astype(BF)
        pieces.append(np.asarray(piece))
        whole = whole - piece.astype(np.float32)
    return np.stack(pieces)


def turns(places, table):
    level = lax.broadcasted_iota(jnp.int32, (16, places.shape[1]), 0).astype(F32)
    hot = jnp.concatenate([(level == places[p : p + 1]).astype(F32) for p in range(3)], axis=0)
    hot = hot.astype(BF)
    return mm_tn(hot, table[0]) + mm_tn(hot, table[1]) + mm_tn(hot, table[2])


def unshuffle():
    i = lax.broadcasted_iota(jnp.int32, (128, 128), 0)
    j = lax.broadcasted_iota(jnp.int32, (128, 128), 1)
    k, dp, r = i // 16, lax.rem(i, 16) // 2, lax.rem(i, 2)
    return (j == dp * 16 + r * 8 + k).astype(F32).astype(BF)


def front_kernel(nz, cfg, *refs):
    (tok, cot, qkv, proj, fc1, fc2, vecs, places, index, ad, table) = refs[:11]
    (out, gres, do_o, q_o, k_o, v_o, o_o, lse_o, n1_o, red_o, wq_o, dn, up, pall, idxs,
     gap, gbp, ga1, gb1, ga2, gb2, vf) = refs[11:33]
    (buf4, wq, wp, w1, w2, q, kv, att, accs, res, n2s,
     vall, selb, adall, small, tab, ssem, rsem, lsem) = refs[33:]
    (r_p_s, r_1_s, g_r2_s, r_2_s, g_r1_s) = [small.at[i] for i in range(5)]
    k = Links(ssem, rsem, lsem, nz)
    c, d, s = k.c, k.d, k.s
    ndp = 2 * nz
    slope, o, gatt, gn2 = kv, q, att, gres
    seqs = [k.core, k.xn, k.diag]
    dps = [(lax.rem(d + j, ndp), s) for j in range(1, ndp)]
    k.barrier(seqs + [k.yn] + [p for p in dps])
    late = []

    def push(src, dst, land, dev):
        i = k.new()
        cp = k.remote(i, src, dst, dev)
        cp.start()
        late.append(cp.wait_send)
        return k.remote(i, src, land, dev).wait_recv

    def send_later(src, dst, land, dev):
        i = k.new()
        cp = k.remote(i, src, dst, dev)

        def start():
            cp.start()
            late.append(cp.wait_send)

        return start, k.remote(i, src, land, dev).wait_recv

    def keep(src, dst):
        i = k.newl()
        cp = k.local(i, src, dst)
        cp.start()
        return cp.wait

    idxs[d] = index[...]
    wait_idx = [
        push(index, idxs.at[d], idxs.at[lax.rem(d + ndp - j, ndp)], dps[j - 1])
        for j in range(1, ndp)
    ]
    vall[s] = vecs[...]
    seq_of = [s + 1 - 2 * c, s + 2 - 4 * k.x, 3 - s]
    wait_vec = [push(vecs, vall.at[s], vall.at[seq_of[r]], seqs[r]) for r in range(3)]
    pall[0] = places[...]
    wait_pos = [push(places, pall.at[r + 1], pall.at[r + 1], seqs[r]) for r in range(3)]
    own_tok = keep(tok, buf4.at[0])
    tok_core = push(tok, buf4.at[1], buf4.at[1], k.core)
    halves = [pl.ds(0, 256), pl.ds(256, 256)]
    tok_x = [send_later(tok.at[h], buf4.at[2, h], buf4.at[2, h], k.xn) for h in halves]
    tok_on = [k.remote(k.new(), buf4.at[2, h], buf4.at[3, h], k.core) for h in halves]
    cuts, order = cfg
    parts = (
        qkv_parts(k, qkv, wq, cuts[0])
        + wide_parts(k, proj, wp, cuts[1])
        + wide_parts(k, fc1, w1, cuts[2])
        + wide_parts(k, fc2, w2, cuts[3])
    )
    groups = []
    n = 0
    for cs in cuts:
        groups.append(parts[n : n + len(cs)])
        n += len(cs)
    state = {}

    def a_tok(h):
        tok_x[h][0]()

    def a_tokfwd(h):
        tok_x[h][1]()
        tok_on[h].start()

    def a_pick():
        for w in wait_idx:
            w()
        for j in range(ndp):
            dest = lax.rem(d + j, ndp)
            who = idxs[dest]
            total = jnp.zeros((16, 512), F32)
            for a in range(NA):
                total += jnp.where(who[0:1, 0:1] == float(a), ad[a].astype(F32), 0.0)
            selb[j] = total.astype(BF)
        adall[s, d] = selb[0]
        state["ad"] = [
            push(selb.at[j], adall.at[s, d], adall.at[s, lax.rem(d + ndp - j, ndp)], dps[j - 1])
            for j in range(1, ndp)
        ]

    def a_pass():
        for w in state["ad"]:
            w()
        state["ad4"] = [
            push(adall.at[s], adall.at[s], adall.at[seq_of[r]], seqs[r]) for r in range(3)
        ]

    def a_maps():
        for w in state["ad4"]:
            w()
        shuffle = unshuffle()
        for t in range(4):
            rows = mm(shuffle, adall[t].reshape(128, 512)).astype(BF)
            for b in range(8):
                piece = rows[16 * b : 16 * b + 16]
                at = b * 512
                nd = dn.shape[1] // 4
                nu = up.shape[1] // 4
                cut = min(max(nd - at, 0), 512)
                if cut:
                    dn[:, t * nd + at : t * nd + at + cut] = piece[:, :cut]
                if cut < 512:
                    b0 = t * nu + at + cut - nd
                    up[:, b0 : b0 + 512 - cut] = piece[:, cut:]

    def a_vec():
        for w in wait_vec:
            w()
        for t in range(4):
            vf[:, t * 256 : t * 256 + 256] = vall[t].astype(F32)

    def a_norm(slot):
        if slot < 2:
            (own_tok, tok_core)[slot]()
        else:
            for cp in tok_on:
                cp.wait_send() if slot == 2 else cp.wait_recv()
        if slot == 0:
            for w in wait_pos:
                w()
        xhat, _ = norm_parts(buf4[slot].astype(F32))
        buf4[slot] = (xhat * vf[0:1, :] + vf[1:2, :]).astype(BF)

    def a_wq():
        for p in groups[0]:
            p.arrive()
        late.append(keep(wq, wq_o))

    def role_cols(role):
        return pl.ds(pl.multiple_of((4 * (role // 2) + 2 * (role % 2) + c) * 256, 256), 256)

    def role_bias(role):
        lg = pl.multiple_of((2 * (role % 2) + c) * 256, 256)
        return vf[4 + role // 2 : 5 + role // 2, pl.ds(lg, 256)]

    def a_red(slot):
        red_o[slot] = mm_nt(buf4[slot], dn[:, :D]).astype(BF)

    def a_qkv(slot, first, last):
        if first < 4:
            if state.get("tab") != slot:
                tab[...] = turns(pall[slot], table)
                state["tab"] = slot
            cos, sin = tab[:, :128], tab[:, 128:]
        h, low = buf4[slot], red_o[slot]
        rows = pl.ds(slot * 512, 512)
        for role in range(first, last):
            val = mm(h, wq[role_slot(role, c)].reshape(D, 256)) + role_bias(role) + mm(low, up[:, role_cols(role)])
            cols = pl.ds((role % 2) * 256, 256)
            if role < 2:
                q[rows, cols] = (turn(val, cos, sin) * (LOG2E * HD**-0.5)).astype(BF)
            elif role < 4:
                kv[slot, :, (role % 2) * 256 : (role % 2) * 256 + 256] = turn(val, cos, sin).astype(BF)
            else:
                kv[slot, :, 512 + (role % 2) * 256 : 768 + (role % 2) * 256] = val.astype(BF)

    def a_keep():
        state["n1"] = keep(buf4, n1_o)
        state["q"] = keep(q, q_o)
        state["kv"] = [keep(kv.at[:, :, pl.ds(512 * i, 512)], (k_o, v_o)[i]) for i in range(2)]

    def a_att(pair, qb):
        lane_i = lax.broadcasted_iota(jnp.int32, (1, 128), 1)
        if "q" in state:
            state.pop("q")()
        cols = pl.ds(pair * 128, 128)
        rows = pl.ds(qb * QB, QB)
        ks, qs = kv[:, :, cols].reshape(-1, 128), q[rows, cols]
        vt = kv[:, :, pl.ds(512 + pair * 128, 128)].reshape(-1, 128).T
        outs = []
        for e in range(2):
            mine = (lane_i < 64) if e == 0 else (lane_i >= 64)
            st = mm_nt(ks, jnp.where(mine, qs, jnp.zeros_like(qs)))
            top = jnp.max(st, axis=0, keepdims=True)
            pr = jnp.exp2(st - top)
            total = jnp.sum(pr, axis=0, keepdims=True)
            outs.append(mm(vt[64 * e : 64 * e + 64], pr.astype(BF)) / total)
            lse_o[pair, e : e + 1, pl.ds(qb * QB, QB)] = top + jnp.log2(total)
        o[rows, cols] = jnp.concatenate(outs, axis=0).T.astype(BF)

    def a_swap():
        late.append(keep(o, o_o))
        state["att"] = []
        for lg in range(2):
            cols = pl.ds(lg * 256, 256)
            state["att"].append(keep(o.at[pl.ds(0, 512), cols], att.at[2 * lg + c]))
            state["att"].append(
                push(o.at[pl.ds(512, 512), cols], att.at[2 * lg + c], att.at[2 * lg + 1 - c], k.core)
            )

    def a_proj():
        for w in state["att"] + state["kv"]:
            w()
        own = keep(tok, n2s)
        own()
        for p in groups[1]:
            p.arrive()
        low = jnp.zeros((512, 16), F32)
        for g in range(4):
            low += mm_nt(att[g], dn[:, D + g * 256 : D + g * 256 + 256])
        low = low.astype(BF)
        r_p_s[...] = low
        for t in range(4):
            cols = pl.ds(t * 256, 256)
            val = mm(low, up[:, 3 * D + t * 256 : 3 * D + t * 256 + 256]) + vf[7:8, cols]
            for g in range(4):
                val += mm(att[g], wp[t // 2, t % 2, g].reshape(256, 256))
            res[:, cols] = n2s[:, cols].astype(F32) + val

    def a_norm2():
        xhat, _ = norm_parts(res[...])
        n2 = (xhat * vf[2:3, :] + vf[3:4, :]).astype(BF)
        n2s[...] = n2
        r_1_s[...] = mm_nt(n2, dn[:, 2 * D : 3 * D]).astype(BF)
        g_r2_s[...] = mm_nt(cot[...], up[:, 4 * D + FF :]).astype(BF)
        accs[...] = jnp.zeros_like(accs)
        gn2[...] = jnp.zeros_like(gn2)
        state["n1"]()

    def a_fc1(i):
        if i == 0:
            for p in groups[2]:
                p.arrive()
        t, h = i // 2, i % 2
        w = w1[t // 2, t % 2, :, :, :, h * 512 : h * 512 + 512].reshape(D, 512)
        bias = jnp.concatenate(
            [vf[9 + 2 * h + b : 10 + 2 * h + b, t * 256 : t * 256 + 256] for b in range(2)], axis=1
        )
        hid = mm(n2s[...], w) + bias
        hid += mm(r_1_s[...], up[:, 4 * D + i * 512 : 4 * D + i * 512 + 512])
        a, sl = gelu_parts(hid)
        a = a.astype(BF)
        for j in range(4):
            buf4[j, :, i * 128 : i * 128 + 128] = a[:, j * 128 : j * 128 + 128]
            slope[j, :, i * 128 : i * 128 + 128] = sl[:, j * 128 : j * 128 + 128].astype(BF)

    def a_fc2(j):
        groups[3][j].arrive()
        a = buf4[j]
        hcols = [3 * D + i * 512 + j * 128 for i in range(8)]
        d2 = jnp.concatenate([dn[:, h : h + 128] for h in hcols], axis=1)
        low2 = mm_nt(a, d2)
        w = jnp.concatenate(
            [
                w2[t // 2, t % 2, :, :, j * 128 : j * 128 + 128, :].reshape(1024, 256)
                for t in range(4)
            ],
            axis=1,
        )
        g = mm_nt(cot[...], w) + mm(g_r2_s[...], d2)
        accs[...] += mm(a, w)
        gh = (g * slope[j].astype(F32)).astype(BF)
        w = jnp.concatenate(
            [
                w1[i // 4, (i // 2) % 2, :, :, :, (i % 2) * 512 + j * 128 : (i % 2) * 512 + j * 128 + 128].reshape(D, 128)
                for i in range(8)
            ],
            axis=1,
        )
        gn2[...] += mm_nt(gh, w)
        u1 = jnp.concatenate(
            [up[:, 4 * D + i * 512 + j * 128 : 4 * D + i * 512 + j * 128 + 128] for i in range(8)],
            axis=1,
        )
        low1 = mm_nt(gh, u1)
        state["r2"] = low2 if "r2" not in state else state["r2"] + low2
        state["g1"] = low1 if "g1" not in state else state["g1"] + low1
        ga2[j] = mm_tn(g_r2_s[...], a)
        gb1[j] = mm_tn(r_1_s[...], gh)

    def a_end():
        r_2, g_r1 = state["r2"].astype(BF), state["g1"].astype(BF)
        g_n2 = gn2[...] + mm(g_r1, dn[:, 2 * D : 3 * D])
        xhat, inv = norm_parts(res[...])
        g_res = cot[...].astype(F32) + norm_back(g_n2, xhat, inv, vf[2:3, :])
        gres[...] = g_res
        gb = g_res.astype(BF)
        g_rp = mm_nt(gb, up[:, 3 * D : 4 * D]).astype(BF)
        for g in range(4):
            gap[:, g * 256 : g * 256 + 256] = mm_tn(g_rp, att[g])
            val = mm(g_rp, dn[:, D + g * 256 : D + g * 256 + 256])
            for t in range(4):
                w = wp[t // 2, t % 2, g].reshape(256, 256)
                val += mm_nt(gb[:, t * 256 : t * 256 + 256], w)
            gatt[g] = val.astype(BF)
        waits = []
        for lg in range(2):
            cols = pl.ds(lg * 256, 256)
            top, low = pl.ds(0, 512), pl.ds(512, 512)
            waits.append(keep(gatt.at[2 * lg + c], do_o.at[top, cols]))
            waits.append(
                push(gatt.at[2 * lg + 1 - c], do_o.at[low, cols], do_o.at[low, cols], k.core)
            )
        u2 = up[:, 4 * D + FF :]
        out[...] = (res[...] + accs[...] + vf[8:9, :] + mm(r_2, u2)).astype(BF)
        gb2[...] = mm_tn(r_2, cot[...])
        ga1[...] = mm_tn(g_r1, n2s[...])
        gbp[...] = mm_tn(r_p_s[...], gb)
        for w in waits:
            w()

    acts = {
        "tok": a_tok, "tokfwd": a_tokfwd, "pick": a_pick, "pass": a_pass, "maps": a_maps, "vec": a_vec,
        "norm": a_norm, "wq": a_wq, "red": a_red, "qkv": a_qkv, "keep": a_keep, "att": a_att,
        "swap": a_swap, "proj": a_proj, "norm2": a_norm2, "fc1": a_fc1, "fc2": a_fc2, "end": a_end,
    }
    for name, *args in order:
        if isinstance(name, int):
            parts[name].step(args[0])
        else:
            acts[name](*args)
    for w in late:
        w()
    for p in parts:
        p.finish()
    assert k.nr <= NSEM[0] and k.nl <= NSEM[1]


def front(nz, cfg, tok, cot, qkv, proj, fc1, fc2, vecs, places, index, ad):
    anys, vm = pl.BlockSpec(memory_space=pl.ANY), pl.BlockSpec(memory_space=pltpu.VMEM)
    ndp = 2 * nz
    rows = tok.shape[0]
    nd, nu = 3 * D + FF, 5 * D + FF
    outs = [
        (vm, (rows, D), BF), (vm, (rows, D), F32), (anys, (2 * rows, 512), BF),
        (anys, (2 * rows, 512), BF), (anys, (4, rows, 512), BF), (anys, (4, rows, 512), BF),
        (anys, (2 * rows, 512), BF), (vm, (4, 2, 2 * rows), F32), (anys, (4, rows, D), BF),
        (vm, (4, rows, 16), BF), (anys, (2, 4, nz, 2, qkv.shape[1], 256), BF), (vm, (16, nd), BF),
        (vm, (16, nu), BF), (vm, (4, 8, rows), F32), (vm, (ndp, 8, 128), F32),
        (vm, (16, D), F32), (vm, (16, D), F32), (vm, (16, D), F32), (vm, (4, 16, 1024), F32),
        (vm, (4, 16, 1024), F32), (vm, (16, D), F32), (vm, (16, D), F32),
    ]
    scratch = [
        ((4, rows, D), BF), ((2, 4, nz, 2, qkv.shape[1], 256), BF),
        ((2, 2, nz, 2) + proj.shape, BF), ((2, 2, nz, 2) + fc1.shape, BF), ((2, 2, nz, 2) + fc2.shape, BF),
        ((2 * rows, 512), BF), ((4, rows, 1024), BF), ((4, rows, 256), BF), ((rows, D), F32),
        ((rows, D), F32), ((rows, D), BF), ((4, 16, 256), BF),
        ((ndp, 16, 512), BF), ((4, ndp, 16, 512), BF), ((5, rows, 16), BF), ((rows, 256), F32),
    ]
    return pl.pallas_call(
        functools.partial(front_kernel, nz, cfg),
        out_shape=[sds(sh, t) for _, sh, t in outs],
        in_specs=[anys, vm, anys, anys, anys, anys, vm, vm, vm, vm, vm],
        out_specs=[m for m, _, _ in outs],
        scratch_shapes=[pltpu.VMEM(sh, t) for sh, t in scratch]
        + [
            pltpu.SemaphoreType.DMA((NSEM[0],)),
            pltpu.SemaphoreType.DMA((NSEM[0],)),
            pltpu.SemaphoreType.DMA((NSEM[1],)),
        ],
        compiler_params=pltpu.CompilerParams(
            collective_id=0, has_side_effects=True, vmem_limit_bytes=VM
        ),
    )(tok, cot, qkv, proj, fc1, fc2, vecs, places, index, ad, jnp.asarray(row_table()))


def back_kernel(nz, *refs):
    (q_i, k_i, v_i, o_i, do_i, n1_i, wq_i, tok_i, gres_i, lse, red, dn, up, pall, idxs, vf,
     gap, gbp, ga1, gb1, ga2, gb2, table) = refs[:23]
    ig, gdn, gup = refs[23:26]
    (q, kk, vv, o, do, n1, wcat, tok, gres, acc, dl, dk, dv, gm, upc, gaq, gbq, own, part, gd, gu,
     blk, got, selo, selr, ssem, rsem, lsem) = refs[26:]
    k = Links(ssem, rsem, lsem, nz)
    c, d, s = k.c, k.d, k.s
    ndp = 2 * nz
    rows = tok.shape[0]
    nq = 2 * rows
    seqs = [k.core, k.xn, k.diag]
    seq_of = [s + 1 - 2 * c, s + 2 - 4 * k.x, 3 - s]
    dps = [(lax.rem(d + j, ndp), s) for j in range(1, ndp)]
    late = []

    def keep(src, dst):
        i = k.newl()
        cp = k.local(i, src, dst)
        cp.start()
        return cp.wait

    def push(src, dst, land, dev):
        i = k.new()
        cp = k.remote(i, src, dst, dev)
        cp.start()
        late.append(cp.wait_send)
        return k.remote(i, src, land, dev).wait_recv

    first = [keep(a, b) for a, b in ((q_i, q), (k_i, kk), (v_i, vv), (o_i, o), (do_i, do))]
    later = [keep(wq_i.at[role_slot(r, c)], wcat.at[:, pl.ds(256 * r, 256)]) for r in range(6)]
    later += [keep(a, b) for a, b in ((n1_i, n1), (tok_i, tok), (gres_i, gres))]
    meet = k.greet(seqs + dps)
    for w in first:
        w()
    lane = lax.broadcasted_iota(jnp.int32, (1, 128), 1)

    def attend_back(pair, half):
        cols = pl.ds(pair * 128, 128)
        krows = pl.ds(half * nq, nq)
        qs, dos, ks, vs = q[:, cols], do[:, cols], kk[krows, cols], vv[krows, cols]
        if half == 1:
            r8 = lax.broadcasted_iota(jnp.int32, (8, 128), 0)
            l8 = lax.broadcasted_iota(jnp.int32, (8, 128), 1) // 64
            dl[pair] = lax.dot_general(
                (r8 == l8).astype(F32),
                dos.astype(F32) * o[:, cols].astype(F32),
                (((1,), (1,)), ((), ())),
                precision=lax.Precision.HIGHEST,
                preferred_element_type=F32,
            )
        dks, dvs, dqs = [], [], []
        for e in range(2):
            mine = (lane < 64) if e == 0 else (lane >= 64)
            st = mm_nt(jnp.where(mine, ks, jnp.zeros_like(ks)), qs)
            pr = jnp.exp2(st - lse[pair, e : e + 1, :])
            dp = mm_nt(jnp.where(mine, vs, jnp.zeros_like(vs)), dos)
            ds = (pr * (dp - dl[pair, e : e + 1, :])).astype(BF)
            dvs.append(mm(pr.astype(BF), dos))
            dks.append(mm(ds, qs))
            dqs.append(mm(ks.T[64 * e : 64 * e + 64], ds))
        dk[:, cols] = jnp.where(lane < 64, dks[0], dks[1]) * LN2
        dv[:, cols] = jnp.where(lane < 64, dvs[0], dvs[1])
        dq = jnp.concatenate(dqs, axis=0)
        frows = pl.ds(pair * 128, 128)
        if half == 1:
            acc[frows, :] = dq
        else:
            acc[frows, :] += dq

    def mixed(slot):
        tab = turns(pall[slot], table)
        cos, sin = tab[:, :128], -tab[:, 128:]
        at = pl.ds((slot % 2) * rows, rows)
        f = 0 if slot < 2 else 512
        for role in range(0 if slot < 2 else 2, 6):
            cols = pl.ds((role % 2) * 256, 256)
            if role < 2:
                g = acc[cols, at].T * (HD**-0.5)
                g = turn(g, cos, sin)
            elif role < 4:
                g = turn(dk[at, cols], cos, sin)
            else:
                g = dv[at, cols]
            gm[at, role * 256 : role * 256 + 256] = g.astype(BF)
        g = gm[at, f:]
        low = mm_nt(g, upc[:, f:]).astype(BF)
        ta, tb = mm_tn(low, n1[slot]), mm_tn(red[slot], g)
        if slot == 2:
            gaq[...] = ta
            gbq[:, :512] = jnp.zeros((16, 512), F32)
            gbq[:, f:] = tb
        else:
            gaq[...] += ta
            gbq[:, f:] += tb
        return low

    def into_h(slot, low):
        at = pl.ds((slot % 2) * rows, rows)
        f = 0 if slot < 2 else 512
        return mm_nt(gm[at, f:], wcat[:, f:]) + mm(low, dn[:, :D])

    for pair in range(4):
        attend_back(pair, 1)
    for w in later:
        w()
    for role in range(6):
        at = pl.multiple_of((4 * (role // 2) + 2 * (role % 2) + c) * 256, 256)
        upc[:, role * 256 : role * 256 + 256] = up[:, pl.ds(at, 256)]
    low2 = mixed(2)
    low3 = mixed(3)
    part[0] = into_h(3, low3).astype(BF)
    meet()
    from_core = push(part.at[0], part.at[1], part.at[1], k.core)
    own[...] = into_h(2, low2)
    from_core()
    part[2] = (own[...] + part[1].astype(F32)).astype(BF)
    from_x = push(part.at[2], part.at[3], part.at[3], k.xn)
    gd[:, D : 2 * D] = gap[...]
    gd[:, 2 * D : 3 * D] = ga1[...]
    gu[:, : 3 * D] = jnp.zeros((16, 3 * D), F32)
    gu[:, 3 * D : 4 * D] = gbp[...]
    gu[:, 4 * D + FF :] = gb2[...]
    for j in range(4):
        for i in range(8):
            at = i * 512 + j * 128
            gd[:, 3 * D + at : 3 * D + at + 128] = ga2[j, :, i * 128 : i * 128 + 128]
            gu[:, 4 * D + at : 4 * D + at + 128] = gb1[j, :, i * 128 : i * 128 + 128]
    for pair in range(4):
        attend_back(pair, 0)
    low1 = mixed(1)
    low0 = mixed(0)
    gd[:, :D] = gaq[...]
    for role in range(6):
        at = pl.multiple_of((4 * (role // 2) + 2 * (role % 2) + c) * 256, 256)
        gu[:, pl.ds(at, 256)] = gbq[:, role * 256 : role * 256 + 256]
    nd, nu = gd.shape[1] // 4, gu.shape[1] // 4
    for t in range(4):
        blk[t, :, :nd] = gd[:, t * nd : t * nd + nd].astype(BF)
        blk[t, :, nd:] = gu[:, t * nu : t * nu + nu].astype(BF)
    sums = [push(blk.at[seq_of[r]], got.at[r], got.at[r], seqs[r]) for r in range(3)]
    part[4] = into_h(1, low1).astype(BF)
    from_core = push(part.at[4], part.at[5], part.at[5], k.core)
    for w in sums:
        w()
    total = blk[s].astype(F32)
    for r in range(3):
        total += got[r].astype(F32)
    total = total.astype(BF)
    stack = jnp.concatenate([total[:, b * 512 : b * 512 + 512] for b in range(8)], axis=0)
    selo[...] = mm_tn(unshuffle(), stack).astype(BF).reshape(ndp, 16, 512)
    selr[d] = selo[d]
    ends = [
        push(selo.at[lax.rem(d + j, ndp)], selr.at[d], selr.at[lax.rem(d + ndp - j, ndp)], dps[j - 1])
        for j in range(1, ndp)
    ]
    own[...] = into_h(0, low0)
    xhat, inv = norm_parts(tok[...].astype(F32))
    from_core()
    from_x()
    g_n1 = own[...] + part[5].astype(F32) + part[3].astype(F32)
    ig[...] = (gres[...] + norm_back(g_n1, xhat, inv, vf[0:1, :])).astype(BF)
    for w in ends:
        w()
    for a in range(NA):
        out = jnp.zeros((16, 512), F32)
        for j in range(ndp):
            out += jnp.where(idxs[j][0:1, 0:1] == float(a), selr[j].astype(F32), 0.0)
        for r in range(2):
            row = jnp.concatenate([out[8 * r + b : 8 * r + b + 1] for b in range(8)], axis=1)
            gdn[a, r : r + 1, :] = row[:, :nd]
            gup[a, r : r + 1, :] = row[:, nd:]
    for w in late:
        w()
    assert k.nr <= 40 and k.nl <= 20


def back(nz, *args):
    anys, vm = pl.BlockSpec(memory_space=pl.ANY), pl.BlockSpec(memory_space=pltpu.VMEM)
    rows = args[7].shape[0]
    nq = 2 * rows
    ndp = 2 * nz
    scratch = [
        ((nq, 512), BF), ((2 * nq, 512), BF), ((2 * nq, 512), BF), ((nq, 512), BF), ((nq, 512), BF),
        ((4, rows, D), BF), ((D, 1536), BF), ((rows, D), BF), ((rows, D), F32),
        ((512, nq), F32), ((4, 8, nq), F32), ((nq, 512), F32), ((nq, 512), F32),
        ((nq, 1536), BF), ((16, 1536), BF), ((16, D), F32), ((16, 1536), F32), ((rows, D), F32),
        ((6, rows, D), BF), ((16, 3 * D + FF), F32), ((16, 5 * D + FF), F32),
        ((4, 16, 4096), BF), ((3, 16, 4096), BF), ((ndp, 16, 512), BF), ((ndp, 16, 512), BF),
    ]
    return pl.pallas_call(
        functools.partial(back_kernel, nz),
        out_shape=[
            sds((rows, D), BF), sds((NA, 2, (3 * D + FF) // 4), F32), sds((NA, 2, (5 * D + FF) // 4), F32)
        ],
        in_specs=[anys] * 9 + [vm] * (len(args) - 8),
        out_specs=[vm, vm, vm],
        scratch_shapes=[pltpu.VMEM(sh, t) for sh, t in scratch]
        + [
            pltpu.SemaphoreType.DMA((40,)),
            pltpu.SemaphoreType.DMA((40,)),
            pltpu.SemaphoreType.DMA((20,)),
        ],
        compiler_params=pltpu.CompilerParams(
            collective_id=1, has_side_effects=True, vmem_limit_bytes=VM
        ),
    )(*args, jnp.asarray(row_table()))


def fast_shards(
    nz, tokens, positions, adapter_index, qkv_weight, proj_weight, fc1_weight, fc2_weight,
    vectors, fc1_bias, adapter_down, adapter_up, cotangent,
):
    blocks = qkv_weight.reshape(-1, 3, 256)
    blocks = jnp.stack([blocks[:, i] for i in (0, 2, 1)])
    vecs = jnp.concatenate([vectors, fc1_bias.reshape(4, 256), jnp.zeros((3, 256), BF)], axis=0)
    places = jnp.pad(positions[:, 0].astype(F32), ((0, 5), (0, 0)))
    index = jnp.broadcast_to(adapter_index.astype(F32), (8, 128))
    ad = jnp.concatenate([adapter_down, adapter_up], axis=-1).reshape(NA, 16, 512)
    (output, gres, do, q, k, v, o, lse, n1, red, wq, dn, up, pall, idxs,
     gap, gbp, ga1, gb1, ga2, gb2, vf) = front(
        nz, PLAN, tokens[0], cotangent[0], blocks, proj_weight, fc1_weight, fc2_weight,
        vecs, places, index, ad,
    )
    input_grad, down_grad, up_grad = back(
        nz, q, k.reshape(-1, 512), v.reshape(-1, 512), o, do, n1, wq.reshape(2, 4, D, 256), tokens[0],
        gres, lse, red, dn, up, pall, idxs, vf, gap, gbp, ga1, gb1, ga2, gb2,
    )
    return output[None], input_grad[None], down_grad, up_grad


def solution(mesh):
    in_specs = (
        P("dp", "seq", None),
        P(None, "dp", "seq"),
        P("dp", None),
        P("dp", "seq"),
        P("dp", "seq"),
        P("dp", "seq"),
        P("dp", "seq"),
        P(None, "seq"),
        P("seq"),
        P(None, "dp", "seq"),
        P(None, "dp", "seq"),
        P("dp", "seq", None),
    )
    out_specs = (
        P("dp", "seq", None),
        P("dp", "seq", None),
        P(None, "dp", "seq"),
        P(None, "dp", "seq"),
    )
    body = shards
    if mesh.shape["seq"] == 4 and mesh.shape["dp"] == 8:

        def body(tokens, *rest):
            if tokens.shape[0] == 1 and tokens.shape[1] == 512:
                return fast_shards(mesh.shape["dp"] // 2, tokens, *rest)
            return shards(tokens, *rest)

    return jax.shard_map(body, mesh=mesh, in_specs=in_specs, out_specs=out_specs, check_vma=False)
```

```python
import functools
import math

import jax
import jax.numpy as jnp
import numpy as np
from jax import lax
from jax.experimental import pallas as pl
from jax.experimental.pallas import tpu as pltpu
from jax.sharding import PartitionSpec as P

D = 1024
HEADS = 16
HD = 64
FF = 4096
NA = 8


def layer_norm(values, gain_row, shift_row):
    centre = values - jnp.mean(values, axis=-1, keepdims=True)
    spread = jnp.mean(centre * centre, axis=-1, keepdims=True)
    return centre * lax.rsqrt(spread + 1e-06) * gain_row + shift_row


def rotate(values, places, direction):
    rot_span = 2 * (values.shape[-1] // 3 // 2)
    half_span = rot_span // 2
    inverse_freq = 10000.0 ** (-jnp.arange(half_span, dtype=jnp.float32) / half_span)
    pieces = []
    for axis_id in range(3):
        segment = values[..., axis_id * rot_span : (axis_id + 1) * rot_span]
        angles = places[axis_id].astype(jnp.float32)[..., None, None] * inverse_freq
        cosine = jnp.cos(angles)
        sine_wave = direction * jnp.sin(angles)
        lower_part = segment[..., :half_span]
        upper_part = segment[..., half_span:]
        pieces.append(lower_part * cosine - upper_part * sine_wave)
        pieces.append(lower_part * sine_wave + upper_part * cosine)
    pieces.append(values[..., 3 * rot_span :])
    return jnp.concatenate(pieces, axis=-1)


def exact_gelu(values):
    return jax.nn.gelu(values, approximate=False)


def fetch_weight(weight):
    joined = lax.all_gather(weight, "seq", axis=1, tiled=True)
    return lax.all_gather(joined, "dp", axis=0, tiled=True)


def adapted(inputs, weight, shift_row, down_part, up_part):
    base = jnp.einsum("cti,io->cto", inputs, weight, preferred_element_type=jnp.float32)
    reduced = jnp.einsum(
        "cti,cri->ctr", inputs, down_part, preferred_element_type=jnp.float32
    ).astype(jnp.bfloat16)
    result = (
        base
        + shift_row
        + jnp.einsum("ctr,cro->cto", reduced, up_part, preferred_element_type=jnp.float32)
    )
    return (result, reduced)


def adapted_back(grad_out, inputs, weight, down_part, up_part, reduced):
    grad_in = jnp.einsum("cto,io->cti", grad_out, weight, preferred_element_type=jnp.float32)
    grad_reduced = jnp.einsum(
        "cto,cro->ctr", grad_out, up_part, preferred_element_type=jnp.float32
    ).astype(jnp.bfloat16)
    grad_in = grad_in + jnp.einsum(
        "ctr,cri->cti", grad_reduced, down_part, preferred_element_type=jnp.float32
    )
    grad_down = jnp.einsum("ctr,cti->cri", grad_reduced, inputs, preferred_element_type=jnp.float32)
    grad_up = jnp.einsum("ctr,cto->cro", reduced, grad_out, preferred_element_type=jnp.float32)
    return (grad_in, grad_down, grad_up)


def split_tokens(source, split_count):
    old_shape = source.shape
    shaped = source.reshape(
        (old_shape[0], split_count, old_shape[1] // split_count) + old_shape[2:]
    )
    return jnp.moveaxis(shaped, 1, 0)


def score_grads(
    query_block, key_block, value_block, grad_block, log_block, delta_block, score_scale
):
    scores = (
        jnp.einsum("cqhd,ckhd->chqk", query_block, key_block, preferred_element_type=jnp.float32)
        * score_scale
    )
    probabilities = jnp.exp(scores - log_block[..., None])
    grad_probs = jnp.einsum(
        "cqhd,ckhd->chqk", grad_block, value_block, preferred_element_type=jnp.float32
    )
    grad_scores = (probabilities * (grad_probs - delta_block[..., None])).astype(jnp.bfloat16)
    return (probabilities.astype(jnp.bfloat16), grad_scores)


def shards(
    tokens,
    positions,
    adapter_index,
    qkv_weight,
    proj_weight,
    fc1_weight,
    fc2_weight,
    vectors,
    fc1_bias,
    adapter_down,
    adapter_up,
    cotangent,
):
    clip_count, tok_count = (tokens.shape[0], tokens.shape[1])
    head_shape = (clip_count, tok_count, HEADS, HD)
    score_scale = HD ** (-0.5)
    small_parts = (
        lax.all_gather(adapter_down, "seq", axis=2, tiled=True),
        lax.all_gather(adapter_up, "seq", axis=2, tiled=True),
        lax.all_gather(vectors, "seq", axis=1, tiled=True),
        lax.all_gather(fc1_bias, "seq", axis=0, tiled=True),
    )
    down_all, up_all = (
        lax.all_gather(small_parts[0], "dp", axis=1, tiled=True),
        lax.all_gather(small_parts[1], "dp", axis=1, tiled=True),
    )
    vector_rows = small_parts[2].astype(jnp.float32)
    hidden_bias = small_parts[3].astype(jnp.float32)
    choose = (adapter_index == jnp.arange(NA, dtype=jnp.int32)[None, :]).astype(jnp.bfloat16)
    down_sel = jnp.einsum(
        "ca,ari->cri", choose, down_all, preferred_element_type=jnp.float32
    ).astype(jnp.bfloat16)
    up_sel = jnp.einsum("ca,aro->cro", choose, up_all, preferred_element_type=jnp.float32).astype(
        jnp.bfloat16
    )
    down_parts = (
        down_sel[:, :, :D],
        down_sel[:, :, D : 2 * D],
        down_sel[:, :, 2 * D : 3 * D],
        down_sel[:, :, 3 * D :],
    )
    up_parts = (
        up_sel[:, :, : 3 * D],
        up_sel[:, :, 3 * D : 4 * D],
        up_sel[:, :, 4 * D : 4 * D + FF],
        up_sel[:, :, 4 * D + FF :],
    )
    inputs = tokens.astype(jnp.float32)
    normed_one = layer_norm(inputs, vector_rows[0], vector_rows[1]).astype(jnp.bfloat16)
    weight_qkv = fetch_weight(qkv_weight)
    mixed_qkv, reduced_qkv = adapted(
        normed_one, weight_qkv, vector_rows[4:7].reshape(3 * D), down_parts[0], up_parts[0]
    )
    queries = rotate(mixed_qkv[..., :D].reshape(head_shape), positions, 1.0).astype(jnp.bfloat16)
    keys_local = rotate(mixed_qkv[..., D : 2 * D].reshape(head_shape), positions, 1.0).astype(
        jnp.bfloat16
    )
    values_local = mixed_qkv[..., 2 * D :].reshape(head_shape).astype(jnp.bfloat16)
    stat_shape = (clip_count, HEADS, tok_count)
    start_state = (
        jnp.full(stat_shape, -jnp.inf, jnp.float32),
        jnp.zeros(stat_shape, jnp.float32),
        jnp.zeros(stat_shape + (HD,), jnp.float32),
    )
    key_piece = lax.all_gather(keys_local, "seq", axis=1, tiled=True)
    value_piece = lax.all_gather(values_local, "seq", axis=1, tiled=True)
    split_count = key_piece.shape[1] // math.gcd(key_piece.shape[1], 256)

    def inner_step(running, block_pair):
        top_score, row_total, weighted = running
        key_block, value_block = block_pair
        scores = (
            jnp.einsum("cqhd,ckhd->chqk", queries, key_block, preferred_element_type=jnp.float32)
            * score_scale
        )
        new_top = jnp.maximum(top_score, jnp.max(scores, axis=-1))
        factor = jnp.exp(top_score - new_top)
        weights = jnp.exp(scores - new_top[..., None])
        row_total = row_total * factor + jnp.sum(weights, axis=-1)
        weighted = weighted * factor[..., None] + jnp.einsum(
            "chqk,ckhd->chqd",
            weights.astype(jnp.bfloat16),
            value_block,
            preferred_element_type=jnp.float32,
        )
        return ((new_top, row_total, weighted), None)

    result, unused = lax.scan(
        inner_step,
        start_state,
        (split_tokens(key_piece, split_count), split_tokens(value_piece, split_count)),
    )
    top_score, row_total, weighted = result
    log_total = top_score + jnp.log(row_total)
    heads_tok = jnp.swapaxes(weighted / row_total[..., None], 1, 2)
    attended = heads_tok.reshape(clip_count, tok_count, D).astype(jnp.bfloat16)
    weight_proj = fetch_weight(proj_weight)
    projected, reduced_proj = adapted(
        attended, weight_proj, vector_rows[7], down_parts[1], up_parts[1]
    )
    residual = inputs + projected
    normed_two = layer_norm(residual, vector_rows[2], vector_rows[3]).astype(jnp.bfloat16)
    weight_up = fetch_weight(fc1_weight)
    hidden, reduced_up = adapted(normed_two, weight_up, hidden_bias, down_parts[2], up_parts[2])
    activated = exact_gelu(hidden).astype(jnp.bfloat16)
    weight_down = fetch_weight(fc2_weight)
    branch, reduced_down = adapted(
        activated, weight_down, vector_rows[8], down_parts[3], up_parts[3]
    )
    output = (residual + branch).astype(jnp.bfloat16)
    weight_down = fetch_weight(fc2_weight)
    grad_act, gdown_four, gup_four = adapted_back(
        cotangent, activated, weight_down, down_parts[3], up_parts[3], reduced_down
    )
    unused, gelu_back = jax.vjp(exact_gelu, hidden)
    grad_hidden = gelu_back(grad_act)[0].astype(jnp.bfloat16)
    weight_up = fetch_weight(fc1_weight)
    grad_normed_two, gdown_three, gup_three = adapted_back(
        grad_hidden, normed_two, weight_up, down_parts[2], up_parts[2], reduced_up
    )

    def norm_two(values):
        return layer_norm(values, vector_rows[2], vector_rows[3])

    unused, norm_two_back = jax.vjp(norm_two, residual)
    grad_residual = cotangent.astype(jnp.float32) + norm_two_back(grad_normed_two)[0]
    weight_proj = fetch_weight(proj_weight)
    grad_attended, gdown_two, gup_two = adapted_back(
        grad_residual.astype(jnp.bfloat16),
        attended,
        weight_proj,
        down_parts[1],
        up_parts[1],
        reduced_proj,
    )
    grad_tok = grad_attended.astype(jnp.bfloat16).reshape(head_shape)
    delta_heads = jnp.swapaxes(jnp.sum(grad_tok.astype(jnp.float32) * heads_tok, axis=-1), 1, 2)
    whole_keys, whole_values = (
        lax.all_gather(keys_local, "seq", axis=1, tiled=True),
        lax.all_gather(values_local, "seq", axis=1, tiled=True),
    )
    block_count = whole_keys.shape[1] // math.gcd(whole_keys.shape[1], 256)
    key_blocks = split_tokens(whole_keys, block_count)
    value_blocks = split_tokens(whole_values, block_count)
    zero_heads = jnp.zeros(head_shape, jnp.float32)

    def back_step(grad_query, block_pair):
        key_block, value_block = block_pair
        probs_low, grad_scores = score_grads(
            queries, key_block, value_block, grad_tok, log_total, delta_heads, score_scale
        )
        grad_query = (
            grad_query
            + jnp.einsum(
                "chqk,ckhd->cqhd", grad_scores, key_block, preferred_element_type=jnp.float32
            )
            * score_scale
        )
        grad_key = (
            jnp.einsum("chqk,cqhd->ckhd", grad_scores, queries, preferred_element_type=jnp.float32)
            * score_scale
        )
        grad_value = jnp.einsum(
            "chqk,cqhd->ckhd", probs_low, grad_tok, preferred_element_type=jnp.float32
        )
        return (grad_query, jnp.concatenate([grad_key, grad_value], axis=-1))

    grad_query, key_terms = lax.scan(back_step, zero_heads, (key_blocks, value_blocks))
    key_terms = jnp.moveaxis(key_terms, 0, 1).reshape(
        clip_count, whole_keys.shape[1], HEADS, 2 * HD
    )
    summed = lax.psum_scatter(
        key_terms.astype(jnp.bfloat16), "seq", scatter_dimension=1, tiled=True
    ).astype(jnp.float32)
    grad_key = summed[..., :HD]
    grad_value = summed[..., HD:]
    grad_mixed = jnp.concatenate(
        [
            rotate(grad_query, positions, -1.0).reshape(clip_count, tok_count, D),
            rotate(grad_key, positions, -1.0).reshape(clip_count, tok_count, D),
            grad_value.reshape(clip_count, tok_count, D),
        ],
        axis=-1,
    ).astype(jnp.bfloat16)
    weight_qkv = fetch_weight(qkv_weight)
    grad_normed_one, gdown_one, gup_one = adapted_back(
        grad_mixed, normed_one, weight_qkv, down_parts[0], up_parts[0], reduced_qkv
    )

    def norm_one(values):
        return layer_norm(values, vector_rows[0], vector_rows[1])

    unused, norm_one_back = jax.vjp(norm_one, inputs)
    input_grad = (grad_residual + norm_one_back(grad_normed_one)[0]).astype(jnp.bfloat16)
    choose_wide = choose.astype(jnp.float32)
    clip_down = jnp.concatenate([gdown_one, gdown_two, gdown_three, gdown_four], axis=-1)
    clip_up = jnp.concatenate([gup_one, gup_two, gup_three, gup_four], axis=-1)
    down_term = jnp.einsum("ca,cri->ari", choose_wide, clip_down, precision=lax.Precision.HIGHEST)
    up_term = jnp.einsum("ca,cro->aro", choose_wide, clip_up, precision=lax.Precision.HIGHEST)
    down_grad, up_grad = (
        lax.psum_scatter(
            down_term.astype(jnp.bfloat16), "seq", scatter_dimension=2, tiled=True
        ).astype(jnp.float32),
        lax.psum_scatter(
            up_term.astype(jnp.bfloat16), "seq", scatter_dimension=2, tiled=True
        ).astype(jnp.float32),
    )
    down_grad, up_grad = (
        lax.psum_scatter(
            down_grad.astype(jnp.bfloat16), "dp", scatter_dimension=1, tiled=True
        ).astype(jnp.float32),
        lax.psum_scatter(
            up_grad.astype(jnp.bfloat16), "dp", scatter_dimension=1, tiled=True
        ).astype(jnp.float32),
    )
    return (output, input_grad, down_grad, up_grad)

MESH = pl.DeviceIdType.MESH
BF = jnp.bfloat16
F32 = jnp.float32
LOG2E = 1.4426950408889634
LN2 = 0.6931471805599453
VM = 60 * 1024 * 1024


def mm(a, b):
    return lax.dot_general(a, b, (((1,), (0,)), ((), ())), preferred_element_type=F32)


def mm_nt(a, b):
    return lax.dot_general(a, b, (((1,), (1,)), ((), ())), preferred_element_type=F32)


def mm_tn(a, b):
    return lax.dot_general(a, b, (((0,), (0,)), ((), ())), preferred_element_type=F32)


class Links:
    def __init__(self, ssem, rsem, lsem, nz):
        self.ssem, self.rsem, self.lsem = ssem, rsem, lsem
        self.nr, self.nl = 0, 0
        d, s = lax.axis_index("dp"), lax.axis_index("seq")
        self.d, self.s, self.nz = d, s, nz
        self.z, self.y, self.x, self.c = d // 2, lax.rem(d, 2), s // 2, lax.rem(s, 2)
        self.core = (d, s + 1 - 2 * self.c)
        self.xn = (d, s + 2 - 4 * self.x)
        self.diag = (d, 3 - s)
        self.yn = (d + 1 - 2 * self.y, s)
        self.up, self.down = (d + 2, s), (d - 2, s)
        self.zpeer = [(lax.rem(d + 2 * j, 2 * nz), s) for j in range(nz)]

    def greet(self, peers):
        bar = pltpu.get_barrier_semaphore()
        for dev in peers:
            pl.semaphore_signal(bar, inc=1, device_id=dev, device_id_type=MESH)
        return lambda: pl.semaphore_wait(bar, len(peers))

    def barrier(self, peers):
        self.greet(peers)()

    def new(self, count=1):
        self.nr += count
        return self.nr - count

    def newl(self):
        self.nl += 1
        return self.nl - 1

    def remote(self, i, src, dst, dev):
        return pltpu.make_async_remote_copy(
            src_ref=src,
            dst_ref=dst,
            send_sem=self.ssem.at[i],
            recv_sem=self.rsem.at[i],
            device_id=dev,
            device_id_type=MESH,
        )

    def local(self, i, src, dst):
        return pltpu.make_async_copy(src, dst, self.lsem.at[i])


def guard(cond, body):
    if cond is None:
        body()
    else:
        pl.when(cond)(body)


class Part:
    def __init__(self, links, order, own, region, handover):
        self.k, self.order, self.own = links, order, own
        self.placed = own is None
        self.region, self.handover = region, handover
        k = links
        self.s_own = None if self.placed else k.newl()
        n = k.nz - 1
        self.s_z = k.new(2 * n if order == "xyz" else n)
        self.s_f, self.s_g1, self.s_g2 = k.new(), k.new(), k.new()
        self.pend, self.tail = [], []
        xfirst = order != "zyx"
        self.f, self.g = (k.x, k.y) if xfirst else (k.y, k.x)
        self.fd, self.gd = (k.xn, k.yn) if xfirst else (k.yn, k.xn)
        if self.placed:
            self.own = self.reg(self.f, self.g, k.z)

    def reg(self, fi, gi, zs):
        return self.region(gi, zs, fi) if self.order == "zyx" else self.region(fi, zs, gi)

    def hand(self, cond, fi, zs, gi):
        k = self.k
        x, y = (gi, fi) if self.order == "zyx" else (fi, gi)
        loc, rem = self.handover(x, zs, y)
        ls = [(k.newl(), a, b) for a, b in loc]
        rs = [(k.new(), a, b, w) for a, b, w in rem]

        def start():
            for i, a, b in ls:
                k.local(i, a, b).start()
            for i, a, b, _ in rs:
                k.remote(i, a, b, k.core).start()

        def arrive():
            for i, a, b in ls:
                k.local(i, a, b).wait()
            for i, a, b, w in rs:
                k.remote(i, a, w, k.core).wait_recv()

        def sent():
            for i, a, b, _ in rs:
                k.remote(i, a, b, k.core).wait_send()

        guard(cond, start)
        self.pend.append((cond, arrive))
        self.tail.append((cond, sent))

    def go(self, cond, copy):
        guard(cond, copy.start)
        self.tail.append((cond, copy.wait_send))

    def own_start(self):
        if not self.placed:
            self.k.local(self.s_own, self.own, self.reg(self.f, self.g, self.k.z)).start()

    def own_wait(self):
        if not self.placed:
            self.k.local(self.s_own, self.own, self.reg(self.f, self.g, self.k.z)).wait()

    def step(self, name):
        getattr(self, ("l_" if self.order == "xyz" else "z_") + name)()

    def z_s(self):
        k, f, g = self.k, self.f, self.g
        self.own_start()
        for j in range(1, k.nz):
            self.go(None, k.remote(self.s_z + j - 1, self.own, self.reg(f, g, k.z), k.zpeer[j]))

    def z_m(self):
        k, f, g = self.k, self.f, self.g
        al = slice(None)
        for j in range(1, k.nz):
            at = self.reg(f, g, lax.rem(k.z + k.nz - j, k.nz))
            k.remote(self.s_z + j - 1, self.own, at, k.zpeer[j]).wait_recv()
        self.own_wait()
        mine = self.reg(f, g, al)
        self.go(None, k.remote(self.s_f, mine, mine, self.fd))
        self.go(None, k.remote(self.s_g1, mine, mine, self.gd))

    def z_f(self):
        k, f, g = self.k, self.f, self.g
        al = slice(None)
        new = self.reg(1 - f, g, al)
        k.remote(self.s_f, new, new, self.fd).wait_recv()
        self.go(None, k.remote(self.s_g2, new, new, self.gd))
        self.hand(None, al, al, g)

    def z_g(self):
        k, f, g = self.k, self.f, self.g
        al = slice(None)
        for sem, at in ((self.s_g1, f), (self.s_g2, 1 - f)):
            new = self.reg(at, 1 - g, al)
            k.remote(sem, new, new, self.gd).wait_recv()
        self.hand(None, al, al, 1 - g)

    def l_s(self):
        k, f, g, z = self.k, self.f, self.g, self.k.z
        self.own_start()
        self.go(None, k.remote(self.s_f, self.own, self.reg(f, g, z), self.fd))
        self.go(None, k.remote(self.s_g1, self.own, self.reg(f, g, z), self.gd))

    def l_f(self):
        k, f, g, z = self.k, self.f, self.g, self.k.z
        new = self.reg(1 - f, g, z)
        k.remote(self.s_f, self.own, new, self.fd).wait_recv()
        self.go(None, k.remote(self.s_g2, new, new, self.gd))

    def l_m(self):
        k, f, g, z = self.k, self.f, self.g, self.k.z
        al = slice(None)
        k.remote(self.s_g1, self.own, self.reg(f, 1 - g, z), self.gd).wait_recv()
        new = self.reg(1 - f, 1 - g, z)
        k.remote(self.s_g2, new, new, self.gd).wait_recv()
        self.own_wait()
        four = self.reg(al, al, z)
        self.go(z < k.nz - 1, k.remote(self.s_z, four, four, k.up))
        self.go(z > 0, k.remote(self.s_z + k.nz - 1, four, four, k.down))
        self.hand(None, al, z, al)

    def relay(self, r):
        k, z = self.k, self.k.z
        al = slice(None)
        for sem, here, origin, dev, can in (
            (self.s_z, z > r, z - 1 - r, k.up, z < k.nz - 1),
            (self.s_z + k.nz - 1, z + r < k.nz - 1, z + 1 + r, k.down, z > 0),
        ):
            four = self.reg(al, al, origin)
            guard(here, k.remote(sem + r, four, four, dev).wait_recv)
            if r < k.nz - 2:
                self.go(jnp.logical_and(here, can), k.remote(sem + r + 1, four, four, dev))
            self.hand(here, al, origin, al)

    def l_r0(self):
        self.relay(0)

    def l_r1(self):
        self.relay(1)

    def l_r2(self):
        self.relay(2)

    def arrive(self):
        for cond, body in self.pend:
            guard(cond, body)

    def finish(self):
        for cond, body in self.tail:
            guard(cond, body)


def wide_parts(links, shard, buf, cuts):
    c = links.c
    parts = []
    for r0, n, order in cuts:
        rows = pl.ds(r0, n)

        def region(x, z, y, rows=rows):
            return buf.at[x, c, z, y, rows]

        def handover(x, z, y, rows=rows):
            at = buf.at[x, c, z, y, rows]
            return [], [(at, at, buf.at[x, 1 - c, z, y, rows])]

        parts.append(Part(links, order, shard.at[rows], region, handover))
    return parts


def qkv_parts(links, buf, cuts):
    parts = []
    for r0, n, order in cuts:
        rows = pl.ds(r0, n)

        def region(x, z, y, rows=rows):
            return buf.at[x, pl.ds(0, 3), z, y, rows]

        def handover(x, z, y, rows=rows):
            return [], [
                (buf.at[x, 2, z, y, rows], buf.at[x, 3, z, y, rows], buf.at[x, 3, z, y, rows])
            ]

        parts.append(Part(links, order, None, region, handover))
    return parts


def role_slot(role, c):
    return role // 3, (3 * c, 1 - c, 3 - 2 * c)[role % 3]


def norm_parts(values):
    centre = values - jnp.mean(values, axis=-1, keepdims=True)
    inv = lax.rsqrt(jnp.mean(centre * centre, axis=-1, keepdims=True) + 1e-06)
    return centre * inv, inv


def swap_pairs(v):
    n = v.shape[1]
    j = lax.rem(lax.broadcasted_iota(jnp.int32, (1, n), 1), HD)
    lower = lax.rem(j, 20) < 10
    return jnp.where(lower, pltpu.roll(v, n - 10, 1), pltpu.roll(v, 10, 1))


def turn(v, cos, sin):
    cc, ss = jnp.concatenate([cos, cos], axis=1), jnp.concatenate([sin, sin], axis=1)
    return v * cc + swap_pairs(v) * ss


def norm_back(grad, xhat, inv, gain):
    q = grad * gain
    return inv * (
        q - jnp.mean(q, axis=-1, keepdims=True) - xhat * jnp.mean(q * xhat, axis=-1, keepdims=True)
    )


def sds(shape, dtype):
    return jax.ShapeDtypeStruct(shape, dtype)


PLAN = (
    (((0, 48, 'zxy'), (48, 48, 'zxy'), (96, 32, 'xyz')), ((0, 128, 'zyx'),), ((0, 48, 'zxy'), (48, 48, 'zxy'), (96, 32, 'zyx')), ((0, 128, 'xyz'), (128, 128, 'zxy'), (256, 128, 'zyx'), (384, 128, 'zxy'))),
    (
        (0, 's'), (2, 's'), (7, 's'), ('tok', 0), (1, 's'), (3, 's'), ('vec',), ('norm', 0), (2, 'f'),
        (7, 'f'), ('pick',), (0, 'm'), (1, 'm'), ('pass',), (4, 's'), ('tok', 1), (3, 'm'), (2, 'm'),
        (0, 'f'), ('maps',), (2, 'r0'), ('norm', 1), ('tokfwd', 0), (1, 'f'), (2, 'r1'), (5, 's'), (4, 'm'),
        (9, 's'), (0, 'g'), (7, 'm'), (6, 's'), (8, 's'), ('red', 0), (10, 's'), ('tokfwd', 1), (3, 'f'),
        ('red', 1), (2, 'r2'), (1, 'g'), ('norm', 2), ('norm', 3), ('red', 2), ('red', 3), ('wq',),
        ('qkv', 0, 0, 2), ('qkv', 0, 2, 4), (5, 'm'), ('qkv', 0, 4, 6), ('qkv', 1, 0, 2), ('qkv', 1, 2, 4),
        (9, 'm'), ('qkv', 1, 4, 6), ('qkv', 2, 2, 4), (4, 'f'), ('qkv', 2, 4, 6), ('qkv', 3, 2, 4),
        ('qkv', 3, 4, 6), (7, 'r0'), ('keep',), ('att', 0, 0), (6, 'm'), ('att', 0, 1), ('att', 1, 0),
        ('att', 1, 1), (5, 'f'), (9, 'f'), ('att', 2, 0), (7, 'r1'), ('att', 2, 1), (6, 'f'), ('att', 3, 0),
        (3, 'g'), ('att', 3, 1), ('swap',), (9, 'g'), (8, 'm'), (5, 'g'), (4, 'g'), (10, 'm'), (7, 'r2'),
        (6, 'g'), ('proj',), ('norm2',), ('fc1', 0), ('fc1', 1), ('fc1', 2), (8, 'f'), ('fc1', 3),
        ('fc1', 4), (10, 'f'), ('fc1', 5), ('fc1', 6), ('fc1', 7), ('fc2', 0), (8, 'g'), (10, 'g'),
        ('fc2', 2), ('fc2', 1), ('fc2', 3), ('end',),
    ),
)
NSEM = (136, 23)


def gelu_parts(h):
    bell = jnp.exp(-0.5 * h * h)
    t = 1.0 / (1.0 + (0.3275911 * 0.5**0.5) * jnp.abs(h))
    poly = 1.061405429 * t - 1.453152027
    for co in (1.421413741, -0.284496736, 0.254829592):
        poly = poly * t + co
    tail = 0.5 * poly * t * bell
    cdf = jnp.where(h < 0.0, tail, 1.0 - tail)
    return h * cdf, cdf + h * bell * 0.3989422804014327


def row_table():
    half = 10
    freq = 10000.0 ** (-np.arange(half) / half)
    ang = np.arange(16)[:, None] * freq
    whole = np.zeros((48, 256))
    for p in range(3):
        rows = slice(16 * p, 16 * p + 16)
        for head in range(2):
            at = head * HD + p * 2 * half
            whole[rows, at : at + half] = np.cos(ang)
            whole[rows, at + half : at + 2 * half] = np.cos(ang)
            whole[rows, 128 + at : 128 + at + half] = -np.sin(ang)
            whole[rows, 128 + at + half : 128 + at + 2 * half] = np.sin(ang)
    for head in range(2):
        whole[:16, head * HD + 60 : head * HD + HD] = 1.0
    whole = whole.astype(np.float32)
    pieces = []
    for _ in range(3):
        piece = whole.astype(BF)
        pieces.append(np.asarray(piece))
        whole = whole - piece.astype(np.float32)
    return np.stack(pieces)


def turns(places, table):
    level = lax.broadcasted_iota(jnp.int32, (16, places.shape[1]), 0).astype(F32)
    hot = jnp.concatenate([(level == places[p : p + 1]).astype(F32) for p in range(3)], axis=0)
    hot = hot.astype(BF)
    return mm_tn(hot, table[0]) + mm_tn(hot, table[1]) + mm_tn(hot, table[2])


def unshuffle():
    i = lax.broadcasted_iota(jnp.int32, (128, 128), 0)
    j = lax.broadcasted_iota(jnp.int32, (128, 128), 1)
    k, dp, r = i // 16, lax.rem(i, 16) // 2, lax.rem(i, 2)
    return (j == dp * 16 + r * 8 + k).astype(F32).astype(BF)


def front_kernel(nz, cfg, *refs):
    (tok, cot, qkv, proj, fc1, fc2, vectors, bias, places, index, ad_d, ad_u, table) = refs[:13]
    (out, gres, do_o, q_o, k_o, v_o, o_o, lse_o, n1_o, red_o, wq_o, dn, up, pall, idxs,
     gap, gbp, ga1, gb1, ga2, gb2, vf) = refs[13:35]
    (buf4, wq, wp, w1, w2, q, kv, att, accs, res, n2s,
     vall, selb, adall, small, tab, du, adr, ssem, rsem, lsem) = refs[35:]
    (r_p_s, r_1_s, g_r2_s, r_2_s, g_r1_s) = [small.at[i] for i in range(5)]
    k = Links(ssem, rsem, lsem, nz)
    c, d, s = k.c, k.d, k.s
    ndp = 2 * nz
    slope, o, gatt, gn2 = kv, q, att, gres
    seqs = [k.core, k.xn, k.diag]
    dps = [(lax.rem(d + j, ndp), s) for j in range(1, ndp)]
    meet = k.greet(seqs + dps)
    late = []

    def push(src, dst, land, dev):
        i = k.new()
        cp = k.remote(i, src, dst, dev)
        cp.start()
        late.append(cp.wait_send)
        return k.remote(i, src, land, dev).wait_recv

    def send_later(src, dst, land, dev):
        i = k.new()
        cp = k.remote(i, src, dst, dev)

        def start():
            cp.start()
            late.append(cp.wait_send)

        return start, k.remote(i, src, land, dev).wait_recv

    def keep(src, dst):
        i = k.newl()
        cp = k.local(i, src, dst)
        cp.start()
        return cp.wait

    placed = [
        keep(qkv.at[:, pl.ds(256 * b, 256)], wq.at[k.x, (0, 2, 1)[b], k.z, k.y]) for b in range(3)
    ]
    own_tok = keep(tok, buf4.at[0])
    idxs[d] = jnp.broadcast_to(index[...].astype(F32), (8, 128))
    vall[s] = jnp.zeros_like(vall[0])
    vall[s, 0:9, :] = vectors[...].astype(F32)
    vall[s, 9:13, :] = bias[...].astype(F32)
    pall[0] = jnp.zeros_like(pall[0])
    for p in range(3):
        pall[0, p : p + 1, :] = places[p].astype(F32)
    for r in range(2):
        n = ad_d.shape[2]
        adr[:, r * 4096 : r * 4096 + n] = ad_d[...].astype(F32)[:, r, :].astype(BF)
        adr[:, r * 4096 + n : r * 4096 + 4096] = ad_u[...].astype(F32)[:, r, :].astype(BF)
    for w in placed:
        w()
    meet()
    wait_idx = [
        push(idxs.at[d], idxs.at[d], idxs.at[lax.rem(d + ndp - j, ndp)], dps[j - 1])
        for j in range(1, ndp)
    ]
    seq_of = [s + 1 - 2 * c, s + 2 - 4 * k.x, 3 - s]
    wait_vec = [push(vall.at[s], vall.at[s], vall.at[seq_of[r]], seqs[r]) for r in range(3)]
    wait_pos = [push(pall.at[0], pall.at[r + 1], pall.at[r + 1], seqs[r]) for r in range(3)]
    tok_core = push(tok, buf4.at[1], buf4.at[1], k.core)
    halves = [pl.ds(0, 256), pl.ds(256, 256)]
    tok_x = [send_later(tok.at[h], buf4.at[2, h], buf4.at[2, h], k.xn) for h in halves]
    tok_on = [k.remote(k.new(), buf4.at[2, h], buf4.at[3, h], k.core) for h in halves]
    cuts, order = cfg
    parts = (
        qkv_parts(k, wq, cuts[0])
        + wide_parts(k, proj, wp, cuts[1])
        + wide_parts(k, fc1, w1, cuts[2])
        + wide_parts(k, fc2, w2, cuts[3])
    )
    groups = []
    n = 0
    for cs in cuts:
        groups.append(parts[n : n + len(cs)])
        n += len(cs)
    state = {}

    def a_tok(h):
        tok_x[h][0]()

    def a_tokfwd(h):
        tok_x[h][1]()
        tok_on[h].start()

    def a_pick():
        for w in wait_idx:
            w()
        spots = lax.broadcasted_iota(jnp.int32, (1, NA), 1).astype(F32)
        hot = [(idxs[lax.rem(d + j, ndp)][0:1, :NA] == spots).astype(F32) for j in range(ndp)]
        sel = mm(jnp.concatenate(hot, axis=0).astype(BF), adr[...]).astype(BF)
        stack = jnp.concatenate([sel[:, p * 512 : p * 512 + 512] for p in range(16)], axis=0)
        r = lax.broadcasted_iota(jnp.int32, (128, 128), 0)
        q_ = lax.broadcasted_iota(jnp.int32, (128, 128), 1)
        swap = (q_ == lax.rem(r, 16) * 8 + r // 16).astype(F32).astype(BF)
        selb[...] = mm(swap, stack).astype(BF).reshape(ndp, 16, 512)
        adall[s, d] = selb[0]
        state["ad"] = [
            push(selb.at[j], adall.at[s, d], adall.at[s, lax.rem(d + ndp - j, ndp)], dps[j - 1])
            for j in range(1, ndp)
        ]

    def a_pass():
        for w in state["ad"]:
            w()
        state["ad4"] = [
            push(adall.at[s], adall.at[s], adall.at[seq_of[r]], seqs[r]) for r in range(3)
        ]

    def a_maps():
        for w in state["ad4"]:
            w()
        shuffle = unshuffle()
        for t in range(4):
            rows = mm(shuffle, adall[t].reshape(128, 512)).astype(BF)
            for b in range(8):
                piece = rows[16 * b : 16 * b + 16]
                at = b * 512
                nd = dn.shape[1] // 4
                nu = up.shape[1] // 4
                cut = min(max(nd - at, 0), 512)
                if cut:
                    dn[:, t * nd + at : t * nd + at + cut] = piece[:, :cut]
                if cut < 512:
                    b0 = t * nu + at + cut - nd
                    up[:, b0 : b0 + 512 - cut] = piece[:, cut:]
        for j in range(4):
            for i in range(8):
                at = i * 512 + j * 128
                du[0, j, :, i * 128 : i * 128 + 128] = dn[:, 3 * D + at : 3 * D + at + 128]
                du[1, j, :, i * 128 : i * 128 + 128] = up[:, 4 * D + at : 4 * D + at + 128]
        g_r2_s[...] = mm_nt(cot[...], up[:, 4 * D + FF :]).astype(BF)

    def a_vec():
        for w in wait_vec:
            w()
        for t in range(4):
            vf[:, t * 256 : t * 256 + 256] = vall[t]

    def a_norm(slot):
        if slot < 2:
            (own_tok, tok_core)[slot]()
        else:
            for cp in tok_on:
                cp.wait_send() if slot == 2 else cp.wait_recv()
        if slot == 0:
            for w in wait_pos:
                w()
        xhat, _ = norm_parts(buf4[slot].astype(F32))
        buf4[slot] = (xhat * vf[0:1, :] + vf[1:2, :]).astype(BF)

    def a_wq():
        for p in groups[0]:
            p.arrive()
        late.append(keep(wq, wq_o))

    def role_cols(role):
        return pl.ds(pl.multiple_of((4 * (role // 2) + 2 * (role % 2) + c) * 256, 256), 256)

    def role_bias(role):
        lg = pl.multiple_of((2 * (role % 2) + c) * 256, 256)
        return vf[4 + role // 2 : 5 + role // 2, pl.ds(lg, 256)]

    def a_red(slot):
        red_o[slot] = mm_nt(buf4[slot], dn[:, :D]).astype(BF)

    def a_qkv(slot, first, last):
        if first < 4:
            if state.get("tab") != slot:
                tab[...] = turns(pall[slot], table)
                state["tab"] = slot
            cos, sin = tab[:, :128], tab[:, 128:]
        h, low = buf4[slot], red_o[slot]
        rows = pl.ds(slot * 512, 512)
        for role in range(first, last):
            val = mm(h, wq[role_slot(role, c)].reshape(D, 256)) + role_bias(role) + mm(low, up[:, role_cols(role)])
            cols = pl.ds((role % 2) * 256, 256)
            if role < 2:
                q[rows, cols] = (turn(val, cos, sin) * (LOG2E * HD**-0.5)).astype(BF)
            elif role < 4:
                kv[slot, :, (role % 2) * 256 : (role % 2) * 256 + 256] = turn(val, cos, sin).astype(BF)
            else:
                kv[slot, :, 512 + (role % 2) * 256 : 768 + (role % 2) * 256] = val.astype(BF)

    def a_keep():
        state["n1"] = keep(buf4, n1_o)
        state["q"] = keep(q, q_o)
        state["kv"] = [keep(kv.at[:, :, pl.ds(512 * i, 512)], (k_o, v_o)[i]) for i in range(2)]

    def a_att(pair, qb):
        lane_i = lax.broadcasted_iota(jnp.int32, (1, 128), 1)
        if "q" in state:
            state.pop("q")()
        cols = pl.ds(pair * 128, 128)
        rows = pl.ds(qb * 512, 512)
        ks, qs = kv[:, :, cols].reshape(-1, 128), q[rows, cols]
        vt = kv[:, :, pl.ds(512 + pair * 128, 128)].reshape(-1, 128).T
        outs = []
        for e in range(2):
            mine = (lane_i < 64) if e == 0 else (lane_i >= 64)
            st = mm_nt(ks, jnp.where(mine, qs, jnp.zeros_like(qs)))
            top = jnp.max(st, axis=0, keepdims=True)
            pr = jnp.exp2(st - top)
            total = jnp.sum(pr, axis=0, keepdims=True)
            outs.append(mm(vt[64 * e : 64 * e + 64], pr.astype(BF)) / total)
            lse_o[pair, e : e + 1, pl.ds(qb * 512, 512)] = top + jnp.log2(total)
        o[rows, cols] = jnp.concatenate(outs, axis=0).T.astype(BF)

    def a_swap():
        late.append(keep(o, o_o))
        state["att"] = []
        for lg in range(2):
            cols = pl.ds(lg * 256, 256)
            here, there = group(2 * lg + c), group(2 * lg + 1 - c)
            state["att"].append(keep(o.at[pl.ds(0, 512), cols], att.at[:, here]))
            state["att"].append(
                push(o.at[pl.ds(512, 512), cols], att.at[:, here], att.at[:, there], k.core)
            )

    def group(g):
        return pl.ds(pl.multiple_of(g * 256, 256), 256)

    def a_proj():
        for w in state["att"] + state["kv"]:
            w()
        own = keep(tok, n2s)
        own()
        for p in groups[1]:
            p.arrive()
        low = mm_nt(att[...], dn[:, D : 2 * D]).astype(BF)
        r_p_s[...] = low
        for t in range(4):
            cols = pl.ds(t * 256, 256)
            val = mm(low, up[:, 3 * D + t * 256 : 3 * D + t * 256 + 256]) + vf[7:8, cols]
            val += mm(att[...], wp[t // 2, t % 2].reshape(D, 256))
            res[:, cols] = n2s[:, cols].astype(F32) + val

    def a_norm2():
        xhat, _ = norm_parts(res[...])
        n2 = (xhat * vf[2:3, :] + vf[3:4, :]).astype(BF)
        n2s[...] = n2
        r_1_s[...] = mm_nt(n2, dn[:, 2 * D : 3 * D]).astype(BF)
        state["n1"]()

    def a_fc1(i):
        if i == 0:
            for p in groups[2]:
                p.arrive()
        t, h = i // 2, i % 2
        w = w1[t // 2, t % 2, :, :, :, h * 512 : h * 512 + 512].reshape(D, 512)
        bias = jnp.concatenate(
            [vf[9 + 2 * h + b : 10 + 2 * h + b, t * 256 : t * 256 + 256] for b in range(2)], axis=1
        )
        hid = mm(n2s[...], w) + bias
        hid += mm(r_1_s[...], up[:, 4 * D + i * 512 : 4 * D + i * 512 + 512])
        a, sl = gelu_parts(hid)
        a = a.astype(BF)
        for j in range(4):
            buf4[j, :, i * 128 : i * 128 + 128] = a[:, j * 128 : j * 128 + 128]
            slope[j, :, i * 128 : i * 128 + 128] = sl[:, j * 128 : j * 128 + 128].astype(BF)

    def a_fc2(j):
        groups[3][j].arrive()
        a = buf4[j]
        d2 = du[0, j]
        low2 = mm_nt(a, d2)
        w = jnp.concatenate(
            [
                w2[t // 2, t % 2, :, :, j * 128 : j * 128 + 128, :].reshape(1024, 256)
                for t in range(4)
            ],
            axis=1,
        )
        g = mm_nt(cot[...], w) + mm(g_r2_s[...], d2)
        first = "r2" not in state
        accs[...] = mm(a, w) if first else accs[...] + mm(a, w)
        gh = (g * slope[j].astype(F32)).astype(BF)
        w = jnp.concatenate(
            [
                w1[i // 4, (i // 2) % 2, :, :, :, (i % 2) * 512 + j * 128 : (i % 2) * 512 + j * 128 + 128].reshape(D, 128)
                for i in range(8)
            ],
            axis=1,
        )
        gn2[...] = mm_nt(gh, w) if first else gn2[...] + mm_nt(gh, w)
        low1 = mm_nt(gh, du[1, j])
        state["r2"] = low2 if "r2" not in state else state["r2"] + low2
        state["g1"] = low1 if "g1" not in state else state["g1"] + low1
        ga2[j] = mm_tn(g_r2_s[...], a)
        gb1[j] = mm_tn(r_1_s[...], gh)

    def a_end():
        r_2, g_r1 = state["r2"].astype(BF), state["g1"].astype(BF)
        g_n2 = gn2[...] + mm(g_r1, dn[:, 2 * D : 3 * D])
        xhat, inv = norm_parts(res[...])
        g_res = cot[...].astype(F32) + norm_back(g_n2, xhat, inv, vf[2:3, :])
        gres[...] = g_res
        gb = g_res.astype(BF)
        g_rp = mm_nt(gb, up[:, 3 * D : 4 * D]).astype(BF)
        gap[...] = mm_tn(g_rp, att[...])
        w = jnp.concatenate([wp[t // 2, t % 2].reshape(D, 256) for t in range(4)], axis=1)
        gatt[...] = (mm_nt(gb, w) + mm(g_rp, dn[:, D : 2 * D])).astype(BF)
        waits = []
        for lg in range(2):
            cols = pl.ds(lg * 256, 256)
            top, low = pl.ds(0, 512), pl.ds(512, 512)
            waits.append(keep(gatt.at[:, group(2 * lg + c)], do_o.at[top, cols]))
            there = gatt.at[:, group(2 * lg + 1 - c)]
            waits.append(push(there, do_o.at[low, cols], do_o.at[low, cols], k.core))
        u2 = up[:, 4 * D + FF :]
        out[...] = (res[...] + accs[...] + vf[8:9, :] + mm(r_2, u2)).astype(BF)
        gb2[...] = mm_tn(r_2, cot[...])
        ga1[...] = mm_tn(g_r1, n2s[...])
        gbp[...] = mm_tn(r_p_s[...], gb)
        for w in waits:
            w()

    acts = {
        "tok": a_tok, "tokfwd": a_tokfwd, "pick": a_pick, "pass": a_pass, "maps": a_maps, "vec": a_vec,
        "norm": a_norm, "wq": a_wq, "red": a_red, "qkv": a_qkv, "keep": a_keep, "att": a_att,
        "swap": a_swap, "proj": a_proj, "norm2": a_norm2, "fc1": a_fc1, "fc2": a_fc2, "end": a_end,
    }
    for name, *args in order:
        if isinstance(name, int):
            parts[name].step(args[0])
        else:
            acts[name](*args)
    for w in late:
        w()
    for p in parts:
        p.finish()
    assert k.nr <= NSEM[0] and k.nl <= NSEM[1]


def front(nz, cfg, tok, cot, qkv, proj, fc1, fc2, vectors, bias, places, index, ad_d, ad_u):
    anys, vm = pl.BlockSpec(memory_space=pl.ANY), pl.BlockSpec(memory_space=pltpu.VMEM)
    ndp = 2 * nz
    rows = tok.shape[0]
    nd, nu = 3 * D + FF, 5 * D + FF
    outs = [
        (vm, (rows, D), BF), (vm, (rows, D), F32), (anys, (2 * rows, 512), BF),
        (anys, (2 * rows, 512), BF), (anys, (4, rows, 512), BF), (anys, (4, rows, 512), BF),
        (anys, (2 * rows, 512), BF), (vm, (4, 2, 2 * rows), F32), (anys, (4, rows, D), BF),
        (vm, (4, rows, 16), BF), (anys, (2, 4, nz, 2, qkv.shape[0], 256), BF), (vm, (16, nd), BF),
        (vm, (16, nu), BF), (vm, (4, 8, rows), F32), (vm, (ndp, 8, 128), F32),
        (vm, (16, D), F32), (vm, (16, D), F32), (vm, (16, D), F32), (vm, (4, 16, 1024), F32),
        (vm, (4, 16, 1024), F32), (vm, (16, D), F32), (vm, (16, D), F32),
    ]
    scratch = [
        ((4, rows, D), BF), ((2, 4, nz, 2, qkv.shape[0], 256), BF),
        ((2, 2, nz, 2) + proj.shape, BF), ((2, 2, nz, 2) + fc1.shape, BF), ((2, 2, nz, 2) + fc2.shape, BF),
        ((2 * rows, 512), BF), ((4, rows, 1024), BF), ((rows, D), BF), ((rows, D), F32),
        ((rows, D), F32), ((rows, D), BF), ((4, 16, 256), F32),
        ((ndp, 16, 512), BF), ((4, ndp, 16, 512), BF), ((5, rows, 16), BF), ((rows, 256), F32), ((2, 4, 16, 1024), BF), ((NA, 8192), BF),
    ]
    return pl.pallas_call(
        functools.partial(front_kernel, nz, cfg),
        out_shape=[sds(sh, t) for _, sh, t in outs],
        in_specs=[anys, vm, anys, anys, anys, anys] + [vm] * 7,
        out_specs=[m for m, _, _ in outs],
        scratch_shapes=[pltpu.VMEM(sh, t) for sh, t in scratch]
        + [
            pltpu.SemaphoreType.DMA((NSEM[0],)),
            pltpu.SemaphoreType.DMA((NSEM[0],)),
            pltpu.SemaphoreType.DMA((NSEM[1],)),
        ],
        compiler_params=pltpu.CompilerParams(
            collective_id=0, has_side_effects=True, vmem_limit_bytes=VM
        ),
    )(
        tok, cot, qkv, proj, fc1, fc2, vectors, bias, places, index, ad_d, ad_u,
        jnp.asarray(row_table()),
    )


def back_kernel(nz, *refs):
    (q_i, k_i, v_i, o_i, do_i, n1_i, wq_i, tok_i, gres_i, lse, red, dn, up, pall, idxs, vf,
     gap, gbp, ga1, gb1, ga2, gb2, table) = refs[:23]
    ig, gdn, gup = refs[23:26]
    (q, kk, vv, o, do, n1, wcat, tok, gres, acc, dl, dk, dv, gm, upc, gaq, gbq, own, part, gd, gu,
     blk, got, selo, selr, ssem, rsem, lsem) = refs[26:]
    k = Links(ssem, rsem, lsem, nz)
    c, d, s = k.c, k.d, k.s
    ndp = 2 * nz
    rows = tok.shape[0]
    nq = 2 * rows
    seqs = [k.core, k.xn, k.diag]
    seq_of = [s + 1 - 2 * c, s + 2 - 4 * k.x, 3 - s]
    dps = [(lax.rem(d + j, ndp), s) for j in range(1, ndp)]
    late = []

    def keep(src, dst):
        i = k.newl()
        cp = k.local(i, src, dst)
        cp.start()
        return cp.wait

    def push(src, dst, land, dev):
        i = k.new()
        cp = k.remote(i, src, dst, dev)
        cp.start()
        late.append(cp.wait_send)
        return k.remote(i, src, land, dev).wait_recv

    first = [keep(a, b) for a, b in ((q_i, q), (k_i, kk), (v_i, vv), (o_i, o), (do_i, do))]
    meet = k.greet(seqs + dps)
    for w in first:
        w()
    later = [keep(wq_i.at[role_slot(r, c)], wcat.at[:, pl.ds(256 * r, 256)]) for r in range(6)]
    later += [keep(a, b) for a, b in ((n1_i, n1), (tok_i, tok), (gres_i, gres))]
    lane = lax.broadcasted_iota(jnp.int32, (1, 128), 1)

    def attend_back(pair, half, at, size):
        cols = pl.ds(pair * 128, 128)
        krows, outs = pl.ds(half * nq + at, size), pl.ds(at, size)
        begin = half == 1 and at > 0
        qs, dos, ks, vs = q[:, cols], do[:, cols], kk[krows, cols], vv[krows, cols]
        if begin:
            r8 = lax.broadcasted_iota(jnp.int32, (8, 128), 0)
            l8 = lax.broadcasted_iota(jnp.int32, (8, 128), 1) // 64
            dl[pair] = lax.dot_general(
                (r8 == l8).astype(F32),
                dos.astype(F32) * o[:, cols].astype(F32),
                (((1,), (1,)), ((), ())),
                precision=lax.Precision.HIGHEST,
                preferred_element_type=F32,
            )
        dks, dvs, dqs = [], [], []
        for e in range(2):
            mine = (lane < 64) if e == 0 else (lane >= 64)
            st = mm_nt(jnp.where(mine, ks, jnp.zeros_like(ks)), qs)
            pr = jnp.exp2(st - lse[pair, e : e + 1, :])
            dp = mm_nt(jnp.where(mine, vs, jnp.zeros_like(vs)), dos)
            ds = (pr * (dp - dl[pair, e : e + 1, :])).astype(BF)
            dvs.append(mm(pr.astype(BF), dos))
            dks.append(mm(ds, qs))
            dqs.append(mm(ks.T[64 * e : 64 * e + 64], ds))
        dk[outs, cols] = jnp.where(lane < 64, dks[0], dks[1]) * LN2
        dv[outs, cols] = jnp.where(lane < 64, dvs[0], dvs[1])
        dq = jnp.concatenate(dqs, axis=0)
        frows = pl.ds(pair * 128, 128)
        if begin:
            acc[frows, :] = dq
        else:
            acc[frows, :] += dq

    def mixed(slot):
        tab = turns(pall[slot], table)
        cos, sin = tab[:, :128], -tab[:, 128:]
        at = pl.ds((slot % 2) * rows, rows)
        f = 0 if slot < 2 else 512
        for role in range(0 if slot < 2 else 2, 6):
            cols = pl.ds((role % 2) * 256, 256)
            if role < 2:
                g = acc[cols, at].T * (HD**-0.5)
                g = turn(g, cos, sin)
            elif role < 4:
                g = turn(dk[at, cols], cos, sin)
            else:
                g = dv[at, cols]
            gm[at, role * 256 : role * 256 + 256] = g.astype(BF)
        g = gm[at, f:]
        low = mm_nt(g, upc[:, f:]).astype(BF)
        ta, tb = mm_tn(low, n1[slot]), mm_tn(red[slot], g)
        if slot == 3:
            gaq[...] = ta
            gbq[:, :512] = jnp.zeros((16, 512), F32)
            gbq[:, f:] = tb
        else:
            gaq[...] += ta
            gbq[:, f:] += tb
        return low

    def into_h(slot, low):
        at = pl.ds((slot % 2) * rows, rows)
        f = 0 if slot < 2 else 512
        return mm_nt(gm[at, f:], wcat[:, f:]) + mm(low, dn[:, :D])

    for pair in range(4):
        attend_back(pair, 1, rows, rows)
    for w in later:
        w()
    for role in range(6):
        at = pl.multiple_of((4 * (role // 2) + 2 * (role % 2) + c) * 256, 256)
        upc[:, role * 256 : role * 256 + 256] = up[:, pl.ds(at, 256)]
    part[0] = into_h(3, mixed(3)).astype(BF)
    meet()
    from_core = push(part.at[0], part.at[1], part.at[1], k.core)
    for pair in range(4):
        attend_back(pair, 1, 0, rows)
    own[...] = into_h(2, mixed(2))
    from_core()
    part[2] = (own[...] + part[1].astype(F32)).astype(BF)
    from_x = push(part.at[2], part.at[3], part.at[3], k.xn)
    gd[:, D : 2 * D] = gap[...]
    gd[:, 2 * D : 3 * D] = ga1[...]
    gu[:, : 3 * D] = jnp.zeros((16, 3 * D), F32)
    gu[:, 3 * D : 4 * D] = gbp[...]
    gu[:, 4 * D + FF :] = gb2[...]
    for j in range(4):
        for i in range(8):
            at = i * 512 + j * 128
            gd[:, 3 * D + at : 3 * D + at + 128] = ga2[j, :, i * 128 : i * 128 + 128]
            gu[:, 4 * D + at : 4 * D + at + 128] = gb1[j, :, i * 128 : i * 128 + 128]
    for pair in range(4):
        attend_back(pair, 0, 0, nq)
    low1 = mixed(1)
    low0 = mixed(0)
    gd[:, :D] = gaq[...]
    for role in range(6):
        at = pl.multiple_of((4 * (role // 2) + 2 * (role % 2) + c) * 256, 256)
        gu[:, pl.ds(at, 256)] = gbq[:, role * 256 : role * 256 + 256]
    nd, nu = gd.shape[1] // 4, gu.shape[1] // 4
    for t in range(4):
        blk[t, :, :nd] = gd[:, t * nd : t * nd + nd].astype(BF)
        blk[t, :, nd:] = gu[:, t * nu : t * nu + nu].astype(BF)
    sums = [push(blk.at[seq_of[r]], got.at[r], got.at[r], seqs[r]) for r in range(3)]
    part[4] = into_h(1, low1).astype(BF)
    from_core = push(part.at[4], part.at[5], part.at[5], k.core)
    own[...] = into_h(0, low0)
    xhat, inv = norm_parts(tok[...].astype(F32))
    for w in sums:
        w()
    total = blk[s].astype(F32)
    for r in range(3):
        total += got[r].astype(F32)
    total = total.astype(BF)
    stack = jnp.concatenate([total[:, b * 512 : b * 512 + 512] for b in range(8)], axis=0)
    selo[...] = mm_tn(unshuffle(), stack).astype(BF).reshape(ndp, 16, 512)
    selr[d] = selo[d]
    ends = [
        push(selo.at[lax.rem(d + j, ndp)], selr.at[d], selr.at[lax.rem(d + ndp - j, ndp)], dps[j - 1])
        for j in range(1, ndp)
    ]
    from_core()
    from_x()
    g_n1 = own[...] + part[5].astype(F32) + part[3].astype(F32)
    ig[...] = (gres[...] + norm_back(g_n1, xhat, inv, vf[0:1, :])).astype(BF)
    for w in ends:
        w()
    for a in range(NA):
        out = jnp.zeros((16, 512), F32)
        for j in range(ndp):
            out += jnp.where(idxs[j][0:1, 0:1] == float(a), selr[j].astype(F32), 0.0)
        for r in range(2):
            row = jnp.concatenate([out[8 * r + b : 8 * r + b + 1] for b in range(8)], axis=1)
            gdn[a, r : r + 1, :] = row[:, :nd]
            gup[a, r : r + 1, :] = row[:, nd:]
    for w in late:
        w()
    assert k.nr <= 40 and k.nl <= 20


def back(nz, *args):
    anys, vm = pl.BlockSpec(memory_space=pl.ANY), pl.BlockSpec(memory_space=pltpu.VMEM)
    rows = args[7].shape[0]
    nq = 2 * rows
    ndp = 2 * nz
    scratch = [
        ((nq, 512), BF), ((2 * nq, 512), BF), ((2 * nq, 512), BF), ((nq, 512), BF), ((nq, 512), BF),
        ((4, rows, D), BF), ((D, 1536), BF), ((rows, D), BF), ((rows, D), F32),
        ((512, nq), F32), ((4, 8, nq), F32), ((nq, 512), F32), ((nq, 512), F32),
        ((nq, 1536), BF), ((16, 1536), BF), ((16, D), F32), ((16, 1536), F32), ((rows, D), F32),
        ((6, rows, D), BF), ((16, 3 * D + FF), F32), ((16, 5 * D + FF), F32),
        ((4, 16, 4096), BF), ((3, 16, 4096), BF), ((ndp, 16, 512), BF), ((ndp, 16, 512), BF),
    ]
    return pl.pallas_call(
        functools.partial(back_kernel, nz),
        out_shape=[
            sds((rows, D), BF), sds((NA, 2, (3 * D + FF) // 4), F32), sds((NA, 2, (5 * D + FF) // 4), F32)
        ],
        in_specs=[anys] * 9 + [vm] * (len(args) - 8),
        out_specs=[vm, vm, vm],
        scratch_shapes=[pltpu.VMEM(sh, t) for sh, t in scratch]
        + [
            pltpu.SemaphoreType.DMA((40,)),
            pltpu.SemaphoreType.DMA((40,)),
            pltpu.SemaphoreType.DMA((20,)),
        ],
        compiler_params=pltpu.CompilerParams(
            collective_id=1, has_side_effects=True, vmem_limit_bytes=VM
        ),
    )(*args, jnp.asarray(row_table()))


def fast_shards(
    nz, tokens, positions, adapter_index, qkv_weight, proj_weight, fc1_weight, fc2_weight,
    vectors, fc1_bias, adapter_down, adapter_up, cotangent,
):
    (output, gres, do, q, k, v, o, lse, n1, red, wq, dn, up, pall, idxs,
     gap, gbp, ga1, gb1, ga2, gb2, vf) = front(
        nz, PLAN, tokens[0], cotangent[0], qkv_weight, proj_weight, fc1_weight, fc2_weight,
        vectors, fc1_bias.reshape(4, 256), positions, adapter_index, adapter_down, adapter_up,
    )
    input_grad, down_grad, up_grad = back(
        nz, q, k.reshape(-1, 512), v.reshape(-1, 512), o, do, n1, wq.reshape(2, 4, D, 256), tokens[0],
        gres, lse, red, dn, up, pall, idxs, vf, gap, gbp, ga1, gb1, ga2, gb2,
    )
    return output[None], input_grad[None], down_grad, up_grad


def solution(mesh):
    in_specs = (
        P("dp", "seq", None),
        P(None, "dp", "seq"),
        P("dp", None),
        P("dp", "seq"),
        P("dp", "seq"),
        P("dp", "seq"),
        P("dp", "seq"),
        P(None, "seq"),
        P("seq"),
        P(None, "dp", "seq"),
        P(None, "dp", "seq"),
        P("dp", "seq", None),
    )
    out_specs = (
        P("dp", "seq", None),
        P("dp", "seq", None),
        P(None, "dp", "seq"),
        P(None, "dp", "seq"),
    )
    body = shards
    if mesh.shape["seq"] == 4 and mesh.shape["dp"] == 8:

        def body(tokens, *rest):
            if tokens.shape[0] == 1 and tokens.shape[1] == 512:
                return fast_shards(mesh.shape["dp"] // 2, tokens, *rest)
            return shards(tokens, *rest)

    return jax.shard_map(body, mesh=mesh, in_specs=in_specs, out_specs=out_specs, check_vma=False)
```

```python
import functools
import math

import jax
import jax.numpy as jnp
import numpy as np
from jax import lax
from jax.experimental import pallas as pl
from jax.experimental.pallas import tpu as pltpu
from jax.sharding import PartitionSpec as P

D = 1024
HEADS = 16
HD = 64
FF = 4096
NA = 8


def layer_norm(values, gain_row, shift_row):
    centre = values - jnp.mean(values, axis=-1, keepdims=True)
    spread = jnp.mean(centre * centre, axis=-1, keepdims=True)
    return centre * lax.rsqrt(spread + 1e-06) * gain_row + shift_row


def rotate(values, places, direction):
    rot_span = 2 * (values.shape[-1] // 3 // 2)
    half_span = rot_span // 2
    inverse_freq = 10000.0 ** (-jnp.arange(half_span, dtype=jnp.float32) / half_span)
    pieces = []
    for axis_id in range(3):
        segment = values[..., axis_id * rot_span : (axis_id + 1) * rot_span]
        angles = places[axis_id].astype(jnp.float32)[..., None, None] * inverse_freq
        cosine = jnp.cos(angles)
        sine_wave = direction * jnp.sin(angles)
        lower_part = segment[..., :half_span]
        upper_part = segment[..., half_span:]
        pieces.append(lower_part * cosine - upper_part * sine_wave)
        pieces.append(lower_part * sine_wave + upper_part * cosine)
    pieces.append(values[..., 3 * rot_span :])
    return jnp.concatenate(pieces, axis=-1)


def exact_gelu(values):
    return jax.nn.gelu(values, approximate=False)


def fetch_weight(weight):
    joined = lax.all_gather(weight, "seq", axis=1, tiled=True)
    return lax.all_gather(joined, "dp", axis=0, tiled=True)


def adapted(inputs, weight, shift_row, down_part, up_part):
    base = jnp.einsum("cti,io->cto", inputs, weight, preferred_element_type=jnp.float32)
    reduced = jnp.einsum(
        "cti,cri->ctr", inputs, down_part, preferred_element_type=jnp.float32
    ).astype(jnp.bfloat16)
    result = (
        base
        + shift_row
        + jnp.einsum("ctr,cro->cto", reduced, up_part, preferred_element_type=jnp.float32)
    )
    return (result, reduced)


def adapted_back(grad_out, inputs, weight, down_part, up_part, reduced):
    grad_in = jnp.einsum("cto,io->cti", grad_out, weight, preferred_element_type=jnp.float32)
    grad_reduced = jnp.einsum(
        "cto,cro->ctr", grad_out, up_part, preferred_element_type=jnp.float32
    ).astype(jnp.bfloat16)
    grad_in = grad_in + jnp.einsum(
        "ctr,cri->cti", grad_reduced, down_part, preferred_element_type=jnp.float32
    )
    grad_down = jnp.einsum("ctr,cti->cri", grad_reduced, inputs, preferred_element_type=jnp.float32)
    grad_up = jnp.einsum("ctr,cto->cro", reduced, grad_out, preferred_element_type=jnp.float32)
    return (grad_in, grad_down, grad_up)


def split_tokens(source, split_count):
    old_shape = source.shape
    shaped = source.reshape(
        (old_shape[0], split_count, old_shape[1] // split_count) + old_shape[2:]
    )
    return jnp.moveaxis(shaped, 1, 0)


def score_grads(
    query_block, key_block, value_block, grad_block, log_block, delta_block, score_scale
):
    scores = (
        jnp.einsum("cqhd,ckhd->chqk", query_block, key_block, preferred_element_type=jnp.float32)
        * score_scale
    )
    probabilities = jnp.exp(scores - log_block[..., None])
    grad_probs = jnp.einsum(
        "cqhd,ckhd->chqk", grad_block, value_block, preferred_element_type=jnp.float32
    )
    grad_scores = (probabilities * (grad_probs - delta_block[..., None])).astype(jnp.bfloat16)
    return (probabilities.astype(jnp.bfloat16), grad_scores)


def shards(
    tokens,
    positions,
    adapter_index,
    qkv_weight,
    proj_weight,
    fc1_weight,
    fc2_weight,
    vectors,
    fc1_bias,
    adapter_down,
    adapter_up,
    cotangent,
):
    clip_count, tok_count = (tokens.shape[0], tokens.shape[1])
    head_shape = (clip_count, tok_count, HEADS, HD)
    score_scale = HD ** (-0.5)
    small_parts = (
        lax.all_gather(adapter_down, "seq", axis=2, tiled=True),
        lax.all_gather(adapter_up, "seq", axis=2, tiled=True),
        lax.all_gather(vectors, "seq", axis=1, tiled=True),
        lax.all_gather(fc1_bias, "seq", axis=0, tiled=True),
    )
    down_all, up_all = (
        lax.all_gather(small_parts[0], "dp", axis=1, tiled=True),
        lax.all_gather(small_parts[1], "dp", axis=1, tiled=True),
    )
    vector_rows = small_parts[2].astype(jnp.float32)
    hidden_bias = small_parts[3].astype(jnp.float32)
    choose = (adapter_index == jnp.arange(NA, dtype=jnp.int32)[None, :]).astype(jnp.bfloat16)
    down_sel = jnp.einsum(
        "ca,ari->cri", choose, down_all, preferred_element_type=jnp.float32
    ).astype(jnp.bfloat16)
    up_sel = jnp.einsum("ca,aro->cro", choose, up_all, preferred_element_type=jnp.float32).astype(
        jnp.bfloat16
    )
    down_parts = (
        down_sel[:, :, :D],
        down_sel[:, :, D : 2 * D],
        down_sel[:, :, 2 * D : 3 * D],
        down_sel[:, :, 3 * D :],
    )
    up_parts = (
        up_sel[:, :, : 3 * D],
        up_sel[:, :, 3 * D : 4 * D],
        up_sel[:, :, 4 * D : 4 * D + FF],
        up_sel[:, :, 4 * D + FF :],
    )
    inputs = tokens.astype(jnp.float32)
    normed_one = layer_norm(inputs, vector_rows[0], vector_rows[1]).astype(jnp.bfloat16)
    weight_qkv = fetch_weight(qkv_weight)
    mixed_qkv, reduced_qkv = adapted(
        normed_one, weight_qkv, vector_rows[4:7].reshape(3 * D), down_parts[0], up_parts[0]
    )
    queries = rotate(mixed_qkv[..., :D].reshape(head_shape), positions, 1.0).astype(jnp.bfloat16)
    keys_local = rotate(mixed_qkv[..., D : 2 * D].reshape(head_shape), positions, 1.0).astype(
        jnp.bfloat16
    )
    values_local = mixed_qkv[..., 2 * D :].reshape(head_shape).astype(jnp.bfloat16)
    stat_shape = (clip_count, HEADS, tok_count)
    start_state = (
        jnp.full(stat_shape, -jnp.inf, jnp.float32),
        jnp.zeros(stat_shape, jnp.float32),
        jnp.zeros(stat_shape + (HD,), jnp.float32),
    )
    key_piece = lax.all_gather(keys_local, "seq", axis=1, tiled=True)
    value_piece = lax.all_gather(values_local, "seq", axis=1, tiled=True)
    split_count = key_piece.shape[1] // math.gcd(key_piece.shape[1], 256)

    def inner_step(running, block_pair):
        top_score, row_total, weighted = running
        key_block, value_block = block_pair
        scores = (
            jnp.einsum("cqhd,ckhd->chqk", queries, key_block, preferred_element_type=jnp.float32)
            * score_scale
        )
        new_top = jnp.maximum(top_score, jnp.max(scores, axis=-1))
        factor = jnp.exp(top_score - new_top)
        weights = jnp.exp(scores - new_top[..., None])
        row_total = row_total * factor + jnp.sum(weights, axis=-1)
        weighted = weighted * factor[..., None] + jnp.einsum(
            "chqk,ckhd->chqd",
            weights.astype(jnp.bfloat16),
            value_block,
            preferred_element_type=jnp.float32,
        )
        return ((new_top, row_total, weighted), None)

    result, unused = lax.scan(
        inner_step,
        start_state,
        (split_tokens(key_piece, split_count), split_tokens(value_piece, split_count)),
    )
    top_score, row_total, weighted = result
    log_total = top_score + jnp.log(row_total)
    heads_tok = jnp.swapaxes(weighted / row_total[..., None], 1, 2)
    attended = heads_tok.reshape(clip_count, tok_count, D).astype(jnp.bfloat16)
    weight_proj = fetch_weight(proj_weight)
    projected, reduced_proj = adapted(
        attended, weight_proj, vector_rows[7], down_parts[1], up_parts[1]
    )
    residual = inputs + projected
    normed_two = layer_norm(residual, vector_rows[2], vector_rows[3]).astype(jnp.bfloat16)
    weight_up = fetch_weight(fc1_weight)
    hidden, reduced_up = adapted(normed_two, weight_up, hidden_bias, down_parts[2], up_parts[2])
    activated = exact_gelu(hidden).astype(jnp.bfloat16)
    weight_down = fetch_weight(fc2_weight)
    branch, reduced_down = adapted(
        activated, weight_down, vector_rows[8], down_parts[3], up_parts[3]
    )
    output = (residual + branch).astype(jnp.bfloat16)
    weight_down = fetch_weight(fc2_weight)
    grad_act, gdown_four, gup_four = adapted_back(
        cotangent, activated, weight_down, down_parts[3], up_parts[3], reduced_down
    )
    unused, gelu_back = jax.vjp(exact_gelu, hidden)
    grad_hidden = gelu_back(grad_act)[0].astype(jnp.bfloat16)
    weight_up = fetch_weight(fc1_weight)
    grad_normed_two, gdown_three, gup_three = adapted_back(
        grad_hidden, normed_two, weight_up, down_parts[2], up_parts[2], reduced_up
    )

    def norm_two(values):
        return layer_norm(values, vector_rows[2], vector_rows[3])

    unused, norm_two_back = jax.vjp(norm_two, residual)
    grad_residual = cotangent.astype(jnp.float32) + norm_two_back(grad_normed_two)[0]
    weight_proj = fetch_weight(proj_weight)
    grad_attended, gdown_two, gup_two = adapted_back(
        grad_residual.astype(jnp.bfloat16),
        attended,
        weight_proj,
        down_parts[1],
        up_parts[1],
        reduced_proj,
    )
    grad_tok = grad_attended.astype(jnp.bfloat16).reshape(head_shape)
    delta_heads = jnp.swapaxes(jnp.sum(grad_tok.astype(jnp.float32) * heads_tok, axis=-1), 1, 2)
    whole_keys, whole_values = (
        lax.all_gather(keys_local, "seq", axis=1, tiled=True),
        lax.all_gather(values_local, "seq", axis=1, tiled=True),
    )
    block_count = whole_keys.shape[1] // math.gcd(whole_keys.shape[1], 256)
    key_blocks = split_tokens(whole_keys, block_count)
    value_blocks = split_tokens(whole_values, block_count)
    zero_heads = jnp.zeros(head_shape, jnp.float32)

    def back_step(grad_query, block_pair):
        key_block, value_block = block_pair
        probs_low, grad_scores = score_grads(
            queries, key_block, value_block, grad_tok, log_total, delta_heads, score_scale
        )
        grad_query = (
            grad_query
            + jnp.einsum(
                "chqk,ckhd->cqhd", grad_scores, key_block, preferred_element_type=jnp.float32
            )
            * score_scale
        )
        grad_key = (
            jnp.einsum("chqk,cqhd->ckhd", grad_scores, queries, preferred_element_type=jnp.float32)
            * score_scale
        )
        grad_value = jnp.einsum(
            "chqk,cqhd->ckhd", probs_low, grad_tok, preferred_element_type=jnp.float32
        )
        return (grad_query, jnp.concatenate([grad_key, grad_value], axis=-1))

    grad_query, key_terms = lax.scan(back_step, zero_heads, (key_blocks, value_blocks))
    key_terms = jnp.moveaxis(key_terms, 0, 1).reshape(
        clip_count, whole_keys.shape[1], HEADS, 2 * HD
    )
    summed = lax.psum_scatter(
        key_terms.astype(jnp.bfloat16), "seq", scatter_dimension=1, tiled=True
    ).astype(jnp.float32)
    grad_key = summed[..., :HD]
    grad_value = summed[..., HD:]
    grad_mixed = jnp.concatenate(
        [
            rotate(grad_query, positions, -1.0).reshape(clip_count, tok_count, D),
            rotate(grad_key, positions, -1.0).reshape(clip_count, tok_count, D),
            grad_value.reshape(clip_count, tok_count, D),
        ],
        axis=-1,
    ).astype(jnp.bfloat16)
    weight_qkv = fetch_weight(qkv_weight)
    grad_normed_one, gdown_one, gup_one = adapted_back(
        grad_mixed, normed_one, weight_qkv, down_parts[0], up_parts[0], reduced_qkv
    )

    def norm_one(values):
        return layer_norm(values, vector_rows[0], vector_rows[1])

    unused, norm_one_back = jax.vjp(norm_one, inputs)
    input_grad = (grad_residual + norm_one_back(grad_normed_one)[0]).astype(jnp.bfloat16)
    choose_wide = choose.astype(jnp.float32)
    clip_down = jnp.concatenate([gdown_one, gdown_two, gdown_three, gdown_four], axis=-1)
    clip_up = jnp.concatenate([gup_one, gup_two, gup_three, gup_four], axis=-1)
    down_term = jnp.einsum("ca,cri->ari", choose_wide, clip_down, precision=lax.Precision.HIGHEST)
    up_term = jnp.einsum("ca,cro->aro", choose_wide, clip_up, precision=lax.Precision.HIGHEST)
    down_grad, up_grad = (
        lax.psum_scatter(
            down_term.astype(jnp.bfloat16), "seq", scatter_dimension=2, tiled=True
        ).astype(jnp.float32),
        lax.psum_scatter(
            up_term.astype(jnp.bfloat16), "seq", scatter_dimension=2, tiled=True
        ).astype(jnp.float32),
    )
    down_grad, up_grad = (
        lax.psum_scatter(
            down_grad.astype(jnp.bfloat16), "dp", scatter_dimension=1, tiled=True
        ).astype(jnp.float32),
        lax.psum_scatter(
            up_grad.astype(jnp.bfloat16), "dp", scatter_dimension=1, tiled=True
        ).astype(jnp.float32),
    )
    return (output, input_grad, down_grad, up_grad)

MESH = pl.DeviceIdType.MESH
BF = jnp.bfloat16
F32 = jnp.float32
LOG2E = 1.4426950408889634
LN2 = 0.6931471805599453
VM = 60 * 1024 * 1024


def mm(a, b):
    return lax.dot_general(a, b, (((1,), (0,)), ((), ())), preferred_element_type=F32)


def mm_nt(a, b):
    return lax.dot_general(a, b, (((1,), (1,)), ((), ())), preferred_element_type=F32)


def mm_tn(a, b):
    return lax.dot_general(a, b, (((0,), (0,)), ((), ())), preferred_element_type=F32)


class Links:
    def __init__(self, ssem, rsem, lsem, nz):
        self.ssem, self.rsem, self.lsem = ssem, rsem, lsem
        self.nr, self.nl = 0, 0
        d, s = lax.axis_index("dp"), lax.axis_index("seq")
        self.d, self.s, self.nz = d, s, nz
        self.z, self.y, self.x, self.c = d // 2, lax.rem(d, 2), s // 2, lax.rem(s, 2)
        self.core = (d, s + 1 - 2 * self.c)
        self.xn = (d, s + 2 - 4 * self.x)
        self.diag = (d, 3 - s)
        self.yn = (d + 1 - 2 * self.y, s)
        self.up, self.down = (d + 2, s), (d - 2, s)
        self.zpeer = [(lax.rem(d + 2 * j, 2 * nz), s) for j in range(nz)]

    def greet(self, peers):
        bar = pltpu.get_barrier_semaphore()
        for dev in peers:
            pl.semaphore_signal(bar, inc=1, device_id=dev, device_id_type=MESH)
        return lambda: pl.semaphore_wait(bar, len(peers))

    def barrier(self, peers):
        self.greet(peers)()

    def new(self, count=1):
        self.nr += count
        return self.nr - count

    def newl(self):
        self.nl += 1
        return self.nl - 1

    def remote(self, i, src, dst, dev):
        return pltpu.make_async_remote_copy(
            src_ref=src,
            dst_ref=dst,
            send_sem=self.ssem.at[i],
            recv_sem=self.rsem.at[i],
            device_id=dev,
            device_id_type=MESH,
        )

    def local(self, i, src, dst):
        return pltpu.make_async_copy(src, dst, self.lsem.at[i])


def guard(cond, body):
    if cond is None:
        body()
    else:
        pl.when(cond)(body)


class Part:
    def __init__(self, links, order, own, region, handover):
        self.k, self.order, self.own = links, order, own
        self.placed = own is None
        self.region, self.handover = region, handover
        k = links
        self.s_own = None if self.placed else k.newl()
        n = k.nz - 1
        self.s_z = k.new(2 * n if order == "xyz" else n)
        self.s_f, self.s_g1, self.s_g2 = k.new(), k.new(), k.new()
        self.pend, self.tail = [], []
        xfirst = order != "zyx"
        self.f, self.g = (k.x, k.y) if xfirst else (k.y, k.x)
        self.fd, self.gd = (k.xn, k.yn) if xfirst else (k.yn, k.xn)
        if self.placed:
            self.own = self.reg(self.f, self.g, k.z)

    def reg(self, fi, gi, zs):
        return self.region(gi, zs, fi) if self.order == "zyx" else self.region(fi, zs, gi)

    def hand(self, cond, fi, zs, gi):
        k = self.k
        x, y = (gi, fi) if self.order == "zyx" else (fi, gi)
        loc, rem = self.handover(x, zs, y)
        ls = [(k.newl(), a, b) for a, b in loc]
        rs = [(k.new(), a, b, w) for a, b, w in rem]

        def start():
            for i, a, b in ls:
                k.local(i, a, b).start()
            for i, a, b, _ in rs:
                k.remote(i, a, b, k.core).start()

        def arrive():
            for i, a, b in ls:
                k.local(i, a, b).wait()
            for i, a, b, w in rs:
                k.remote(i, a, w, k.core).wait_recv()

        def sent():
            for i, a, b, _ in rs:
                k.remote(i, a, b, k.core).wait_send()

        guard(cond, start)
        self.pend.append((cond, arrive))
        self.tail.append((cond, sent))

    def go(self, cond, copy):
        guard(cond, copy.start)
        self.tail.append((cond, copy.wait_send))

    def own_start(self):
        if not self.placed:
            self.k.local(self.s_own, self.own, self.reg(self.f, self.g, self.k.z)).start()

    def own_wait(self):
        if not self.placed:
            self.k.local(self.s_own, self.own, self.reg(self.f, self.g, self.k.z)).wait()

    def step(self, name):
        getattr(self, ("l_" if self.order == "xyz" else "z_") + name)()

    def z_s(self):
        k, f, g = self.k, self.f, self.g
        self.own_start()
        for j in range(1, k.nz):
            self.go(None, k.remote(self.s_z + j - 1, self.own, self.reg(f, g, k.z), k.zpeer[j]))

    def z_m(self):
        k, f, g = self.k, self.f, self.g
        al = slice(None)
        for j in range(1, k.nz):
            at = self.reg(f, g, lax.rem(k.z + k.nz - j, k.nz))
            k.remote(self.s_z + j - 1, self.own, at, k.zpeer[j]).wait_recv()
        self.own_wait()
        mine = self.reg(f, g, al)
        self.go(None, k.remote(self.s_f, mine, mine, self.fd))
        self.go(None, k.remote(self.s_g1, mine, mine, self.gd))

    def z_f(self):
        k, f, g = self.k, self.f, self.g
        al = slice(None)
        new = self.reg(1 - f, g, al)
        k.remote(self.s_f, new, new, self.fd).wait_recv()
        self.go(None, k.remote(self.s_g2, new, new, self.gd))
        self.hand(None, al, al, g)

    def z_g(self):
        k, f, g = self.k, self.f, self.g
        al = slice(None)
        for sem, at in ((self.s_g1, f), (self.s_g2, 1 - f)):
            new = self.reg(at, 1 - g, al)
            k.remote(sem, new, new, self.gd).wait_recv()
        self.hand(None, al, al, 1 - g)

    def l_s(self):
        k, f, g, z = self.k, self.f, self.g, self.k.z
        self.own_start()
        self.go(None, k.remote(self.s_f, self.own, self.reg(f, g, z), self.fd))
        self.go(None, k.remote(self.s_g1, self.own, self.reg(f, g, z), self.gd))

    def l_f(self):
        k, f, g, z = self.k, self.f, self.g, self.k.z
        new = self.reg(1 - f, g, z)
        k.remote(self.s_f, self.own, new, self.fd).wait_recv()
        self.go(None, k.remote(self.s_g2, new, new, self.gd))

    def l_m(self):
        k, f, g, z = self.k, self.f, self.g, self.k.z
        al = slice(None)
        k.remote(self.s_g1, self.own, self.reg(f, 1 - g, z), self.gd).wait_recv()
        new = self.reg(1 - f, 1 - g, z)
        k.remote(self.s_g2, new, new, self.gd).wait_recv()
        self.own_wait()
        four = self.reg(al, al, z)
        self.go(z < k.nz - 1, k.remote(self.s_z, four, four, k.up))
        self.go(z > 0, k.remote(self.s_z + k.nz - 1, four, four, k.down))
        self.hand(None, al, z, al)

    def relay(self, r):
        k, z = self.k, self.k.z
        al = slice(None)
        for sem, here, origin, dev, can in (
            (self.s_z, z > r, z - 1 - r, k.up, z < k.nz - 1),
            (self.s_z + k.nz - 1, z + r < k.nz - 1, z + 1 + r, k.down, z > 0),
        ):
            four = self.reg(al, al, origin)
            guard(here, k.remote(sem + r, four, four, dev).wait_recv)
            if r < k.nz - 2:
                self.go(jnp.logical_and(here, can), k.remote(sem + r + 1, four, four, dev))
            self.hand(here, al, origin, al)

    def l_r0(self):
        self.relay(0)

    def l_r1(self):
        self.relay(1)

    def l_r2(self):
        self.relay(2)

    def arrive(self):
        for cond, body in self.pend:
            guard(cond, body)

    def finish(self):
        for cond, body in self.tail:
            guard(cond, body)


def wide_parts(links, shard, buf, cuts):
    c = links.c
    parts = []
    for r0, n, order in cuts:
        rows = pl.ds(r0, n)

        def region(x, z, y, rows=rows):
            return buf.at[x, c, z, y, rows]

        def handover(x, z, y, rows=rows):
            at = buf.at[x, c, z, y, rows]
            return [], [(at, at, buf.at[x, 1 - c, z, y, rows])]

        parts.append(Part(links, order, shard.at[rows], region, handover))
    return parts


def qkv_parts(links, buf, cuts):
    parts = []
    for r0, n, order in cuts:
        rows = pl.ds(r0, n)

        def region(x, z, y, rows=rows):
            return buf.at[x, pl.ds(0, 3), z, y, rows]

        def handover(x, z, y, rows=rows):
            return [], [
                (buf.at[x, 2, z, y, rows], buf.at[x, 3, z, y, rows], buf.at[x, 3, z, y, rows])
            ]

        parts.append(Part(links, order, None, region, handover))
    return parts


def role_slot(role, c):
    return role // 3, (3 * c, 1 - c, 3 - 2 * c)[role % 3]


def norm_parts(values):
    centre = values - jnp.mean(values, axis=-1, keepdims=True)
    inv = lax.rsqrt(jnp.mean(centre * centre, axis=-1, keepdims=True) + 1e-06)
    return centre * inv, inv


def swap_pairs(v):
    n = v.shape[1]
    j = lax.rem(lax.broadcasted_iota(jnp.int32, (1, n), 1), HD)
    lower = lax.rem(j, 20) < 10
    return jnp.where(lower, pltpu.roll(v, n - 10, 1), pltpu.roll(v, 10, 1))


def turn(v, cos, sin):
    cc, ss = jnp.concatenate([cos, cos], axis=1), jnp.concatenate([sin, sin], axis=1)
    return v * cc + swap_pairs(v) * ss


def norm_back(grad, xhat, inv, gain):
    q = grad * gain
    return inv * (
        q - jnp.mean(q, axis=-1, keepdims=True) - xhat * jnp.mean(q * xhat, axis=-1, keepdims=True)
    )


def sds(shape, dtype):
    return jax.ShapeDtypeStruct(shape, dtype)


PLAN = (
    (((0, 48, 'zxy'), (48, 48, 'zxy'), (96, 32, 'xyz')), ((0, 128, 'zyx'),), ((0, 48, 'zxy'), (48, 48, 'zxy'), (96, 32, 'zyx')), ((0, 128, 'xyz'), (128, 128, 'zxy'), (256, 128, 'zyx'), (384, 128, 'zxy'))),
    (
        (0, 's'), (2, 's'), (7, 's'), ('tok', 0), (1, 's'), (3, 's'), ('vec',), ('norm', 0), (2, 'f'),
        (7, 'f'), ('pick',), (0, 'm'), (1, 'm'), ('pass',), (4, 's'), ('tok', 1), (3, 'm'), (2, 'm'),
        (0, 'f'), ('maps',), (2, 'r0'), ('norm', 1), ('tokfwd', 0), (1, 'f'), (2, 'r1'), (5, 's'), (4, 'm'),
        (9, 's'), (0, 'g'), (7, 'm'), (6, 's'), (8, 's'), ('red', 0), (10, 's'), ('tokfwd', 1), (3, 'f'),
        ('red', 1), (2, 'r2'), (1, 'g'), ('norm', 2), ('norm', 3), ('red', 2), ('red', 3), ('wq',),
        ('qkv', 0, 0, 2), ('qkv', 0, 2, 4), (5, 'm'), ('qkv', 0, 4, 6), ('qkv', 1, 0, 2), ('qkv', 1, 2, 4),
        (9, 'm'), ('qkv', 1, 4, 6), ('qkv', 2, 2, 4), (4, 'f'), ('qkv', 2, 4, 6), ('qkv', 3, 2, 4),
        ('qkv', 3, 4, 6), (7, 'r0'), ('keep',), ('att', 0, 0), (6, 'm'), ('att', 0, 1), ('att', 1, 0),
        ('att', 1, 1), (5, 'f'), (9, 'f'), ('att', 2, 0), (7, 'r1'), ('att', 2, 1), (6, 'f'), ('att', 3, 0),
        (3, 'g'), ('att', 3, 1), ('swap',), (9, 'g'), (8, 'm'), (5, 'g'), (4, 'g'), (10, 'm'), (7, 'r2'),
        (6, 'g'), ('proj',), ('norm2',), ('fc1', 0), ('fc1', 1), ('fc1', 2), (8, 'f'), ('fc1', 3),
        ('fc1', 4), (10, 'f'), ('fc1', 5), ('fc1', 6), ('fc1', 7), ('fc2', 0), (8, 'g'), (10, 'g'),
        ('fc2', 2), ('fc2', 1), ('fc2', 3), ('end',),
    ),
)
NSEM = (136, 23)


def gelu_parts(h):
    bell = jnp.exp(-0.5 * h * h)
    t = 1.0 / (1.0 + (0.3275911 * 0.5**0.5) * jnp.abs(h))
    poly = 1.061405429 * t - 1.453152027
    for co in (1.421413741, -0.284496736, 0.254829592):
        poly = poly * t + co
    tail = 0.5 * poly * t * bell
    cdf = jnp.where(h < 0.0, tail, 1.0 - tail)
    return h * cdf, cdf + h * bell * 0.3989422804014327


def row_table():
    half = 10
    freq = 10000.0 ** (-np.arange(half) / half)
    ang = np.arange(16)[:, None] * freq
    whole = np.zeros((48, 256))
    for p in range(3):
        rows = slice(16 * p, 16 * p + 16)
        for head in range(2):
            at = head * HD + p * 2 * half
            whole[rows, at : at + half] = np.cos(ang)
            whole[rows, at + half : at + 2 * half] = np.cos(ang)
            whole[rows, 128 + at : 128 + at + half] = -np.sin(ang)
            whole[rows, 128 + at + half : 128 + at + 2 * half] = np.sin(ang)
    for head in range(2):
        whole[:16, head * HD + 60 : head * HD + HD] = 1.0
    whole = whole.astype(np.float32)
    pieces = []
    for _ in range(3):
        piece = whole.astype(BF)
        pieces.append(np.asarray(piece))
        whole = whole - piece.astype(np.float32)
    return np.stack(pieces)


def turns(places, table):
    level = lax.broadcasted_iota(jnp.int32, (16, places.shape[1]), 0).astype(F32)
    hot = jnp.concatenate([(level == places[p : p + 1]).astype(F32) for p in range(3)], axis=0)
    hot = hot.astype(BF)
    return mm_tn(hot, table[0]) + mm_tn(hot, table[1]) + mm_tn(hot, table[2])


def unshuffle():
    i = lax.broadcasted_iota(jnp.int32, (128, 128), 0)
    j = lax.broadcasted_iota(jnp.int32, (128, 128), 1)
    k, dp, r = i // 16, lax.rem(i, 16) // 2, lax.rem(i, 2)
    return (j == dp * 16 + r * 8 + k).astype(F32).astype(BF)


def front_kernel(nz, cfg, *refs):
    (tok, cot, qkv, proj, fc1, fc2, vectors, bias, places, index, ad_d, ad_u, table) = refs[:13]
    (out, gres, do_o, q_o, k_o, v_o, o_o, lse_o, n1_o, red_o, wq_o, dn, up, pall, idxs,
     gap, gbp, ga1, gb1, ga2, gb2, vf) = refs[13:35]
    (buf4, wq, wp, w1, w2, q, kv, att, accs, res, n2s,
     vall, selb, adall, small, tab, du, adr, ssem, rsem, lsem) = refs[35:]
    (r_p_s, r_1_s, g_r2_s, r_2_s, g_r1_s) = [small.at[i] for i in range(5)]
    k = Links(ssem, rsem, lsem, nz)
    c, d, s = k.c, k.d, k.s
    ndp = 2 * nz
    slope, o, gatt, gn2 = kv, q, att, gres
    seqs = [k.core, k.xn, k.diag]
    dps = [(lax.rem(d + j, ndp), s) for j in range(1, ndp)]
    meet = k.greet(seqs + dps)
    late = []

    def push(src, dst, land, dev):
        i = k.new()
        cp = k.remote(i, src, dst, dev)
        cp.start()
        late.append(cp.wait_send)
        return k.remote(i, src, land, dev).wait_recv

    def send_later(src, dst, land, dev):
        i = k.new()
        cp = k.remote(i, src, dst, dev)

        def start():
            cp.start()
            late.append(cp.wait_send)

        return start, k.remote(i, src, land, dev).wait_recv

    def keep(src, dst):
        i = k.newl()
        cp = k.local(i, src, dst)
        cp.start()
        return cp.wait

    placed = [
        keep(qkv.at[:, pl.ds(256 * b, 256)], wq.at[k.x, (0, 2, 1)[b], k.z, k.y]) for b in range(3)
    ]
    own_tok = keep(tok, buf4.at[0])
    idxs[d] = jnp.broadcast_to(index[...].astype(F32), (8, 128))
    vall[s] = jnp.zeros_like(vall[0])
    vall[s, 0:9, :] = vectors[...].astype(F32)
    for r in range(8):
        half = (r % 2) * 128
        vall[s, 9 + r // 2 : 10 + r // 2, half : half + 128] = bias[r : r + 1, :].astype(F32)
    pall[0] = jnp.zeros_like(pall[0])
    for p in range(3):
        pall[0, p : p + 1, :] = places[p].astype(F32)
    for r in range(2):
        n = ad_d.shape[2]
        adr[:, r * 4096 : r * 4096 + n] = ad_d[...].astype(F32)[:, r, :].astype(BF)
        adr[:, r * 4096 + n : r * 4096 + 4096] = ad_u[...].astype(F32)[:, r, :].astype(BF)
    for w in placed:
        w()
    meet()
    wait_idx = [
        push(idxs.at[d], idxs.at[d], idxs.at[lax.rem(d + ndp - j, ndp)], dps[j - 1])
        for j in range(1, ndp)
    ]
    seq_of = [s + 1 - 2 * c, s + 2 - 4 * k.x, 3 - s]
    wait_vec = [push(vall.at[s], vall.at[s], vall.at[seq_of[r]], seqs[r]) for r in range(3)]
    wait_pos = [push(pall.at[0], pall.at[r + 1], pall.at[r + 1], seqs[r]) for r in range(3)]
    tok_core = push(tok, buf4.at[1], buf4.at[1], k.core)
    halves = [pl.ds(0, 256), pl.ds(256, 256)]
    tok_x = [send_later(tok.at[h], buf4.at[2, h], buf4.at[2, h], k.xn) for h in halves]
    tok_on = [k.remote(k.new(), buf4.at[2, h], buf4.at[3, h], k.core) for h in halves]
    cuts, order = cfg
    parts = (
        qkv_parts(k, wq, cuts[0])
        + wide_parts(k, proj, wp, cuts[1])
        + wide_parts(k, fc1, w1, cuts[2])
        + wide_parts(k, fc2, w2, cuts[3])
    )
    groups = []
    n = 0
    for cs in cuts:
        groups.append(parts[n : n + len(cs)])
        n += len(cs)
    state = {}

    def a_tok(h):
        tok_x[h][0]()

    def a_tokfwd(h):
        tok_x[h][1]()
        tok_on[h].start()

    def a_pick():
        for w in wait_idx:
            w()
        spots = lax.broadcasted_iota(jnp.int32, (1, NA), 1).astype(F32)
        hot = [(idxs[lax.rem(d + j, ndp)][0:1, :NA] == spots).astype(F32) for j in range(ndp)]
        sel = mm(jnp.concatenate(hot, axis=0).astype(BF), adr[...]).astype(BF)
        stack = jnp.concatenate([sel[:, p * 512 : p * 512 + 512] for p in range(16)], axis=0)
        r = lax.broadcasted_iota(jnp.int32, (128, 128), 0)
        q_ = lax.broadcasted_iota(jnp.int32, (128, 128), 1)
        swap = (q_ == lax.rem(r, 16) * 8 + r // 16).astype(F32).astype(BF)
        selb[...] = mm(swap, stack).astype(BF).reshape(ndp, 16, 512)
        adall[s, d] = selb[0]
        state["ad"] = [
            push(selb.at[j], adall.at[s, d], adall.at[s, lax.rem(d + ndp - j, ndp)], dps[j - 1])
            for j in range(1, ndp)
        ]

    def a_pass():
        for w in state["ad"]:
            w()
        state["ad4"] = [
            push(adall.at[s], adall.at[s], adall.at[seq_of[r]], seqs[r]) for r in range(3)
        ]

    def a_maps():
        for w in state["ad4"]:
            w()
        shuffle = unshuffle()
        for t in range(4):
            rows = mm(shuffle, adall[t].reshape(128, 512)).astype(BF)
            for b in range(8):
                piece = rows[16 * b : 16 * b + 16]
                at = b * 512
                nd = dn.shape[1] // 4
                nu = up.shape[1] // 4
                cut = min(max(nd - at, 0), 512)
                if cut:
                    dn[:, t * nd + at : t * nd + at + cut] = piece[:, :cut]
                if cut < 512:
                    b0 = t * nu + at + cut - nd
                    up[:, b0 : b0 + 512 - cut] = piece[:, cut:]
        for j in range(4):
            for i in range(8):
                at = i * 512 + j * 128
                du[0, j, :, i * 128 : i * 128 + 128] = dn[:, 3 * D + at : 3 * D + at + 128]
                du[1, j, :, i * 128 : i * 128 + 128] = up[:, 4 * D + at : 4 * D + at + 128]
        g_r2_s[...] = mm_nt(cot[...], up[:, 4 * D + FF :]).astype(BF)

    def a_vec():
        for w in wait_vec:
            w()
        for t in range(4):
            vf[:, t * 256 : t * 256 + 256] = vall[t]

    def a_norm(slot):
        if slot < 2:
            (own_tok, tok_core)[slot]()
        else:
            for cp in tok_on:
                cp.wait_send() if slot == 2 else cp.wait_recv()
        if slot == 0:
            for w in wait_pos:
                w()
        xhat, _ = norm_parts(buf4[slot].astype(F32))
        buf4[slot] = (xhat * vf[0:1, :] + vf[1:2, :]).astype(BF)

    def a_wq():
        for p in groups[0]:
            p.arrive()
        late.append(keep(wq, wq_o))

    def role_cols(role):
        return pl.ds(pl.multiple_of((4 * (role // 2) + 2 * (role % 2) + c) * 256, 256), 256)

    def role_bias(role):
        lg = pl.multiple_of((2 * (role % 2) + c) * 256, 256)
        return vf[4 + role // 2 : 5 + role // 2, pl.ds(lg, 256)]

    def a_red(slot):
        red_o[slot] = mm_nt(buf4[slot], dn[:, :D]).astype(BF)

    def a_qkv(slot, first, last):
        if first < 4:
            if state.get("tab") != slot:
                tab[...] = turns(pall[slot], table)
                state["tab"] = slot
            cos, sin = tab[:, :128], tab[:, 128:]
        h, low = buf4[slot], red_o[slot]
        rows = pl.ds(slot * 512, 512)
        for role in range(first, last):
            val = mm(h, wq[role_slot(role, c)].reshape(D, 256)) + role_bias(role) + mm(low, up[:, role_cols(role)])
            cols = pl.ds((role % 2) * 256, 256)
            if role < 2:
                q[rows, cols] = (turn(val, cos, sin) * (LOG2E * HD**-0.5)).astype(BF)
            elif role < 4:
                kv[slot, :, (role % 2) * 256 : (role % 2) * 256 + 256] = turn(val, cos, sin).astype(BF)
            else:
                kv[slot, :, 512 + (role % 2) * 256 : 768 + (role % 2) * 256] = val.astype(BF)

    def a_keep():
        state["n1"] = keep(buf4, n1_o)
        state["q"] = keep(q, q_o)
        state["kv"] = [keep(kv.at[:, :, pl.ds(512 * i, 512)], (k_o, v_o)[i]) for i in range(2)]

    def a_att(pair, qb):
        if "q" in state:
            state.pop("q")()
        lane_i = lax.broadcasted_iota(jnp.int32, (1, 128), 1)
        cols = pl.ds(pair * 128, 128)
        rows = pl.ds(qb * 512, 512)
        qs = q[rows, cols]
        qm = [jnp.where((lane_i < 64) == (e == 0), qs, jnp.zeros_like(qs)) for e in range(2)]
        ks = [kv[2 * b : 2 * b + 2, :, cols].reshape(-1, 128) for b in range(2)]
        vcols = pl.ds(512 + pair * 128, 128)
        vt = [kv[2 * b : 2 * b + 2, :, vcols].reshape(-1, 128).T for b in range(2)]
        steps = [(b, e) for b in range(2) for e in range(2)]
        top, total, acc = [None] * 2, [None] * 2, [None] * 2
        ahead = mm_nt(ks[0], qm[0])
        for n, (b, e) in enumerate(steps):
            st = ahead
            if n < 3:
                ahead = mm_nt(ks[steps[n + 1][0]], qm[steps[n + 1][1]])
            new = jnp.max(st, axis=0, keepdims=True)
            v_ = vt[b][64 * e : 64 * e + 64]
            if b == 0:
                pr = jnp.exp2(st - new)
                total[e] = jnp.sum(pr, axis=0, keepdims=True)
                acc[e] = mm(v_, pr.astype(BF))
            else:
                new = jnp.maximum(new, top[e])
                fall = jnp.exp2(top[e] - new)
                pr = jnp.exp2(st - new)
                total[e] = total[e] * fall + jnp.sum(pr, axis=0, keepdims=True)
                acc[e] = acc[e] * fall + mm(v_, pr.astype(BF))
            top[e] = new
        for e in range(2):
            lse_o[pair, e : e + 1, pl.ds(qb * 512, 512)] = top[e] + jnp.log2(total[e])
        o[rows, cols] = jnp.concatenate([acc[e] / total[e] for e in range(2)], axis=0).T.astype(BF)

    def a_swap():
        late.append(keep(o, o_o))
        state["att"] = []
        for lg in range(2):
            cols = pl.ds(lg * 256, 256)
            here, there = group(2 * lg + c), group(2 * lg + 1 - c)
            state["att"].append(keep(o.at[pl.ds(0, 512), cols], att.at[:, here]))
            state["att"].append(
                push(o.at[pl.ds(512, 512), cols], att.at[:, here], att.at[:, there], k.core)
            )

    def group(g):
        return pl.ds(pl.multiple_of(g * 256, 256), 256)

    def a_proj():
        for w in state["att"] + state["kv"]:
            w()
        own = keep(tok, n2s)
        own()
        for p in groups[1]:
            p.arrive()
        low = mm_nt(att[...], dn[:, D : 2 * D]).astype(BF)
        r_p_s[...] = low
        for t in range(4):
            cols = pl.ds(t * 256, 256)
            val = mm(low, up[:, 3 * D + t * 256 : 3 * D + t * 256 + 256]) + vf[7:8, cols]
            val += mm(att[...], wp[t // 2, t % 2].reshape(D, 256))
            res[:, cols] = n2s[:, cols].astype(F32) + val

    def a_norm2():
        xhat, _ = norm_parts(res[...])
        n2 = (xhat * vf[2:3, :] + vf[3:4, :]).astype(BF)
        n2s[...] = n2
        r_1_s[...] = mm_nt(n2, dn[:, 2 * D : 3 * D]).astype(BF)
        state["n1"]()

    def a_fc1(i):
        if i == 0:
            for p in groups[2]:
                p.arrive()
        t, h = i // 2, i % 2
        w = w1[t // 2, t % 2, :, :, :, h * 512 : h * 512 + 512].reshape(D, 512)
        bias = jnp.concatenate(
            [vf[9 + 2 * h + b : 10 + 2 * h + b, t * 256 : t * 256 + 256] for b in range(2)], axis=1
        )
        hid = mm(n2s[...], w) + bias
        hid += mm(r_1_s[...], up[:, 4 * D + i * 512 : 4 * D + i * 512 + 512])
        a, sl = gelu_parts(hid)
        a = a.astype(BF)
        for j in range(4):
            buf4[j, :, i * 128 : i * 128 + 128] = a[:, j * 128 : j * 128 + 128]
            slope[j, :, i * 128 : i * 128 + 128] = sl[:, j * 128 : j * 128 + 128].astype(BF)

    def a_fc2(j):
        groups[3][j].arrive()
        a = buf4[j]
        d2 = du[0, j]
        low2 = mm_nt(a, d2)
        w = jnp.concatenate(
            [
                w2[t // 2, t % 2, :, :, j * 128 : j * 128 + 128, :].reshape(1024, 256)
                for t in range(4)
            ],
            axis=1,
        )
        g = mm_nt(cot[...], w) + mm(g_r2_s[...], d2)
        first = "r2" not in state
        accs[...] = mm(a, w) if first else accs[...] + mm(a, w)
        gh = (g * slope[j].astype(F32)).astype(BF)
        w = jnp.concatenate(
            [
                w1[i // 4, (i // 2) % 2, :, :, :, (i % 2) * 512 + j * 128 : (i % 2) * 512 + j * 128 + 128].reshape(D, 128)
                for i in range(8)
            ],
            axis=1,
        )
        gn2[...] = mm_nt(gh, w) if first else gn2[...] + mm_nt(gh, w)
        low1 = mm_nt(gh, du[1, j])
        state["r2"] = low2 if "r2" not in state else state["r2"] + low2
        state["g1"] = low1 if "g1" not in state else state["g1"] + low1
        ga2[j] = mm_tn(g_r2_s[...], a)
        gb1[j] = mm_tn(r_1_s[...], gh)

    def a_end():
        r_2, g_r1 = state["r2"].astype(BF), state["g1"].astype(BF)
        g_n2 = gn2[...] + mm(g_r1, dn[:, 2 * D : 3 * D])
        xhat, inv = norm_parts(res[...])
        g_res = cot[...].astype(F32) + norm_back(g_n2, xhat, inv, vf[2:3, :])
        gres[...] = g_res
        gb = g_res.astype(BF)
        g_rp = mm_nt(gb, up[:, 3 * D : 4 * D]).astype(BF)
        gap[...] = mm_tn(g_rp, att[...])
        w = jnp.concatenate([wp[t // 2, t % 2].reshape(D, 256) for t in range(4)], axis=1)
        gatt[...] = (mm_nt(gb, w) + mm(g_rp, dn[:, D : 2 * D])).astype(BF)
        waits = []
        for lg in range(2):
            cols = pl.ds(lg * 256, 256)
            top, low = pl.ds(0, 512), pl.ds(512, 512)
            waits.append(keep(gatt.at[:, group(2 * lg + c)], do_o.at[top, cols]))
            there = gatt.at[:, group(2 * lg + 1 - c)]
            waits.append(push(there, do_o.at[low, cols], do_o.at[low, cols], k.core))
        u2 = up[:, 4 * D + FF :]
        out[...] = (res[...] + accs[...] + vf[8:9, :] + mm(r_2, u2)).astype(BF)
        gb2[...] = mm_tn(r_2, cot[...])
        ga1[...] = mm_tn(g_r1, n2s[...])
        gbp[...] = mm_tn(r_p_s[...], gb)
        for w in waits:
            w()

    acts = {
        "tok": a_tok, "tokfwd": a_tokfwd, "pick": a_pick, "pass": a_pass, "maps": a_maps, "vec": a_vec,
        "norm": a_norm, "wq": a_wq, "red": a_red, "qkv": a_qkv, "keep": a_keep, "att": a_att,
        "swap": a_swap, "proj": a_proj, "norm2": a_norm2, "fc1": a_fc1, "fc2": a_fc2, "end": a_end,
    }
    for name, *args in order:
        if isinstance(name, int):
            parts[name].step(args[0])
        else:
            acts[name](*args)
    for w in late:
        w()
    for p in parts:
        p.finish()
    assert k.nr <= NSEM[0] and k.nl <= NSEM[1]


def front(nz, cfg, tok, cot, qkv, proj, fc1, fc2, vectors, bias, places, index, ad_d, ad_u):
    anys, vm = pl.BlockSpec(memory_space=pl.ANY), pl.BlockSpec(memory_space=pltpu.VMEM)
    ndp = 2 * nz
    rows = tok.shape[0]
    nd, nu = 3 * D + FF, 5 * D + FF
    outs = [
        (vm, (rows, D), BF), (vm, (rows, D), F32), (anys, (2 * rows, 512), BF),
        (anys, (2 * rows, 512), BF), (anys, (4, rows, 512), BF), (anys, (4, rows, 512), BF),
        (anys, (2 * rows, 512), BF), (vm, (4, 2, 2 * rows), F32), (anys, (4, rows, D), BF),
        (vm, (4, rows, 16), BF), (anys, (2, 4, nz, 2, qkv.shape[0], 256), BF), (vm, (16, nd), BF),
        (vm, (16, nu), BF), (vm, (4, 8, rows), F32), (vm, (ndp, 8, 128), F32),
        (vm, (16, D), F32), (vm, (16, D), F32), (vm, (16, D), F32), (vm, (4, 16, 1024), F32),
        (vm, (4, 16, 1024), F32), (vm, (16, D), F32), (vm, (16, D), F32),
    ]
    scratch = [
        ((4, rows, D), BF), ((2, 4, nz, 2, qkv.shape[0], 256), BF),
        ((2, 2, nz, 2) + proj.shape, BF), ((2, 2, nz, 2) + fc1.shape, BF), ((2, 2, nz, 2) + fc2.shape, BF),
        ((2 * rows, 512), BF), ((4, rows, 1024), BF), ((rows, D), BF), ((rows, D), F32),
        ((rows, D), F32), ((rows, D), BF), ((4, 16, 256), F32),
        ((ndp, 16, 512), BF), ((4, ndp, 16, 512), BF), ((5, rows, 16), BF), ((rows, 256), F32), ((2, 4, 16, 1024), BF), ((NA, 8192), BF),
    ]
    return pl.pallas_call(
        functools.partial(front_kernel, nz, cfg),
        out_shape=[sds(sh, t) for _, sh, t in outs],
        in_specs=[anys, vm, anys, anys, anys, anys] + [vm] * 7,
        out_specs=[m for m, _, _ in outs],
        scratch_shapes=[pltpu.VMEM(sh, t) for sh, t in scratch]
        + [
            pltpu.SemaphoreType.DMA((NSEM[0],)),
            pltpu.SemaphoreType.DMA((NSEM[0],)),
            pltpu.SemaphoreType.DMA((NSEM[1],)),
        ],
        compiler_params=pltpu.CompilerParams(
            collective_id=0, has_side_effects=True, vmem_limit_bytes=VM
        ),
    )(
        tok, cot, qkv, proj, fc1, fc2, vectors, bias, places, index, ad_d, ad_u,
        jnp.asarray(row_table()),
    )


def back_kernel(nz, *refs):
    (q_i, k_i, v_i, o_i, do_i, n1_i, wq_i, tok_i, gres_i, lse, red, dn, up, pall, idxs, vf,
     gap, gbp, ga1, gb1, ga2, gb2, table) = refs[:23]
    ig, gdn, gup = refs[23:26]
    (q, kk, vv, o, do, n1, wcat, tok, gres, acc, dl, dk, dv, gm, upc, gaq, gbq, own, part, gd, gu,
     blk, got, selo, selr, ssem, rsem, lsem) = refs[26:]
    k = Links(ssem, rsem, lsem, nz)
    c, d, s = k.c, k.d, k.s
    ndp = 2 * nz
    rows = tok.shape[0]
    nq = 2 * rows
    seqs = [k.core, k.xn, k.diag]
    seq_of = [s + 1 - 2 * c, s + 2 - 4 * k.x, 3 - s]
    dps = [(lax.rem(d + j, ndp), s) for j in range(1, ndp)]
    late = []

    def keep(src, dst):
        i = k.newl()
        cp = k.local(i, src, dst)
        cp.start()
        return cp.wait

    def push(src, dst, land, dev):
        i = k.new()
        cp = k.remote(i, src, dst, dev)
        cp.start()
        late.append(cp.wait_send)
        return k.remote(i, src, land, dev).wait_recv

    last, rest = pl.ds(3 * rows, rows), pl.ds(0, 3 * rows)
    first = [keep(a, b) for a, b in ((q_i, q), (do_i, do), (o_i, o))]
    first += [keep(a.at[last], b.at[last]) for a, b in ((k_i, kk), (v_i, vv))]
    meet = k.greet(seqs + dps)
    for w in first:
        w()
    later = [keep(a.at[rest], b.at[rest]) for a, b in ((k_i, kk), (v_i, vv))]
    later += [keep(wq_i.at[role_slot(r, c)], wcat.at[:, pl.ds(256 * r, 256)]) for r in range(6)]
    later += [keep(a, b) for a, b in ((n1_i, n1), (tok_i, tok), (gres_i, gres))]
    lane = lax.broadcasted_iota(jnp.int32, (1, 128), 1)

    def attend_back(pair, half, at, size):
        cols = pl.ds(pair * 128, 128)
        krows, outs = pl.ds(half * nq + at, size), pl.ds(at, size)
        begin = half == 1 and at > 0
        qs, dos, ks, vs = q[:, cols], do[:, cols], kk[krows, cols], vv[krows, cols]
        if begin:
            r8 = lax.broadcasted_iota(jnp.int32, (8, 128), 0)
            l8 = lax.broadcasted_iota(jnp.int32, (8, 128), 1) // 64
            dl[pair] = lax.dot_general(
                (r8 == l8).astype(F32),
                dos.astype(F32) * o[:, cols].astype(F32),
                (((1,), (1,)), ((), ())),
                precision=lax.Precision.HIGHEST,
                preferred_element_type=F32,
            )
        dks, dvs, dqs = [], [], []
        for e in range(2):
            mine = (lane < 64) if e == 0 else (lane >= 64)
            st = mm_nt(jnp.where(mine, ks, jnp.zeros_like(ks)), qs)
            pr = jnp.exp2(st - lse[pair, e : e + 1, :])
            dp = mm_nt(jnp.where(mine, vs, jnp.zeros_like(vs)), dos)
            ds = (pr * (dp - dl[pair, e : e + 1, :])).astype(BF)
            dvs.append(mm(pr.astype(BF), dos))
            dks.append(mm(ds, qs))
            dqs.append(mm(ks.T[64 * e : 64 * e + 64], ds))
        dk[outs, cols] = jnp.where(lane < 64, dks[0], dks[1]) * LN2
        dv[outs, cols] = jnp.where(lane < 64, dvs[0], dvs[1])
        dq = jnp.concatenate(dqs, axis=0)
        frows = pl.ds(pair * 128, 128)
        if begin:
            acc[frows, :] = dq
        else:
            acc[frows, :] += dq

    def mixed(slot):
        tab = turns(pall[slot], table)
        cos, sin = tab[:, :128], -tab[:, 128:]
        at = pl.ds((slot % 2) * rows, rows)
        f = 0 if slot < 2 else 512
        for role in range(0 if slot < 2 else 2, 6):
            cols = pl.ds((role % 2) * 256, 256)
            if role < 2:
                g = acc[cols, at].T * (HD**-0.5)
                g = turn(g, cos, sin)
            elif role < 4:
                g = turn(dk[at, cols], cos, sin)
            else:
                g = dv[at, cols]
            gm[at, role * 256 : role * 256 + 256] = g.astype(BF)
        g = gm[at, f:]
        low = mm_nt(g, upc[:, f:]).astype(BF)
        ta, tb = mm_tn(low, n1[slot]), mm_tn(red[slot], g)
        if slot == 3:
            gaq[...] = ta
            gbq[:, :512] = jnp.zeros((16, 512), F32)
            gbq[:, f:] = tb
        else:
            gaq[...] += ta
            gbq[:, f:] += tb
        return low

    def into_h(slot, low):
        at = pl.ds((slot % 2) * rows, rows)
        f = 0 if slot < 2 else 512
        return mm_nt(gm[at, f:], wcat[:, f:]) + mm(low, dn[:, :D])

    for pair in range(4):
        attend_back(pair, 1, rows, rows)
    for w in later:
        w()
    for role in range(6):
        at = pl.multiple_of((4 * (role // 2) + 2 * (role % 2) + c) * 256, 256)
        upc[:, role * 256 : role * 256 + 256] = up[:, pl.ds(at, 256)]
    part[0] = into_h(3, mixed(3)).astype(BF)
    meet()
    from_core = push(part.at[0], part.at[1], part.at[1], k.core)
    for pair in range(4):
        attend_back(pair, 1, 0, rows)
    own[...] = into_h(2, mixed(2))
    from_core()
    part[2] = (own[...] + part[1].astype(F32)).astype(BF)
    from_x = push(part.at[2], part.at[3], part.at[3], k.xn)
    gd[:, D : 2 * D] = gap[...]
    gd[:, 2 * D : 3 * D] = ga1[...]
    gu[:, : 3 * D] = jnp.zeros((16, 3 * D), F32)
    gu[:, 3 * D : 4 * D] = gbp[...]
    gu[:, 4 * D + FF :] = gb2[...]
    for j in range(4):
        for i in range(8):
            at = i * 512 + j * 128
            gd[:, 3 * D + at : 3 * D + at + 128] = ga2[j, :, i * 128 : i * 128 + 128]
            gu[:, 4 * D + at : 4 * D + at + 128] = gb1[j, :, i * 128 : i * 128 + 128]
    for pair in range(4):
        attend_back(pair, 0, 0, nq)
    low1 = mixed(1)
    low0 = mixed(0)
    gd[:, :D] = gaq[...]
    for role in range(6):
        at = pl.multiple_of((4 * (role // 2) + 2 * (role % 2) + c) * 256, 256)
        gu[:, pl.ds(at, 256)] = gbq[:, role * 256 : role * 256 + 256]
    nd, nu = gd.shape[1] // 4, gu.shape[1] // 4
    for t in range(4):
        blk[t, :, :nd] = gd[:, t * nd : t * nd + nd].astype(BF)
        blk[t, :, nd:] = gu[:, t * nu : t * nu + nu].astype(BF)
    sums = [push(blk.at[seq_of[r]], got.at[r], got.at[r], seqs[r]) for r in range(3)]
    part[4] = into_h(1, low1).astype(BF)
    from_core = push(part.at[4], part.at[5], part.at[5], k.core)
    own[...] = into_h(0, low0)
    xhat, inv = norm_parts(tok[...].astype(F32))
    for w in sums:
        w()
    total = blk[s].astype(F32)
    for r in range(3):
        total += got[r].astype(F32)
    total = total.astype(BF)
    stack = jnp.concatenate([total[:, b * 512 : b * 512 + 512] for b in range(8)], axis=0)
    selo[...] = mm_tn(unshuffle(), stack).astype(BF).reshape(ndp, 16, 512)
    selr[d] = selo[d]
    ends = [
        push(selo.at[lax.rem(d + j, ndp)], selr.at[d], selr.at[lax.rem(d + ndp - j, ndp)], dps[j - 1])
        for j in range(1, ndp)
    ]
    from_core()
    from_x()
    g_n1 = own[...] + part[5].astype(F32) + part[3].astype(F32)
    ig[...] = (gres[...] + norm_back(g_n1, xhat, inv, vf[0:1, :])).astype(BF)
    for w in ends:
        w()
    for a in range(NA):
        out = jnp.zeros((16, 512), F32)
        for j in range(ndp):
            out += jnp.where(idxs[j][0:1, 0:1] == float(a), selr[j].astype(F32), 0.0)
        for r in range(2):
            row = jnp.concatenate([out[8 * r + b : 8 * r + b + 1] for b in range(8)], axis=1)
            gdn[a, r : r + 1, :] = row[:, :nd]
            gup[a, r : r + 1, :] = row[:, nd:]
    for w in late:
        w()
    assert k.nr <= 40 and k.nl <= 20


def back(nz, *args):
    anys, vm = pl.BlockSpec(memory_space=pl.ANY), pl.BlockSpec(memory_space=pltpu.VMEM)
    rows = args[7].shape[0]
    nq = 2 * rows
    ndp = 2 * nz
    scratch = [
        ((nq, 512), BF), ((2 * nq, 512), BF), ((2 * nq, 512), BF), ((nq, 512), BF), ((nq, 512), BF),
        ((4, rows, D), BF), ((D, 1536), BF), ((rows, D), BF), ((rows, D), F32),
        ((512, nq), F32), ((4, 8, nq), F32), ((nq, 512), F32), ((nq, 512), F32),
        ((nq, 1536), BF), ((16, 1536), BF), ((16, D), F32), ((16, 1536), F32), ((rows, D), F32),
        ((6, rows, D), BF), ((16, 3 * D + FF), F32), ((16, 5 * D + FF), F32),
        ((4, 16, 4096), BF), ((3, 16, 4096), BF), ((ndp, 16, 512), BF), ((ndp, 16, 512), BF),
    ]
    return pl.pallas_call(
        functools.partial(back_kernel, nz),
        out_shape=[
            sds((rows, D), BF), sds((NA, 2, (3 * D + FF) // 4), F32), sds((NA, 2, (5 * D + FF) // 4), F32)
        ],
        in_specs=[anys] * 9 + [vm] * (len(args) - 8),
        out_specs=[vm, vm, vm],
        scratch_shapes=[pltpu.VMEM(sh, t) for sh, t in scratch]
        + [
            pltpu.SemaphoreType.DMA((40,)),
            pltpu.SemaphoreType.DMA((40,)),
            pltpu.SemaphoreType.DMA((20,)),
        ],
        compiler_params=pltpu.CompilerParams(
            collective_id=1, has_side_effects=True, vmem_limit_bytes=VM
        ),
    )(*args, jnp.asarray(row_table()))


def fast_shards(
    nz, tokens, positions, adapter_index, qkv_weight, proj_weight, fc1_weight, fc2_weight,
    vectors, fc1_bias, adapter_down, adapter_up, cotangent,
):
    (output, gres, do, q, k, v, o, lse, n1, red, wq, dn, up, pall, idxs,
     gap, gbp, ga1, gb1, ga2, gb2, vf) = front(
        nz, PLAN, tokens[0], cotangent[0], qkv_weight, proj_weight, fc1_weight, fc2_weight,
        vectors, fc1_bias.reshape(8, 128), positions, adapter_index, adapter_down, adapter_up,
    )
    input_grad, down_grad, up_grad = back(
        nz, q, k.reshape(-1, 512), v.reshape(-1, 512), o, do, n1, wq.reshape(2, 4, D, 256), tokens[0],
        gres, lse, red, dn, up, pall, idxs, vf, gap, gbp, ga1, gb1, ga2, gb2,
    )
    return output[None], input_grad[None], down_grad, up_grad


def solution(mesh):
    in_specs = (
        P("dp", "seq", None),
        P(None, "dp", "seq"),
        P("dp", None),
        P("dp", "seq"),
        P("dp", "seq"),
        P("dp", "seq"),
        P("dp", "seq"),
        P(None, "seq"),
        P("seq"),
        P(None, "dp", "seq"),
        P(None, "dp", "seq"),
        P("dp", "seq", None),
    )
    out_specs = (
        P("dp", "seq", None),
        P("dp", "seq", None),
        P(None, "dp", "seq"),
        P(None, "dp", "seq"),
    )
    body = shards
    if mesh.shape["seq"] == 4 and mesh.shape["dp"] == 8:

        def body(tokens, *rest):
            if tokens.shape[0] == 1 and tokens.shape[1] == 512:
                return fast_shards(mesh.shape["dp"] // 2, tokens, *rest)
            return shards(tokens, *rest)

    return jax.shard_map(body, mesh=mesh, in_specs=in_specs, out_specs=out_specs, check_vma=False)
```

```python
import functools
import math

import jax
import jax.numpy as jnp
import numpy as np
from jax import lax
from jax.experimental import pallas as pl
from jax.experimental.pallas import tpu as pltpu
from jax.sharding import PartitionSpec as P

D = 1024
HEADS = 16
HD = 64
FF = 4096
NA = 8


def layer_norm(values, gain_row, shift_row):
    centre = values - jnp.mean(values, axis=-1, keepdims=True)
    spread = jnp.mean(centre * centre, axis=-1, keepdims=True)
    return centre * lax.rsqrt(spread + 1e-06) * gain_row + shift_row


def rotate(values, places, direction):
    rot_span = 2 * (values.shape[-1] // 3 // 2)
    half_span = rot_span // 2
    inverse_freq = 10000.0 ** (-jnp.arange(half_span, dtype=jnp.float32) / half_span)
    pieces = []
    for axis_id in range(3):
        segment = values[..., axis_id * rot_span : (axis_id + 1) * rot_span]
        angles = places[axis_id].astype(jnp.float32)[..., None, None] * inverse_freq
        cosine = jnp.cos(angles)
        sine_wave = direction * jnp.sin(angles)
        lower_part = segment[..., :half_span]
        upper_part = segment[..., half_span:]
        pieces.append(lower_part * cosine - upper_part * sine_wave)
        pieces.append(lower_part * sine_wave + upper_part * cosine)
    pieces.append(values[..., 3 * rot_span :])
    return jnp.concatenate(pieces, axis=-1)


def exact_gelu(values):
    return jax.nn.gelu(values, approximate=False)


def fetch_weight(weight):
    joined = lax.all_gather(weight, "seq", axis=1, tiled=True)
    return lax.all_gather(joined, "dp", axis=0, tiled=True)


def adapted(inputs, weight, shift_row, down_part, up_part):
    base = jnp.einsum("cti,io->cto", inputs, weight, preferred_element_type=jnp.float32)
    reduced = jnp.einsum(
        "cti,cri->ctr", inputs, down_part, preferred_element_type=jnp.float32
    ).astype(jnp.bfloat16)
    result = (
        base
        + shift_row
        + jnp.einsum("ctr,cro->cto", reduced, up_part, preferred_element_type=jnp.float32)
    )
    return (result, reduced)


def adapted_back(grad_out, inputs, weight, down_part, up_part, reduced):
    grad_in = jnp.einsum("cto,io->cti", grad_out, weight, preferred_element_type=jnp.float32)
    grad_reduced = jnp.einsum(
        "cto,cro->ctr", grad_out, up_part, preferred_element_type=jnp.float32
    ).astype(jnp.bfloat16)
    grad_in = grad_in + jnp.einsum(
        "ctr,cri->cti", grad_reduced, down_part, preferred_element_type=jnp.float32
    )
    grad_down = jnp.einsum("ctr,cti->cri", grad_reduced, inputs, preferred_element_type=jnp.float32)
    grad_up = jnp.einsum("ctr,cto->cro", reduced, grad_out, preferred_element_type=jnp.float32)
    return (grad_in, grad_down, grad_up)


def split_tokens(source, split_count):
    old_shape = source.shape
    shaped = source.reshape(
        (old_shape[0], split_count, old_shape[1] // split_count) + old_shape[2:]
    )
    return jnp.moveaxis(shaped, 1, 0)


def score_grads(
    query_block, key_block, value_block, grad_block, log_block, delta_block, score_scale
):
    scores = (
        jnp.einsum("cqhd,ckhd->chqk", query_block, key_block, preferred_element_type=jnp.float32)
        * score_scale
    )
    probabilities = jnp.exp(scores - log_block[..., None])
    grad_probs = jnp.einsum(
        "cqhd,ckhd->chqk", grad_block, value_block, preferred_element_type=jnp.float32
    )
    grad_scores = (probabilities * (grad_probs - delta_block[..., None])).astype(jnp.bfloat16)
    return (probabilities.astype(jnp.bfloat16), grad_scores)


def shards(
    tokens,
    positions,
    adapter_index,
    qkv_weight,
    proj_weight,
    fc1_weight,
    fc2_weight,
    vectors,
    fc1_bias,
    adapter_down,
    adapter_up,
    cotangent,
):
    clip_count, tok_count = (tokens.shape[0], tokens.shape[1])
    head_shape = (clip_count, tok_count, HEADS, HD)
    score_scale = HD ** (-0.5)
    small_parts = (
        lax.all_gather(adapter_down, "seq", axis=2, tiled=True),
        lax.all_gather(adapter_up, "seq", axis=2, tiled=True),
        lax.all_gather(vectors, "seq", axis=1, tiled=True),
        lax.all_gather(fc1_bias, "seq", axis=0, tiled=True),
    )
    down_all, up_all = (
        lax.all_gather(small_parts[0], "dp", axis=1, tiled=True),
        lax.all_gather(small_parts[1], "dp", axis=1, tiled=True),
    )
    vector_rows = small_parts[2].astype(jnp.float32)
    hidden_bias = small_parts[3].astype(jnp.float32)
    choose = (adapter_index == jnp.arange(NA, dtype=jnp.int32)[None, :]).astype(jnp.bfloat16)
    down_sel = jnp.einsum(
        "ca,ari->cri", choose, down_all, preferred_element_type=jnp.float32
    ).astype(jnp.bfloat16)
    up_sel = jnp.einsum("ca,aro->cro", choose, up_all, preferred_element_type=jnp.float32).astype(
        jnp.bfloat16
    )
    down_parts = (
        down_sel[:, :, :D],
        down_sel[:, :, D : 2 * D],
        down_sel[:, :, 2 * D : 3 * D],
        down_sel[:, :, 3 * D :],
    )
    up_parts = (
        up_sel[:, :, : 3 * D],
        up_sel[:, :, 3 * D : 4 * D],
        up_sel[:, :, 4 * D : 4 * D + FF],
        up_sel[:, :, 4 * D + FF :],
    )
    inputs = tokens.astype(jnp.float32)
    normed_one = layer_norm(inputs, vector_rows[0], vector_rows[1]).astype(jnp.bfloat16)
    weight_qkv = fetch_weight(qkv_weight)
    mixed_qkv, reduced_qkv = adapted(
        normed_one, weight_qkv, vector_rows[4:7].reshape(3 * D), down_parts[0], up_parts[0]
    )
    queries = rotate(mixed_qkv[..., :D].reshape(head_shape), positions, 1.0).astype(jnp.bfloat16)
    keys_local = rotate(mixed_qkv[..., D : 2 * D].reshape(head_shape), positions, 1.0).astype(
        jnp.bfloat16
    )
    values_local = mixed_qkv[..., 2 * D :].reshape(head_shape).astype(jnp.bfloat16)
    stat_shape = (clip_count, HEADS, tok_count)
    start_state = (
        jnp.full(stat_shape, -jnp.inf, jnp.float32),
        jnp.zeros(stat_shape, jnp.float32),
        jnp.zeros(stat_shape + (HD,), jnp.float32),
    )
    key_piece = lax.all_gather(keys_local, "seq", axis=1, tiled=True)
    value_piece = lax.all_gather(values_local, "seq", axis=1, tiled=True)
    split_count = key_piece.shape[1] // math.gcd(key_piece.shape[1], 256)

    def inner_step(running, block_pair):
        top_score, row_total, weighted = running
        key_block, value_block = block_pair
        scores = (
            jnp.einsum("cqhd,ckhd->chqk", queries, key_block, preferred_element_type=jnp.float32)
            * score_scale
        )
        new_top = jnp.maximum(top_score, jnp.max(scores, axis=-1))
        factor = jnp.exp(top_score - new_top)
        weights = jnp.exp(scores - new_top[..., None])
        row_total = row_total * factor + jnp.sum(weights, axis=-1)
        weighted = weighted * factor[..., None] + jnp.einsum(
            "chqk,ckhd->chqd",
            weights.astype(jnp.bfloat16),
            value_block,
            preferred_element_type=jnp.float32,
        )
        return ((new_top, row_total, weighted), None)

    result, unused = lax.scan(
        inner_step,
        start_state,
        (split_tokens(key_piece, split_count), split_tokens(value_piece, split_count)),
    )
    top_score, row_total, weighted = result
    log_total = top_score + jnp.log(row_total)
    heads_tok = jnp.swapaxes(weighted / row_total[..., None], 1, 2)
    attended = heads_tok.reshape(clip_count, tok_count, D).astype(jnp.bfloat16)
    weight_proj = fetch_weight(proj_weight)
    projected, reduced_proj = adapted(
        attended, weight_proj, vector_rows[7], down_parts[1], up_parts[1]
    )
    residual = inputs + projected
    normed_two = layer_norm(residual, vector_rows[2], vector_rows[3]).astype(jnp.bfloat16)
    weight_up = fetch_weight(fc1_weight)
    hidden, reduced_up = adapted(normed_two, weight_up, hidden_bias, down_parts[2], up_parts[2])
    activated = exact_gelu(hidden).astype(jnp.bfloat16)
    weight_down = fetch_weight(fc2_weight)
    branch, reduced_down = adapted(
        activated, weight_down, vector_rows[8], down_parts[3], up_parts[3]
    )
    output = (residual + branch).astype(jnp.bfloat16)
    weight_down = fetch_weight(fc2_weight)
    grad_act, gdown_four, gup_four = adapted_back(
        cotangent, activated, weight_down, down_parts[3], up_parts[3], reduced_down
    )
    unused, gelu_back = jax.vjp(exact_gelu, hidden)
    grad_hidden = gelu_back(grad_act)[0].astype(jnp.bfloat16)
    weight_up = fetch_weight(fc1_weight)
    grad_normed_two, gdown_three, gup_three = adapted_back(
        grad_hidden, normed_two, weight_up, down_parts[2], up_parts[2], reduced_up
    )

    def norm_two(values):
        return layer_norm(values, vector_rows[2], vector_rows[3])

    unused, norm_two_back = jax.vjp(norm_two, residual)
    grad_residual = cotangent.astype(jnp.float32) + norm_two_back(grad_normed_two)[0]
    weight_proj = fetch_weight(proj_weight)
    grad_attended, gdown_two, gup_two = adapted_back(
        grad_residual.astype(jnp.bfloat16),
        attended,
        weight_proj,
        down_parts[1],
        up_parts[1],
        reduced_proj,
    )
    grad_tok = grad_attended.astype(jnp.bfloat16).reshape(head_shape)
    delta_heads = jnp.swapaxes(jnp.sum(grad_tok.astype(jnp.float32) * heads_tok, axis=-1), 1, 2)
    whole_keys, whole_values = (
        lax.all_gather(keys_local, "seq", axis=1, tiled=True),
        lax.all_gather(values_local, "seq", axis=1, tiled=True),
    )
    block_count = whole_keys.shape[1] // math.gcd(whole_keys.shape[1], 256)
    key_blocks = split_tokens(whole_keys, block_count)
    value_blocks = split_tokens(whole_values, block_count)
    zero_heads = jnp.zeros(head_shape, jnp.float32)

    def back_step(grad_query, block_pair):
        key_block, value_block = block_pair
        probs_low, grad_scores = score_grads(
            queries, key_block, value_block, grad_tok, log_total, delta_heads, score_scale
        )
        grad_query = (
            grad_query
            + jnp.einsum(
                "chqk,ckhd->cqhd", grad_scores, key_block, preferred_element_type=jnp.float32
            )
            * score_scale
        )
        grad_key = (
            jnp.einsum("chqk,cqhd->ckhd", grad_scores, queries, preferred_element_type=jnp.float32)
            * score_scale
        )
        grad_value = jnp.einsum(
            "chqk,cqhd->ckhd", probs_low, grad_tok, preferred_element_type=jnp.float32
        )
        return (grad_query, jnp.concatenate([grad_key, grad_value], axis=-1))

    grad_query, key_terms = lax.scan(back_step, zero_heads, (key_blocks, value_blocks))
    key_terms = jnp.moveaxis(key_terms, 0, 1).reshape(
        clip_count, whole_keys.shape[1], HEADS, 2 * HD
    )
    summed = lax.psum_scatter(
        key_terms.astype(jnp.bfloat16), "seq", scatter_dimension=1, tiled=True
    ).astype(jnp.float32)
    grad_key = summed[..., :HD]
    grad_value = summed[..., HD:]
    grad_mixed = jnp.concatenate(
        [
            rotate(grad_query, positions, -1.0).reshape(clip_count, tok_count, D),
            rotate(grad_key, positions, -1.0).reshape(clip_count, tok_count, D),
            grad_value.reshape(clip_count, tok_count, D),
        ],
        axis=-1,
    ).astype(jnp.bfloat16)
    weight_qkv = fetch_weight(qkv_weight)
    grad_normed_one, gdown_one, gup_one = adapted_back(
        grad_mixed, normed_one, weight_qkv, down_parts[0], up_parts[0], reduced_qkv
    )

    def norm_one(values):
        return layer_norm(values, vector_rows[0], vector_rows[1])

    unused, norm_one_back = jax.vjp(norm_one, inputs)
    input_grad = (grad_residual + norm_one_back(grad_normed_one)[0]).astype(jnp.bfloat16)
    choose_wide = choose.astype(jnp.float32)
    clip_down = jnp.concatenate([gdown_one, gdown_two, gdown_three, gdown_four], axis=-1)
    clip_up = jnp.concatenate([gup_one, gup_two, gup_three, gup_four], axis=-1)
    down_term = jnp.einsum("ca,cri->ari", choose_wide, clip_down, precision=lax.Precision.HIGHEST)
    up_term = jnp.einsum("ca,cro->aro", choose_wide, clip_up, precision=lax.Precision.HIGHEST)
    down_grad, up_grad = (
        lax.psum_scatter(
            down_term.astype(jnp.bfloat16), "seq", scatter_dimension=2, tiled=True
        ).astype(jnp.float32),
        lax.psum_scatter(
            up_term.astype(jnp.bfloat16), "seq", scatter_dimension=2, tiled=True
        ).astype(jnp.float32),
    )
    down_grad, up_grad = (
        lax.psum_scatter(
            down_grad.astype(jnp.bfloat16), "dp", scatter_dimension=1, tiled=True
        ).astype(jnp.float32),
        lax.psum_scatter(
            up_grad.astype(jnp.bfloat16), "dp", scatter_dimension=1, tiled=True
        ).astype(jnp.float32),
    )
    return (output, input_grad, down_grad, up_grad)

MESH = pl.DeviceIdType.MESH
BF = jnp.bfloat16
F32 = jnp.float32
LOG2E = 1.4426950408889634
LN2 = 0.6931471805599453
VM = 60 * 1024 * 1024


def mm(a, b):
    return lax.dot_general(a, b, (((1,), (0,)), ((), ())), preferred_element_type=F32)


def mm_nt(a, b):
    return lax.dot_general(a, b, (((1,), (1,)), ((), ())), preferred_element_type=F32)


def mm_tn(a, b):
    return lax.dot_general(a, b, (((0,), (0,)), ((), ())), preferred_element_type=F32)


class Links:
    def __init__(self, ssem, rsem, lsem, nz):
        self.ssem, self.rsem, self.lsem = ssem, rsem, lsem
        self.nr, self.nl = 0, 0
        d, s = lax.axis_index("dp"), lax.axis_index("seq")
        self.d, self.s, self.nz = d, s, nz
        self.z, self.y, self.x, self.c = d // 2, lax.rem(d, 2), s // 2, lax.rem(s, 2)
        self.core = (d, s + 1 - 2 * self.c)
        self.xn = (d, s + 2 - 4 * self.x)
        self.diag = (d, 3 - s)
        self.yn = (d + 1 - 2 * self.y, s)
        self.up, self.down = (d + 2, s), (d - 2, s)
        self.zpeer = [(lax.rem(d + 2 * j, 2 * nz), s) for j in range(nz)]

    def greet(self, peers):
        bar = pltpu.get_barrier_semaphore()
        for dev in peers:
            pl.semaphore_signal(bar, inc=1, device_id=dev, device_id_type=MESH)
        return lambda: pl.semaphore_wait(bar, len(peers))

    def barrier(self, peers):
        self.greet(peers)()

    def new(self, count=1):
        self.nr += count
        return self.nr - count

    def newl(self):
        self.nl += 1
        return self.nl - 1

    def remote(self, i, src, dst, dev):
        return pltpu.make_async_remote_copy(
            src_ref=src,
            dst_ref=dst,
            send_sem=self.ssem.at[i],
            recv_sem=self.rsem.at[i],
            device_id=dev,
            device_id_type=MESH,
        )

    def local(self, i, src, dst):
        return pltpu.make_async_copy(src, dst, self.lsem.at[i])


def guard(cond, body):
    if cond is None:
        body()
    else:
        pl.when(cond)(body)


class Part:
    def __init__(self, links, order, own, region, handover):
        self.k, self.order, self.own = links, order, own
        self.placed = own is None
        self.region, self.handover = region, handover
        k = links
        self.s_own = None if self.placed else k.newl()
        n = k.nz - 1
        self.s_z = k.new(2 * n if order == "xyz" else n)
        self.s_f, self.s_g1, self.s_g2 = k.new(), k.new(), k.new()
        self.pend, self.tail = [], []
        xfirst = order != "zyx"
        self.f, self.g = (k.x, k.y) if xfirst else (k.y, k.x)
        self.fd, self.gd = (k.xn, k.yn) if xfirst else (k.yn, k.xn)
        if self.placed:
            self.own = self.reg(self.f, self.g, k.z)

    def reg(self, fi, gi, zs):
        return self.region(gi, zs, fi) if self.order == "zyx" else self.region(fi, zs, gi)

    def hand(self, cond, fi, zs, gi):
        k = self.k
        x, y = (gi, fi) if self.order == "zyx" else (fi, gi)
        loc, rem = self.handover(x, zs, y)
        ls = [(k.newl(), a, b) for a, b in loc]
        rs = [(k.new(), a, b, w) for a, b, w in rem]

        def start():
            for i, a, b in ls:
                k.local(i, a, b).start()
            for i, a, b, _ in rs:
                k.remote(i, a, b, k.core).start()

        def arrive():
            for i, a, b in ls:
                k.local(i, a, b).wait()
            for i, a, b, w in rs:
                k.remote(i, a, w, k.core).wait_recv()

        def sent():
            for i, a, b, _ in rs:
                k.remote(i, a, b, k.core).wait_send()

        guard(cond, start)
        self.pend.append((cond, arrive))
        self.tail.append((cond, sent))

    def go(self, cond, copy):
        guard(cond, copy.start)
        self.tail.append((cond, copy.wait_send))

    def own_start(self):
        if not self.placed:
            self.k.local(self.s_own, self.own, self.reg(self.f, self.g, self.k.z)).start()

    def own_wait(self):
        if not self.placed:
            self.k.local(self.s_own, self.own, self.reg(self.f, self.g, self.k.z)).wait()

    def step(self, name):
        getattr(self, ("l_" if self.order == "xyz" else "z_") + name)()

    def z_s(self):
        k, f, g = self.k, self.f, self.g
        self.own_start()
        for j in range(1, k.nz):
            self.go(None, k.remote(self.s_z + j - 1, self.own, self.reg(f, g, k.z), k.zpeer[j]))

    def z_m(self):
        k, f, g = self.k, self.f, self.g
        al = slice(None)
        for j in range(1, k.nz):
            at = self.reg(f, g, lax.rem(k.z + k.nz - j, k.nz))
            k.remote(self.s_z + j - 1, self.own, at, k.zpeer[j]).wait_recv()
        self.own_wait()
        mine = self.reg(f, g, al)
        self.go(None, k.remote(self.s_f, mine, mine, self.fd))
        self.go(None, k.remote(self.s_g1, mine, mine, self.gd))

    def z_f(self):
        k, f, g = self.k, self.f, self.g
        al = slice(None)
        new = self.reg(1 - f, g, al)
        k.remote(self.s_f, new, new, self.fd).wait_recv()
        self.go(None, k.remote(self.s_g2, new, new, self.gd))
        self.hand(None, al, al, g)

    def z_g(self):
        k, f, g = self.k, self.f, self.g
        al = slice(None)
        for sem, at in ((self.s_g1, f), (self.s_g2, 1 - f)):
            new = self.reg(at, 1 - g, al)
            k.remote(sem, new, new, self.gd).wait_recv()
        self.hand(None, al, al, 1 - g)

    def l_s(self):
        k, f, g, z = self.k, self.f, self.g, self.k.z
        self.own_start()
        self.go(None, k.remote(self.s_f, self.own, self.reg(f, g, z), self.fd))
        self.go(None, k.remote(self.s_g1, self.own, self.reg(f, g, z), self.gd))

    def l_f(self):
        k, f, g, z = self.k, self.f, self.g, self.k.z
        new = self.reg(1 - f, g, z)
        k.remote(self.s_f, self.own, new, self.fd).wait_recv()
        self.go(None, k.remote(self.s_g2, new, new, self.gd))

    def l_m(self):
        k, f, g, z = self.k, self.f, self.g, self.k.z
        al = slice(None)
        k.remote(self.s_g1, self.own, self.reg(f, 1 - g, z), self.gd).wait_recv()
        new = self.reg(1 - f, 1 - g, z)
        k.remote(self.s_g2, new, new, self.gd).wait_recv()
        self.own_wait()
        four = self.reg(al, al, z)
        self.go(z < k.nz - 1, k.remote(self.s_z, four, four, k.up))
        self.go(z > 0, k.remote(self.s_z + k.nz - 1, four, four, k.down))
        self.hand(None, al, z, al)

    def relay(self, r):
        k, z = self.k, self.k.z
        al = slice(None)
        for sem, here, origin, dev, can in (
            (self.s_z, z > r, z - 1 - r, k.up, z < k.nz - 1),
            (self.s_z + k.nz - 1, z + r < k.nz - 1, z + 1 + r, k.down, z > 0),
        ):
            four = self.reg(al, al, origin)
            guard(here, k.remote(sem + r, four, four, dev).wait_recv)
            if r < k.nz - 2:
                self.go(jnp.logical_and(here, can), k.remote(sem + r + 1, four, four, dev))
            self.hand(here, al, origin, al)

    def l_r0(self):
        self.relay(0)

    def l_r1(self):
        self.relay(1)

    def l_r2(self):
        self.relay(2)

    def arrive(self):
        for cond, body in self.pend:
            guard(cond, body)

    def finish(self):
        for cond, body in self.tail:
            guard(cond, body)


def wide_parts(links, shard, buf, cuts):
    c = links.c
    parts = []
    for r0, n, order in cuts:
        rows = pl.ds(r0, n)

        def region(x, z, y, rows=rows):
            return buf.at[x, c, z, y, rows]

        def handover(x, z, y, rows=rows):
            at = buf.at[x, c, z, y, rows]
            return [], [(at, at, buf.at[x, 1 - c, z, y, rows])]

        parts.append(Part(links, order, shard.at[rows], region, handover))
    return parts


def qkv_parts(links, buf, cuts):
    parts = []
    for r0, n, order in cuts:
        rows = pl.ds(r0, n)

        def region(x, z, y, rows=rows):
            return buf.at[x, pl.ds(0, 3), z, y, rows]

        def handover(x, z, y, rows=rows):
            return [], [
                (buf.at[x, 2, z, y, rows], buf.at[x, 3, z, y, rows], buf.at[x, 3, z, y, rows])
            ]

        parts.append(Part(links, order, None, region, handover))
    return parts


def role_slot(role, c):
    return role // 3, (3 * c, 1 - c, 3 - 2 * c)[role % 3]


def norm_parts(values):
    centre = values - jnp.mean(values, axis=-1, keepdims=True)
    inv = lax.rsqrt(jnp.mean(centre * centre, axis=-1, keepdims=True) + 1e-06)
    return centre * inv, inv


def swap_pairs(v):
    n = v.shape[1]
    j = lax.rem(lax.broadcasted_iota(jnp.int32, (1, n), 1), HD)
    lower = lax.rem(j, 20) < 10
    return jnp.where(lower, pltpu.roll(v, n - 10, 1), pltpu.roll(v, 10, 1))


def turn(v, cos, sin):
    cc, ss = jnp.concatenate([cos, cos], axis=1), jnp.concatenate([sin, sin], axis=1)
    return v * cc + swap_pairs(v) * ss


def norm_back(grad, xhat, inv, gain):
    q = grad * gain
    return inv * (
        q - jnp.mean(q, axis=-1, keepdims=True) - xhat * jnp.mean(q * xhat, axis=-1, keepdims=True)
    )


def sds(shape, dtype):
    return jax.ShapeDtypeStruct(shape, dtype)


PLAN = (
    (((0, 48, 'zxy'), (48, 48, 'zxy'), (96, 32, 'xyz')), ((0, 128, 'zxy'),), ((0, 48, 'zxy'), (48, 48, 'zyx'), (96, 32, 'zyx')), ((0, 128, 'xyz'), (128, 128, 'zxy'), (256, 128, 'zyx'), (384, 128, 'zxy'))),
    (
        (2, 's'), (1, 's'), ('tok', 0), (0, 's'), ('vec',), (7, 's'), ('norm', 0), ('pick',), (2, 'f'),
        (1, 'm'), (2, 'm'), (0, 'm'), ('tok', 1), (8, 's'), (2, 'r0'), (1, 'f'), (6, 's'), ('pass',),
        (0, 'f'), (2, 'r1'), (3, 's'), (4, 's'), (7, 'f'), (1, 'g'), ('maps',), ('norm', 1), ('red', 0),
        (5, 's'), ('tokfwd', 0), (10, 's'), (6, 'm'), ('red', 1), (0, 'g'), ('tokfwd', 1), (7, 'm'),
        (9, 's'), (3, 'm'), (2, 'r2'), ('norm', 2), ('norm', 3), (6, 'f'), ('red', 2), ('red', 3), ('wq',),
        (4, 'm'), ('qkv', 0, 0, 2), ('qkv', 0, 2, 4), ('qkv', 0, 4, 6), ('qkv', 1, 0, 2), ('qkv', 1, 2, 4),
        ('qkv', 1, 4, 6), (5, 'm'), (3, 'f'), ('qkv', 2, 2, 4), ('qkv', 2, 4, 6), ('qkv', 3, 2, 4),
        ('qkv', 3, 4, 6), ('keep',), ('att', 0, 0), ('att', 0, 1), ('att', 1, 0), (5, 'f'), (10, 'm'),
        ('att', 1, 1), ('att', 2, 0), (4, 'f'), ('att', 2, 1), (9, 'm'), ('att', 3, 0), (3, 'g'),
        ('att', 3, 1), ('swap',), (7, 'r0'), (10, 'f'), (8, 'm'), (6, 'g'), (5, 'g'), (4, 'g'), ('proj',),
        ('norm2',), (9, 'f'), ('fc1', 0), ('fc1', 1), ('fc1', 2), ('fc1', 3), (8, 'f'), ('fc1', 4),
        (7, 'r1'), (9, 'g'), ('fc1', 5), (10, 'g'), ('fc1', 6), ('fc1', 7), (8, 'g'), ('fc2', 2), ('fc2', 1),
        (7, 'r2'), ('fc2', 3), ('fc2', 0), ('end',),
    ),
)
NSEM = (136, 23)


def gelu_parts(h):
    bell = jnp.exp(-0.5 * h * h)
    t = 1.0 / (1.0 + (0.3275911 * 0.5**0.5) * jnp.abs(h))
    poly = 1.061405429 * t - 1.453152027
    for co in (1.421413741, -0.284496736, 0.254829592):
        poly = poly * t + co
    tail = 0.5 * poly * t * bell
    cdf = jnp.where(h < 0.0, tail, 1.0 - tail)
    return h * cdf, cdf + h * bell * 0.3989422804014327


def row_table():
    half = 10
    freq = 10000.0 ** (-np.arange(half) / half)
    ang = np.arange(16)[:, None] * freq
    whole = np.zeros((48, 256))
    for p in range(3):
        rows = slice(16 * p, 16 * p + 16)
        for head in range(2):
            at = head * HD + p * 2 * half
            whole[rows, at : at + half] = np.cos(ang)
            whole[rows, at + half : at + 2 * half] = np.cos(ang)
            whole[rows, 128 + at : 128 + at + half] = -np.sin(ang)
            whole[rows, 128 + at + half : 128 + at + 2 * half] = np.sin(ang)
    for head in range(2):
        whole[:16, head * HD + 60 : head * HD + HD] = 1.0
    whole = whole.astype(np.float32)
    pieces = []
    for _ in range(3):
        piece = whole.astype(BF)
        pieces.append(np.asarray(piece))
        whole = whole - piece.astype(np.float32)
    return np.stack(pieces)


def turns(places, table):
    level = lax.broadcasted_iota(jnp.int32, (16, places.shape[1]), 0).astype(F32)
    hot = jnp.concatenate([(level == places[p : p + 1]).astype(F32) for p in range(3)], axis=0)
    hot = hot.astype(BF)
    return mm_tn(hot, table[0]) + mm_tn(hot, table[1]) + mm_tn(hot, table[2])


def unshuffle():
    i = lax.broadcasted_iota(jnp.int32, (128, 128), 0)
    j = lax.broadcasted_iota(jnp.int32, (128, 128), 1)
    k, dp, r = i // 16, lax.rem(i, 16) // 2, lax.rem(i, 2)
    return (j == dp * 16 + r * 8 + k).astype(F32).astype(BF)


def front_kernel(nz, cfg, *refs):
    (tok, cot, qkv, proj, fc1, fc2, vectors, bias, places, index, ad_d, ad_u, table) = refs[:13]
    (out, gres, do_o, q_o, k_o, v_o, o_o, lse_o, n1_o, red_o, wq_o, dn, up, pall, idxs,
     gap, gbp, ga1, gb1, ga2, gb2, vf) = refs[13:35]
    (buf4, wq, wp, w1, w2, q, kv, att, accs, res, n2s,
     vall, selb, adall, small, tab, du, adr, ssem, rsem, lsem) = refs[35:]
    (r_p_s, r_1_s, g_r2_s, r_2_s, g_r1_s) = [small.at[i] for i in range(5)]
    k = Links(ssem, rsem, lsem, nz)
    c, d, s = k.c, k.d, k.s
    ndp = 2 * nz
    slope, o, gatt, gn2 = kv, q, att, gres
    seqs = [k.core, k.xn, k.diag]
    dps = [(lax.rem(d + j, ndp), s) for j in range(1, ndp)]
    meet = k.greet(seqs + dps)
    late = []

    def push(src, dst, land, dev):
        i = k.new()
        cp = k.remote(i, src, dst, dev)
        cp.start()
        late.append(cp.wait_send)
        return k.remote(i, src, land, dev).wait_recv

    def send_later(src, dst, land, dev):
        i = k.new()
        cp = k.remote(i, src, dst, dev)

        def start():
            cp.start()
            late.append(cp.wait_send)

        return start, k.remote(i, src, land, dev).wait_recv

    def keep(src, dst):
        i = k.newl()
        cp = k.local(i, src, dst)
        cp.start()
        return cp.wait

    placed = [
        keep(qkv.at[:, pl.ds(256 * b, 256)], wq.at[k.x, (0, 2, 1)[b], k.z, k.y]) for b in range(3)
    ]
    own_tok = keep(tok, buf4.at[0])
    idxs[d] = jnp.broadcast_to(index[...].astype(F32), (8, 128))
    vall[s] = jnp.zeros_like(vall[0])
    vall[s, 0:9, :] = vectors[...].astype(F32)
    for r in range(8):
        half = (r % 2) * 128
        vall[s, 9 + r // 2 : 10 + r // 2, half : half + 128] = bias[r : r + 1, :].astype(F32)
    pall[0] = jnp.zeros_like(pall[0])
    for p in range(3):
        pall[0, p : p + 1, :] = places[p].astype(F32)
    for r in range(2):
        n = ad_d.shape[2]
        adr[:, r * 4096 : r * 4096 + n] = ad_d[...].astype(F32)[:, r, :].astype(BF)
        adr[:, r * 4096 + n : r * 4096 + 4096] = ad_u[...].astype(F32)[:, r, :].astype(BF)
    for w in placed:
        w()
    meet()
    wait_idx = [
        push(idxs.at[d], idxs.at[d], idxs.at[lax.rem(d + ndp - j, ndp)], dps[j - 1])
        for j in range(1, ndp)
    ]
    seq_of = [s + 1 - 2 * c, s + 2 - 4 * k.x, 3 - s]
    wait_vec = [push(vall.at[s], vall.at[s], vall.at[seq_of[r]], seqs[r]) for r in range(3)]
    wait_pos = [push(pall.at[0], pall.at[r + 1], pall.at[r + 1], seqs[r]) for r in range(3)]
    tok_core = push(tok, buf4.at[1], buf4.at[1], k.core)
    halves = [pl.ds(0, 256), pl.ds(256, 256)]
    tok_x = [send_later(tok.at[h], buf4.at[2, h], buf4.at[2, h], k.xn) for h in halves]
    tok_on = [k.remote(k.new(), buf4.at[2, h], buf4.at[3, h], k.core) for h in halves]
    cuts, order = cfg
    parts = (
        qkv_parts(k, wq, cuts[0])
        + wide_parts(k, proj, wp, cuts[1])
        + wide_parts(k, fc1, w1, cuts[2])
        + wide_parts(k, fc2, w2, cuts[3])
    )
    groups = []
    n = 0
    for cs in cuts:
        groups.append(parts[n : n + len(cs)])
        n += len(cs)
    state = {}

    def a_tok(h):
        tok_x[h][0]()

    def a_tokfwd(h):
        tok_x[h][1]()
        tok_on[h].start()

    def a_pick():
        for w in wait_idx:
            w()
        spots = lax.broadcasted_iota(jnp.int32, (1, NA), 1).astype(F32)
        hot = [(idxs[lax.rem(d + j, ndp)][0:1, :NA] == spots).astype(F32) for j in range(ndp)]
        sel = mm(jnp.concatenate(hot, axis=0).astype(BF), adr[...]).astype(BF)
        stack = jnp.concatenate([sel[:, p * 512 : p * 512 + 512] for p in range(16)], axis=0)
        r = lax.broadcasted_iota(jnp.int32, (128, 128), 0)
        q_ = lax.broadcasted_iota(jnp.int32, (128, 128), 1)
        swap = (q_ == lax.rem(r, 16) * 8 + r // 16).astype(F32).astype(BF)
        selb[...] = mm(swap, stack).astype(BF).reshape(ndp, 16, 512)
        adall[s, d] = selb[0]
        state["ad"] = [
            push(selb.at[j], adall.at[s, d], adall.at[s, lax.rem(d + ndp - j, ndp)], dps[j - 1])
            for j in range(1, ndp)
        ]

    def a_pass():
        for w in state["ad"]:
            w()
        state["ad4"] = [
            push(adall.at[s], adall.at[s], adall.at[seq_of[r]], seqs[r]) for r in range(3)
        ]

    def a_maps():
        for w in state["ad4"]:
            w()
        shuffle = unshuffle()
        for t in range(4):
            rows = mm(shuffle, adall[t].reshape(128, 512)).astype(BF)
            for b in range(8):
                piece = rows[16 * b : 16 * b + 16]
                at = b * 512
                nd = dn.shape[1] // 4
                nu = up.shape[1] // 4
                cut = min(max(nd - at, 0), 512)
                if cut:
                    dn[:, t * nd + at : t * nd + at + cut] = piece[:, :cut]
                if cut < 512:
                    b0 = t * nu + at + cut - nd
                    up[:, b0 : b0 + 512 - cut] = piece[:, cut:]
        for j in range(4):
            for i in range(8):
                at = i * 512 + j * 128
                du[0, j, :, i * 128 : i * 128 + 128] = dn[:, 3 * D + at : 3 * D + at + 128]
                du[1, j, :, i * 128 : i * 128 + 128] = up[:, 4 * D + at : 4 * D + at + 128]
        g_r2_s[...] = mm_nt(cot[...], up[:, 4 * D + FF :]).astype(BF)

    def a_vec():
        for w in wait_vec:
            w()
        for t in range(4):
            vf[:, t * 256 : t * 256 + 256] = vall[t]

    def a_norm(slot):
        if slot < 2:
            (own_tok, tok_core)[slot]()
        else:
            for cp in tok_on:
                cp.wait_send() if slot == 2 else cp.wait_recv()
        if slot == 0:
            for w in wait_pos:
                w()
        xhat, _ = norm_parts(buf4[slot].astype(F32))
        buf4[slot] = (xhat * vf[0:1, :] + vf[1:2, :]).astype(BF)

    def a_wq():
        for p in groups[0]:
            p.arrive()
        late.append(keep(wq, wq_o))

    def role_cols(role):
        return pl.ds(pl.multiple_of((4 * (role // 2) + 2 * (role % 2) + c) * 256, 256), 256)

    def role_bias(role):
        lg = pl.multiple_of((2 * (role % 2) + c) * 256, 256)
        return vf[4 + role // 2 : 5 + role // 2, pl.ds(lg, 256)]

    def a_red(slot):
        red_o[slot] = mm_nt(buf4[slot], dn[:, :D]).astype(BF)

    def a_qkv(slot, first, last):
        if first < 4:
            if state.get("tab") != slot:
                tab[...] = turns(pall[slot], table)
                state["tab"] = slot
            cos, sin = tab[:, :128], tab[:, 128:]
        h, low = buf4[slot], red_o[slot]
        rows = pl.ds(slot * 512, 512)
        for role in range(first, last):
            val = mm(h, wq[role_slot(role, c)].reshape(D, 256)) + role_bias(role) + mm(low, up[:, role_cols(role)])
            cols = pl.ds((role % 2) * 256, 256)
            if role < 2:
                q[rows, cols] = (turn(val, cos, sin) * (LOG2E * HD**-0.5)).astype(BF)
            elif role < 4:
                kv[slot, :, (role % 2) * 256 : (role % 2) * 256 + 256] = turn(val, cos, sin).astype(BF)
            else:
                kv[slot, :, 512 + (role % 2) * 256 : 768 + (role % 2) * 256] = val.astype(BF)

    def a_keep():
        state["n1"] = keep(buf4, n1_o)
        state["q"] = keep(q, q_o)
        state["kv"] = [keep(kv.at[:, :, pl.ds(512 * i, 512)], (k_o, v_o)[i]) for i in range(2)]

    def a_att(pair, qb):
        if "q" in state:
            state.pop("q")()
        lane_i = lax.broadcasted_iota(jnp.int32, (1, 128), 1)
        cols = pl.ds(pair * 128, 128)
        rows = pl.ds(qb * 512, 512)
        qs = q[rows, cols]
        qm = [jnp.where((lane_i < 64) == (e == 0), qs, jnp.zeros_like(qs)) for e in range(2)]
        ks = [kv[2 * b : 2 * b + 2, :, cols].reshape(-1, 128) for b in range(2)]
        vcols = pl.ds(512 + pair * 128, 128)
        vt = [kv[2 * b : 2 * b + 2, :, vcols].reshape(-1, 128).T for b in range(2)]
        steps = [(b, e) for b in range(2) for e in range(2)]
        top, total, acc = [None] * 2, [None] * 2, [None] * 2
        ahead = mm_nt(ks[0], qm[0])
        for n, (b, e) in enumerate(steps):
            st = ahead
            if n < 3:
                ahead = mm_nt(ks[steps[n + 1][0]], qm[steps[n + 1][1]])
            new = jnp.max(st, axis=0, keepdims=True)
            v_ = vt[b][64 * e : 64 * e + 64]
            if b == 0:
                pr = jnp.exp2(st - new)
                total[e] = jnp.sum(pr, axis=0, keepdims=True)
                acc[e] = mm(v_, pr.astype(BF))
            else:
                new = jnp.maximum(new, top[e])
                fall = jnp.exp2(top[e] - new)
                pr = jnp.exp2(st - new)
                total[e] = total[e] * fall + jnp.sum(pr, axis=0, keepdims=True)
                acc[e] = acc[e] * fall + mm(v_, pr.astype(BF))
            top[e] = new
        for e in range(2):
            lse_o[pair, e : e + 1, pl.ds(qb * 512, 512)] = top[e] + jnp.log2(total[e])
        o[rows, cols] = jnp.concatenate([acc[e] / total[e] for e in range(2)], axis=0).T.astype(BF)

    def a_swap():
        late.append(keep(o, o_o))
        state["att"] = []
        for lg in range(2):
            cols = pl.ds(lg * 256, 256)
            here, there = group(2 * lg + c), group(2 * lg + 1 - c)
            state["att"].append(keep(o.at[pl.ds(0, 512), cols], att.at[:, here]))
            state["att"].append(
                push(o.at[pl.ds(512, 512), cols], att.at[:, here], att.at[:, there], k.core)
            )

    def group(g):
        return pl.ds(pl.multiple_of(g * 256, 256), 256)

    def a_proj():
        for w in state["att"] + state["kv"]:
            w()
        own = keep(tok, n2s)
        own()
        for p in groups[1]:
            p.arrive()
        low = mm_nt(att[...], dn[:, D : 2 * D]).astype(BF)
        r_p_s[...] = low
        for t in range(4):
            cols = pl.ds(t * 256, 256)
            val = mm(low, up[:, 3 * D + t * 256 : 3 * D + t * 256 + 256]) + vf[7:8, cols]
            val += mm(att[...], wp[t // 2, t % 2].reshape(D, 256))
            res[:, cols] = n2s[:, cols].astype(F32) + val

    def a_norm2():
        xhat, _ = norm_parts(res[...])
        n2 = (xhat * vf[2:3, :] + vf[3:4, :]).astype(BF)
        n2s[...] = n2
        r_1_s[...] = mm_nt(n2, dn[:, 2 * D : 3 * D]).astype(BF)
        state["n1"]()

    def a_fc1(i):
        if i == 0:
            for p in groups[2]:
                p.arrive()
        t, h = i // 2, i % 2
        w = w1[t // 2, t % 2, :, :, :, h * 512 : h * 512 + 512].reshape(D, 512)
        bias = jnp.concatenate(
            [vf[9 + 2 * h + b : 10 + 2 * h + b, t * 256 : t * 256 + 256] for b in range(2)], axis=1
        )
        hid = mm(n2s[...], w) + bias
        hid += mm(r_1_s[...], up[:, 4 * D + i * 512 : 4 * D + i * 512 + 512])
        a, sl = gelu_parts(hid)
        a = a.astype(BF)
        for j in range(4):
            buf4[j, :, i * 128 : i * 128 + 128] = a[:, j * 128 : j * 128 + 128]
            slope[j, :, i * 128 : i * 128 + 128] = sl[:, j * 128 : j * 128 + 128].astype(BF)

    def a_fc2(j):
        groups[3][j].arrive()
        a = buf4[j]
        d2 = du[0, j]
        low2 = mm_nt(a, d2)
        w = jnp.concatenate(
            [
                w2[t // 2, t % 2, :, :, j * 128 : j * 128 + 128, :].reshape(1024, 256)
                for t in range(4)
            ],
            axis=1,
        )
        g = mm_nt(cot[...], w) + mm(g_r2_s[...], d2)
        first = "r2" not in state
        accs[...] = mm(a, w) if first else accs[...] + mm(a, w)
        gh = (g * slope[j].astype(F32)).astype(BF)
        w = jnp.concatenate(
            [
                w1[i // 4, (i // 2) % 2, :, :, :, (i % 2) * 512 + j * 128 : (i % 2) * 512 + j * 128 + 128].reshape(D, 128)
                for i in range(8)
            ],
            axis=1,
        )
        gn2[...] = mm_nt(gh, w) if first else gn2[...] + mm_nt(gh, w)
        low1 = mm_nt(gh, du[1, j])
        state["r2"] = low2 if "r2" not in state else state["r2"] + low2
        state["g1"] = low1 if "g1" not in state else state["g1"] + low1
        ga2[j] = mm_tn(g_r2_s[...], a)
        gb1[j] = mm_tn(r_1_s[...], gh)

    def a_end():
        r_2, g_r1 = state["r2"].astype(BF), state["g1"].astype(BF)
        g_n2 = gn2[...] + mm(g_r1, dn[:, 2 * D : 3 * D])
        xhat, inv = norm_parts(res[...])
        g_res = cot[...].astype(F32) + norm_back(g_n2, xhat, inv, vf[2:3, :])
        gres[...] = g_res
        gb = g_res.astype(BF)
        g_rp = mm_nt(gb, up[:, 3 * D : 4 * D]).astype(BF)
        gap[...] = mm_tn(g_rp, att[...])
        w = jnp.concatenate([wp[t // 2, t % 2].reshape(D, 256) for t in range(4)], axis=1)
        gatt[...] = (mm_nt(gb, w) + mm(g_rp, dn[:, D : 2 * D])).astype(BF)
        waits = []
        for lg in range(2):
            cols = pl.ds(lg * 256, 256)
            top, low = pl.ds(0, 512), pl.ds(512, 512)
            waits.append(keep(gatt.at[:, group(2 * lg + c)], do_o.at[top, cols]))
            there = gatt.at[:, group(2 * lg + 1 - c)]
            waits.append(push(there, do_o.at[low, cols], do_o.at[low, cols], k.core))
        u2 = up[:, 4 * D + FF :]
        out[...] = (res[...] + accs[...] + vf[8:9, :] + mm(r_2, u2)).astype(BF)
        gb2[...] = mm_tn(r_2, cot[...])
        ga1[...] = mm_tn(g_r1, n2s[...])
        gbp[...] = mm_tn(r_p_s[...], gb)
        for w in waits:
            w()

    acts = {
        "tok": a_tok, "tokfwd": a_tokfwd, "pick": a_pick, "pass": a_pass, "maps": a_maps, "vec": a_vec,
        "norm": a_norm, "wq": a_wq, "red": a_red, "qkv": a_qkv, "keep": a_keep, "att": a_att,
        "swap": a_swap, "proj": a_proj, "norm2": a_norm2, "fc1": a_fc1, "fc2": a_fc2, "end": a_end,
    }
    for name, *args in order:
        if isinstance(name, int):
            parts[name].step(args[0])
        else:
            acts[name](*args)
    for w in late:
        w()
    for p in parts:
        p.finish()
    assert k.nr <= NSEM[0] and k.nl <= NSEM[1]


def front(nz, cfg, tok, cot, qkv, proj, fc1, fc2, vectors, bias, places, index, ad_d, ad_u):
    anys, vm = pl.BlockSpec(memory_space=pl.ANY), pl.BlockSpec(memory_space=pltpu.VMEM)
    ndp = 2 * nz
    rows = tok.shape[0]
    nd, nu = 3 * D + FF, 5 * D + FF
    outs = [
        (vm, (rows, D), BF), (vm, (rows, D), F32), (anys, (2 * rows, 512), BF),
        (anys, (2 * rows, 512), BF), (anys, (4, rows, 512), BF), (anys, (4, rows, 512), BF),
        (anys, (2 * rows, 512), BF), (vm, (4, 2, 2 * rows), F32), (anys, (4, rows, D), BF),
        (vm, (4, rows, 16), BF), (anys, (2, 4, nz, 2, qkv.shape[0], 256), BF), (vm, (16, nd), BF),
        (vm, (16, nu), BF), (vm, (4, 8, rows), F32), (vm, (ndp, 8, 128), F32),
        (vm, (16, D), F32), (vm, (16, D), F32), (vm, (16, D), F32), (vm, (4, 16, 1024), F32),
        (vm, (4, 16, 1024), F32), (vm, (16, D), F32), (vm, (16, D), F32),
    ]
    scratch = [
        ((4, rows, D), BF), ((2, 4, nz, 2, qkv.shape[0], 256), BF),
        ((2, 2, nz, 2) + proj.shape, BF), ((2, 2, nz, 2) + fc1.shape, BF), ((2, 2, nz, 2) + fc2.shape, BF),
        ((2 * rows, 512), BF), ((4, rows, 1024), BF), ((rows, D), BF), ((rows, D), F32),
        ((rows, D), F32), ((rows, D), BF), ((4, 16, 256), F32),
        ((ndp, 16, 512), BF), ((4, ndp, 16, 512), BF), ((5, rows, 16), BF), ((rows, 256), F32), ((2, 4, 16, 1024), BF), ((NA, 8192), BF),
    ]
    return pl.pallas_call(
        functools.partial(front_kernel, nz, cfg),
        out_shape=[sds(sh, t) for _, sh, t in outs],
        in_specs=[anys, vm, anys, anys, anys, anys] + [vm] * 7,
        out_specs=[m for m, _, _ in outs],
        scratch_shapes=[pltpu.VMEM(sh, t) for sh, t in scratch]
        + [
            pltpu.SemaphoreType.DMA((NSEM[0],)),
            pltpu.SemaphoreType.DMA((NSEM[0],)),
            pltpu.SemaphoreType.DMA((NSEM[1],)),
        ],
        compiler_params=pltpu.CompilerParams(
            collective_id=0, has_side_effects=True, vmem_limit_bytes=VM
        ),
    )(
        tok, cot, qkv, proj, fc1, fc2, vectors, bias, places, index, ad_d, ad_u,
        jnp.asarray(row_table()),
    )


def back_kernel(nz, *refs):
    (q_i, k_i, v_i, o_i, do_i, n1_i, wq_i, tok_i, gres_i, lse, red, dn, up, pall, idxs, vf,
     gap, gbp, ga1, gb1, ga2, gb2, table) = refs[:23]
    ig, gdn, gup = refs[23:26]
    (q, kk, vv, o, do, n1, wcat, tok, gres, acc, dl, dk, dv, gm, upc, gaq, gbq, own, part, gd, gu,
     blk, got, selo, selr, ssem, rsem, lsem) = refs[26:]
    k = Links(ssem, rsem, lsem, nz)
    c, d, s = k.c, k.d, k.s
    ndp = 2 * nz
    rows = tok.shape[0]
    nq = 2 * rows
    seqs = [k.core, k.xn, k.diag]
    seq_of = [s + 1 - 2 * c, s + 2 - 4 * k.x, 3 - s]
    dps = [(lax.rem(d + j, ndp), s) for j in range(1, ndp)]
    late = []

    def keep(src, dst):
        i = k.newl()
        cp = k.local(i, src, dst)
        cp.start()
        return cp.wait

    def push(src, dst, land, dev):
        i = k.new()
        cp = k.remote(i, src, dst, dev)
        cp.start()
        late.append(cp.wait_send)
        return k.remote(i, src, land, dev).wait_recv

    last, rest = pl.ds(3 * rows, rows), pl.ds(0, 3 * rows)
    first = [keep(a, b) for a, b in ((q_i, q), (do_i, do), (o_i, o))]
    first += [keep(a.at[last], b.at[last]) for a, b in ((k_i, kk), (v_i, vv))]
    meet = k.greet(seqs + dps)
    for w in first:
        w()
    later = [keep(a.at[rest], b.at[rest]) for a, b in ((k_i, kk), (v_i, vv))]
    later += [keep(wq_i.at[role_slot(r, c)], wcat.at[:, pl.ds(256 * r, 256)]) for r in range(6)]
    later += [keep(a, b) for a, b in ((n1_i, n1), (tok_i, tok), (gres_i, gres))]
    lane = lax.broadcasted_iota(jnp.int32, (1, 128), 1)

    def attend_back(pair, half, at, size):
        cols = pl.ds(pair * 128, 128)
        krows, outs = pl.ds(half * nq + at, size), pl.ds(at, size)
        begin = half == 1 and at > 0
        qs, dos, ks, vs = q[:, cols], do[:, cols], kk[krows, cols], vv[krows, cols]
        if begin:
            r8 = lax.broadcasted_iota(jnp.int32, (8, 128), 0)
            l8 = lax.broadcasted_iota(jnp.int32, (8, 128), 1) // 64
            dl[pair] = lax.dot_general(
                (r8 == l8).astype(F32),
                dos.astype(F32) * o[:, cols].astype(F32),
                (((1,), (1,)), ((), ())),
                precision=lax.Precision.HIGHEST,
                preferred_element_type=F32,
            )
        dks, dvs, dqs = [], [], []
        for e in range(2):
            mine = (lane < 64) if e == 0 else (lane >= 64)
            st = mm_nt(jnp.where(mine, ks, jnp.zeros_like(ks)), qs)
            pr = jnp.exp2(st - lse[pair, e : e + 1, :])
            dp = mm_nt(jnp.where(mine, vs, jnp.zeros_like(vs)), dos)
            ds = (pr * (dp - dl[pair, e : e + 1, :])).astype(BF)
            dvs.append(mm(pr.astype(BF), dos))
            dks.append(mm(ds, qs))
            dqs.append(mm(ks.T[64 * e : 64 * e + 64], ds))
        dk[outs, cols] = jnp.where(lane < 64, dks[0], dks[1]) * LN2
        dv[outs, cols] = jnp.where(lane < 64, dvs[0], dvs[1])
        dq = jnp.concatenate(dqs, axis=0)
        frows = pl.ds(pair * 128, 128)
        if begin:
            acc[frows, :] = dq
        else:
            acc[frows, :] += dq

    def mixed(slot):
        tab = turns(pall[slot], table)
        cos, sin = tab[:, :128], -tab[:, 128:]
        at = pl.ds((slot % 2) * rows, rows)
        f = 0 if slot < 2 else 512
        for role in range(0 if slot < 2 else 2, 6):
            cols = pl.ds((role % 2) * 256, 256)
            if role < 2:
                g = acc[cols, at].T * (HD**-0.5)
                g = turn(g, cos, sin)
            elif role < 4:
                g = turn(dk[at, cols], cos, sin)
            else:
                g = dv[at, cols]
            gm[at, role * 256 : role * 256 + 256] = g.astype(BF)
        g = gm[at, f:]
        low = mm_nt(g, upc[:, f:]).astype(BF)
        ta, tb = mm_tn(low, n1[slot]), mm_tn(red[slot], g)
        if slot == 3:
            gaq[...] = ta
            gbq[:, :512] = jnp.zeros((16, 512), F32)
            gbq[:, f:] = tb
        else:
            gaq[...] += ta
            gbq[:, f:] += tb
        return low

    def into_h(slot, low):
        at = pl.ds((slot % 2) * rows, rows)
        f = 0 if slot < 2 else 512
        return mm_nt(gm[at, f:], wcat[:, f:]) + mm(low, dn[:, :D])

    for pair in range(4):
        attend_back(pair, 1, rows, rows)
    for w in later:
        w()
    for role in range(6):
        at = pl.multiple_of((4 * (role // 2) + 2 * (role % 2) + c) * 256, 256)
        upc[:, role * 256 : role * 256 + 256] = up[:, pl.ds(at, 256)]
    part[0] = into_h(3, mixed(3)).astype(BF)
    meet()
    from_core = push(part.at[0], part.at[1], part.at[1], k.core)
    for pair in range(4):
        attend_back(pair, 1, 0, rows)
    own[...] = into_h(2, mixed(2))
    from_core()
    part[2] = (own[...] + part[1].astype(F32)).astype(BF)
    from_x = push(part.at[2], part.at[3], part.at[3], k.xn)
    gd[:, D : 2 * D] = gap[...]
    gd[:, 2 * D : 3 * D] = ga1[...]
    gu[:, : 3 * D] = jnp.zeros((16, 3 * D), F32)
    gu[:, 3 * D : 4 * D] = gbp[...]
    gu[:, 4 * D + FF :] = gb2[...]
    for j in range(4):
        for i in range(8):
            at = i * 512 + j * 128
            gd[:, 3 * D + at : 3 * D + at + 128] = ga2[j, :, i * 128 : i * 128 + 128]
            gu[:, 4 * D + at : 4 * D + at + 128] = gb1[j, :, i * 128 : i * 128 + 128]
    for pair in range(4):
        attend_back(pair, 0, 0, nq)
    low1 = mixed(1)
    low0 = mixed(0)
    gd[:, :D] = gaq[...]
    for role in range(6):
        at = pl.multiple_of((4 * (role // 2) + 2 * (role % 2) + c) * 256, 256)
        gu[:, pl.ds(at, 256)] = gbq[:, role * 256 : role * 256 + 256]
    nd, nu = gd.shape[1] // 4, gu.shape[1] // 4
    for t in range(4):
        blk[t, :, :nd] = gd[:, t * nd : t * nd + nd].astype(BF)
        blk[t, :, nd:] = gu[:, t * nu : t * nu + nu].astype(BF)
    sums = [push(blk.at[seq_of[r]], got.at[r], got.at[r], seqs[r]) for r in range(3)]
    part[4] = into_h(1, low1).astype(BF)
    from_core = push(part.at[4], part.at[5], part.at[5], k.core)
    own[...] = into_h(0, low0)
    xhat, inv = norm_parts(tok[...].astype(F32))
    for w in sums:
        w()
    total = blk[s].astype(F32)
    for r in range(3):
        total += got[r].astype(F32)
    total = total.astype(BF)
    stack = jnp.concatenate([total[:, b * 512 : b * 512 + 512] for b in range(8)], axis=0)
    selo[...] = mm_tn(unshuffle(), stack).astype(BF).reshape(ndp, 16, 512)
    selr[d] = selo[d]
    ends = [
        push(selo.at[lax.rem(d + j, ndp)], selr.at[d], selr.at[lax.rem(d + ndp - j, ndp)], dps[j - 1])
        for j in range(1, ndp)
    ]
    from_core()
    from_x()
    g_n1 = own[...] + part[5].astype(F32) + part[3].astype(F32)
    ig[...] = (gres[...] + norm_back(g_n1, xhat, inv, vf[0:1, :])).astype(BF)
    for w in ends:
        w()
    for a in range(NA):
        out = jnp.zeros((16, 512), F32)
        for j in range(ndp):
            out += jnp.where(idxs[j][0:1, 0:1] == float(a), selr[j].astype(F32), 0.0)
        for r in range(2):
            row = jnp.concatenate([out[8 * r + b : 8 * r + b + 1] for b in range(8)], axis=1)
            gdn[a, r : r + 1, :] = row[:, :nd]
            gup[a, r : r + 1, :] = row[:, nd:]
    for w in late:
        w()
    assert k.nr <= 16 and k.nl <= 18


def back(nz, *args):
    anys, vm = pl.BlockSpec(memory_space=pl.ANY), pl.BlockSpec(memory_space=pltpu.VMEM)
    rows = args[7].shape[0]
    nq = 2 * rows
    ndp = 2 * nz
    scratch = [
        ((nq, 512), BF), ((2 * nq, 512), BF), ((2 * nq, 512), BF), ((nq, 512), BF), ((nq, 512), BF),
        ((4, rows, D), BF), ((D, 1536), BF), ((rows, D), BF), ((rows, D), F32),
        ((512, nq), F32), ((4, 8, nq), F32), ((nq, 512), F32), ((nq, 512), F32),
        ((nq, 1536), BF), ((16, 1536), BF), ((16, D), F32), ((16, 1536), F32), ((rows, D), F32),
        ((6, rows, D), BF), ((16, 3 * D + FF), F32), ((16, 5 * D + FF), F32),
        ((4, 16, 4096), BF), ((3, 16, 4096), BF), ((ndp, 16, 512), BF), ((ndp, 16, 512), BF),
    ]
    return pl.pallas_call(
        functools.partial(back_kernel, nz),
        out_shape=[
            sds((rows, D), BF), sds((NA, 2, (3 * D + FF) // 4), F32), sds((NA, 2, (5 * D + FF) // 4), F32)
        ],
        in_specs=[anys] * 9 + [vm] * (len(args) - 8),
        out_specs=[vm, vm, vm],
        scratch_shapes=[pltpu.VMEM(sh, t) for sh, t in scratch]
        + [
            pltpu.SemaphoreType.DMA((16,)),
            pltpu.SemaphoreType.DMA((16,)),
            pltpu.SemaphoreType.DMA((18,)),
        ],
        compiler_params=pltpu.CompilerParams(
            collective_id=1, has_side_effects=True, vmem_limit_bytes=VM
        ),
    )(*args, jnp.asarray(row_table()))


def fast_shards(
    nz, tokens, positions, adapter_index, qkv_weight, proj_weight, fc1_weight, fc2_weight,
    vectors, fc1_bias, adapter_down, adapter_up, cotangent,
):
    (output, gres, do, q, k, v, o, lse, n1, red, wq, dn, up, pall, idxs,
     gap, gbp, ga1, gb1, ga2, gb2, vf) = front(
        nz, PLAN, tokens[0], cotangent[0], qkv_weight, proj_weight, fc1_weight, fc2_weight,
        vectors, fc1_bias.reshape(8, 128), positions, adapter_index, adapter_down, adapter_up,
    )
    input_grad, down_grad, up_grad = back(
        nz, q, k.reshape(-1, 512), v.reshape(-1, 512), o, do, n1, wq.reshape(2, 4, D, 256), tokens[0],
        gres, lse, red, dn, up, pall, idxs, vf, gap, gbp, ga1, gb1, ga2, gb2,
    )
    return output[None], input_grad[None], down_grad, up_grad


def solution(mesh):
    in_specs = (
        P("dp", "seq", None),
        P(None, "dp", "seq"),
        P("dp", None),
        P("dp", "seq"),
        P("dp", "seq"),
        P("dp", "seq"),
        P("dp", "seq"),
        P(None, "seq"),
        P("seq"),
        P(None, "dp", "seq"),
        P(None, "dp", "seq"),
        P("dp", "seq", None),
    )
    out_specs = (
        P("dp", "seq", None),
        P("dp", "seq", None),
        P(None, "dp", "seq"),
        P(None, "dp", "seq"),
    )
    body = shards
    if mesh.shape["seq"] == 4 and mesh.shape["dp"] == 8:

        def body(tokens, *rest):
            if tokens.shape[0] == 1 and tokens.shape[1] == 512:
                return fast_shards(mesh.shape["dp"] // 2, tokens, *rest)
            return shards(tokens, *rest)

    return jax.shard_map(body, mesh=mesh, in_specs=in_specs, out_specs=out_specs, check_vma=False)
```
